32 devices in a mesh: seq: 4 (over x, core), wshard: 8 (over z, y).
Axes of the slice: x: 2, y: 2, z: 4, core: 2. Of those that a mesh axis runs over, the one named last changes fastest.
Arguments:
- block_in: bfloat16 [8, 1024, 1024], P('wshard', 'seq'), may hold values from -6 to 6
- cotangent: bfloat16 [8, 1024, 1024], P('wshard', 'seq'), may hold values from -6 to 6
- in_weight: float32 [1024, 4384], P('wshard'), may hold values from -0.1875 to 0.1875
- in_first: float32 [1024, 4384], P('wshard'), may hold values from -32 to 32
- in_second: float32 [1024, 4384], P('wshard'), may hold values from 106.496 to 434.176
- out_weight: float32 [2048, 1024], P('wshard'), may hold values from -0.125 to 0.125
- out_first: float32 [2048, 1024], P('wshard'), may hold values from -64 to 64
- out_second: float32 [2048, 1024], P('wshard'), may hold values from 434.176 to 1720.32
- vec_weight: float32 [14688], replicated, may hold values from -7 to 3, as said below
- vec_first: float32 [14688], replicated, may hold values from -325.8348 to 325.8348, as said below
- vec_second: float32 [14688], replicated, may hold values from 32.768 to 114688, as said below
Outputs:
- block_out: float32 [8, 1024, 1024], P('wshard', 'seq')
- block_in_grad: float32 [8, 1024, 1024], P('wshard', 'seq')
- in_first_new: float32 [1024, 4384], P('wshard')
- in_second_new: float32 [1024, 4384], P('wshard')
- in_weight_new: float32 [1024, 4384], P('wshard')
- out_first_new: float32 [2048, 1024], P('wshard')
- out_second_new: float32 [2048, 1024], P('wshard')
- out_weight_new: float32 [2048, 1024], P('wshard')
- vec_first_new: float32 [14688], replicated
- vec_second_new: float32 [14688], replicated
- vec_weight_new: float32 [14688], replicated
The draws below stay inside these ranges and needn't reach their ends.
Inputs may be any that keep to these rules, and one draw needn't show every extreme that they name: `vec_weight`: gains near one, a_log the logarithm of a positive rate, dt_bias an inverse softplus of a small step. `vec_first`: both signs. `vec_second`: entries are positive.
All inputs are finite; a program needn't handle non-finite values.
Results may differ from the reference program's by a relative error of at most 0.018.
Values may be sent and summed in bfloat16 or wider, within the bound.
No kernel may reach another device: no remote copies, remote signals or barrier semaphores. Data moves between devices by JAX's collectives and lax.ppermute only.
A program may use at most 192 MiB of HBM per device.

```python
import math
import jax
import jax.numpy as jnp
from jax import lax

D = 1024
HEADS = 32
HEADDIM = 64
STATE = 128
WIDTH = 4
BLOCK = 256
STEP = 10
DI = 2048
CONVCH = 2304
PROJ = 4384
VEC = 14688
L = 1024
SEQS = 8
TOKENS = 8192


def segment_scale():
    pieces = [jnp.full((D,), 0.5, jnp.float32), jnp.full((DI,), 1.0, jnp.float32), jnp.full((WIDTH * CONVCH,), 0.5, jnp.float32), jnp.full((CONVCH,), 0.5, jnp.float32), jnp.full((HEADS,), 1.0, jnp.float32), jnp.full((HEADS,), 0.3, jnp.float32), jnp.full((HEADS,), 8.0, jnp.float32)]
    return jnp.concatenate(pieces)


def draw_vec_weight(key, part):
    key = jax.random.fold_in(key, 11)
    keys = jax.random.split(key, 7)
    gain_one = 1.0 + 0.2 * jax.random.uniform(keys[0], (D,), jnp.float32, -1.0, 1.0)
    gain_two = 1.0 + 0.2 * jax.random.uniform(keys[1], (DI,), jnp.float32, -1.0, 1.0)
    kernel = 0.5 * jax.random.truncated_normal(keys[2], -4.0, 4.0, (WIDTH * CONVCH,), jnp.float32)
    conv_bias = 0.2 * jax.random.truncated_normal(keys[3], -4.0, 4.0, (CONVCH,), jnp.float32)
    a_log = jnp.log(jax.random.uniform(keys[4], (HEADS,), jnp.float32, 1.0, 16.0))
    step_size = jnp.exp(jax.random.uniform(keys[5], (HEADS,), jnp.float32, jnp.log(0.001), jnp.log(0.1)))
    dt_bias = step_size + jnp.log(-jnp.expm1(-step_size))
    d_skip = jax.random.uniform(keys[6], (HEADS,), jnp.float32, 0.5, 1.5)
    return jnp.concatenate([gain_one, gain_two, kernel, conv_bias, a_log, dt_bias, d_skip])


def draw_vec_first(key, part):
    key = jax.random.fold_in(key, 23)
    normal = jax.random.truncated_normal(key, -4.0, 4.0, (VEC,), jnp.float32)
    return normal * 0.11 * segment_scale() * jnp.sqrt(jnp.float32(TOKENS))


def draw_vec_second(key, part):
    key = jax.random.fold_in(key, 37)
    factor = jnp.exp(jax.random.uniform(key, (VEC,), jnp.float32, 0.0, jnp.log(4.0)))
    scale = segment_scale()
    return factor * 0.053 * scale * scale * jnp.float32(TOKENS)


def block_levels(stream_key, shape, cuts, smallest, high):
    factor_of = 1.0
    for position, shards_of in cuts:
        draws = jax.random.uniform(jax.random.fold_in(jax.random.fold_in(stream_key, 6), position), (shards_of,), jnp.float32, smallest / len(cuts), high / len(cuts))
        factor_of = factor_of * jnp.repeat(jnp.exp(draws), shape[position] // shards_of).reshape((-1,) + (1,) * (len(shape) - 1 - position))
    return factor_of


def scatter_about(stream_key, dims, spread, most, cuts=(), dtype=jnp.bfloat16):
    result = jax.random.normal(stream_key, dims, jnp.float32) * spread
    if len(cuts) > 0:
        result = block_levels(stream_key, dims, cuts, -0.22, 0.18) * result
    return jnp.clip(result, min=-most, max=most).astype(dtype)


def setup_inputs(seed: int = 0) -> dict:
    key_list = jax.random.split(jax.random.key(seed), 12)
    block_in = scatter_about(key_list[0], (SEQS, L, D), 1.0, 6.0, ((0, 8), (1, 4)))
    cotangent = scatter_about(key_list[1], (SEQS, L, D), 1.0, 6.0, ((0, 8), (1, 4)))
    in_weight = scatter_about(key_list[2], (D, PROJ), D ** -0.5, 0.1875, ((0, 8),), jnp.float32)
    in_first = scatter_about(key_list[3], (D, PROJ), (0.055 * TOKENS ** 0.5), 32.0, ((0, 8),), jnp.float32)
    in_second = jnp.clip(jnp.exp(math.log(434.176) - 1.40534252 * jax.random.uniform(key_list[4], (D, PROJ), jnp.float32) ** block_levels(key_list[4], (D, PROJ), ((0, 8),), -0.2, 0.2)), 106.496, 434.176)
    out_weight = scatter_about(key_list[5], (DI, D), DI ** -0.5, 0.125, ((0, 8),), jnp.float32)
    out_first = scatter_about(key_list[6], (DI, D), (0.11 * TOKENS ** 0.5), 64.0, ((0, 8),), jnp.float32)
    out_second = jnp.clip(jnp.exp(math.log(1720.32) - 1.3768156 * jax.random.uniform(key_list[7], (DI, D), jnp.float32) ** block_levels(key_list[7], (DI, D), ((0, 8),), -0.2, 0.2)), 434.176, 1720.32)
    vec_weight = draw_vec_weight(jax.random.fold_in(key_list[11], 71), 0)
    vec_first = draw_vec_first(jax.random.fold_in(key_list[11], 71), 0)
    vec_second = draw_vec_second(jax.random.fold_in(key_list[11], 71), 0)
    return dict(block_in=block_in, cotangent=cotangent, in_weight=in_weight, in_first=in_first, in_second=in_second, out_weight=out_weight, out_first=out_first, out_second=out_second, vec_weight=vec_weight, vec_first=vec_first, vec_second=vec_second)


@jax.custom_vjp
def low(v):
    return lax.optimization_barrier(v.astype(jnp.bfloat16)).astype(jnp.float32)

@jax.custom_vjp
def low_back(v):
    return v

def low_keep(v):
    return (low(v), None)

def low_pass(kept, grad):
    return (grad,)

def back_keep(v):
    return (v, None)

def back_low(kept, grad):
    return (low(grad),)
low.defvjp(low_keep, low_pass)
low_back.defvjp(back_keep, back_low)
precise = lax.Precision.HIGHEST
norm_eps = 1e-05
beta_one = 0.9
beta_two = 0.95
adam_eps = 1e-08
matrix_rate = 0.05
matrix_decay = 0.1
vector_rate = 0.5

def rms_scale(values):
    return values * lax.rsqrt(lax.optimization_barrier(jnp.mean(values * values, axis=-1, keepdims=True)) + norm_eps)

def split_vector(vector):
    extents = [D, DI, WIDTH * CONVCH, CONVCH, HEADS, HEADS, HEADS]
    pieces = []
    offset = 0
    for extent in extents:
        pieces.append(vector[offset:offset + extent])
        offset = offset + extent
    pieces[2] = pieces[2].reshape(WIDTH, CONVCH)
    return pieces

def convolve(extended, kernel, conv_bias):
    rows_out = extended.shape[0] - kernel.shape[0] + 1
    summed = jnp.broadcast_to(conv_bias[None, :], (rows_out, kernel.shape[1]))
    for offset in range(kernel.shape[0]):
        summed = summed + kernel[offset][None, :] * extended[offset:offset + rows_out]
    return jax.nn.silu(summed)

def state_scan(inputs_x, step_size, a_log, b_rows, c_rows, d_skip):
    length, head_count, head_width = inputs_x.shape
    blocks = length // BLOCK
    log_decay = step_size * (-jnp.exp(a_log))[None, :]
    weighted = inputs_x * step_size[:, :, None]
    causal = jnp.tril(jnp.ones((BLOCK, BLOCK), jnp.float32))

    def advance(carry_state, pieces):
        x_block, r_block, b_block, c_block = pieces
        cumulative = jnp.cumsum(r_block.T, axis=1)
        differ = (cumulative[:, :, None] - cumulative[:, None, :]) * causal[None]
        decay_mat = jnp.exp(differ) * causal[None]
        scores = jnp.dot(c_block, b_block.T, precision=precise)
        within = jnp.einsum('hij,jhp->ihp', decay_mat * scores[None], x_block, precision=precise)
        carried = jnp.einsum('in,hpn->ihp', c_block, carry_state, precision=precise)
        carried = carried * jnp.exp(cumulative.T)[:, :, None]
        to_end = jnp.exp(cumulative[:, -1:] - cumulative)
        fresh = jnp.einsum('jn,jhp->hpn', b_block, x_block * to_end.T[:, :, None], precision=precise)
        carry_state = carry_state * jnp.exp(cumulative[:, -1])[:, None, None] + fresh
        return (carry_state, within + carried)
    initial = jnp.zeros((head_count, head_width, b_rows.shape[1]), jnp.float32)
    pieces = (weighted.reshape(blocks, BLOCK, head_count, head_width), log_decay.reshape(blocks, BLOCK, head_count), b_rows.reshape(blocks, BLOCK, b_rows.shape[1]), c_rows.reshape(blocks, BLOCK, c_rows.shape[1]))
    last_state, outputs = lax.scan(advance, initial, pieces)
    return outputs.reshape(length, head_count, head_width) + d_skip[None, :, None] * inputs_x

def block_forward(hidden, in_low, out_low, vector):
    gain_one, gain_two, kernel, conv_bias, a_log, dt_bias, d_skip = split_vector(vector)
    normed = low(rms_scale(hidden) * gain_one[None, :])
    projected = low_back(jnp.dot(normed, in_low, precision=precise))
    gating = projected[:, :DI]
    conv_in = projected[:, DI:DI + CONVCH]
    dt_raw = projected[:, DI + CONVCH:]
    padding = jnp.zeros((WIDTH - 1, CONVCH), jnp.float32)
    conv_out = convolve(jnp.concatenate([padding, conv_in], 0), kernel, conv_bias)
    inputs_x = low(low_back(conv_out[:, :DI])).reshape(-1, HEADS, HEADDIM)
    b_and_c = low(conv_out[:, DI:])
    dt_low = low(low_back(dt_raw))
    step_size = jax.nn.softplus(dt_low + dt_bias[None, :])
    scanned = state_scan(inputs_x, step_size, a_log, b_and_c[:, :STATE], b_and_c[:, STATE:], d_skip)
    scanned = low(low_back(scanned.reshape(-1, DI)))
    gated = rms_scale(scanned * jax.nn.silu(gating)) * gain_two[None, :]
    return hidden + jnp.dot(low(gated), out_low, precision=precise)

def adamw_step(weight, first, second, grad, rate, decay):
    first_new = beta_one * first + (1.0 - beta_one) * grad
    second_new = beta_two * second + (1.0 - beta_two) * grad * grad
    fix_one = 1.0 - beta_one ** STEP
    fix_two = 1.0 - beta_two ** STEP
    normalized = first_new / fix_one / (jnp.sqrt(second_new / fix_two) + adam_eps)
    return (first_new, second_new, weight - rate * (normalized + decay * weight))

def reference(block_in, cotangent, in_weight, in_first, in_second, out_weight, out_first, out_second, vec_weight, vec_first, vec_second):
    hidden = block_in.astype(jnp.float32)

    def forward(hidden_all, in_master, out_master, vector):
        in_low = low(in_master)
        out_low = low(out_master)
        one_seq = jax.checkpoint(lambda sequence: block_forward(sequence, in_low, out_low, vector))
        return lax.map(one_seq, hidden_all)
    block_out, pullback = jax.vjp(forward, hidden, in_weight, out_weight, vec_weight)
    block_grad, grad_in, grad_out, grad_vec = pullback(cotangent.astype(jnp.float32))
    in_first_new, in_second_new, in_weight_new = adamw_step(in_weight, in_first, in_second, grad_in, matrix_rate, matrix_decay)
    out_first_new, out_second_new, out_weight_new = adamw_step(out_weight, out_first, out_second, grad_out, matrix_rate, matrix_decay)
    vec_first_new, vec_second_new, vec_weight_new = adamw_step(vec_weight, vec_first, vec_second, grad_vec, vector_rate, 0.0)
    return (block_out, block_grad, in_first_new, in_second_new, in_weight_new, out_first_new, out_second_new, out_weight_new, vec_first_new, vec_second_new, vec_weight_new)
```

```python
import jax
import jax.numpy as jnp
from jax import lax
from jax.sharding import PartitionSpec as P

D = 1024
HEADS = 32
HEADDIM = 64
STATE = 128
WIDTH = 4
BLOCK = 256
STEP = 10
DI = 2048
CONVCH = 2304


precise = lax.Precision.HIGHEST
norm_eps = 1e-05
beta_one = 0.9
beta_two = 0.95
adam_eps = 1e-08
matrix_rate = 0.05
matrix_decay = 0.1
vector_rate = 0.5


def rms_scale(values):
    return values * lax.rsqrt(jnp.mean(values * values, axis=-1, keepdims=True) + norm_eps)


def split_vector(vector):
    extents = [D, DI, WIDTH * CONVCH, CONVCH, HEADS, HEADS, HEADS]
    pieces = []
    offset = 0
    for extent in extents:
        pieces.append(vector[offset : offset + extent])
        offset = offset + extent
    pieces[2] = pieces[2].reshape(WIDTH, CONVCH)
    return pieces


def convolve(extended, kernel, conv_bias):
    rows_out = extended.shape[0] - kernel.shape[0] + 1
    summed = jnp.broadcast_to(conv_bias[None, :], (rows_out, kernel.shape[1]))
    for offset in range(kernel.shape[0]):
        summed = summed + kernel[offset][None, :] * extended[offset : offset + rows_out]
    return jax.nn.silu(summed)


def state_scan(inputs_x, step_size, a_log, b_rows, c_rows, d_skip):
    length, head_count, head_width = inputs_x.shape
    blocks = length // BLOCK
    log_decay = step_size * (-jnp.exp(a_log))[None, :]
    weighted = inputs_x * step_size[:, :, None]
    causal = jnp.tril(jnp.ones((BLOCK, BLOCK), jnp.float32))
    lower = causal > 0.5

    def advance(carry_state, pieces):
        x_block, r_block, b_block, c_block = pieces
        cumulative = jnp.cumsum(r_block.T, axis=1)
        differ = (cumulative[:, :, None] - cumulative[:, None, :]) * causal[None]
        scores = jnp.dot(c_block, b_block.T, precision=precise)
        decay_mat = jnp.where(lower[None], jnp.exp(differ), 0.0) * scores[None]
        within = jnp.einsum("hij,jhp->ihp", decay_mat, x_block, precision=precise)
        carried = jnp.einsum("in,hpn->ihp", c_block, carry_state, precision=precise)
        carried = carried * jnp.exp(cumulative.T)[:, :, None]
        to_end = jnp.exp(cumulative[:, -1:] - cumulative)
        fresh = jnp.einsum(
            "jn,jhp->hpn", b_block, x_block * to_end.T[:, :, None], precision=precise
        )
        carry_state = carry_state * jnp.exp(cumulative[:, -1])[:, None, None] + fresh
        return (carry_state, within + carried)

    initial = jnp.zeros((head_count, head_width, b_rows.shape[1]), jnp.float32)
    pieces = (
        weighted.reshape(blocks, BLOCK, head_count, head_width),
        log_decay.reshape(blocks, BLOCK, head_count),
        b_rows.reshape(blocks, BLOCK, b_rows.shape[1]),
        c_rows.reshape(blocks, BLOCK, c_rows.shape[1]),
    )
    last_state, outputs = lax.scan(jax.checkpoint(advance), initial, pieces)
    return outputs.reshape(length, head_count, head_width) + d_skip[None, :, None] * inputs_x


def head_mixer(inputs_x, dt_part, both_rows, decay_part, bias_part, skip_part):
    step_size = jax.nn.softplus(dt_part + bias_part[None, :])
    return state_scan(
        inputs_x, step_size, decay_part, both_rows[:, :STATE], both_rows[:, STATE:], skip_part
    )


def adamw_step(weight, first, second, grad, rate, decay):
    first_new = beta_one * first + (1.0 - beta_one) * grad
    second_new = beta_two * second + (1.0 - beta_two) * grad * grad
    fix_one = 1.0 - beta_one**STEP
    fix_two = 1.0 - beta_two**STEP
    normalized = first_new / fix_one / (jnp.sqrt(second_new / fix_two) + adam_eps)
    return (first_new, second_new, weight - rate * (normalized + decay * weight))


def pick_heads(values, axis, width, index, groups):
    shape = values.shape
    split = shape[:axis] + (HEADS // groups, groups, width) + shape[axis + 1 :]
    taken = lax.dynamic_index_in_dim(values.reshape(split), index, axis + 1, keepdims=False)
    return taken.reshape(shape[:axis] + (HEADS // groups * width,) + shape[axis + 1 :])


def merge_heads(stacked, axis, width):
    groups = stacked.shape[0]
    shape = stacked.shape[1:]
    split = (groups,) + shape[:axis] + (HEADS // groups, width) + shape[axis + 1 :]
    moved = jnp.moveaxis(stacked.reshape(split), 0, axis + 1)
    return moved.reshape(shape[:axis] + (HEADS * width,) + shape[axis + 1 :])


def seq_sum_rows(partial):
    return lax.psum_scatter(
        partial.astype(jnp.bfloat16), "seq", scatter_dimension=0, tiled=True
    ).astype(jnp.float32)


def gather_out(out_low, seq_index, groups):
    rows = out_low.shape[0]
    if rows % (groups * HEADDIM) == 0:
        mine = pick_rows(out_low, seq_index, groups)
        return lax.all_gather(mine, "wshard", axis=0, tiled=True)
    whole = lax.all_gather(out_low, "wshard", axis=0, tiled=True)
    return pick_heads(whole, 0, HEADDIM, seq_index, groups)


def pick_rows(values, seq_index, groups):
    rows = values.shape[0]
    split = values.reshape(rows // (groups * HEADDIM), groups, HEADDIM, values.shape[1])
    return lax.dynamic_index_in_dim(split, seq_index, 1, keepdims=False).reshape(
        rows // groups, values.shape[1]
    )


def sum_out_grad(grad, rows, seq_index, groups):
    grad = grad.astype(jnp.bfloat16)
    if rows % (groups * HEADDIM) == 0:
        mine = lax.psum_scatter(grad, "wshard", scatter_dimension=0, tiled=True)
        every = lax.all_gather(mine, "seq", axis=0, tiled=False)
        split = every.reshape(groups, rows // (groups * HEADDIM), HEADDIM, grad.shape[1])
        return jnp.moveaxis(split, 0, 1).reshape(rows, grad.shape[1]).astype(jnp.float32)
    blocks = grad.reshape(HEADS // groups, 1, HEADDIM, grad.shape[1])
    here = (jnp.arange(groups) == seq_index)[None, :, None, None]
    spread = jnp.where(here, blocks, jnp.zeros((), jnp.bfloat16)).reshape(DI, grad.shape[1])
    mine = lax.psum_scatter(spread, "wshard", scatter_dimension=0, tiled=True)
    return lax.psum(mine.astype(jnp.float32), "seq")


def shards(
    block_in,
    cotangent,
    in_weight,
    in_first,
    in_second,
    out_weight,
    out_first,
    out_second,
    vec_weight,
    vec_first,
    vec_second,
):
    rows_here = block_in.shape[1]
    groups = lax.axis_size("seq")
    seq_index = lax.axis_index("seq")
    local_heads = HEADS // groups
    local_di = DI // groups
    hidden_rows = block_in.reshape(rows_here, D)
    cot_rows = cotangent.reshape(rows_here, D)
    gain_one, gain_two, kernel, conv_bias, a_log, dt_bias, d_skip = split_vector(vec_weight)

    def heads_of(values, axis, width):
        return pick_heads(values, axis, width, seq_index, groups)

    in_low = in_weight.astype(jnp.bfloat16)
    in_mine = jnp.concatenate(
        [
            heads_of(in_low[:, :DI], 1, HEADDIM),
            heads_of(in_low[:, DI : 2 * DI], 1, HEADDIM),
            in_low[:, 2 * DI : 2 * DI + 2 * STATE],
            heads_of(in_low[:, DI + CONVCH :], 1, 1),
        ],
        1,
    )
    hidden_low = lax.all_gather(hidden_rows, "seq", axis=0, tiled=True)
    in_mine = lax.all_gather(in_mine, "wshard", axis=0, tiled=True)
    cot = lax.all_gather(cot_rows, "seq", axis=0, tiled=True)
    out_mine = gather_out(out_weight.astype(jnp.bfloat16), seq_index, groups)
    length = hidden_low.shape[0]
    my_gain_two = heads_of(gain_two, 0, HEADDIM)
    my_kernel = jnp.concatenate([heads_of(kernel[:, :DI], 1, HEADDIM), kernel[:, DI:]], 1)
    my_bias = jnp.concatenate([heads_of(conv_bias[:DI], 0, HEADDIM), conv_bias[DI:]], 0)

    hidden = hidden_low.astype(jnp.float32)
    unit = rms_scale(hidden)
    normed_low = (unit * gain_one[None, :]).astype(jnp.bfloat16)
    projected = jnp.dot(normed_low, in_mine, preferred_element_type=jnp.float32)
    gating = projected[:, :local_di]
    conv_in = projected[:, local_di : 2 * local_di + 2 * STATE]
    dt_low = projected[:, 2 * local_di + 2 * STATE :].astype(jnp.bfloat16)
    padding = jnp.zeros((WIDTH - 1, conv_in.shape[1]), jnp.float32)
    conv_out, conv_pullback = jax.vjp(
        convolve, jnp.concatenate([padding, conv_in], 0), my_kernel, my_bias
    )
    conv_low = conv_out.astype(jnp.bfloat16).astype(jnp.float32)
    scanned, scan_pullback = jax.vjp(
        head_mixer,
        conv_low[:, :local_di].reshape(length, local_heads, HEADDIM),
        dt_low.astype(jnp.float32),
        conv_low[:, local_di:],
        heads_of(a_log, 0, 1),
        heads_of(dt_bias, 0, 1),
        heads_of(d_skip, 0, 1),
    )
    mixed = scanned.astype(jnp.bfloat16).reshape(length, local_di).astype(jnp.float32)
    gate, gate_pullback = jax.vjp(jax.nn.silu, gating)
    gated = mixed * gate
    d_gnorm = jnp.dot(cot, out_mine.T, preferred_element_type=jnp.float32)
    d_unit = d_gnorm * my_gain_two[None, :]
    sums = jnp.stack([jnp.sum(gated * gated, axis=1), jnp.sum(d_unit * gated, axis=1)])
    sums = jnp.sum(lax.all_gather(sums, "seq", axis=0, tiled=False), axis=0) / DI
    scale = lax.rsqrt(sums[0] + norm_eps)[:, None]
    unit_two = gated * scale
    gnorm_low = (unit_two * my_gain_two[None, :]).astype(jnp.bfloat16)
    block_part = jnp.dot(gnorm_low, out_mine, preferred_element_type=jnp.float32)
    block_out = hidden_rows.astype(jnp.float32) + seq_sum_rows(block_part)
    grad_out = jnp.dot(gnorm_low.T, cot, preferred_element_type=jnp.float32)
    d_gain_two = jnp.sum(d_gnorm * unit_two, axis=0)
    d_gated = scale * d_unit - unit_two * (scale * scale * sums[1][:, None])
    (d_gating,) = gate_pullback(d_gated * mixed)
    d_scanned = (d_gated * gate).astype(jnp.bfloat16).astype(jnp.float32)
    d_inner, d_dt, d_both, d_a_log, d_dt_bias, d_skip_part = scan_pullback(
        d_scanned.reshape(length, local_heads, HEADDIM)
    )
    d_conv_out = jnp.concatenate([d_inner.reshape(length, local_di), d_both], 1)
    d_extended, d_kernel, d_conv_bias = conv_pullback(d_conv_out)
    d_projected = jnp.concatenate([d_gating, d_extended[WIDTH - 1 :], d_dt], 1).astype(
        jnp.bfloat16
    )
    d_normed_part = jnp.dot(d_projected, in_mine.T, preferred_element_type=jnp.float32)
    grad_in = jnp.dot(normed_low.T, d_projected, preferred_element_type=jnp.float32)
    d_gain_one = jnp.sum(d_normed_part * unit, axis=0)
    d_normed = seq_sum_rows(d_normed_part)
    own_hidden = hidden_rows.astype(jnp.float32)
    own_scale = lax.rsqrt(jnp.mean(own_hidden * own_hidden, axis=-1, keepdims=True) + norm_eps)
    own_unit = own_hidden * own_scale
    d_own = d_normed * gain_one[None, :]
    d_hidden = own_scale * (
        d_own - own_unit * jnp.mean(d_own * own_unit, axis=-1, keepdims=True)
    )
    block_grad = cot_rows.astype(jnp.float32) + d_hidden

    def spread_heads(values, axis, width):
        here = (jnp.arange(groups) == seq_index).reshape((groups,) + (1,) * values.ndim)
        return merge_heads(jnp.where(here, values[None], 0.0), axis, width)

    vec_grad = jnp.concatenate(
        [
            d_gain_one,
            spread_heads(d_gain_two, 0, HEADDIM),
            jnp.concatenate(
                [spread_heads(d_kernel[:, :local_di], 1, HEADDIM), d_kernel[:, local_di:]], 1
            ).reshape(-1),
            spread_heads(d_conv_bias[:local_di], 0, HEADDIM),
            d_conv_bias[local_di:],
            spread_heads(d_a_log, 0, 1),
            spread_heads(d_dt_bias, 0, 1),
            spread_heads(d_skip_part, 0, 1),
        ]
    )
    vec_total = lax.psum(vec_grad, ("seq", "wshard"))
    vec_first_new, vec_second_new, vec_weight_new = adamw_step(
        vec_weight, vec_first, vec_second, vec_total, vector_rate, 0.0
    )
    out_total = sum_out_grad(grad_out, out_weight.shape[0], seq_index, groups)
    in_part = lax.psum_scatter(
        grad_in.astype(jnp.bfloat16), "wshard", scatter_dimension=0, tiled=True
    )
    in_every = lax.all_gather(in_part, "seq", axis=0, tiled=False)
    both_end = 2 * local_di + 2 * STATE
    in_total = jnp.concatenate(
        [
            merge_heads(in_every[:, :, :local_di], 1, HEADDIM),
            merge_heads(in_every[:, :, local_di : 2 * local_di], 1, HEADDIM),
            jnp.sum(in_every[:, :, 2 * local_di : both_end].astype(jnp.float32), axis=0).astype(
                jnp.bfloat16
            ),
            merge_heads(in_every[:, :, both_end:], 1, 1),
        ],
        1,
    ).astype(jnp.float32)
    in_first_new, in_second_new, in_weight_new = adamw_step(
        in_weight, in_first, in_second, in_total, matrix_rate, matrix_decay
    )
    out_first_new, out_second_new, out_weight_new = adamw_step(
        out_weight, out_first, out_second, out_total, matrix_rate, matrix_decay
    )
    return (
        block_out.reshape(1, rows_here, D),
        block_grad.reshape(1, rows_here, D),
        in_first_new,
        in_second_new,
        in_weight_new,
        out_first_new,
        out_second_new,
        out_weight_new,
        vec_first_new,
        vec_second_new,
        vec_weight_new,
    )


def solution(mesh):
    return jax.shard_map(
        shards,
        mesh=mesh,
        in_specs=(
            P("wshard", "seq", None),
            P("wshard", "seq", None),
            P("wshard", None),
            P("wshard", None),
            P("wshard", None),
            P("wshard", None),
            P("wshard", None),
            P("wshard", None),
            P(),
            P(),
            P(),
        ),
        out_specs=(
            P("wshard", "seq", None),
            P("wshard", "seq", None),
            P("wshard", None),
            P("wshard", None),
            P("wshard", None),
            P("wshard", None),
            P("wshard", None),
            P("wshard", None),
            P(),
            P(),
            P(),
        ),
        check_vma=False,
    )
```

```python
import jax
import jax.numpy as jnp
from jax import lax
from jax.experimental import pallas as pl
from jax.experimental.pallas import tpu as pltpu
from jax.sharding import PartitionSpec as P

D = 1024
HEADS = 32
HEADDIM = 64
STATE = 128
WIDTH = 4
BLOCK = 256
STEP = 10
DI = 2048
CONVCH = 2304


precise = lax.Precision.HIGHEST
norm_eps = 1e-05
beta_one = 0.9
beta_two = 0.95
adam_eps = 1e-08
matrix_rate = 0.05
matrix_decay = 0.1
vector_rate = 0.5


def rms_scale(values):
    return values * lax.rsqrt(jnp.mean(values * values, axis=-1, keepdims=True) + norm_eps)


def split_vector(vector):
    extents = [D, DI, WIDTH * CONVCH, CONVCH, HEADS, HEADS, HEADS]
    pieces = []
    offset = 0
    for extent in extents:
        pieces.append(vector[offset : offset + extent])
        offset = offset + extent
    pieces[2] = pieces[2].reshape(WIDTH, CONVCH)
    return pieces


def wide(extent):
    return pl.BlockSpec((BLOCK, extent), lambda q: (q, 0))


def wide_back(extent, count):
    return pl.BlockSpec((BLOCK, extent), lambda q: (count - 1 - q, 0))


def whole(*shape):
    return pl.BlockSpec(shape, lambda q: (0,) * len(shape))


def dot_nt(left, right, precision=None):
    return lax.dot_general(
        left,
        right,
        (((1,), (1,)), ((), ())),
        precision=precision,
        preferred_element_type=jnp.float32,
    )


def dot_tn(left, right):
    return lax.dot_general(
        left, right, (((0,), (0,)), ((), ())), preferred_element_type=jnp.float32
    )


def dot_nn(left, right, precision=None):
    return jnp.dot(left, right, precision=precision, preferred_element_type=jnp.float32)


def sigmoid(values):
    return 1.0 / (1.0 + jnp.exp(-values))


def low(values):
    return values.astype(jnp.bfloat16)


def lower_mask():
    rows = lax.broadcasted_iota(jnp.int32, (BLOCK, BLOCK), 0)
    return rows >= lax.broadcasted_iota(jnp.int32, (BLOCK, BLOCK), 1)


def decay_sums(dt_raw, dt_bias, a_log, expand):
    shifted = dt_raw + dt_bias
    step = jnp.maximum(shifted, 0.0) + jnp.log1p(jnp.exp(-jnp.abs(shifted)))
    log_decay = -jnp.exp(a_log) * step
    ones = jnp.where(lower_mask(), 1.0, 0.0)
    running = dot_nn(ones, log_decay, precise)
    step_wide = dot_nn(step, expand, precise)
    running_wide = dot_nn(running, expand, precise)
    return shifted, step, log_decay, running, step_wide, running_wide


def forward_kernel(
    hidden_ref,
    cot_ref,
    in_ref,
    dt_weight_ref,
    out_ref,
    gain_one_ref,
    gain_two_ref,
    conv_ref,
    bias_ref,
    a_log_ref,
    dt_bias_ref,
    skip_ref,
    expand_ref,
    normed_ref,
    gating_ref,
    conv_in_ref,
    conv_pre_ref,
    dt_ref,
    y_ref,
    scanned_ref,
    state_ref,
    d_gnorm_ref,
    sums_ref,
    ext,
    state,
):
    local_di = gating_ref.shape[1]
    heads = local_di // HEADDIM

    @pl.when(pl.program_id(0) == 0)
    def _():
        ext[0:8, :] = jnp.zeros((8, ext.shape[1]), jnp.float32)
        state[...] = jnp.zeros_like(state)

    hidden = hidden_ref[...].astype(jnp.float32)
    normed = low(rms_scale(hidden) * gain_one_ref[...])
    normed_ref[...] = normed
    projected = dot_nn(normed, in_ref[...])
    gating = projected[:, :local_di]
    gating_ref[...] = gating
    conv_in = projected[:, local_di:]
    conv_in_ref[...] = conv_in
    ext[8 : 8 + BLOCK, :] = conv_in
    conv_pre = bias_ref[...] + conv_ref[WIDTH - 1 : WIDTH, :] * conv_in
    for tap in range(WIDTH - 1):
        first = 8 - WIDTH + 1 + tap
        conv_pre = conv_pre + conv_ref[tap : tap + 1, :] * ext[first : first + BLOCK, :]
    conv_pre_ref[...] = conv_pre
    ext[8 - WIDTH + 1 : 8, :] = ext[8 + BLOCK - WIDTH + 1 : 8 + BLOCK, :]
    conv_low = low(conv_pre * sigmoid(conv_pre))
    inner = conv_low[:, :local_di]
    b_rows = conv_low[:, local_di : local_di + STATE]
    c_rows = conv_low[:, local_di + STATE :]
    dt_raw = low(dot_nn(normed, dt_weight_ref[...])).astype(jnp.float32)
    dt_ref[...] = dt_raw

    _, _, _, running, step_wide, running_wide = decay_sums(
        dt_raw, dt_bias_ref[...], a_log_ref[...], expand_ref[...]
    )
    running_t = running.T
    b_t = low(b_rows.astype(jnp.float32).T)
    scores = dot_nn(c_rows, b_t)
    mask = lower_mask()
    inner_wide = inner.astype(jnp.float32)
    stepped = step_wide * inner_wide
    stepped_low = low(stepped)
    first_half = lax.broadcasted_iota(jnp.int32, (BLOCK, 2 * HEADDIM), 1) < HEADDIM
    zero = jnp.zeros((), jnp.bfloat16)
    state_ref[...] = state[...].reshape(state_ref.shape)
    held = state[...]
    carried = jnp.exp(running_wide) * dot_nn(c_rows, low(held))
    for pair in range(heads // 2):
        span = slice(pair * 2 * HEADDIM, (pair + 1) * 2 * HEADDIM)
        both = stepped_low[:, span]
        total = carried[:, span]
        for half in range(2):
            head = 2 * pair + half
            differ = running[:, head : head + 1] - running_t[head : head + 1, :]
            mixed = low(jnp.exp(jnp.where(mask, differ, -jnp.inf)) * scores)
            mine = jnp.where(first_half if half == 0 else ~first_half, both, zero)
            total = total + dot_nn(mixed, mine)
        y_ref[:, span] = total
    last = running_wide[BLOCK - 1 : BLOCK, :]
    to_end = jnp.exp(last - running_wide)
    state[...] = jnp.exp(last) * held + dot_nn(b_t, low(to_end * stepped))
    scanned = low(y_ref[...] + skip_ref[...] * inner_wide)
    scanned_ref[...] = scanned
    gated = scanned.astype(jnp.float32) * (gating * sigmoid(gating))
    d_gnorm = dot_nt(cot_ref[...], out_ref[...])
    d_gnorm_ref[...] = d_gnorm
    ones = jnp.ones((8, local_di), jnp.float32)
    squares = dot_nt(ones, gated * gated, precise)
    products = dot_nt(ones, d_gnorm * gain_two_ref[...] * gated, precise)
    sums_ref[...] = jnp.where(
        lax.broadcasted_iota(jnp.int32, squares.shape, 0) == 0, squares, products
    )


def middle_kernel(
    scanned_ref,
    gating_ref,
    d_gnorm_ref,
    cot_ref,
    normed_ref,
    scale_ref,
    slope_ref,
    out_ref,
    gain_two_ref,
    block_ref,
    d_gating_ref,
    d_scanned_ref,
    grad_out_ref,
    grad_gate_ref,
    d_gain_two_ref,
    out_sum,
    gate_sum,
):
    chunk = pl.program_id(0)

    @pl.when(chunk == 0)
    def _():
        out_sum[...] = jnp.zeros_like(out_sum)
        gate_sum[...] = jnp.zeros_like(gate_sum)
        d_gain_two_ref[...] = jnp.zeros_like(d_gain_two_ref)

    gating = gating_ref[...]
    open_part = sigmoid(gating)
    gate = gating * open_part
    scanned = scanned_ref[...].astype(jnp.float32)
    scale = scale_ref[:, :1]
    unit = scanned * gate * scale
    d_gnorm = d_gnorm_ref[...]
    gain_two = gain_two_ref[...]
    gnorm = low(unit * gain_two)
    block_ref[...] = low(dot_nn(gnorm, out_ref[...]))
    out_sum[...] += dot_tn(gnorm, cot_ref[...])
    d_gain_two_ref[...] += jnp.sum(d_gnorm * unit, axis=0, keepdims=True)
    d_gated = scale * (d_gnorm * gain_two) - unit * slope_ref[:, :1]
    d_gating = low(d_gated * scanned * (open_part * (1.0 + gating * (1.0 - open_part))))
    d_gating_ref[...] = d_gating
    d_scanned_ref[...] = low(d_gated * gate)
    gate_sum[...] += dot_tn(normed_ref[...], d_gating)

    @pl.when(chunk == pl.num_programs(0) - 1)
    def _():
        grad_out_ref[...] = low(out_sum[...])
        grad_gate_ref[...] = low(gate_sum[...])


def backward_kernel(
    hidden_ref,
    normed_ref,
    conv_in_ref,
    conv_pre_ref,
    dt_ref,
    y_ref,
    state_ref,
    d_scanned_ref,
    d_gating_ref,
    in_ref,
    dt_weight_ref,
    conv_ref,
    a_log_ref,
    dt_bias_ref,
    skip_ref,
    expand_ref,
    d_normed_ref,
    grad_conv_ref,
    grad_dt_ref,
    d_gain_one_ref,
    d_kernel_ref,
    d_conv_bias_ref,
    d_skip_ref,
    d_head_ref,
    ext,
    d_state,
    later_state,
    conv_sum,
    dt_sum,
):
    local_di = y_ref.shape[1]
    heads = local_di // HEADDIM
    chunk = pl.program_id(0)

    @pl.when(chunk == 0)
    def _():
        ext[BLOCK : BLOCK + 8, :] = jnp.zeros((8, ext.shape[1]), jnp.float32)
        d_state[...] = jnp.zeros_like(d_state)
        later_state[...] = jnp.zeros_like(later_state)
        conv_sum[...] = jnp.zeros_like(conv_sum)
        dt_sum[...] = jnp.zeros_like(dt_sum)
        d_gain_one_ref[...] = jnp.zeros_like(d_gain_one_ref)
        d_kernel_ref[...] = jnp.zeros_like(d_kernel_ref)
        d_conv_bias_ref[...] = jnp.zeros_like(d_conv_bias_ref)
        d_skip_ref[...] = jnp.zeros_like(d_skip_ref)
        d_head_ref[...] = jnp.zeros_like(d_head_ref)

    expand = expand_ref[...]
    conv_pre = conv_pre_ref[...]
    open_part = sigmoid(conv_pre)
    conv_low = low(conv_pre * open_part)
    inner = conv_low[:, :local_di].astype(jnp.float32)
    b_rows = conv_low[:, local_di : local_di + STATE]
    c_rows = conv_low[:, local_di + STATE :]
    a_log = a_log_ref[...]
    shifted, _, log_decay, running, step_wide, running_wide = decay_sums(
        dt_ref[...], dt_bias_ref[...], a_log, expand
    )
    running_t = running.T
    b_t = low(b_rows.astype(jnp.float32).T)
    c_t = low(c_rows.astype(jnp.float32).T)
    scores = dot_nn(c_rows, b_t)
    scores_t = dot_nn(b_rows, c_t)
    mask = lower_mask()
    rows = lax.broadcasted_iota(jnp.int32, (BLOCK, BLOCK), 0)
    mask_t = rows <= lax.broadcasted_iota(jnp.int32, (BLOCK, BLOCK), 1)
    d_y_low = d_scanned_ref[...]
    d_y = d_y_low.astype(jnp.float32)
    stepped_low = low(step_wide * inner)
    stepped = stepped_low.astype(jnp.float32)
    last = running_wide[BLOCK - 1 : BLOCK, :]
    to_end = jnp.exp(last - running_wide)
    d_later = d_state[...]
    d_later_low = low(d_later)
    held = state_ref[...].reshape(d_state.shape)
    decayed_dy = low(jnp.exp(running_wide) * d_y)
    d_c = dot_nt(decayed_dy, low(held))
    d_b = dot_nt(low(to_end * stepped), d_later_low)
    d_stepped = to_end * dot_nn(b_rows, d_later_low)
    cross = jnp.sum(later_state[...] * d_later, axis=0, keepdims=True)
    d_state[...] = jnp.exp(last) * d_later + dot_nn(c_t, decayed_dy)
    later_state[...] = held
    first_half = lax.broadcasted_iota(jnp.int32, (BLOCK, 2 * HEADDIM), 1) < HEADDIM
    zero = jnp.zeros((), jnp.bfloat16)
    d_scores = jnp.zeros((BLOCK, BLOCK), jnp.float32)
    pieces = []
    for pair in range(heads // 2):
        span = slice(pair * 2 * HEADDIM, (pair + 1) * 2 * HEADDIM)
        total = d_stepped[:, span]
        for half in range(2):
            head = 2 * pair + half
            mine = jnp.where(first_half if half == 0 else ~first_half, d_y_low[:, span], zero)
            column = running[:, head : head + 1]
            row = running_t[head : head + 1, :]
            decay = jnp.exp(jnp.where(mask, column - row, -jnp.inf))
            decay_t = jnp.exp(jnp.where(mask_t, row - column, -jnp.inf))
            d_scores = d_scores + dot_nt(mine, stepped_low[:, span]) * decay
            total = total + dot_nn(low(decay_t * scores_t), mine)
        pieces.append(total)
    d_stepped = jnp.concatenate(pieces, 1)
    d_scores_low = low(d_scores)
    d_c = d_c + dot_nn(d_scores_low, b_rows)
    d_b = d_b + dot_nn(low(d_scores.T), c_rows)
    d_inner = step_wide * d_stepped + skip_ref[...] * d_y
    d_running = dot_nt(d_y * y_ref[...] - d_stepped * stepped, expand, precise)
    upper = jnp.where(mask_t, 1.0, 0.0)
    d_log = dot_nn(upper, d_running, precise) + dot_nt(cross, expand, precise)
    d_step = dot_nt(d_stepped * inner, expand, precise) - jnp.exp(a_log) * d_log
    d_dt = d_step * sigmoid(shifted)
    d_head_ref[0:1, :] += jnp.sum(d_log * log_decay, axis=0, keepdims=True)
    d_head_ref[1:2, :] += jnp.sum(d_dt, axis=0, keepdims=True)
    d_skip_ref[...] += jnp.sum(d_y * inner, axis=0, keepdims=True)

    d_conv_out = jnp.concatenate([d_inner, d_b, d_c], 1)
    d_pre = d_conv_out * (open_part * (1.0 + conv_pre * (1.0 - open_part)))
    ext[0:BLOCK, :] = d_pre
    d_conv_bias_ref[...] += jnp.sum(d_pre, axis=0, keepdims=True)
    conv_in = conv_in_ref[...]
    d_conv_in = jnp.zeros_like(conv_in)
    for tap in range(WIDTH):
        moved = ext[WIDTH - 1 - tap : WIDTH - 1 - tap + BLOCK, :]
        d_conv_in = d_conv_in + conv_ref[tap : tap + 1, :] * moved
        d_kernel_ref[tap : tap + 1, :] += jnp.sum(moved * conv_in, axis=0, keepdims=True)
    ext[BLOCK : BLOCK + 8, :] = ext[0:8, :]
    d_conv_low = low(d_conv_in)
    d_dt_low = low(d_dt)
    normed = normed_ref[...]
    conv_sum[...] += dot_tn(normed, d_conv_low)
    dt_sum[...] += dot_tn(normed, d_dt_low)
    d_normed = dot_nt(d_gating_ref[...], in_ref[:, :local_di])
    d_normed = d_normed + dot_nt(d_conv_low, in_ref[:, local_di:])
    d_normed = d_normed + dot_nt(d_dt_low, dt_weight_ref[...])
    d_normed_ref[...] = low(d_normed)
    unit = rms_scale(hidden_ref[...].astype(jnp.float32))
    d_gain_one_ref[...] += jnp.sum(d_normed * unit, axis=0, keepdims=True)

    @pl.when(chunk == pl.num_programs(0) - 1)
    def _():
        grad_conv_ref[...] = low(conv_sum[...])
        grad_dt_ref[...] = low(dt_sum[...])


def kernel_params():
    return pltpu.CompilerParams(
        dimension_semantics=("arbitrary",), vmem_limit_bytes=50 * 1024 * 1024
    )


def run_forward(hidden, cot, in_low, dt_weight, out_low, gains, conv, heads_vectors, expand):
    length = hidden.shape[0]
    chunks = length // BLOCK
    local_di = out_low.shape[0]
    channels = in_low.shape[1] - local_di
    lanes = dt_weight.shape[1]
    shape = jax.ShapeDtypeStruct
    f32, bf16 = jnp.float32, jnp.bfloat16
    return pl.pallas_call(
        forward_kernel,
        grid=(chunks,),
        in_specs=[
            wide(D),
            wide(D),
            whole(D, local_di + channels),
            whole(D, lanes),
            whole(local_di, D),
            whole(1, D),
            whole(1, local_di),
            whole(WIDTH, channels),
            whole(1, channels),
            whole(1, lanes),
            whole(1, lanes),
            whole(1, local_di),
            whole(lanes, local_di),
        ],
        out_specs=[
            wide(D),
            wide(local_di),
            wide(channels),
            wide(channels),
            wide(lanes),
            wide(local_di),
            wide(local_di),
            pl.BlockSpec((1, STATE, local_di), lambda q: (q, 0, 0)),
            wide(local_di),
            pl.BlockSpec((8, BLOCK), lambda q: (0, q)),
        ],
        out_shape=[
            shape((length, D), bf16),
            shape((length, local_di), f32),
            shape((length, channels), f32),
            shape((length, channels), f32),
            shape((length, lanes), f32),
            shape((length, local_di), f32),
            shape((length, local_di), bf16),
            shape((chunks, STATE, local_di), f32),
            shape((length, local_di), f32),
            shape((8, length), f32),
        ],
        scratch_shapes=[
            pltpu.VMEM((8 + BLOCK, channels), f32),
            pltpu.VMEM((STATE, local_di), f32),
        ],
        compiler_params=kernel_params(),
        cost_estimate=pl.CostEstimate(
            flops=8_000_000_000, bytes_accessed=25_000_000, transcendentals=8_000_000
        ),
        name="forward",
    )(hidden, cot, in_low, dt_weight, out_low, *gains, *conv, *heads_vectors, expand)


def run_middle(scanned, gating, d_gnorm, cot, normed, scale, slope, out_low, gain_two):
    length, local_di = scanned.shape
    shape = jax.ShapeDtypeStruct
    f32, bf16 = jnp.float32, jnp.bfloat16
    return pl.pallas_call(
        middle_kernel,
        grid=(length // BLOCK,),
        in_specs=[
            wide(local_di),
            wide(local_di),
            wide(local_di),
            wide(D),
            wide(D),
            wide(1),
            wide(1),
            whole(local_di, D),
            whole(1, local_di),
        ],
        out_specs=[
            wide(D),
            wide(local_di),
            wide(local_di),
            whole(local_di, D),
            whole(D, local_di),
            whole(1, local_di),
        ],
        out_shape=[
            shape((length, D), bf16),
            shape((length, local_di), bf16),
            shape((length, local_di), bf16),
            shape((local_di, D), bf16),
            shape((D, local_di), bf16),
            shape((1, local_di), f32),
        ],
        scratch_shapes=[pltpu.VMEM((local_di, D), f32), pltpu.VMEM((D, local_di), f32)],
        compiler_params=kernel_params(),
        cost_estimate=pl.CostEstimate(
            flops=4_000_000_000, bytes_accessed=15_000_000, transcendentals=500_000
        ),
        name="middle",
    )(scanned, gating, d_gnorm, cot, normed, scale, slope, out_low, gain_two)


def run_backward(
    hidden,
    normed,
    conv_in,
    conv_pre,
    dt_raw,
    y,
    states,
    d_scanned,
    d_gating,
    in_low,
    dt_weight,
    kernel,
    heads_vectors,
    expand,
):
    length, local_di = y.shape
    chunks = length // BLOCK
    channels = conv_in.shape[1]
    lanes = dt_weight.shape[1]
    shape = jax.ShapeDtypeStruct
    f32, bf16 = jnp.float32, jnp.bfloat16

    def back(extent):
        return wide_back(extent, chunks)

    return pl.pallas_call(
        backward_kernel,
        grid=(chunks,),
        in_specs=[
            back(D),
            back(D),
            back(channels),
            back(channels),
            back(lanes),
            back(local_di),
            pl.BlockSpec((1, STATE, local_di), lambda q: (chunks - 1 - q, 0, 0)),
            back(local_di),
            back(local_di),
            whole(D, local_di + channels),
            whole(D, lanes),
            whole(WIDTH, channels),
            whole(1, lanes),
            whole(1, lanes),
            whole(1, local_di),
            whole(lanes, local_di),
        ],
        out_specs=[
            back(D),
            whole(D, channels),
            whole(D, lanes),
            whole(1, D),
            whole(WIDTH, channels),
            whole(1, channels),
            whole(1, local_di),
            whole(2, lanes),
        ],
        out_shape=[
            shape((length, D), bf16),
            shape((D, channels), bf16),
            shape((D, lanes), bf16),
            shape((1, D), f32),
            shape((WIDTH, channels), f32),
            shape((1, channels), f32),
            shape((1, local_di), f32),
            shape((2, lanes), f32),
        ],
        scratch_shapes=[
            pltpu.VMEM((BLOCK + 8, channels), f32),
            pltpu.VMEM((STATE, local_di), f32),
            pltpu.VMEM((STATE, local_di), f32),
            pltpu.VMEM((D, channels), f32),
            pltpu.VMEM((D, lanes), f32),
        ],
        compiler_params=kernel_params(),
        cost_estimate=pl.CostEstimate(
            flops=16_000_000_000, bytes_accessed=25_000_000, transcendentals=10_000_000
        ),
        name="backward",
    )(
        hidden,
        normed,
        conv_in,
        conv_pre,
        dt_raw,
        y,
        states,
        d_scanned,
        d_gating,
        in_low,
        dt_weight,
        kernel,
        *heads_vectors,
        expand,
    )


def adamw_step(weight, first, second, grad, rate, decay):
    first_new = beta_one * first + (1.0 - beta_one) * grad
    second_new = beta_two * second + (1.0 - beta_two) * grad * grad
    fix_one = 1.0 - beta_one**STEP
    fix_two = 1.0 - beta_two**STEP
    normalized = first_new / fix_one / (jnp.sqrt(second_new / fix_two) + adam_eps)
    return (first_new, second_new, weight - rate * (normalized + decay * weight))


def pick_heads(values, axis, width, index, groups):
    shape = values.shape
    split = shape[:axis] + (HEADS // groups, groups, width) + shape[axis + 1 :]
    taken = lax.dynamic_index_in_dim(values.reshape(split), index, axis + 1, keepdims=False)
    return taken.reshape(shape[:axis] + (HEADS // groups * width,) + shape[axis + 1 :])


def merge_heads(stacked, axis, width):
    groups = stacked.shape[0]
    shape = stacked.shape[1:]
    split = (groups,) + shape[:axis] + (HEADS // groups, width) + shape[axis + 1 :]
    moved = jnp.moveaxis(stacked.reshape(split), 0, axis + 1)
    return moved.reshape(shape[:axis] + (HEADS * width,) + shape[axis + 1 :])


def seq_sum_rows(partial):
    return lax.psum_scatter(
        partial.astype(jnp.bfloat16), "seq", scatter_dimension=0, tiled=True
    ).astype(jnp.float32)


def gather_out(out_low, seq_index, groups):
    rows = out_low.shape[0]
    if rows % (groups * HEADDIM) == 0:
        mine = pick_rows(out_low, seq_index, groups)
        return lax.all_gather(mine, "wshard", axis=0, tiled=True)
    whole = lax.all_gather(out_low, "wshard", axis=0, tiled=True)
    return pick_heads(whole, 0, HEADDIM, seq_index, groups)


def pick_rows(values, seq_index, groups):
    rows = values.shape[0]
    split = values.reshape(rows // (groups * HEADDIM), groups, HEADDIM, values.shape[1])
    return lax.dynamic_index_in_dim(split, seq_index, 1, keepdims=False).reshape(
        rows // groups, values.shape[1]
    )


def sum_out_grad(grad, rows, seq_index, groups):
    grad = grad.astype(jnp.bfloat16)
    if rows % (groups * HEADDIM) == 0:
        mine = lax.psum_scatter(grad, "wshard", scatter_dimension=0, tiled=True)
        every = lax.all_gather(mine, "seq", axis=0, tiled=False)
        split = every.reshape(groups, rows // (groups * HEADDIM), HEADDIM, grad.shape[1])
        return jnp.moveaxis(split, 0, 1).reshape(rows, grad.shape[1]).astype(jnp.float32)
    blocks = grad.reshape(HEADS // groups, 1, HEADDIM, grad.shape[1])
    here = (jnp.arange(groups) == seq_index)[None, :, None, None]
    spread = jnp.where(here, blocks, jnp.zeros((), jnp.bfloat16)).reshape(DI, grad.shape[1])
    mine = lax.psum_scatter(spread, "wshard", scatter_dimension=0, tiled=True)
    return lax.psum(mine.astype(jnp.float32), "seq")


def shards(
    block_in,
    cotangent,
    in_weight,
    in_first,
    in_second,
    out_weight,
    out_first,
    out_second,
    vec_weight,
    vec_first,
    vec_second,
):
    rows_here = block_in.shape[1]
    groups = lax.axis_size("seq")
    seq_index = lax.axis_index("seq")
    local_heads = HEADS // groups
    local_di = DI // groups
    hidden_rows = block_in.reshape(rows_here, D)
    cot_rows = cotangent.reshape(rows_here, D)
    gain_one, gain_two, kernel, conv_bias, a_log, dt_bias, d_skip = split_vector(vec_weight)

    def heads_of(values, axis, width):
        return pick_heads(values, axis, width, seq_index, groups)

    in_low = in_weight.astype(jnp.bfloat16)
    in_mine = jnp.concatenate(
        [
            heads_of(in_low[:, :DI], 1, HEADDIM),
            heads_of(in_low[:, DI : 2 * DI], 1, HEADDIM),
            in_low[:, 2 * DI : 2 * DI + 2 * STATE],
            heads_of(in_low[:, DI + CONVCH :], 1, 1),
        ],
        1,
    )
    hidden_low = lax.all_gather(hidden_rows, "seq", axis=0, tiled=True)
    in_mine = lax.all_gather(in_mine, "wshard", axis=0, tiled=True)
    cot = lax.all_gather(cot_rows, "seq", axis=0, tiled=True)
    out_mine = gather_out(out_weight.astype(jnp.bfloat16), seq_index, groups)
    my_gain_two = heads_of(gain_two, 0, HEADDIM)
    my_kernel = jnp.concatenate([heads_of(kernel[:, :DI], 1, HEADDIM), kernel[:, DI:]], 1)
    my_bias = jnp.concatenate([heads_of(conv_bias[:DI], 0, HEADDIM), conv_bias[DI:]], 0)

    lanes = 128
    in_main = in_mine[:, : 2 * local_di + 2 * STATE]
    dt_weight = jnp.pad(in_mine[:, 2 * local_di + 2 * STATE :], ((0, 0), (0, lanes - local_heads)))
    my_skip = heads_of(d_skip, 0, 1)

    def on_lanes(values):
        return jnp.pad(values, (0, lanes - local_heads))[None, :]

    heads_vectors = (
        on_lanes(heads_of(a_log, 0, 1)),
        on_lanes(heads_of(dt_bias, 0, 1)),
        jnp.repeat(my_skip, HEADDIM)[None, :],
    )
    expand = (
        jnp.arange(lanes)[:, None] == jnp.arange(local_di)[None, :] // HEADDIM
    ).astype(jnp.float32)
    (
        normed_low,
        gating,
        conv_in,
        conv_pre,
        dt_raw,
        y,
        scanned,
        states,
        d_gnorm,
        sums,
    ) = run_forward(
        hidden_low,
        cot,
        in_main,
        dt_weight,
        out_mine,
        (gain_one[None, :], my_gain_two[None, :]),
        (my_kernel, my_bias[None, :]),
        heads_vectors,
        expand,
    )
    sums = jnp.sum(lax.all_gather(sums[:2], "seq", axis=0, tiled=False), axis=0) / DI
    scale = lax.rsqrt(sums[0] + norm_eps)
    slope = scale * scale * sums[1]
    block_part, d_gating, d_scanned, grad_out, grad_gate, d_gain_two = run_middle(
        scanned,
        gating,
        d_gnorm,
        cot,
        normed_low,
        scale[:, None],
        slope[:, None],
        out_mine,
        my_gain_two[None, :],
    )
    block_out = hidden_rows.astype(jnp.float32) + seq_sum_rows(block_part)
    (
        d_normed_part,
        grad_conv,
        grad_dt,
        d_gain_one,
        d_kernel,
        d_conv_bias,
        d_skip_wide,
        d_head,
    ) = run_backward(
        hidden_low,
        normed_low,
        conv_in,
        conv_pre,
        dt_raw,
        y,
        states,
        d_scanned,
        d_gating,
        in_main,
        dt_weight,
        my_kernel,
        heads_vectors,
        expand,
    )
    d_gain_one = d_gain_one[0]
    d_gain_two = d_gain_two[0]
    d_conv_bias = d_conv_bias[0]
    d_a_log = d_head[0, :local_heads]
    d_dt_bias = d_head[1, :local_heads]
    d_skip_part = jnp.sum(d_skip_wide.reshape(local_heads, HEADDIM), axis=1)
    grad_in = jnp.concatenate([grad_gate, grad_conv, grad_dt[:, :local_heads]], 1)
    d_normed = seq_sum_rows(d_normed_part)
    own_hidden = hidden_rows.astype(jnp.float32)
    own_scale = lax.rsqrt(jnp.mean(own_hidden * own_hidden, axis=-1, keepdims=True) + norm_eps)
    own_unit = own_hidden * own_scale
    d_own = d_normed * gain_one[None, :]
    d_hidden = own_scale * (
        d_own - own_unit * jnp.mean(d_own * own_unit, axis=-1, keepdims=True)
    )
    block_grad = cot_rows.astype(jnp.float32) + d_hidden

    def spread_heads(values, axis, width):
        here = (jnp.arange(groups) == seq_index).reshape((groups,) + (1,) * values.ndim)
        return merge_heads(jnp.where(here, values[None], 0.0), axis, width)

    vec_grad = jnp.concatenate(
        [
            d_gain_one,
            spread_heads(d_gain_two, 0, HEADDIM),
            jnp.concatenate(
                [spread_heads(d_kernel[:, :local_di], 1, HEADDIM), d_kernel[:, local_di:]], 1
            ).reshape(-1),
            spread_heads(d_conv_bias[:local_di], 0, HEADDIM),
            d_conv_bias[local_di:],
            spread_heads(d_a_log, 0, 1),
            spread_heads(d_dt_bias, 0, 1),
            spread_heads(d_skip_part, 0, 1),
        ]
    )
    vec_total = lax.psum(vec_grad, ("seq", "wshard"))
    vec_first_new, vec_second_new, vec_weight_new = adamw_step(
        vec_weight, vec_first, vec_second, vec_total, vector_rate, 0.0
    )
    out_total = sum_out_grad(grad_out, out_weight.shape[0], seq_index, groups)
    in_part = lax.psum_scatter(
        grad_in.astype(jnp.bfloat16), "wshard", scatter_dimension=0, tiled=True
    )
    in_every = lax.all_gather(in_part, "seq", axis=0, tiled=False).astype(jnp.float32)
    both_end = 2 * local_di + 2 * STATE
    in_total = jnp.concatenate(
        [
            merge_heads(in_every[:, :, :local_di], 1, HEADDIM),
            merge_heads(in_every[:, :, local_di : 2 * local_di], 1, HEADDIM),
            jnp.sum(in_every[:, :, 2 * local_di : both_end], axis=0),
            merge_heads(in_every[:, :, both_end:], 1, 1),
        ],
        1,
    )
    in_first_new, in_second_new, in_weight_new = adamw_step(
        in_weight, in_first, in_second, in_total, matrix_rate, matrix_decay
    )
    out_first_new, out_second_new, out_weight_new = adamw_step(
        out_weight, out_first, out_second, out_total, matrix_rate, matrix_decay
    )
    return (
        block_out.reshape(1, rows_here, D),
        block_grad.reshape(1, rows_here, D),
        in_first_new,
        in_second_new,
        in_weight_new,
        out_first_new,
        out_second_new,
        out_weight_new,
        vec_first_new,
        vec_second_new,
        vec_weight_new,
    )


def solution(mesh):
    return jax.shard_map(
        shards,
        mesh=mesh,
        in_specs=(
            P("wshard", "seq", None),
            P("wshard", "seq", None),
            P("wshard", None),
            P("wshard", None),
            P("wshard", None),
            P("wshard", None),
            P("wshard", None),
            P("wshard", None),
            P(),
            P(),
            P(),
        ),
        out_specs=(
            P("wshard", "seq", None),
            P("wshard", "seq", None),
            P("wshard", None),
            P("wshard", None),
            P("wshard", None),
            P("wshard", None),
            P("wshard", None),
            P("wshard", None),
            P(),
            P(),
            P(),
        ),
        check_vma=False,
    )
```

```python
import jax
import jax.numpy as jnp
from jax import lax
from jax.experimental import pallas as pl
from jax.experimental.pallas import tpu as pltpu
from jax.sharding import PartitionSpec as P

D = 1024
HEADS = 32
HEADDIM = 64
STATE = 128
WIDTH = 4
BLOCK = 256
STEP = 10
DI = 2048
CONVCH = 2304


precise = lax.Precision.HIGHEST
norm_eps = 1e-05
beta_one = 0.9
beta_two = 0.95
adam_eps = 1e-08
matrix_rate = 0.05
matrix_decay = 0.1
vector_rate = 0.5


def rms_scale(values):
    return values * lax.rsqrt(jnp.mean(values * values, axis=-1, keepdims=True) + norm_eps)


def split_vector(vector):
    extents = [D, DI, WIDTH * CONVCH, CONVCH, HEADS, HEADS, HEADS]
    pieces = []
    offset = 0
    for extent in extents:
        pieces.append(vector[offset : offset + extent])
        offset = offset + extent
    pieces[2] = pieces[2].reshape(WIDTH, CONVCH)
    return pieces


def wide(extent):
    return pl.BlockSpec((BLOCK, extent), lambda q: (q, 0))


def wide_back(extent, count):
    return pl.BlockSpec((BLOCK, extent), lambda q: (count - 1 - q, 0))


def whole(*shape):
    return pl.BlockSpec(shape, lambda q: (0,) * len(shape))


def dot_nt(left, right, precision=None):
    return lax.dot_general(
        left,
        right,
        (((1,), (1,)), ((), ())),
        precision=precision,
        preferred_element_type=jnp.float32,
    )


def dot_tn(left, right):
    return lax.dot_general(
        left, right, (((0,), (0,)), ((), ())), preferred_element_type=jnp.float32
    )


def dot_nn(left, right, precision=None):
    return jnp.dot(left, right, precision=precision, preferred_element_type=jnp.float32)


def sigmoid(values):
    return 1.0 / (1.0 + jnp.exp(-values))


def low(values):
    return values.astype(jnp.bfloat16)


def lower_mask():
    rows = lax.broadcasted_iota(jnp.int32, (BLOCK, BLOCK), 0)
    return rows >= lax.broadcasted_iota(jnp.int32, (BLOCK, BLOCK), 1)


def decay_sums(dt_raw, dt_bias, a_log, expand):
    shifted = dt_raw + dt_bias
    step = jnp.maximum(shifted, 0.0) + jnp.log1p(jnp.exp(-jnp.abs(shifted)))
    log_decay = -jnp.exp(a_log) * step
    ones = jnp.where(lower_mask(), 1.0, 0.0)
    running = dot_nn(ones, log_decay, precise)
    step_wide = dot_nn(step, expand, precise)
    running_wide = dot_nn(running, expand, precise)
    return shifted, step, log_decay, running, step_wide, running_wide


def forward_kernel(
    hidden_ref,
    conv_weight_ref,
    dt_weight_ref,
    gain_one_ref,
    conv_ref,
    bias_ref,
    a_log_ref,
    dt_bias_ref,
    skip_ref,
    expand_ref,
    normed_ref,
    conv_in_ref,
    conv_pre_ref,
    dt_ref,
    y_ref,
    scanned_ref,
    state_ref,
    ext,
    state,
):
    local_di = y_ref.shape[1]
    heads = local_di // HEADDIM

    @pl.when(pl.program_id(0) == 0)
    def _():
        ext[0:8, :] = jnp.zeros((8, ext.shape[1]), jnp.float32)
        state[...] = jnp.zeros_like(state)

    hidden = hidden_ref[...].astype(jnp.float32)
    normed = low(rms_scale(hidden) * gain_one_ref[...])
    normed_ref[...] = normed
    conv_in = dot_nn(normed, conv_weight_ref[...])
    conv_in_ref[...] = conv_in
    ext[8 : 8 + BLOCK, :] = conv_in
    conv_pre = bias_ref[...] + conv_ref[WIDTH - 1 : WIDTH, :] * conv_in
    for tap in range(WIDTH - 1):
        first = 8 - WIDTH + 1 + tap
        conv_pre = conv_pre + conv_ref[tap : tap + 1, :] * ext[first : first + BLOCK, :]
    conv_pre_ref[...] = conv_pre
    ext[8 - WIDTH + 1 : 8, :] = ext[8 + BLOCK - WIDTH + 1 : 8 + BLOCK, :]
    conv_low = low(conv_pre * sigmoid(conv_pre))
    inner = conv_low[:, :local_di]
    b_rows = conv_low[:, local_di : local_di + STATE]
    c_rows = conv_low[:, local_di + STATE :]
    dt_raw = low(dot_nn(normed, dt_weight_ref[...])).astype(jnp.float32)
    dt_ref[...] = dt_raw

    _, _, _, running, step_wide, running_wide = decay_sums(
        dt_raw, dt_bias_ref[...], a_log_ref[...], expand_ref[...]
    )
    running_t = running.T
    b_t = low(b_rows.astype(jnp.float32).T)
    scores = dot_nn(c_rows, b_t)
    mask = lower_mask()
    inner_wide = inner.astype(jnp.float32)
    stepped = step_wide * inner_wide
    stepped_low = low(stepped)
    first_half = lax.broadcasted_iota(jnp.int32, (BLOCK, 2 * HEADDIM), 1) < HEADDIM
    zero = jnp.zeros((), jnp.bfloat16)
    state_ref[...] = state[...].reshape(state_ref.shape)
    held = state[...]
    carried = jnp.exp(running_wide) * dot_nn(c_rows, low(held))
    for pair in range(heads // 2):
        span = slice(pair * 2 * HEADDIM, (pair + 1) * 2 * HEADDIM)
        both = stepped_low[:, span]
        total = carried[:, span]
        for half in range(2):
            head = 2 * pair + half
            differ = running[:, head : head + 1] - running_t[head : head + 1, :]
            mixed = low(jnp.exp(jnp.where(mask, differ, -jnp.inf)) * scores)
            mine = jnp.where(first_half if half == 0 else ~first_half, both, zero)
            total = total + dot_nn(mixed, mine)
        y_ref[:, span] = total
    last = running_wide[BLOCK - 1 : BLOCK, :]
    to_end = jnp.exp(last - running_wide)
    state[...] = jnp.exp(last) * held + dot_nn(b_t, low(to_end * stepped))
    scanned_ref[...] = low(y_ref[...] + skip_ref[...] * inner_wide)


def out_halves(packed_ref):
    packed = packed_ref[...].reshape(-1, 2, HEADDIM, packed_ref.shape[1])
    extent = packed_ref.shape[0] // 2
    return (
        packed[:, 0].reshape(extent, packed_ref.shape[1]),
        packed[:, 1].reshape(extent, packed_ref.shape[1]),
    )


def gate_kernel(
    normed_ref,
    scanned_ref,
    cot_ref,
    gate_weight_ref,
    out_ref,
    gain_two_ref,
    gating_ref,
    d_gnorm_ref,
    sums_ref,
):
    local_di = gating_ref.shape[1]
    gating = dot_nn(normed_ref[...], gate_weight_ref[...])
    gating_ref[...] = gating
    out_left, out_right = out_halves(out_ref)
    half = out_left.shape[1]
    d_gnorm = dot_nt(cot_ref[:, :half], out_left) + dot_nt(cot_ref[:, half:], out_right)
    d_gnorm_ref[...] = d_gnorm
    gated = scanned_ref[...].astype(jnp.float32) * (gating * sigmoid(gating))
    ones = jnp.ones((8, local_di), jnp.float32)
    squares = dot_nt(ones, gated * gated, precise)
    products = dot_nt(ones, d_gnorm * gain_two_ref[...] * gated, precise)
    sums_ref[...] = jnp.where(
        lax.broadcasted_iota(jnp.int32, squares.shape, 0) == 0, squares, products
    )


def middle_kernel(
    scanned_ref,
    gating_ref,
    d_gnorm_ref,
    cot_ref,
    normed_ref,
    scale_ref,
    slope_ref,
    out_ref,
    gain_two_ref,
    block_ref,
    d_gating_ref,
    d_scanned_ref,
    grad_ref,
    d_gain_two_ref,
    left_sum,
    right_sum,
    gate_sum,
):
    chunk = pl.program_id(0)

    @pl.when(chunk == 0)
    def _():
        left_sum[...] = jnp.zeros_like(left_sum)
        right_sum[...] = jnp.zeros_like(right_sum)
        gate_sum[...] = jnp.zeros_like(gate_sum)
        d_gain_two_ref[...] = jnp.zeros_like(d_gain_two_ref)

    gating = gating_ref[...]
    open_part = sigmoid(gating)
    gate = gating * open_part
    scanned = scanned_ref[...].astype(jnp.float32)
    scale = scale_ref[:, :1]
    unit = scanned * gate * scale
    d_gnorm = d_gnorm_ref[...]
    gain_two = gain_two_ref[...]
    gnorm = low(unit * gain_two)
    out_left, out_right = out_halves(out_ref)
    half = out_left.shape[1]
    block_ref[:, :half] = low(dot_nn(gnorm, out_left))
    block_ref[:, half:] = low(dot_nn(gnorm, out_right))
    left_sum[...] += dot_tn(gnorm, cot_ref[:, :half])
    right_sum[...] += dot_tn(gnorm, cot_ref[:, half:])
    d_gain_two_ref[...] += jnp.sum(d_gnorm * unit, axis=0, keepdims=True)
    d_gated = scale * (d_gnorm * gain_two) - unit * slope_ref[:, :1]
    d_gating = low(d_gated * scanned * (open_part * (1.0 + gating * (1.0 - open_part))))
    d_gating_ref[...] = d_gating
    d_scanned_ref[...] = low(d_gated * gate)
    gate_sum[...] += dot_tn(normed_ref[...], d_gating)

    @pl.when(chunk == pl.num_programs(0) - 1)
    def _():
        local_di = gating_ref.shape[1]
        grad_ref[:, :local_di] = low(gate_sum[...])
        for head in range(local_di // HEADDIM):
            rows = slice(head * HEADDIM, (head + 1) * HEADDIM)
            base = 2 * head * HEADDIM
            grad_ref[base : base + HEADDIM, local_di:] = low(left_sum[rows, :])
            grad_ref[base + HEADDIM : base + 2 * HEADDIM, local_di:] = low(right_sum[rows, :])


def backward_kernel(
    normed_ref,
    conv_in_ref,
    conv_pre_ref,
    dt_ref,
    y_ref,
    state_ref,
    d_scanned_ref,
    conv_ref,
    a_log_ref,
    dt_bias_ref,
    skip_ref,
    expand_ref,
    d_rest_ref,
    grad_ref,
    d_kernel_ref,
    d_conv_bias_ref,
    d_skip_ref,
    d_head_ref,
    ext,
    d_state,
    later_state,
    rest_sum,
):
    local_di = y_ref.shape[1]
    heads = local_di // HEADDIM
    chunk = pl.program_id(0)

    @pl.when(chunk == 0)
    def _():
        ext[BLOCK : BLOCK + 8, :] = jnp.zeros((8, ext.shape[1]), jnp.float32)
        d_state[...] = jnp.zeros_like(d_state)
        later_state[...] = jnp.zeros_like(later_state)
        rest_sum[...] = jnp.zeros_like(rest_sum)
        d_kernel_ref[...] = jnp.zeros_like(d_kernel_ref)
        d_conv_bias_ref[...] = jnp.zeros_like(d_conv_bias_ref)
        d_skip_ref[...] = jnp.zeros_like(d_skip_ref)
        d_head_ref[...] = jnp.zeros_like(d_head_ref)

    expand = expand_ref[...]
    conv_pre = conv_pre_ref[...]
    open_part = sigmoid(conv_pre)
    conv_low = low(conv_pre * open_part)
    inner = conv_low[:, :local_di].astype(jnp.float32)
    b_rows = conv_low[:, local_di : local_di + STATE]
    c_rows = conv_low[:, local_di + STATE :]
    a_log = a_log_ref[...]
    shifted, _, log_decay, running, step_wide, running_wide = decay_sums(
        dt_ref[...], dt_bias_ref[...], a_log, expand
    )
    running_t = running.T
    b_t = low(b_rows.astype(jnp.float32).T)
    c_t = low(c_rows.astype(jnp.float32).T)
    scores = dot_nn(c_rows, b_t)
    scores_t = dot_nn(b_rows, c_t)
    mask = lower_mask()
    rows = lax.broadcasted_iota(jnp.int32, (BLOCK, BLOCK), 0)
    mask_t = rows <= lax.broadcasted_iota(jnp.int32, (BLOCK, BLOCK), 1)
    d_y_low = d_scanned_ref[...]
    d_y = d_y_low.astype(jnp.float32)
    stepped_low = low(step_wide * inner)
    stepped = stepped_low.astype(jnp.float32)
    last = running_wide[BLOCK - 1 : BLOCK, :]
    to_end = jnp.exp(last - running_wide)
    d_later = d_state[...]
    d_later_low = low(d_later)
    held = state_ref[...].reshape(d_state.shape)
    decayed_dy = low(jnp.exp(running_wide) * d_y)
    d_c = dot_nt(decayed_dy, low(held))
    d_b = dot_nt(low(to_end * stepped), d_later_low)
    d_stepped = to_end * dot_nn(b_rows, d_later_low)
    cross = jnp.sum(later_state[...] * d_later, axis=0, keepdims=True)
    d_state[...] = jnp.exp(last) * d_later + dot_nn(c_t, decayed_dy)
    later_state[...] = held
    first_half = lax.broadcasted_iota(jnp.int32, (BLOCK, 2 * HEADDIM), 1) < HEADDIM
    zero = jnp.zeros((), jnp.bfloat16)
    d_scores = jnp.zeros((BLOCK, BLOCK), jnp.float32)
    pieces = []
    for pair in range(heads // 2):
        span = slice(pair * 2 * HEADDIM, (pair + 1) * 2 * HEADDIM)
        total = d_stepped[:, span]
        for half in range(2):
            head = 2 * pair + half
            mine = jnp.where(first_half if half == 0 else ~first_half, d_y_low[:, span], zero)
            column = running[:, head : head + 1]
            row = running_t[head : head + 1, :]
            decay = jnp.exp(jnp.where(mask, column - row, -jnp.inf))
            decay_t = jnp.exp(jnp.where(mask_t, row - column, -jnp.inf))
            d_scores = d_scores + dot_nt(mine, stepped_low[:, span]) * decay
            total = total + dot_nn(low(decay_t * scores_t), mine)
        pieces.append(total)
    d_stepped = jnp.concatenate(pieces, 1)
    d_scores_low = low(d_scores)
    d_c = d_c + dot_nn(d_scores_low, b_rows)
    d_b = d_b + dot_nn(low(d_scores.T), c_rows)
    d_inner = step_wide * d_stepped + skip_ref[...] * d_y
    d_running = dot_nt(d_y * y_ref[...] - d_stepped * stepped, expand, precise)
    upper = jnp.where(mask_t, 1.0, 0.0)
    d_log = dot_nn(upper, d_running, precise) + dot_nt(cross, expand, precise)
    d_step = dot_nt(d_stepped * inner, expand, precise) - jnp.exp(a_log) * d_log
    d_dt = d_step * sigmoid(shifted)
    d_head_ref[0:1, :] += jnp.sum(d_log * log_decay, axis=0, keepdims=True)
    d_head_ref[1:2, :] += jnp.sum(d_dt, axis=0, keepdims=True)
    d_skip_ref[...] += jnp.sum(d_y * inner, axis=0, keepdims=True)

    d_conv_out = jnp.concatenate([d_inner, d_b, d_c], 1)
    d_pre = d_conv_out * (open_part * (1.0 + conv_pre * (1.0 - open_part)))
    ext[0:BLOCK, :] = d_pre
    d_conv_bias_ref[...] += jnp.sum(d_pre, axis=0, keepdims=True)
    conv_in = conv_in_ref[...]
    d_conv_in = jnp.zeros_like(conv_in)
    for tap in range(WIDTH):
        moved = ext[WIDTH - 1 - tap : WIDTH - 1 - tap + BLOCK, :]
        d_conv_in = d_conv_in + conv_ref[tap : tap + 1, :] * moved
        d_kernel_ref[tap : tap + 1, :] += jnp.sum(moved * conv_in, axis=0, keepdims=True)
    ext[BLOCK : BLOCK + 8, :] = ext[0:8, :]
    d_rest = jnp.concatenate([low(d_conv_in), low(d_dt)], 1)
    d_rest_ref[...] = d_rest
    rest_sum[...] += dot_tn(normed_ref[...], d_rest)

    @pl.when(chunk == pl.num_programs(0) - 1)
    def _():
        grad_ref[...] = low(rest_sum[...])


def normed_kernel(
    hidden_ref,
    d_gating_ref,
    d_rest_ref,
    gate_weight_ref,
    rest_weight_ref,
    d_normed_ref,
    d_gain_one_ref,
):
    @pl.when(pl.program_id(0) == 0)
    def _():
        d_gain_one_ref[...] = jnp.zeros_like(d_gain_one_ref)

    d_normed = dot_nt(d_gating_ref[...], gate_weight_ref[...])
    d_normed = d_normed + dot_nt(d_rest_ref[...], rest_weight_ref[...])
    d_normed_ref[...] = low(d_normed)
    unit = rms_scale(hidden_ref[...].astype(jnp.float32))
    d_gain_one_ref[...] += jnp.sum(d_normed * unit, axis=0, keepdims=True)


def kernel_params():
    return pltpu.CompilerParams(
        dimension_semantics=("arbitrary",), vmem_limit_bytes=50 * 1024 * 1024
    )


def cost(flops, moved, transcendentals):
    return pl.CostEstimate(flops=flops, bytes_accessed=moved, transcendentals=transcendentals)


def run_forward(hidden, rest_weight, gain_one, conv, heads_vectors, expand):
    length = hidden.shape[0]
    chunks = length // BLOCK
    lanes, local_di = expand.shape
    channels = rest_weight.shape[1] - lanes
    shape = jax.ShapeDtypeStruct
    f32, bf16 = jnp.float32, jnp.bfloat16
    return pl.pallas_call(
        forward_kernel,
        grid=(chunks,),
        in_specs=[
            wide(D),
            whole(D, channels),
            pl.BlockSpec((D, lanes), lambda q: (0, channels // lanes)),
            whole(1, D),
            whole(WIDTH, channels),
            whole(1, channels),
            whole(1, lanes),
            whole(1, lanes),
            whole(1, local_di),
            whole(lanes, local_di),
        ],
        out_specs=[
            wide(D),
            wide(channels),
            wide(channels),
            wide(lanes),
            wide(local_di),
            wide(local_di),
            pl.BlockSpec((1, STATE, local_di), lambda q: (q, 0, 0)),
        ],
        out_shape=[
            shape((length, D), bf16),
            shape((length, channels), f32),
            shape((length, channels), f32),
            shape((length, lanes), f32),
            shape((length, local_di), f32),
            shape((length, local_di), bf16),
            shape((chunks, STATE, local_di), f32),
        ],
        scratch_shapes=[
            pltpu.VMEM((8 + BLOCK, channels), f32),
            pltpu.VMEM((STATE, local_di), f32),
        ],
        compiler_params=kernel_params(),
        cost_estimate=cost(6_000_000_000, 30_000_000, 8_000_000),
        name="forward",
    )(hidden, rest_weight, rest_weight, gain_one, *conv, *heads_vectors, expand)


def run_gate(normed, scanned, cot, gate_out, gain_two):
    length, local_di = scanned.shape
    half = D // 2
    shape = jax.ShapeDtypeStruct
    return pl.pallas_call(
        gate_kernel,
        grid=(length // BLOCK,),
        in_specs=[
            wide(D),
            wide(local_di),
            wide(D),
            pl.BlockSpec((D, local_di), lambda q: (0, 0)),
            pl.BlockSpec((2 * local_di, half), lambda q: (0, local_di // half)),
            whole(1, local_di),
        ],
        out_specs=[
            wide(local_di),
            wide(local_di),
            pl.BlockSpec((8, BLOCK), lambda q: (0, q)),
        ],
        out_shape=[
            shape((length, local_di), jnp.float32),
            shape((length, local_di), jnp.float32),
            shape((8, length), jnp.float32),
        ],
        compiler_params=kernel_params(),
        cost_estimate=cost(2_500_000_000, 12_000_000, 1_000_000),
        name="gate",
    )(normed, scanned, cot, gate_out, gate_out, gain_two)


def run_middle(scanned, gating, d_gnorm, cot, normed, scale, slope, gate_out, gain_two):
    length, local_di = scanned.shape
    half = D // 2
    shape = jax.ShapeDtypeStruct
    f32, bf16 = jnp.float32, jnp.bfloat16
    return pl.pallas_call(
        middle_kernel,
        grid=(length // BLOCK,),
        in_specs=[
            wide(local_di),
            wide(local_di),
            wide(local_di),
            wide(D),
            wide(D),
            wide(1),
            wide(1),
            pl.BlockSpec((2 * local_di, half), lambda q: (0, local_di // half)),
            whole(1, local_di),
        ],
        out_specs=[
            wide(D),
            wide(local_di),
            wide(local_di),
            whole(D, local_di + half),
            whole(1, local_di),
        ],
        out_shape=[
            shape((length, D), bf16),
            shape((length, local_di), bf16),
            shape((length, local_di), bf16),
            shape((D, local_di + half), bf16),
            shape((1, local_di), f32),
        ],
        scratch_shapes=[
            pltpu.VMEM((local_di, half), f32),
            pltpu.VMEM((local_di, half), f32),
            pltpu.VMEM((D, local_di), f32),
        ],
        compiler_params=kernel_params(),
        cost_estimate=cost(4_000_000_000, 15_000_000, 500_000),
        name="middle",
    )(scanned, gating, d_gnorm, cot, normed, scale, slope, gate_out, gain_two)


def run_backward(
    normed, conv_in, conv_pre, dt_raw, y, states, d_scanned, kernel, heads_vectors, expand
):
    length, local_di = y.shape
    chunks = length // BLOCK
    channels = conv_in.shape[1]
    lanes = expand.shape[0]
    shape = jax.ShapeDtypeStruct
    f32, bf16 = jnp.float32, jnp.bfloat16

    def back(extent):
        return wide_back(extent, chunks)

    return pl.pallas_call(
        backward_kernel,
        grid=(chunks,),
        in_specs=[
            back(D),
            back(channels),
            back(channels),
            back(lanes),
            back(local_di),
            pl.BlockSpec((1, STATE, local_di), lambda q: (chunks - 1 - q, 0, 0)),
            back(local_di),
            whole(WIDTH, channels),
            whole(1, lanes),
            whole(1, lanes),
            whole(1, local_di),
            whole(lanes, local_di),
        ],
        out_specs=[
            back(channels + lanes),
            whole(D, channels + lanes),
            whole(WIDTH, channels),
            whole(1, channels),
            whole(1, local_di),
            whole(2, lanes),
        ],
        out_shape=[
            shape((length, channels + lanes), bf16),
            shape((D, channels + lanes), bf16),
            shape((WIDTH, channels), f32),
            shape((1, channels), f32),
            shape((1, local_di), f32),
            shape((2, lanes), f32),
        ],
        scratch_shapes=[
            pltpu.VMEM((BLOCK + 8, channels), f32),
            pltpu.VMEM((STATE, local_di), f32),
            pltpu.VMEM((STATE, local_di), f32),
            pltpu.VMEM((D, channels + lanes), f32),
        ],
        compiler_params=kernel_params(),
        cost_estimate=cost(14_000_000_000, 40_000_000, 10_000_000),
        name="backward",
    )(normed, conv_in, conv_pre, dt_raw, y, states, d_scanned, kernel, *heads_vectors, expand)


def run_normed(hidden, d_gating, d_rest, gate_out, rest_weight):
    length, local_di = d_gating.shape
    rest = d_rest.shape[1]
    return pl.pallas_call(
        normed_kernel,
        grid=(length // BLOCK,),
        in_specs=[wide(D), wide(local_di), wide(rest), whole(D, local_di), whole(D, rest)],
        out_specs=[wide(D), whole(1, D)],
        out_shape=[
            jax.ShapeDtypeStruct((length, D), jnp.bfloat16),
            jax.ShapeDtypeStruct((1, D), jnp.float32),
        ],
        compiler_params=kernel_params(),
        cost_estimate=cost(3_000_000_000, 9_000_000, 1000),
        name="normed",
    )(hidden, d_gating, d_rest, gate_out, rest_weight)


def adamw_step(weight, first, second, grad, rate, decay):
    first_new = beta_one * first + (1.0 - beta_one) * grad
    second_new = beta_two * second + (1.0 - beta_two) * grad * grad
    fix_one = 1.0 - beta_one**STEP
    fix_two = 1.0 - beta_two**STEP
    normalized = first_new / fix_one / (jnp.sqrt(second_new / fix_two) + adam_eps)
    return (first_new, second_new, weight - rate * (normalized + decay * weight))


def pick_heads(values, axis, width, index, groups):
    shape = values.shape
    split = shape[:axis] + (HEADS // groups, groups, width) + shape[axis + 1 :]
    taken = lax.dynamic_index_in_dim(values.reshape(split), index, axis + 1, keepdims=False)
    return taken.reshape(shape[:axis] + (HEADS // groups * width,) + shape[axis + 1 :])


def merge_heads(stacked, axis, width):
    groups = stacked.shape[0]
    shape = stacked.shape[1:]
    split = (groups,) + shape[:axis] + (HEADS // groups, width) + shape[axis + 1 :]
    moved = jnp.moveaxis(stacked.reshape(split), 0, axis + 1)
    return moved.reshape(shape[:axis] + (HEADS * width,) + shape[axis + 1 :])


def swap(values, axis, mask):
    route = [(i, i ^ mask) for i in range(lax.axis_size(axis))]
    return lax.ppermute(values, axis, route)


def put_block(buffer, block, index):
    return lax.dynamic_update_slice_in_dim(buffer, block, index * block.shape[0], 0)


def seq_gather(rows):
    count = lax.axis_size("seq")
    if count != 4:
        return lax.all_gather(rows, "seq", axis=0, tiled=True)
    index = lax.axis_index("seq")
    far = swap(rows, "seq", 2)
    blocks = [rows, swap(rows, "seq", 1), far, swap(far, "seq", 1)]
    result = jnp.zeros((count * rows.shape[0],) + rows.shape[1:], rows.dtype)
    for mask, block in enumerate(blocks):
        result = put_block(result, block, index ^ mask)
    return result


def take_block(values, index, rows):
    return lax.dynamic_slice_in_dim(values, index * rows, rows, 0)


def seq_scatter(partial):
    count = lax.axis_size("seq")
    if count != 4:
        return lax.psum_scatter(partial, "seq", scatter_dimension=0, tiled=True).astype(
            jnp.float32
        )
    index = lax.axis_index("seq")
    rows = partial.shape[0] // count
    total = take_block(partial, index, rows).astype(jnp.float32)
    for mask in range(1, count):
        piece = swap(take_block(partial, index ^ mask, rows), "seq", mask)
        total = total + piece.astype(jnp.float32)
    return total


def seq_scatter_near(partial):
    count = lax.axis_size("seq")
    if count != 4:
        return seq_scatter(partial)
    index = lax.axis_index("seq")
    rows = partial.shape[0] // count

    def near(mask):
        arrived = swap(take_block(partial, index ^ 1 ^ mask, rows), "seq", 1)
        mine = take_block(partial, index ^ mask, rows)
        return arrived.astype(jnp.float32) + mine.astype(jnp.float32)

    far = swap(low(near(2)), "seq", 2)
    return near(0) + far.astype(jnp.float32)


def ring_route(count):
    return [(i, (i + 2) % count) for i in range(count)]


def shard_gather(rows):
    count = lax.axis_size("wshard")
    if count != 8:
        return lax.all_gather(rows, "wshard", axis=0, tiled=True)
    index = lax.axis_index("wshard")
    result = jnp.zeros((count * rows.shape[0],) + rows.shape[1:], rows.dtype)
    held = rows
    for step in range(count // 2):
        source = (index + count - 2 * step) % count
        result = put_block(result, held, source)
        result = put_block(result, swap(held, "wshard", 1), source ^ 1)
        if step < count // 2 - 1:
            held = lax.ppermute(held, "wshard", ring_route(count))
    return result


def shard_scatter(partial):
    count = lax.axis_size("wshard")
    if count != 8:
        return lax.psum_scatter(partial, "wshard", scatter_dimension=0, tiled=True)
    index = lax.axis_index("wshard")
    rows = partial.shape[0] // count
    total = None
    for step in range(1, count // 2 + 1):
        target = (index + count - 2 * step) % count
        arrived = swap(take_block(partial, target ^ 1, rows), "wshard", 1)
        mine = take_block(partial, target, rows).astype(jnp.float32)
        mine = mine + arrived.astype(jnp.float32)
        if total is not None:
            mine = mine + lax.ppermute(total, "wshard", ring_route(count)).astype(jnp.float32)
        total = low(mine)
    return total


def shard_total(values):
    count = lax.axis_size("wshard")
    mask = 1
    while mask < count:
        values = values + swap(values, "wshard", mask)
        mask = 2 * mask
    return values


def pack_out(rows):
    split = rows.reshape(-1, HEADDIM, 2, rows.shape[1] // 2)
    return jnp.swapaxes(split, 1, 2).reshape(2 * rows.shape[0], rows.shape[1] // 2)


def unpack_out(packed):
    split = packed.reshape(-1, 2, HEADDIM, packed.shape[1])
    return jnp.swapaxes(split, 1, 2).reshape(packed.shape[0] // 2, 2 * packed.shape[1])


def gather_out(out_low, seq_index, groups):
    rows = out_low.shape[0]
    if rows % (groups * HEADDIM) == 0:
        mine = pick_rows(out_low, seq_index, groups)
        return lax.all_gather(mine, "wshard", axis=0, tiled=True)
    whole = lax.all_gather(out_low, "wshard", axis=0, tiled=True)
    return pick_heads(whole, 0, HEADDIM, seq_index, groups)


def pick_rows(values, seq_index, groups):
    rows = values.shape[0]
    split = values.reshape(rows // (groups * HEADDIM), groups, HEADDIM, values.shape[1])
    return lax.dynamic_index_in_dim(split, seq_index, 1, keepdims=False).reshape(
        rows // groups, values.shape[1]
    )


def sum_out_grad(grad, rows, seq_index, groups):
    grad = grad.astype(jnp.bfloat16)
    if rows % (groups * HEADDIM) == 0:
        mine = lax.psum_scatter(grad, "wshard", scatter_dimension=0, tiled=True)
        every = lax.all_gather(mine, "seq", axis=0, tiled=False)
        split = every.reshape(groups, rows // (groups * HEADDIM), HEADDIM, grad.shape[1])
        return jnp.moveaxis(split, 0, 1).reshape(rows, grad.shape[1]).astype(jnp.float32)
    blocks = grad.reshape(HEADS // groups, 1, HEADDIM, grad.shape[1])
    here = (jnp.arange(groups) == seq_index)[None, :, None, None]
    spread = jnp.where(here, blocks, jnp.zeros((), jnp.bfloat16)).reshape(DI, grad.shape[1])
    mine = lax.psum_scatter(spread, "wshard", scatter_dimension=0, tiled=True)
    return lax.psum(mine.astype(jnp.float32), "seq")


def shards(
    block_in,
    cotangent,
    in_weight,
    in_first,
    in_second,
    out_weight,
    out_first,
    out_second,
    vec_weight,
    vec_first,
    vec_second,
):
    rows_here = block_in.shape[1]
    groups = lax.axis_size("seq")
    seq_index = lax.axis_index("seq")
    local_heads = HEADS // groups
    local_di = DI // groups
    hidden_rows = block_in.reshape(rows_here, D)
    cot_rows = cotangent.reshape(rows_here, D)
    gain_one, gain_two, kernel, conv_bias, a_log, dt_bias, d_skip = split_vector(vec_weight)

    def heads_of(values, axis, width):
        return pick_heads(values, axis, width, seq_index, groups)

    lanes = 128
    channels = local_di + 2 * STATE
    packs = out_weight.shape[0] == groups * HEADDIM
    in_low = low(in_weight)
    rest_mine = jnp.concatenate(
        [
            heads_of(in_low[:, DI : 2 * DI], 1, HEADDIM),
            in_low[:, 2 * DI : 2 * DI + 2 * STATE],
            jnp.pad(heads_of(in_low[:, DI + CONVCH :], 1, 1), ((0, 0), (0, lanes - local_heads))),
        ],
        1,
    )
    gate_mine = heads_of(in_low[:, :DI], 1, HEADDIM)
    rest_weight = shard_gather(rest_mine)
    hidden_low = seq_gather(hidden_rows)
    if packs:
        out_mine = pack_out(pick_rows(low(out_weight), seq_index, groups))
        gate_out = lax.all_gather(
            jnp.concatenate([gate_mine, out_mine], 1), "wshard", axis=0, tiled=True
        )
    else:
        gate_out = jnp.concatenate(
            [
                lax.all_gather(gate_mine, "wshard", axis=0, tiled=True),
                pack_out(gather_out(low(out_weight), seq_index, groups)),
            ],
            1,
        )
    cot = seq_gather(cot_rows)
    my_gain_two = heads_of(gain_two, 0, HEADDIM)[None, :]
    my_kernel = jnp.concatenate([heads_of(kernel[:, :DI], 1, HEADDIM), kernel[:, DI:]], 1)
    my_bias = jnp.concatenate([heads_of(conv_bias[:DI], 0, HEADDIM), conv_bias[DI:]], 0)

    def on_lanes(values):
        return jnp.pad(values, (0, lanes - local_heads))[None, :]

    heads_vectors = (
        on_lanes(heads_of(a_log, 0, 1)),
        on_lanes(heads_of(dt_bias, 0, 1)),
        jnp.repeat(heads_of(d_skip, 0, 1), HEADDIM)[None, :],
    )
    expand = (
        jnp.arange(lanes)[:, None] == jnp.arange(local_di)[None, :] // HEADDIM
    ).astype(jnp.float32)
    normed_low, conv_in, conv_pre, dt_raw, y, scanned, states = run_forward(
        hidden_low,
        rest_weight,
        gain_one[None, :],
        (my_kernel, my_bias[None, :]),
        heads_vectors,
        expand,
    )
    gating, d_gnorm, sums = run_gate(normed_low, scanned, cot, gate_out, my_gain_two)
    sums = sums[:2]
    for mask in (1, 2) if groups == 4 else ():
        sums = sums + swap(sums, "seq", mask)
    if groups != 4:
        sums = lax.psum(sums, "seq")
    sums = sums / DI
    scale = lax.rsqrt(sums[0] + norm_eps)
    slope = scale * scale * sums[1]
    block_part, d_gating, d_scanned, grad_gate_out, d_gain_two = run_middle(
        scanned,
        gating,
        d_gnorm,
        cot,
        normed_low,
        scale[:, None],
        slope[:, None],
        gate_out,
        my_gain_two,
    )
    block_out = hidden_rows.astype(jnp.float32) + seq_scatter(block_part)
    d_rest, grad_rest, d_kernel, d_conv_bias, d_skip_wide, d_head = run_backward(
        normed_low,
        conv_in,
        conv_pre,
        dt_raw,
        y,
        states,
        d_scanned,
        my_kernel,
        heads_vectors,
        expand,
    )
    rest_part = shard_scatter(grad_rest)
    d_normed_part, d_gain_one = run_normed(hidden_low, d_gating, d_rest, gate_out, rest_weight)
    d_normed = seq_scatter_near(d_normed_part)
    own_hidden = hidden_rows.astype(jnp.float32)
    own_scale = lax.rsqrt(jnp.mean(own_hidden * own_hidden, axis=-1, keepdims=True) + norm_eps)
    own_unit = own_hidden * own_scale
    d_own = d_normed * gain_one[None, :]
    d_hidden = own_scale * (
        d_own - own_unit * jnp.mean(d_own * own_unit, axis=-1, keepdims=True)
    )
    block_grad = cot_rows.astype(jnp.float32) + d_hidden

    d_skip_part = jnp.sum(d_skip_wide.reshape(local_heads, HEADDIM), axis=1)
    shared = jnp.concatenate(
        [d_gain_one[0], d_kernel[:, local_di:].reshape(-1), d_conv_bias[0, local_di:]]
    )
    apart = jnp.concatenate(
        [
            d_gain_two[0],
            d_kernel[:, :local_di].reshape(-1),
            d_conv_bias[0, :local_di],
            d_head[:, :local_heads].reshape(-1),
            d_skip_part,
        ]
    )
    vec_part = shard_total(jnp.concatenate([shared, apart]))
    shared = vec_part[: shared.shape[0]]
    every = seq_gather(vec_part[None, shared.shape[0] :])
    for mask in (1, 2) if groups == 4 else ():
        shared = shared + swap(shared, "seq", mask)
    if groups != 4:
        shared = lax.psum(shared, "seq")
    kernel_end = local_di * (1 + WIDTH)
    heads_at = kernel_end + local_di
    both_kernel = D + 2 * STATE * WIDTH
    vec_total = jnp.concatenate(
        [
            shared[:D],
            merge_heads(every[:, :local_di], 0, HEADDIM),
            jnp.concatenate(
                [
                    merge_heads(
                        every[:, local_di:kernel_end].reshape(groups, WIDTH, local_di), 1, HEADDIM
                    ),
                    shared[D:both_kernel].reshape(WIDTH, 2 * STATE),
                ],
                1,
            ).reshape(-1),
            merge_heads(every[:, kernel_end:heads_at], 0, HEADDIM),
            shared[both_kernel:],
            merge_heads(every[:, heads_at : heads_at + local_heads], 0, 1),
            merge_heads(every[:, heads_at + local_heads : heads_at + 2 * local_heads], 0, 1),
            merge_heads(every[:, heads_at + 2 * local_heads :], 0, 1),
        ]
    )
    vec_first_new, vec_second_new, vec_weight_new = adamw_step(
        vec_weight, vec_first, vec_second, vec_total, vector_rate, 0.0
    )
    rows_in = in_weight.shape[0]
    if packs:
        gate_out_part = lax.psum_scatter(grad_gate_out, "wshard", scatter_dimension=0, tiled=True)
        gate_out_every = seq_gather(gate_out_part).reshape(groups, rows_in, -1)
        gate_every = gate_out_every[:, :, :local_di]
        out_total = unpack_out(
            gate_out_every[:, :, local_di:].reshape(groups * rows_in, -1)
        ).astype(jnp.float32)
    else:
        gate_part = lax.psum_scatter(
            grad_gate_out[:, :local_di], "wshard", scatter_dimension=0, tiled=True
        )
        gate_every = lax.all_gather(gate_part, "seq", axis=0, tiled=False)
        out_total = sum_out_grad(
            unpack_out(grad_gate_out[:, local_di:]), out_weight.shape[0], seq_index, groups
        )
    rest_every = seq_gather(rest_part).reshape(groups, rows_in, -1).astype(jnp.float32)
    both_total = jnp.sum(rest_every, axis=0)
    in_total = jnp.concatenate(
        [
            merge_heads(gate_every.astype(jnp.float32), 1, HEADDIM),
            merge_heads(rest_every[:, :, :local_di], 1, HEADDIM),
            both_total[:, local_di:channels],
            merge_heads(rest_every[:, :, channels : channels + local_heads], 1, 1),
        ],
        1,
    )
    in_first_new, in_second_new, in_weight_new = adamw_step(
        in_weight, in_first, in_second, in_total, matrix_rate, matrix_decay
    )
    out_first_new, out_second_new, out_weight_new = adamw_step(
        out_weight, out_first, out_second, out_total, matrix_rate, matrix_decay
    )
    return (
        block_out.reshape(1, rows_here, D),
        block_grad.reshape(1, rows_here, D),
        in_first_new,
        in_second_new,
        in_weight_new,
        out_first_new,
        out_second_new,
        out_weight_new,
        vec_first_new,
        vec_second_new,
        vec_weight_new,
    )


def solution(mesh):
    return jax.shard_map(
        shards,
        mesh=mesh,
        in_specs=(
            P("wshard", "seq", None),
            P("wshard", "seq", None),
            P("wshard", None),
            P("wshard", None),
            P("wshard", None),
            P("wshard", None),
            P("wshard", None),
            P("wshard", None),
            P(),
            P(),
            P(),
        ),
        out_specs=(
            P("wshard", "seq", None),
            P("wshard", "seq", None),
            P("wshard", None),
            P("wshard", None),
            P("wshard", None),
            P("wshard", None),
            P("wshard", None),
            P("wshard", None),
            P(),
            P(),
            P(),
        ),
        check_vma=False,
    )
```

```python
import jax
import jax.numpy as jnp
from jax import lax
from jax.experimental import pallas as pl
from jax.experimental.pallas import tpu as pltpu
from jax.sharding import PartitionSpec as P

D = 1024
HEADS = 32
HEADDIM = 64
STATE = 128
WIDTH = 4
BLOCK = 256
STEP = 10
DI = 2048
CONVCH = 2304


precise = lax.Precision.HIGHEST
norm_eps = 1e-05
beta_one = 0.9
beta_two = 0.95
adam_eps = 1e-08
matrix_rate = 0.05
matrix_decay = 0.1
vector_rate = 0.5


def rms_scale(values):
    return values * lax.rsqrt(jnp.mean(values * values, axis=-1, keepdims=True) + norm_eps)


def split_vector(vector):
    extents = [D, DI, WIDTH * CONVCH, CONVCH, HEADS, HEADS, HEADS]
    pieces = []
    offset = 0
    for extent in extents:
        pieces.append(vector[offset : offset + extent])
        offset = offset + extent
    pieces[2] = pieces[2].reshape(WIDTH, CONVCH)
    return pieces


def wide(extent):
    return pl.BlockSpec((BLOCK, extent), lambda q: (q, 0))


def wide_back(extent, count):
    return pl.BlockSpec((BLOCK, extent), lambda q: (count - 1 - q, 0))


def whole(*shape):
    return pl.BlockSpec(shape, lambda q: (0,) * len(shape))


def dot_nt(left, right, precision=None):
    return lax.dot_general(
        left,
        right,
        (((1,), (1,)), ((), ())),
        precision=precision,
        preferred_element_type=jnp.float32,
    )


def dot_tn(left, right):
    return lax.dot_general(
        left, right, (((0,), (0,)), ((), ())), preferred_element_type=jnp.float32
    )


def dot_nn(left, right, precision=None):
    return jnp.dot(left, right, precision=precision, preferred_element_type=jnp.float32)


def sigmoid(values):
    return 1.0 / (1.0 + jnp.exp(-values))


def low(values):
    return values.astype(jnp.bfloat16)


def lower_mask():
    rows = lax.broadcasted_iota(jnp.int32, (BLOCK, BLOCK), 0)
    return rows >= lax.broadcasted_iota(jnp.int32, (BLOCK, BLOCK), 1)


def decay_sums(dt_raw, dt_bias, a_log, expand):
    shifted = dt_raw + dt_bias
    step = jnp.maximum(shifted, 0.0) + jnp.log1p(jnp.exp(-jnp.abs(shifted)))
    log_decay = -jnp.exp(a_log) * step
    ones = jnp.where(lower_mask(), 1.0, 0.0)
    running = dot_nn(ones, log_decay, precise)
    step_wide = dot_nn(step, expand, precise)
    running_wide = dot_nn(running, expand, precise)
    return shifted, step, log_decay, running, step_wide, running_wide


def forward_kernel(
    hidden_ref,
    conv_weight_ref,
    dt_weight_ref,
    gain_one_ref,
    conv_ref,
    bias_ref,
    a_log_ref,
    dt_bias_ref,
    skip_ref,
    expand_ref,
    normed_ref,
    conv_in_ref,
    conv_pre_ref,
    dt_ref,
    y_ref,
    scanned_ref,
    state_ref,
    ext,
    state,
):
    local_di = y_ref.shape[1]
    heads = local_di // HEADDIM

    @pl.when(pl.program_id(0) == 0)
    def _():
        ext[0:8, :] = jnp.zeros((8, ext.shape[1]), jnp.float32)
        state[...] = jnp.zeros_like(state)

    hidden = hidden_ref[...].astype(jnp.float32)
    normed = low(rms_scale(hidden) * gain_one_ref[...])
    normed_ref[...] = normed
    conv_in = dot_nn(normed, conv_weight_ref[...])
    conv_in_ref[...] = conv_in
    ext[8 : 8 + BLOCK, :] = conv_in
    conv_pre = bias_ref[...] + conv_ref[WIDTH - 1 : WIDTH, :] * conv_in
    for tap in range(WIDTH - 1):
        first = 8 - WIDTH + 1 + tap
        conv_pre = conv_pre + conv_ref[tap : tap + 1, :] * ext[first : first + BLOCK, :]
    conv_pre_ref[...] = conv_pre
    ext[8 - WIDTH + 1 : 8, :] = ext[8 + BLOCK - WIDTH + 1 : 8 + BLOCK, :]
    conv_low = low(conv_pre * sigmoid(conv_pre))
    inner = conv_low[:, :local_di]
    b_rows = conv_low[:, local_di : local_di + STATE]
    c_rows = conv_low[:, local_di + STATE :]
    dt_raw = low(dot_nn(normed, dt_weight_ref[...])).astype(jnp.float32)
    dt_ref[...] = dt_raw

    _, _, _, running, step_wide, running_wide = decay_sums(
        dt_raw, dt_bias_ref[...], a_log_ref[...], expand_ref[...]
    )
    running_t = running.T
    b_t = low(b_rows.astype(jnp.float32).T)
    scores = dot_nn(c_rows, b_t)
    mask = lower_mask()
    inner_wide = inner.astype(jnp.float32)
    stepped = step_wide * inner_wide
    stepped_low = low(stepped)
    first_half = lax.broadcasted_iota(jnp.int32, (BLOCK, 2 * HEADDIM), 1) < HEADDIM
    zero = jnp.zeros((), jnp.bfloat16)
    state_ref[...] = state[...].reshape(state_ref.shape)
    held = state[...]
    carried = jnp.exp(running_wide) * dot_nn(c_rows, low(held))
    for pair in range(heads // 2):
        span = slice(pair * 2 * HEADDIM, (pair + 1) * 2 * HEADDIM)
        both = stepped_low[:, span]
        total = carried[:, span]
        for half in range(2):
            head = 2 * pair + half
            differ = running[:, head : head + 1] - running_t[head : head + 1, :]
            mixed = low(jnp.exp(jnp.where(mask, differ, -jnp.inf)) * scores)
            mine = jnp.where(first_half if half == 0 else ~first_half, both, zero)
            total = total + dot_nn(mixed, mine)
        y_ref[:, span] = total
    last = running_wide[BLOCK - 1 : BLOCK, :]
    to_end = jnp.exp(last - running_wide)
    state[...] = jnp.exp(last) * held + dot_nn(b_t, low(to_end * stepped))
    scanned_ref[...] = low(y_ref[...] + skip_ref[...] * inner_wide)


def out_halves(packed_ref):
    packed = packed_ref[...].reshape(-1, 2, HEADDIM, packed_ref.shape[1])
    extent = packed_ref.shape[0] // 2
    return (
        packed[:, 0].reshape(extent, packed_ref.shape[1]),
        packed[:, 1].reshape(extent, packed_ref.shape[1]),
    )


def gate_kernel(
    normed_ref,
    scanned_ref,
    cot_ref,
    gate_weight_ref,
    out_ref,
    gain_two_ref,
    gating_ref,
    d_gnorm_ref,
    sums_ref,
):
    local_di = gating_ref.shape[1]
    gating = dot_nn(normed_ref[...], gate_weight_ref[...])
    gating_ref[...] = gating
    out_left, out_right = out_halves(out_ref)
    half = out_left.shape[1]
    d_gnorm = dot_nt(cot_ref[:, :half], out_left) + dot_nt(cot_ref[:, half:], out_right)
    d_gnorm_ref[...] = d_gnorm
    gated = scanned_ref[...].astype(jnp.float32) * (gating * sigmoid(gating))
    ones = jnp.ones((8, local_di), jnp.float32)
    squares = dot_nt(ones, gated * gated, precise)
    products = dot_nt(ones, d_gnorm * gain_two_ref[...] * gated, precise)
    sums_ref[...] = jnp.where(
        lax.broadcasted_iota(jnp.int32, squares.shape, 0) == 0, squares, products
    )


def middle_kernel(
    scanned_ref,
    gating_ref,
    d_gnorm_ref,
    cot_ref,
    normed_ref,
    scale_ref,
    slope_ref,
    out_ref,
    gain_two_ref,
    block_ref,
    d_gating_ref,
    d_scanned_ref,
    grad_ref,
    d_gain_two_ref,
    left_sum,
    right_sum,
    gate_sum,
):
    chunk = pl.program_id(0)

    @pl.when(chunk == 0)
    def _():
        left_sum[...] = jnp.zeros_like(left_sum)
        right_sum[...] = jnp.zeros_like(right_sum)
        gate_sum[...] = jnp.zeros_like(gate_sum)
        d_gain_two_ref[...] = jnp.zeros_like(d_gain_two_ref)

    gating = gating_ref[...]
    open_part = sigmoid(gating)
    gate = gating * open_part
    scanned = scanned_ref[...].astype(jnp.float32)
    scale = scale_ref[:, :1]
    unit = scanned * gate * scale
    d_gnorm = d_gnorm_ref[...]
    gain_two = gain_two_ref[...]
    gnorm = low(unit * gain_two)
    out_left, out_right = out_halves(out_ref)
    half = out_left.shape[1]
    block_ref[:, :half] = low(dot_nn(gnorm, out_left))
    block_ref[:, half:] = low(dot_nn(gnorm, out_right))
    left_sum[...] += dot_tn(gnorm, cot_ref[:, :half])
    right_sum[...] += dot_tn(gnorm, cot_ref[:, half:])
    d_gain_two_ref[...] += jnp.sum(d_gnorm * unit, axis=0, keepdims=True)
    d_gated = scale * (d_gnorm * gain_two) - unit * slope_ref[:, :1]
    d_gating = low(d_gated * scanned * (open_part * (1.0 + gating * (1.0 - open_part))))
    d_gating_ref[...] = d_gating
    d_scanned_ref[...] = low(d_gated * gate)
    gate_sum[...] += dot_tn(normed_ref[...], d_gating)

    @pl.when(chunk == pl.num_programs(0) - 1)
    def _():
        local_di = gating_ref.shape[1]
        grad_ref[:, :local_di] = low(gate_sum[...])
        for head in range(local_di // HEADDIM):
            rows = slice(head * HEADDIM, (head + 1) * HEADDIM)
            base = 2 * head * HEADDIM
            grad_ref[base : base + HEADDIM, local_di:] = low(left_sum[rows, :])
            grad_ref[base + HEADDIM : base + 2 * HEADDIM, local_di:] = low(right_sum[rows, :])


def backward_kernel(
    conv_in_ref,
    conv_pre_ref,
    dt_ref,
    y_ref,
    state_ref,
    d_scanned_ref,
    conv_ref,
    a_log_ref,
    dt_bias_ref,
    skip_ref,
    expand_ref,
    d_rest_ref,
    d_kernel_ref,
    d_conv_bias_ref,
    d_skip_ref,
    d_head_ref,
    ext,
    d_state,
    later_state,
):
    local_di = y_ref.shape[1]
    heads = local_di // HEADDIM
    chunk = pl.program_id(0)

    @pl.when(chunk == 0)
    def _():
        ext[BLOCK : BLOCK + 8, :] = jnp.zeros((8, ext.shape[1]), jnp.float32)
        d_state[...] = jnp.zeros_like(d_state)
        later_state[...] = jnp.zeros_like(later_state)
        d_kernel_ref[...] = jnp.zeros_like(d_kernel_ref)
        d_conv_bias_ref[...] = jnp.zeros_like(d_conv_bias_ref)
        d_skip_ref[...] = jnp.zeros_like(d_skip_ref)
        d_head_ref[...] = jnp.zeros_like(d_head_ref)

    expand = expand_ref[...]
    conv_pre = conv_pre_ref[...]
    open_part = sigmoid(conv_pre)
    conv_low = low(conv_pre * open_part)
    inner = conv_low[:, :local_di].astype(jnp.float32)
    b_rows = conv_low[:, local_di : local_di + STATE]
    c_rows = conv_low[:, local_di + STATE :]
    a_log = a_log_ref[...]
    shifted, _, log_decay, running, step_wide, running_wide = decay_sums(
        dt_ref[...], dt_bias_ref[...], a_log, expand
    )
    running_t = running.T
    b_t = low(b_rows.astype(jnp.float32).T)
    c_t = low(c_rows.astype(jnp.float32).T)
    scores = dot_nn(c_rows, b_t)
    scores_t = dot_nn(b_rows, c_t)
    mask = lower_mask()
    rows = lax.broadcasted_iota(jnp.int32, (BLOCK, BLOCK), 0)
    mask_t = rows <= lax.broadcasted_iota(jnp.int32, (BLOCK, BLOCK), 1)
    d_y_low = d_scanned_ref[...]
    d_y = d_y_low.astype(jnp.float32)
    stepped_low = low(step_wide * inner)
    stepped = stepped_low.astype(jnp.float32)
    last = running_wide[BLOCK - 1 : BLOCK, :]
    to_end = jnp.exp(last - running_wide)
    d_later = d_state[...]
    d_later_low = low(d_later)
    held = state_ref[...].reshape(d_state.shape)
    decayed_dy = low(jnp.exp(running_wide) * d_y)
    d_c = dot_nt(decayed_dy, low(held))
    d_b = dot_nt(low(to_end * stepped), d_later_low)
    d_stepped = to_end * dot_nn(b_rows, d_later_low)
    cross = jnp.sum(later_state[...] * d_later, axis=0, keepdims=True)
    d_state[...] = jnp.exp(last) * d_later + dot_nn(c_t, decayed_dy)
    later_state[...] = held
    first_half = lax.broadcasted_iota(jnp.int32, (BLOCK, 2 * HEADDIM), 1) < HEADDIM
    zero = jnp.zeros((), jnp.bfloat16)
    d_scores = jnp.zeros((BLOCK, BLOCK), jnp.float32)
    pieces = []
    for pair in range(heads // 2):
        span = slice(pair * 2 * HEADDIM, (pair + 1) * 2 * HEADDIM)
        total = d_stepped[:, span]
        for half in range(2):
            head = 2 * pair + half
            mine = jnp.where(first_half if half == 0 else ~first_half, d_y_low[:, span], zero)
            column = running[:, head : head + 1]
            row = running_t[head : head + 1, :]
            decay = jnp.exp(jnp.where(mask, column - row, -jnp.inf))
            decay_t = jnp.exp(jnp.where(mask_t, row - column, -jnp.inf))
            d_scores = d_scores + dot_nt(mine, stepped_low[:, span]) * decay
            total = total + dot_nn(low(decay_t * scores_t), mine)
        pieces.append(total)
    d_stepped = jnp.concatenate(pieces, 1)
    d_scores_low = low(d_scores)
    d_c = d_c + dot_nn(d_scores_low, b_rows)
    d_b = d_b + dot_nn(low(d_scores.T), c_rows)
    d_inner = step_wide * d_stepped + skip_ref[...] * d_y
    d_running = dot_nt(d_y * y_ref[...] - d_stepped * stepped, expand, precise)
    upper = jnp.where(mask_t, 1.0, 0.0)
    d_log = dot_nn(upper, d_running, precise) + dot_nt(cross, expand, precise)
    d_step = dot_nt(d_stepped * inner, expand, precise) - jnp.exp(a_log) * d_log
    d_dt = d_step * sigmoid(shifted)
    d_head_ref[0:1, :] += jnp.sum(d_log * log_decay, axis=0, keepdims=True)
    d_head_ref[1:2, :] += jnp.sum(d_dt, axis=0, keepdims=True)
    d_skip_ref[...] += jnp.sum(d_y * inner, axis=0, keepdims=True)

    d_conv_out = jnp.concatenate([d_inner, d_b, d_c], 1)
    d_pre = d_conv_out * (open_part * (1.0 + conv_pre * (1.0 - open_part)))
    ext[0:BLOCK, :] = d_pre
    d_conv_bias_ref[...] += jnp.sum(d_pre, axis=0, keepdims=True)
    conv_in = conv_in_ref[...]
    d_conv_in = jnp.zeros_like(conv_in)
    for tap in range(WIDTH):
        moved = ext[WIDTH - 1 - tap : WIDTH - 1 - tap + BLOCK, :]
        d_conv_in = d_conv_in + conv_ref[tap : tap + 1, :] * moved
        d_kernel_ref[tap : tap + 1, :] += jnp.sum(moved * conv_in, axis=0, keepdims=True)
    ext[BLOCK : BLOCK + 8, :] = ext[0:8, :]
    d_rest_ref[...] = jnp.concatenate([low(d_conv_in), low(d_dt)], 1)


def rest_kernel(normed_ref, d_rest_ref, grad_ref):
    grad_ref[...] = low(dot_tn(normed_ref[...], d_rest_ref[...]))


def normed_first_kernel(*refs):
    @pl.when(pl.program_id(0) == 0)
    def _():
        refs[-1][...] = jnp.zeros_like(refs[-1])

    normed_part(*refs)


def normed_kernel(*refs):
    @pl.when(pl.program_id(0) == 0)
    def _():
        refs[-1][...] = refs[6][...]

    normed_part(*refs[:5], *refs[7:])


def normed_part(
    hidden_ref,
    d_gating_ref,
    d_rest_ref,
    gate_weight_ref,
    rest_weight_ref,
    d_normed_ref,
    d_gain_one_ref,
):
    d_normed = dot_nt(d_gating_ref[...], gate_weight_ref[...])
    d_normed = d_normed + dot_nt(d_rest_ref[...], rest_weight_ref[...])
    d_normed_ref[...] = low(d_normed)
    unit = rms_scale(hidden_ref[...].astype(jnp.float32))
    d_gain_one_ref[...] += jnp.sum(d_normed * unit, axis=0, keepdims=True)


def kernel_params():
    return pltpu.CompilerParams(
        dimension_semantics=("arbitrary",), vmem_limit_bytes=50 * 1024 * 1024
    )


def after(kernel, inputs, arrived):
    def run(*refs):
        kernel(*refs[:inputs], *refs[inputs + arrived :])

    return run


def anywhere(arrived):
    return [pl.BlockSpec(memory_space=pl.ANY)] * len(arrived)


def cost(flops, moved, transcendentals):
    return pl.CostEstimate(flops=flops, bytes_accessed=moved, transcendentals=transcendentals)


def run_forward(hidden, rest_weight, gain_one, conv, heads_vectors, expand, arrived):
    length = hidden.shape[0]
    chunks = length // BLOCK
    lanes, local_di = expand.shape
    channels = rest_weight.shape[1] - lanes
    shape = jax.ShapeDtypeStruct
    f32, bf16 = jnp.float32, jnp.bfloat16
    return pl.pallas_call(
        after(forward_kernel, 10, len(arrived)),
        grid=(chunks,),
        in_specs=[
            wide(D),
            whole(D, channels),
            pl.BlockSpec((D, lanes), lambda q: (0, channels // lanes)),
            whole(1, D),
            whole(WIDTH, channels),
            whole(1, channels),
            whole(1, lanes),
            whole(1, lanes),
            whole(1, local_di),
            whole(lanes, local_di),
        ]
        + anywhere(arrived),
        out_specs=[
            wide(D),
            wide(channels),
            wide(channels),
            wide(lanes),
            wide(local_di),
            wide(local_di),
            pl.BlockSpec((1, STATE, local_di), lambda q: (q, 0, 0)),
        ],
        out_shape=[
            shape((length, D), bf16),
            shape((length, channels), f32),
            shape((length, channels), f32),
            shape((length, lanes), f32),
            shape((length, local_di), f32),
            shape((length, local_di), bf16),
            shape((chunks, STATE, local_di), f32),
        ],
        scratch_shapes=[
            pltpu.VMEM((8 + BLOCK, channels), f32),
            pltpu.VMEM((STATE, local_di), f32),
        ],
        compiler_params=kernel_params(),
        cost_estimate=cost(6_000_000_000, 30_000_000, 8_000_000),
        name="forward",
    )(hidden, rest_weight, rest_weight, gain_one, *conv, *heads_vectors, expand, *arrived)


def run_gate(normed, scanned, cot, gate_out, gain_two):
    length, local_di = scanned.shape
    half = D // 2
    shape = jax.ShapeDtypeStruct
    return pl.pallas_call(
        gate_kernel,
        grid=(length // BLOCK,),
        in_specs=[
            wide(D),
            wide(local_di),
            wide(D),
            pl.BlockSpec((D, local_di), lambda q: (0, 0)),
            pl.BlockSpec((2 * local_di, half), lambda q: (0, local_di // half)),
            whole(1, local_di),
        ],
        out_specs=[
            wide(local_di),
            wide(local_di),
            pl.BlockSpec((8, BLOCK), lambda q: (0, q)),
        ],
        out_shape=[
            shape((length, local_di), jnp.float32),
            shape((length, local_di), jnp.float32),
            shape((8, length), jnp.float32),
        ],
        compiler_params=kernel_params(),
        cost_estimate=cost(2_500_000_000, 12_000_000, 1_000_000),
        name="gate",
    )(normed, scanned, cot, gate_out, gate_out, gain_two)


def run_middle(scanned, gating, d_gnorm, cot, normed, scale, slope, gate_out, gain_two):
    length, local_di = scanned.shape
    half = D // 2
    shape = jax.ShapeDtypeStruct
    f32, bf16 = jnp.float32, jnp.bfloat16
    return pl.pallas_call(
        middle_kernel,
        grid=(length // BLOCK,),
        in_specs=[
            wide(local_di),
            wide(local_di),
            wide(local_di),
            wide(D),
            wide(D),
            wide(1),
            wide(1),
            pl.BlockSpec((2 * local_di, half), lambda q: (0, local_di // half)),
            whole(1, local_di),
        ],
        out_specs=[
            wide(D),
            wide(local_di),
            wide(local_di),
            whole(D, local_di + half),
            whole(1, local_di),
        ],
        out_shape=[
            shape((length, D), bf16),
            shape((length, local_di), bf16),
            shape((length, local_di), bf16),
            shape((D, local_di + half), bf16),
            shape((1, local_di), f32),
        ],
        scratch_shapes=[
            pltpu.VMEM((local_di, half), f32),
            pltpu.VMEM((local_di, half), f32),
            pltpu.VMEM((D, local_di), f32),
        ],
        compiler_params=kernel_params(),
        cost_estimate=cost(4_000_000_000, 15_000_000, 500_000),
        name="middle",
    )(scanned, gating, d_gnorm, cot, normed, scale, slope, gate_out, gain_two)


def run_backward(
    conv_in, conv_pre, dt_raw, y, states, d_scanned, kernel, heads_vectors, expand
):
    length, local_di = y.shape
    chunks = length // BLOCK
    channels = conv_in.shape[1]
    lanes = expand.shape[0]
    shape = jax.ShapeDtypeStruct
    f32, bf16 = jnp.float32, jnp.bfloat16

    def back(extent):
        return wide_back(extent, chunks)

    return pl.pallas_call(
        backward_kernel,
        grid=(chunks,),
        in_specs=[
            back(channels),
            back(channels),
            back(lanes),
            back(local_di),
            pl.BlockSpec((1, STATE, local_di), lambda q: (chunks - 1 - q, 0, 0)),
            back(local_di),
            whole(WIDTH, channels),
            whole(1, lanes),
            whole(1, lanes),
            whole(1, local_di),
            whole(lanes, local_di),
        ],
        out_specs=[
            back(channels + lanes),
            whole(WIDTH, channels),
            whole(1, channels),
            whole(1, local_di),
            whole(2, lanes),
        ],
        out_shape=[
            shape((length, channels + lanes), bf16),
            shape((WIDTH, channels), f32),
            shape((1, channels), f32),
            shape((1, local_di), f32),
            shape((2, lanes), f32),
        ],
        scratch_shapes=[
            pltpu.VMEM((BLOCK + 8, channels), f32),
            pltpu.VMEM((STATE, local_di), f32),
            pltpu.VMEM((STATE, local_di), f32),
        ],
        compiler_params=kernel_params(),
        cost_estimate=cost(14_000_000_000, 40_000_000, 10_000_000),
        name="backward",
    )(conv_in, conv_pre, dt_raw, y, states, d_scanned, kernel, *heads_vectors, expand)


def run_rest(normed, d_rest, arrived):
    length, rest = d_rest.shape
    rows = D // 4
    return pl.pallas_call(
        after(rest_kernel, 2, len(arrived)),
        grid=(4,),
        in_specs=[pl.BlockSpec((length, rows), lambda q: (0, q)), whole(length, rest)]
        + anywhere(arrived),
        out_specs=pl.BlockSpec((rows, rest), lambda q: (q, 0)),
        out_shape=jax.ShapeDtypeStruct((D, rest), jnp.bfloat16),
        compiler_params=kernel_params(),
        cost_estimate=cost(2_000_000_000, 6_000_000, 0),
        name="rest",
    )(normed, d_rest, *arrived)


def run_normed(hidden, d_gating, d_rest, gate_out, rest_weight, before, arrived):
    length, local_di = d_gating.shape
    rest = d_rest.shape[1]
    chunks = length // BLOCK // 2
    first = 0 if not before else chunks

    def part(extent):
        return pl.BlockSpec((BLOCK, extent), lambda q: (q + first, 0))

    kernel = normed_kernel if before else normed_first_kernel
    return pl.pallas_call(
        after(kernel, 5 + len(before), len(arrived)),
        grid=(chunks,),
        in_specs=[part(D), part(local_di), part(rest), whole(D, local_di), whole(D, rest)]
        + [pl.BlockSpec(memory_space=pl.ANY), whole(1, D)][: len(before)]
        + anywhere(arrived),
        out_specs=[part(D), whole(1, D)],
        out_shape=[
            jax.ShapeDtypeStruct((length, D), jnp.bfloat16),
            jax.ShapeDtypeStruct((1, D), jnp.float32),
        ],
        input_output_aliases={5: 0} if before else {},
        compiler_params=kernel_params(),
        cost_estimate=cost(1_500_000_000, 6_000_000, 1000),
        name="normed",
    )(hidden, d_gating, d_rest, gate_out, rest_weight, *before, *arrived)


def adamw_step(weight, first, second, grad, rate, decay):
    first_new = beta_one * first + (1.0 - beta_one) * grad
    second_new = beta_two * second + (1.0 - beta_two) * grad * grad
    fix_one = 1.0 - beta_one**STEP
    fix_two = 1.0 - beta_two**STEP
    normalized = first_new / fix_one / (jnp.sqrt(second_new / fix_two) + adam_eps)
    return (first_new, second_new, weight - rate * (normalized + decay * weight))


def pick_heads(values, axis, width, index, groups):
    shape = values.shape
    split = shape[:axis] + (HEADS // groups, groups, width) + shape[axis + 1 :]
    taken = lax.dynamic_index_in_dim(values.reshape(split), index, axis + 1, keepdims=False)
    return taken.reshape(shape[:axis] + (HEADS // groups * width,) + shape[axis + 1 :])


def merge_heads(stacked, axis, width):
    groups = stacked.shape[0]
    shape = stacked.shape[1:]
    split = (groups,) + shape[:axis] + (HEADS // groups, width) + shape[axis + 1 :]
    moved = jnp.moveaxis(stacked.reshape(split), 0, axis + 1)
    return moved.reshape(shape[:axis] + (HEADS * width,) + shape[axis + 1 :])


def swap(values, axis, mask):
    route = [(i, i ^ mask) for i in range(lax.axis_size(axis))]
    return lax.ppermute(values, axis, route)


def put_block(buffer, block, index):
    return lax.dynamic_update_slice_in_dim(buffer, block, index * block.shape[0], 0)


def seq_gather(rows, far=None):
    count = lax.axis_size("seq")
    if count != 4:
        return lax.all_gather(rows, "seq", axis=0, tiled=True)
    index = lax.axis_index("seq")
    far = swap(rows, "seq", 2) if far is None else far
    blocks = [rows, swap(rows, "seq", 1), far, swap(far, "seq", 1)]
    result = jnp.zeros((count * rows.shape[0],) + rows.shape[1:], rows.dtype)
    for mask, block in enumerate(blocks):
        result = put_block(result, block, index ^ mask)
    return result


def take_block(values, index, rows):
    return lax.dynamic_slice_in_dim(values, index * rows, rows, 0)


def seq_pieces(partial):
    index = lax.axis_index("seq")
    count = lax.axis_size("seq")
    rows = partial.shape[0] // count
    return [
        swap(take_block(partial, index ^ mask, rows), "seq", mask) for mask in range(1, count)
    ]


def seq_scatter(partial, pieces):
    rows = partial.shape[0] // lax.axis_size("seq")
    total = take_block(partial, lax.axis_index("seq"), rows).astype(jnp.float32)
    for piece in pieces:
        total = total + piece.astype(jnp.float32)
    return total


def near_first(partial):
    count = lax.axis_size("seq")
    parity = lax.axis_index("seq") % 2
    rows = partial.shape[0] // count
    split = partial.reshape(count // 2, 2, rows, partial.shape[1])

    def half(parity):
        chosen = lax.dynamic_index_in_dim(split, parity, 1, keepdims=False)
        return chosen.reshape(count // 2 * rows, partial.shape[1])

    return half(parity), swap(half(1 - parity), "seq", 1)


def far_piece(mine, arrived):
    other = 1 - lax.axis_index("seq") // 2
    rows = mine.shape[0] // 2
    total = take_block(mine, other, rows).astype(jnp.float32)
    return swap(low(total + take_block(arrived, other, rows).astype(jnp.float32)), "seq", 2)


def near_sum(mine, arrived, far):
    here = lax.axis_index("seq") // 2
    rows = mine.shape[0] // 2
    total = take_block(mine, here, rows).astype(jnp.float32)
    total = total + take_block(arrived, here, rows).astype(jnp.float32)
    return total + far.astype(jnp.float32)


def ring_route(count):
    return [(i, (i + 2) % count) for i in range(count)]


def shard_gather(rows, late=0):
    count = lax.axis_size("wshard")
    if count != 8:
        return lax.all_gather(rows, "wshard", axis=0, tiled=True), [], []
    index = lax.axis_index("wshard")
    result = jnp.zeros((count * rows.shape[0],) + rows.shape[1:], rows.dtype)
    held = rows
    blocks = []
    missing = []
    for step in range(count // 2):
        source = (index + count - 2 * step) % count
        swapped = swap(held, "wshard", 1)
        result = put_block(result, held, source)
        blocks = blocks + [held]
        if step < count // 2 - late:
            result = put_block(result, swapped, source ^ 1)
            blocks = blocks + [swapped]
        else:
            missing = missing + [(source ^ 1, swapped)]
        if step < count // 2 - 1:
            held = lax.ppermute(held, "wshard", ring_route(count))
    return result, blocks, missing


def add_kernel(target_ref, mine_ref, *refs):
    total = mine_ref[...].astype(jnp.float32)
    for ref in refs[:-1]:
        total = total + ref[...].astype(jnp.float32)
    refs[-1][...] = low(total)


def add_block(partial, target, pieces, arrived):
    rows, columns = pieces[0].shape
    spec = pl.BlockSpec((rows, columns), lambda q, target_ref: (0, 0))
    return pl.pallas_call(
        after(add_kernel, 2 + len(pieces), len(arrived)),
        grid_spec=pltpu.PrefetchScalarGridSpec(
            num_scalar_prefetch=1,
            grid=(1,),
            in_specs=[pl.BlockSpec((rows, columns), lambda q, target_ref: (target_ref[0], 0))]
            + [spec] * len(pieces)
            + anywhere(arrived),
            out_specs=spec,
        ),
        out_shape=jax.ShapeDtypeStruct((rows, columns), jnp.bfloat16),
        compiler_params=kernel_params(),
        cost_estimate=cost(200_000, 900_000, 0),
        name="add",
    )(jnp.reshape(target, (1,)).astype(jnp.int32), partial, *pieces, *arrived)


def place_kernel(target_ref, first_ref, second_ref, whole_ref, result_ref):
    result_ref[...] = jnp.where(pl.program_id(0) == 0, first_ref[...], second_ref[...])


def place_blocks(whole_array, targets, first, second, arrived):
    rows, columns = first.shape
    spec = pl.BlockSpec((rows, columns), lambda q, target_ref: (0, 0))
    return pl.pallas_call(
        after(place_kernel, 4, len(arrived)),
        grid_spec=pltpu.PrefetchScalarGridSpec(
            num_scalar_prefetch=1,
            grid=(2,),
            in_specs=[spec, spec, pl.BlockSpec(memory_space=pl.ANY)] + anywhere(arrived),
            out_specs=pl.BlockSpec((rows, columns), lambda q, target_ref: (target_ref[q], 0)),
        ),
        out_shape=jax.ShapeDtypeStruct(whole_array.shape, whole_array.dtype),
        input_output_aliases={3: 0},
        compiler_params=kernel_params(),
        cost_estimate=cost(1000, 1_000_000, 0),
        name="place",
    )(jnp.stack(targets).astype(jnp.int32), first, second, whole_array, *arrived)


def sum_kernel(*refs):
    total = refs[0][...]
    for ref in refs[1:-1]:
        total = total + ref[...]
    refs[-1][...] = total


def sum_after(terms, arrived):
    return pl.pallas_call(
        after(sum_kernel, len(terms), len(arrived)),
        in_specs=[pl.BlockSpec(memory_space=pltpu.VMEM)] * len(terms) + anywhere(arrived),
        out_specs=pl.BlockSpec(memory_space=pltpu.VMEM),
        out_shape=jax.ShapeDtypeStruct(terms[0].shape, terms[0].dtype),
        compiler_params=pltpu.CompilerParams(vmem_limit_bytes=50 * 1024 * 1024),
        cost_estimate=cost(10_000, 60_000, 0),
        name="sum",
    )(*terms, *arrived)


def ring_target(step):
    count = lax.axis_size("wshard")
    return (lax.axis_index("wshard") + count - 2 * step) % count


def ring_swap(partial, step):
    rows = partial.shape[0] // lax.axis_size("wshard")
    return swap(take_block(partial, ring_target(step) ^ 1, rows), "wshard", 1)


def ring_step(held):
    return lax.ppermute(held, "wshard", ring_route(lax.axis_size("wshard")))


def y_first(partial):
    count = lax.axis_size("wshard")
    parity = lax.axis_index("wshard") % 2
    rows = partial.shape[0] // count
    split = partial.reshape(count // 2, 2, rows, partial.shape[1])

    def half(parity):
        chosen = lax.dynamic_index_in_dim(split, parity, 1, keepdims=False)
        return chosen.reshape(count // 2 * rows, partial.shape[1])

    arrived = swap(half(1 - parity), "wshard", 1)
    return half(parity), arrived


def z_pieces(paired):
    count = lax.axis_size("wshard")
    index = lax.axis_index("wshard")
    rows = paired.shape[0] // (count // 2)
    return [
        swap(take_block(paired, (index ^ mask) // 2, rows), "wshard", mask)
        for mask in range(2, count, 2)
    ]


def pack_out(rows):
    split = rows.reshape(-1, HEADDIM, 2, rows.shape[1] // 2)
    return jnp.swapaxes(split, 1, 2).reshape(2 * rows.shape[0], rows.shape[1] // 2)


def unpack_out(packed):
    split = packed.reshape(-1, 2, HEADDIM, packed.shape[1])
    return jnp.swapaxes(split, 1, 2).reshape(packed.shape[0] // 2, 2 * packed.shape[1])


def gather_out(out_low, seq_index, groups):
    rows = out_low.shape[0]
    if rows % (groups * HEADDIM) == 0:
        mine = pick_rows(out_low, seq_index, groups)
        return lax.all_gather(mine, "wshard", axis=0, tiled=True)
    whole = lax.all_gather(out_low, "wshard", axis=0, tiled=True)
    return pick_heads(whole, 0, HEADDIM, seq_index, groups)


def pick_rows(values, seq_index, groups):
    rows = values.shape[0]
    split = values.reshape(rows // (groups * HEADDIM), groups, HEADDIM, values.shape[1])
    return lax.dynamic_index_in_dim(split, seq_index, 1, keepdims=False).reshape(
        rows // groups, values.shape[1]
    )


def sum_out_grad(grad, rows, seq_index, groups):
    grad = grad.astype(jnp.bfloat16)
    if rows % (groups * HEADDIM) == 0:
        mine = lax.psum_scatter(grad, "wshard", scatter_dimension=0, tiled=True)
        every = lax.all_gather(mine, "seq", axis=0, tiled=False)
        split = every.reshape(groups, rows // (groups * HEADDIM), HEADDIM, grad.shape[1])
        return jnp.moveaxis(split, 0, 1).reshape(rows, grad.shape[1]).astype(jnp.float32)
    blocks = grad.reshape(HEADS // groups, 1, HEADDIM, grad.shape[1])
    here = (jnp.arange(groups) == seq_index)[None, :, None, None]
    spread = jnp.where(here, blocks, jnp.zeros((), jnp.bfloat16)).reshape(DI, grad.shape[1])
    mine = lax.psum_scatter(spread, "wshard", scatter_dimension=0, tiled=True)
    return lax.psum(mine.astype(jnp.float32), "seq")


def shards(
    block_in,
    cotangent,
    in_weight,
    in_first,
    in_second,
    out_weight,
    out_first,
    out_second,
    vec_weight,
    vec_first,
    vec_second,
):
    rows_here = block_in.shape[1]
    groups = lax.axis_size("seq")
    seq_index = lax.axis_index("seq")
    local_heads = HEADS // groups
    local_di = DI // groups
    hidden_rows = block_in.reshape(rows_here, D)
    cot_rows = cotangent.reshape(rows_here, D)
    gain_one, gain_two, kernel, conv_bias, a_log, dt_bias, d_skip = split_vector(vec_weight)

    def heads_of(values, axis, width):
        return pick_heads(values, axis, width, seq_index, groups)

    lanes = 128
    channels = local_di + 2 * STATE
    packs = out_weight.shape[0] == groups * HEADDIM and lax.axis_size("wshard") == 8
    in_low = low(in_weight)
    rest_mine = jnp.concatenate(
        [
            heads_of(in_low[:, DI : 2 * DI], 1, HEADDIM),
            in_low[:, 2 * DI : 2 * DI + 2 * STATE],
            jnp.pad(heads_of(in_low[:, DI + CONVCH :], 1, 1), ((0, 0), (0, lanes - local_heads))),
        ],
        1,
    )
    gate_mine = heads_of(in_low[:, :DI], 1, HEADDIM)
    rest_weight, _, _ = shard_gather(rest_mine)
    hidden_low = seq_gather(hidden_rows)
    if packs:
        out_mine = pack_out(pick_rows(low(out_weight), seq_index, groups))
        gate_out, arrived, late = shard_gather(jnp.concatenate([gate_mine, out_mine], 1), 2)
    else:
        arrived = []
        gate_out = jnp.concatenate(
            [
                lax.all_gather(gate_mine, "wshard", axis=0, tiled=True),
                pack_out(gather_out(low(out_weight), seq_index, groups)),
            ],
            1,
        )
    cot = seq_gather(cot_rows)
    my_gain_two = heads_of(gain_two, 0, HEADDIM)[None, :]
    my_kernel = jnp.concatenate([heads_of(kernel[:, :DI], 1, HEADDIM), kernel[:, DI:]], 1)
    my_bias = jnp.concatenate([heads_of(conv_bias[:DI], 0, HEADDIM), conv_bias[DI:]], 0)

    def on_lanes(values):
        return jnp.pad(values, (0, lanes - local_heads))[None, :]

    heads_vectors = (
        on_lanes(heads_of(a_log, 0, 1)),
        on_lanes(heads_of(dt_bias, 0, 1)),
        jnp.repeat(heads_of(d_skip, 0, 1), HEADDIM)[None, :],
    )
    expand = (
        jnp.arange(lanes)[:, None] == jnp.arange(local_di)[None, :] // HEADDIM
    ).astype(jnp.float32)
    normed_low, conv_in, conv_pre, dt_raw, y, scanned, states = run_forward(
        hidden_low,
        rest_weight,
        gain_one[None, :],
        (my_kernel, my_bias[None, :]),
        heads_vectors,
        expand,
        arrived,
    )
    if packs:
        gate_out = place_blocks(
            gate_out, [late[0][0], late[1][0]], late[0][1], late[1][1], [scanned]
        )
    gating, d_gnorm, sums = run_gate(normed_low, scanned, cot, gate_out, my_gain_two)
    sums = sums[:2]
    for mask in (1, 2) if groups == 4 else ():
        sums = sums + swap(sums, "seq", mask)
    if groups != 4:
        sums = lax.psum(sums, "seq")
    sums = sums / DI
    scale = lax.rsqrt(sums[0] + norm_eps)
    slope = scale * scale * sums[1]
    block_part, d_gating, d_scanned, grad_gate_out, d_gain_two = run_middle(
        scanned,
        gating,
        d_gnorm,
        cot,
        normed_low,
        scale[:, None],
        slope[:, None],
        gate_out,
        my_gain_two,
    )
    if groups == 4:
        block_near = near_first(block_part)
        early = [block_near[1]]
    else:
        block_rows = seq_scatter(block_part, seq_pieces(block_part))
        early = []
    if packs:
        grad_gate, grad_out = grad_gate_out[:, :local_di], grad_gate_out[:, local_di:]
        gate_pieces = z_pieces(grad_gate)
        out_mine, out_arrived = y_first(grad_out)
        early = early + gate_pieces + [out_arrived]
    d_rest, d_kernel, d_conv_bias, d_skip_wide, d_head = run_backward(
        conv_in,
        conv_pre,
        dt_raw,
        y,
        states,
        d_scanned,
        my_kernel,
        heads_vectors,
        expand,
    )
    grad_rest = run_rest(normed_low, d_rest, early)
    before_normed = [grad_rest]
    between_normed = []
    if packs:
        gate_paired = add_block(
            grad_gate, lax.axis_index("wshard") // 2, gate_pieces, [grad_rest]
        )
        out_paired = add_block(out_mine, jnp.int32(0), [out_arrived], [grad_rest])
        rest_swaps = [ring_swap(grad_rest, 1)]
        held = add_block(grad_rest, ring_target(1), rest_swaps, [gate_paired, out_paired])
        before_normed = [held]
        ring_arrived = ring_step(held)
        rest_swaps = [ring_swap(grad_rest, 2)]
        between_normed = [ring_arrived] + rest_swaps
    normed_half = run_normed(
        hidden_low, d_gating, d_rest, gate_out, rest_weight, [], before_normed
    )
    d_normed_part, d_gain_one = run_normed(
        hidden_low, d_gating, d_rest, gate_out, rest_weight, normed_half, between_normed
    )
    shared = jnp.concatenate(
        [d_gain_one[0], d_kernel[:, local_di:].reshape(-1), d_conv_bias[0, local_di:]]
    )
    d_skip_part = jnp.sum(d_skip_wide.reshape(local_heads, HEADDIM), axis=1)
    apart = jnp.concatenate(
        [
            d_gain_two[0],
            d_kernel[:, :local_di].reshape(-1),
            d_conv_bias[0, :local_di],
            d_head[:, :local_heads].reshape(-1),
            d_skip_part,
        ]
    )
    vec_part = jnp.concatenate([shared, apart])[None]
    if packs:
        out_pieces = z_pieces(out_paired)
        shard_rows = gate_paired.shape[0] // 2
        parity = lax.axis_index("wshard") % 2
        gate_arrived = swap(take_block(gate_paired, 1 - parity, shard_rows), "wshard", 1)
        vec_swap = swap(vec_part, "wshard", 1)
        block_far = far_piece(*block_near)
        near = near_first(d_normed_part)
        pieces = rest_swaps + [ring_arrived]
        rest_swaps = [ring_swap(grad_rest, 3)]
        held = add_block(
            grad_rest,
            ring_target(2),
            pieces,
            out_pieces + [gate_arrived, vec_swap, near[1]] + rest_swaps,
        )
        gate_part = add_block(gate_paired, parity, [gate_arrived], [held])
        out_part = add_block(
            out_paired, lax.axis_index("wshard") // 2, out_pieces, [held]
        )
        gate_out_part = jnp.concatenate([gate_part, out_part], 1)
        gate_out_far = swap(gate_out_part, "seq", 2)
        vec_part = sum_after([vec_part, vec_swap], [held])
        vec_swap = swap(vec_part, "wshard", 2)
        pieces = rest_swaps + [ring_step(held)]
        rest_swaps = [ring_swap(grad_rest, 4)]
        held = add_block(
            grad_rest, ring_target(3), pieces, [vec_swap, block_far] + rest_swaps
        )
        vec_part = sum_after([vec_part, vec_swap], [held])
        vec_swap = swap(vec_part, "wshard", 4)
        far = far_piece(*near)
        pieces = rest_swaps + [ring_step(held)]
        rest_part = add_block(
            grad_rest, ring_target(4), pieces, [vec_swap, far, gate_out_far]
        )
        vec_part = sum_after([vec_part, vec_swap], [rest_part])
        block_rows = near_sum(*block_near, block_far)
        d_normed = near_sum(*near, far)
    else:
        if groups == 4:
            block_rows = near_sum(*block_near, far_piece(*block_near))
        rest_part = lax.psum_scatter(grad_rest, "wshard", scatter_dimension=0, tiled=True)
        vec_part = lax.psum(vec_part, "wshard")
        d_normed = seq_scatter(d_normed_part, seq_pieces(d_normed_part))
    block_out = hidden_rows.astype(jnp.float32) + block_rows
    own_hidden = hidden_rows.astype(jnp.float32)
    own_scale = lax.rsqrt(jnp.mean(own_hidden * own_hidden, axis=-1, keepdims=True) + norm_eps)
    own_unit = own_hidden * own_scale
    d_own = d_normed * gain_one[None, :]
    d_hidden = own_scale * (
        d_own - own_unit * jnp.mean(d_own * own_unit, axis=-1, keepdims=True)
    )
    block_grad = cot_rows.astype(jnp.float32) + d_hidden

    every = seq_gather(vec_part)
    shared, every = (
        jnp.sum(every[:, : shared.shape[0]], axis=0),
        every[:, shared.shape[0] :],
    )
    kernel_end = local_di * (1 + WIDTH)
    heads_at = kernel_end + local_di
    both_kernel = D + 2 * STATE * WIDTH
    vec_total = jnp.concatenate(
        [
            shared[:D],
            merge_heads(every[:, :local_di], 0, HEADDIM),
            jnp.concatenate(
                [
                    merge_heads(
                        every[:, local_di:kernel_end].reshape(groups, WIDTH, local_di), 1, HEADDIM
                    ),
                    shared[D:both_kernel].reshape(WIDTH, 2 * STATE),
                ],
                1,
            ).reshape(-1),
            merge_heads(every[:, kernel_end:heads_at], 0, HEADDIM),
            shared[both_kernel:],
            merge_heads(every[:, heads_at : heads_at + local_heads], 0, 1),
            merge_heads(every[:, heads_at + local_heads : heads_at + 2 * local_heads], 0, 1),
            merge_heads(every[:, heads_at + 2 * local_heads :], 0, 1),
        ]
    )
    vec_first_new, vec_second_new, vec_weight_new = adamw_step(
        vec_weight, vec_first, vec_second, vec_total, vector_rate, 0.0
    )
    rows_in = in_weight.shape[0]
    if packs:
        gate_out_every = seq_gather(gate_out_part, gate_out_far).reshape(groups, rows_in, -1)
        gate_every = gate_out_every[:, :, :local_di]
        out_total = unpack_out(
            gate_out_every[:, :, local_di:].reshape(groups * rows_in, -1)
        ).astype(jnp.float32)
    else:
        gate_part = lax.psum_scatter(
            grad_gate_out[:, :local_di], "wshard", scatter_dimension=0, tiled=True
        )
        gate_every = lax.all_gather(gate_part, "seq", axis=0, tiled=False)
        out_total = sum_out_grad(
            unpack_out(grad_gate_out[:, local_di:]), out_weight.shape[0], seq_index, groups
        )
    rest_every = seq_gather(rest_part).reshape(groups, rows_in, -1).astype(jnp.float32)
    both_total = jnp.sum(rest_every, axis=0)
    in_total = jnp.concatenate(
        [
            merge_heads(gate_every.astype(jnp.float32), 1, HEADDIM),
            merge_heads(rest_every[:, :, :local_di], 1, HEADDIM),
            both_total[:, local_di:channels],
            merge_heads(rest_every[:, :, channels : channels + local_heads], 1, 1),
        ],
        1,
    )
    in_first_new, in_second_new, in_weight_new = adamw_step(
        in_weight, in_first, in_second, in_total, matrix_rate, matrix_decay
    )
    out_first_new, out_second_new, out_weight_new = adamw_step(
        out_weight, out_first, out_second, out_total, matrix_rate, matrix_decay
    )
    return (
        block_out.reshape(1, rows_here, D),
        block_grad.reshape(1, rows_here, D),
        in_first_new,
        in_second_new,
        in_weight_new,
        out_first_new,
        out_second_new,
        out_weight_new,
        vec_first_new,
        vec_second_new,
        vec_weight_new,
    )


def solution(mesh):
    return jax.shard_map(
        shards,
        mesh=mesh,
        in_specs=(
            P("wshard", "seq", None),
            P("wshard", "seq", None),
            P("wshard", None),
            P("wshard", None),
            P("wshard", None),
            P("wshard", None),
            P("wshard", None),
            P("wshard", None),
            P(),
            P(),
            P(),
        ),
        out_specs=(
            P("wshard", "seq", None),
            P("wshard", "seq", None),
            P("wshard", None),
            P("wshard", None),
            P("wshard", None),
            P("wshard", None),
            P("wshard", None),
            P("wshard", None),
            P(),
            P(),
            P(),
        ),
        check_vma=False,
    )
```

```python
import jax
import jax.numpy as jnp
from jax import lax
from jax.experimental import pallas as pl
from jax.experimental.pallas import tpu as pltpu
from jax.sharding import PartitionSpec as P

D = 1024
HEADS = 32
HEADDIM = 64
STATE = 128
WIDTH = 4
BLOCK = 256
STEP = 10
DI = 2048
CONVCH = 2304


precise = lax.Precision.HIGHEST
norm_eps = 1e-05
beta_one = 0.9
beta_two = 0.95
adam_eps = 1e-08
matrix_rate = 0.05
matrix_decay = 0.1
vector_rate = 0.5


def rms_scale(values):
    return values * lax.rsqrt(jnp.mean(values * values, axis=-1, keepdims=True) + norm_eps)


def split_vector(vector):
    extents = [D, DI, WIDTH * CONVCH, CONVCH, HEADS, HEADS, HEADS]
    pieces = []
    offset = 0
    for extent in extents:
        pieces.append(vector[offset : offset + extent])
        offset = offset + extent
    pieces[2] = pieces[2].reshape(WIDTH, CONVCH)
    return pieces


def wide_back(extent, count):
    return pl.BlockSpec((BLOCK, extent), lambda q: (count - 1 - q, 0))


def whole(*shape):
    return pl.BlockSpec(shape, lambda q: (0,) * len(shape))


def dot_nt(left, right, precision=None):
    return lax.dot_general(
        left,
        right,
        (((1,), (1,)), ((), ())),
        precision=precision,
        preferred_element_type=jnp.float32,
    )


def dot_tn(left, right):
    return lax.dot_general(
        left, right, (((0,), (0,)), ((), ())), preferred_element_type=jnp.float32
    )


def dot_nn(left, right, precision=None):
    return jnp.dot(left, right, precision=precision, preferred_element_type=jnp.float32)


def sigmoid(values):
    return 1.0 / (1.0 + jnp.exp(-values))


def low(values):
    return values.astype(jnp.bfloat16)


def lower_mask():
    rows = lax.broadcasted_iota(jnp.int32, (BLOCK, BLOCK), 0)
    return rows >= lax.broadcasted_iota(jnp.int32, (BLOCK, BLOCK), 1)


def decay_sums(dt_raw, dt_bias, a_log, expand):
    shifted = dt_raw + dt_bias
    step = jnp.maximum(shifted, 0.0) + jnp.log1p(jnp.exp(-jnp.abs(shifted)))
    log_decay = -jnp.exp(a_log) * step
    ones = jnp.where(lower_mask(), 1.0, 0.0)
    running = dot_nn(ones, log_decay, precise)
    step_wide = dot_nn(step, expand, precise)
    running_wide = dot_nn(running, expand, precise)
    return shifted, step, log_decay, running, step_wide, running_wide


def place(result_ref, places_ref, first, blocks):
    for number, block in enumerate(blocks):
        rows = block.shape[0]
        start = pl.multiple_of(places_ref[first + number] * rows, rows)
        result_ref[pl.ds(start, rows), :] = block[...]


def forward_kernel(hidden_count, rest_count, places_ref, *refs):
    hidden_blocks = refs[:hidden_count]
    rest_blocks = refs[hidden_count : hidden_count + rest_count]
    (
        gain_one_ref,
        conv_ref,
        bias_ref,
        a_log_ref,
        dt_bias_ref,
        skip_ref,
        expand_ref,
        hidden_ref,
        rest_ref,
        normed_ref,
        normed_t_ref,
        conv_in_ref,
        conv_pre_ref,
        dt_ref,
        y_ref,
        scanned_ref,
        state_ref,
        ext,
        state,
    ) = refs[hidden_count + rest_count :]
    local_di = y_ref.shape[1]
    heads = local_di // HEADDIM
    channels = conv_in_ref.shape[1]

    @pl.when(pl.program_id(0) == 0)
    def _():
        ext[0:8, :] = jnp.zeros((8, ext.shape[1]), jnp.float32)
        state[...] = jnp.zeros_like(state)
        place(hidden_ref, places_ref, 0, hidden_blocks)
        place(rest_ref, places_ref, hidden_count, rest_blocks)

    chunk = pl.ds(pl.multiple_of(pl.program_id(0) * BLOCK, BLOCK), BLOCK)
    hidden = hidden_ref[chunk, :].astype(jnp.float32)
    normed = rms_scale(hidden) * gain_one_ref[...]
    normed_t_ref[...] = low(normed.T)
    normed = low(normed)
    normed_ref[...] = normed
    conv_in = dot_nn(normed, rest_ref[:, :channels])
    conv_in_ref[...] = conv_in
    ext[8 : 8 + BLOCK, :] = conv_in
    conv_pre = bias_ref[...] + conv_ref[WIDTH - 1 : WIDTH, :] * conv_in
    for tap in range(WIDTH - 1):
        first = 8 - WIDTH + 1 + tap
        conv_pre = conv_pre + conv_ref[tap : tap + 1, :] * ext[first : first + BLOCK, :]
    conv_pre_ref[...] = conv_pre
    ext[8 - WIDTH + 1 : 8, :] = ext[8 + BLOCK - WIDTH + 1 : 8 + BLOCK, :]
    conv_low = low(conv_pre * sigmoid(conv_pre))
    inner = conv_low[:, :local_di]
    b_rows = conv_low[:, local_di : local_di + STATE]
    c_rows = conv_low[:, local_di + STATE :]
    dt_raw = low(dot_nn(normed, rest_ref[:, channels:])).astype(jnp.float32)
    dt_ref[...] = dt_raw

    _, _, _, running, step_wide, running_wide = decay_sums(
        dt_raw, dt_bias_ref[...], a_log_ref[...], expand_ref[...]
    )
    running_t = running.T
    b_t = low(b_rows.astype(jnp.float32).T)
    scores = dot_nn(c_rows, b_t)
    mask = lower_mask()
    inner_wide = inner.astype(jnp.float32)
    stepped = step_wide * inner_wide
    stepped_low = low(stepped)
    first_half = lax.broadcasted_iota(jnp.int32, (BLOCK, 2 * HEADDIM), 1) < HEADDIM
    zero = jnp.zeros((), jnp.bfloat16)
    state_ref[...] = state[...].reshape(state_ref.shape)
    held = state[...]
    carried = jnp.exp(running_wide) * dot_nn(c_rows, low(held))
    for pair in range(heads // 2):
        span = slice(pair * 2 * HEADDIM, (pair + 1) * 2 * HEADDIM)
        both = stepped_low[:, span]
        total = carried[:, span]
        for half in range(2):
            head = 2 * pair + half
            differ = running[:, head : head + 1] - running_t[head : head + 1, :]
            mixed = low(jnp.exp(jnp.where(mask, differ, -jnp.inf)) * scores)
            mine = jnp.where(first_half if half == 0 else ~first_half, both, zero)
            total = total + dot_nn(mixed, mine)
        y_ref[:, span] = total
    last = running_wide[BLOCK - 1 : BLOCK, :]
    to_end = jnp.exp(last - running_wide)
    state[...] = jnp.exp(last) * held + dot_nn(b_t, low(to_end * stepped))
    scanned_ref[...] = low(y_ref[...] + skip_ref[...] * inner_wide)


def out_halves(packed):
    split = packed.reshape(-1, 2, HEADDIM, packed.shape[1])
    extent = packed.shape[0] // 2
    return (
        split[:, 0].reshape(extent, packed.shape[1]),
        split[:, 1].reshape(extent, packed.shape[1]),
    )


def gate_kernel(cot_count, gate_out_count, places_ref, *refs):
    cot_blocks = refs[:cot_count]
    gate_out_blocks = refs[cot_count : cot_count + gate_out_count]
    (
        normed_ref,
        scanned_ref,
        gain_two_ref,
        cot_ref,
        gate_out_ref,
        gating_ref,
        d_gnorm_ref,
        sums_ref,
    ) = refs[cot_count + gate_out_count :]
    local_di = gating_ref.shape[1]

    @pl.when(pl.program_id(0) == 0)
    def _():
        place(cot_ref, places_ref, 0, cot_blocks)
        place(gate_out_ref, places_ref, cot_count, gate_out_blocks)

    chunk = pl.ds(pl.multiple_of(pl.program_id(0) * BLOCK, BLOCK), BLOCK)
    gating = dot_nn(normed_ref[...], gate_out_ref[:, :local_di])
    gating_ref[...] = gating
    out_left, out_right = out_halves(gate_out_ref[:, local_di:])
    half = out_left.shape[1]
    d_gnorm = dot_nt(cot_ref[chunk, :half], out_left)
    d_gnorm = d_gnorm + dot_nt(cot_ref[chunk, half:], out_right)
    d_gnorm_ref[...] = d_gnorm
    gated = scanned_ref[...].astype(jnp.float32) * (gating * sigmoid(gating))
    ones = jnp.ones((8, local_di), jnp.float32)
    squares = dot_nt(ones, gated * gated, precise)
    products = dot_nt(ones, d_gnorm * gain_two_ref[...] * gated, precise)
    sums_ref[...] = jnp.where(
        lax.broadcasted_iota(jnp.int32, squares.shape, 0) == 0, squares, products
    )


def keep_chunk(value, here, number, mine_ref, send_ref):
    rows = pl.ds(pl.multiple_of(number * BLOCK, BLOCK), BLOCK)

    @pl.when(here)
    def _():
        mine_ref[rows, :] = value

    @pl.when(jnp.logical_not(here))
    def _():
        send_ref[rows, :] = value


def middle_kernel(gate_count, out_count, places_ref, *refs):
    (
        scanned_ref,
        gating_ref,
        d_gnorm_ref,
        cot_ref,
        normed_t_ref,
        scale_ref,
        slope_ref,
        out_ref,
        gain_two_ref,
        mine_ref,
        send_ref,
        d_gating_ref,
        d_scanned_ref,
        d_gain_two_ref,
    ) = refs[:14]
    gate_refs = refs[14 : 14 + gate_count]
    out_refs = refs[14 + gate_count : 14 + gate_count + out_count]
    left_sum, right_sum, gate_sum = refs[14 + gate_count + out_count :]
    chunk = pl.program_id(0)

    @pl.when(chunk == 0)
    def _():
        left_sum[...] = jnp.zeros_like(left_sum)
        right_sum[...] = jnp.zeros_like(right_sum)
        gate_sum[...] = jnp.zeros_like(gate_sum)
        d_gain_two_ref[...] = jnp.zeros_like(d_gain_two_ref)

    gating = gating_ref[...]
    open_part = sigmoid(gating)
    gate = gating * open_part
    scanned = scanned_ref[...].astype(jnp.float32)
    scale = scale_ref[:, :1]
    unit = scanned * gate * scale
    d_gnorm = d_gnorm_ref[...]
    gain_two = gain_two_ref[...]
    gnorm = low(unit * gain_two)
    out_left, out_right = out_halves(out_ref[...])
    half = out_left.shape[1]
    block_part = jnp.concatenate([low(dot_nn(gnorm, out_left)), low(dot_nn(gnorm, out_right))], 1)
    keep_chunk(block_part, chunk % 2 == places_ref[0], chunk // 2, mine_ref, send_ref)
    left_sum[...] += dot_tn(gnorm, cot_ref[:, :half])
    right_sum[...] += dot_tn(gnorm, cot_ref[:, half:])
    d_gain_two_ref[...] += jnp.sum(d_gnorm * unit, axis=0, keepdims=True)
    d_gated = scale * (d_gnorm * gain_two) - unit * slope_ref[:, :1]
    d_gating = low(d_gated * scanned * (open_part * (1.0 + gating * (1.0 - open_part))))
    d_gating_ref[...] = d_gating
    d_scanned_ref[...] = low(d_gated * gate)
    gate_sum[...] += dot_nn(normed_t_ref[...], d_gating)

    @pl.when(chunk == pl.num_programs(0) - 1)
    def _():
        for number, gate_ref in enumerate(gate_refs):
            rows = gate_ref.shape[0]
            start = pl.multiple_of(places_ref[1 + number] * rows, rows)
            gate_ref[...] = low(gate_sum[pl.ds(start, rows), :])
        for number, grad_ref in enumerate(out_refs):
            first = places_ref[1 + gate_count + number]
            for step in range(grad_ref.shape[0] // (2 * HEADDIM)):
                head = first + step * out_count
                rows = pl.ds(pl.multiple_of(head * HEADDIM, HEADDIM), HEADDIM)
                base = 2 * step * HEADDIM
                grad_ref[base : base + HEADDIM, :] = low(left_sum[rows, :])
                grad_ref[base + HEADDIM : base + 2 * HEADDIM, :] = low(right_sum[rows, :])


def backward_kernel(
    conv_in_ref,
    conv_pre_ref,
    dt_ref,
    y_ref,
    state_ref,
    d_scanned_ref,
    conv_ref,
    a_log_ref,
    dt_bias_ref,
    skip_ref,
    expand_ref,
    d_rest_ref,
    d_kernel_ref,
    d_conv_bias_ref,
    d_skip_ref,
    d_head_ref,
    ext,
    d_state,
    later_state,
):
    local_di = y_ref.shape[1]
    heads = local_di // HEADDIM
    chunk = pl.program_id(0)

    @pl.when(chunk == 0)
    def _():
        ext[BLOCK : BLOCK + 8, :] = jnp.zeros((8, ext.shape[1]), jnp.float32)
        d_state[...] = jnp.zeros_like(d_state)
        later_state[...] = jnp.zeros_like(later_state)
        d_kernel_ref[...] = jnp.zeros_like(d_kernel_ref)
        d_conv_bias_ref[...] = jnp.zeros_like(d_conv_bias_ref)
        d_skip_ref[...] = jnp.zeros_like(d_skip_ref)
        d_head_ref[...] = jnp.zeros_like(d_head_ref)

    expand = expand_ref[...]
    conv_pre = conv_pre_ref[...]
    open_part = sigmoid(conv_pre)
    conv_low = low(conv_pre * open_part)
    inner = conv_low[:, :local_di].astype(jnp.float32)
    b_rows = conv_low[:, local_di : local_di + STATE]
    c_rows = conv_low[:, local_di + STATE :]
    a_log = a_log_ref[...]
    shifted, _, log_decay, running, step_wide, running_wide = decay_sums(
        dt_ref[...], dt_bias_ref[...], a_log, expand
    )
    running_t = running.T
    b_t = low(b_rows.astype(jnp.float32).T)
    c_t = low(c_rows.astype(jnp.float32).T)
    scores = dot_nn(c_rows, b_t)
    scores_t = dot_nn(b_rows, c_t)
    mask = lower_mask()
    rows = lax.broadcasted_iota(jnp.int32, (BLOCK, BLOCK), 0)
    mask_t = rows <= lax.broadcasted_iota(jnp.int32, (BLOCK, BLOCK), 1)
    d_y_low = d_scanned_ref[...]
    d_y = d_y_low.astype(jnp.float32)
    stepped_low = low(step_wide * inner)
    stepped = stepped_low.astype(jnp.float32)
    last = running_wide[BLOCK - 1 : BLOCK, :]
    to_end = jnp.exp(last - running_wide)
    d_later = d_state[...]
    d_later_low = low(d_later)
    held = state_ref[...].reshape(d_state.shape)
    decayed_dy = low(jnp.exp(running_wide) * d_y)
    d_c = dot_nt(decayed_dy, low(held))
    d_b = dot_nt(low(to_end * stepped), d_later_low)
    d_stepped = to_end * dot_nn(b_rows, d_later_low)
    cross = jnp.sum(later_state[...] * d_later, axis=0, keepdims=True)
    d_state[...] = jnp.exp(last) * d_later + dot_nn(c_t, decayed_dy)
    later_state[...] = held
    first_half = lax.broadcasted_iota(jnp.int32, (BLOCK, 2 * HEADDIM), 1) < HEADDIM
    zero = jnp.zeros((), jnp.bfloat16)
    d_scores = jnp.zeros((BLOCK, BLOCK), jnp.float32)
    pieces = []
    for pair in range(heads // 2):
        span = slice(pair * 2 * HEADDIM, (pair + 1) * 2 * HEADDIM)
        total = d_stepped[:, span]
        for half in range(2):
            head = 2 * pair + half
            mine = jnp.where(first_half if half == 0 else ~first_half, d_y_low[:, span], zero)
            column = running[:, head : head + 1]
            row = running_t[head : head + 1, :]
            decay = jnp.exp(jnp.where(mask, column - row, -jnp.inf))
            decay_t = jnp.exp(jnp.where(mask_t, row - column, -jnp.inf))
            d_scores = d_scores + dot_nt(mine, stepped_low[:, span]) * decay
            total = total + dot_nn(low(decay_t * scores_t), mine)
        pieces.append(total)
    d_stepped = jnp.concatenate(pieces, 1)
    d_scores_low = low(d_scores)
    d_c = d_c + dot_nn(d_scores_low, b_rows)
    d_b = d_b + dot_nn(low(d_scores.T), c_rows)
    d_inner = step_wide * d_stepped + skip_ref[...] * d_y
    d_running = dot_nt(d_y * y_ref[...] - d_stepped * stepped, expand, precise)
    upper = jnp.where(mask_t, 1.0, 0.0)
    d_log = dot_nn(upper, d_running, precise) + dot_nt(cross, expand, precise)
    d_step = dot_nt(d_stepped * inner, expand, precise) - jnp.exp(a_log) * d_log
    d_dt = d_step * sigmoid(shifted)
    d_head_ref[0:1, :] += jnp.sum(d_log * log_decay, axis=0, keepdims=True)
    d_head_ref[1:2, :] += jnp.sum(d_dt, axis=0, keepdims=True)
    d_skip_ref[...] += jnp.sum(d_y * inner, axis=0, keepdims=True)

    d_conv_out = jnp.concatenate([d_inner, d_b, d_c], 1)
    d_pre = d_conv_out * (open_part * (1.0 + conv_pre * (1.0 - open_part)))
    ext[0:BLOCK, :] = d_pre
    d_conv_bias_ref[...] += jnp.sum(d_pre, axis=0, keepdims=True)
    conv_in = conv_in_ref[...]
    d_conv_in = jnp.zeros_like(conv_in)
    for tap in range(WIDTH):
        moved = ext[WIDTH - 1 - tap : WIDTH - 1 - tap + BLOCK, :]
        d_conv_in = d_conv_in + conv_ref[tap : tap + 1, :] * moved
        d_kernel_ref[tap : tap + 1, :] += jnp.sum(moved * conv_in, axis=0, keepdims=True)
    ext[BLOCK : BLOCK + 8, :] = ext[0:8, :]
    d_rest_ref[...] = jnp.concatenate([low(d_conv_in), low(d_dt)], 1)


def rest_kernel(places_ref, normed_t_ref, d_rest_ref, *grad_refs):
    for number, grad_ref in enumerate(grad_refs):
        rows = grad_ref.shape[0]
        start = pl.multiple_of(places_ref[number] * rows, rows)
        grad_ref[...] = low(dot_nn(normed_t_ref[pl.ds(start, rows), :], d_rest_ref[...]))


def normed_kernel(
    places_ref,
    hidden_ref,
    d_gating_ref,
    d_rest_ref,
    gate_weight_ref,
    rest_weight_ref,
    before_ref,
    mine_ref,
    send_ref,
    d_gain_one_ref,
):
    chunk = pl.program_id(0)

    @pl.when(chunk == 0)
    def _():
        d_gain_one_ref[...] = before_ref[...]

    d_normed = dot_nt(d_gating_ref[...], gate_weight_ref[...])
    d_normed = d_normed + dot_nt(d_rest_ref[...], rest_weight_ref[...])
    keep_chunk(low(d_normed), chunk == places_ref[0], 0, mine_ref, send_ref)
    unit = rms_scale(hidden_ref[...].astype(jnp.float32))
    d_gain_one_ref[...] += jnp.sum(d_normed * unit, axis=0, keepdims=True)


def first_lanes(shape):
    return lax.broadcasted_iota(jnp.int32, shape, 1) < HEADDIM


def prepare_kernel(places_ref, in_ref, out_ref, rest_ref, gate_out_ref):
    index = places_ref[0]
    local_di = gate_out_ref.shape[1] // 2
    lanes = 2 * HEADDIM
    rows = in_ref.shape[0]
    first = first_lanes((rows, lanes))
    odd = lax.broadcasted_iota(jnp.int32, (rows, lanes), 1) * 0 + index % 2 == 1

    def head(base, number):
        start = pl.multiple_of(base + (2 * number + index // 2) * lanes, lanes)
        return in_ref[:, pl.ds(start, lanes)]

    for base, result_ref in ((0, gate_out_ref), (DI, rest_ref)):
        for tile in range(local_di // lanes):
            left, right = head(base, 2 * tile), head(base, 2 * tile + 1)
            left = jnp.where(odd, pltpu.roll(left, HEADDIM, 1), left)
            right = jnp.where(odd, right, pltpu.roll(right, HEADDIM, 1))
            span = slice(tile * lanes, (tile + 1) * lanes)
            result_ref[:, span] = low(jnp.where(first, left, right))
    channels = local_di + 2 * STATE
    rest_ref[:, local_di:channels] = low(in_ref[:, 2 * DI : 2 * DI + 2 * STATE])
    source = lax.broadcasted_iota(jnp.int32, (HEADS, lanes), 0)
    target = lax.broadcasted_iota(jnp.int32, (HEADS, lanes), 1)
    groups = DI // local_di
    chosen = (source == groups * target + index) & (target < HEADS // groups)
    steps = low(in_ref[:, DI + CONVCH :])
    rest_ref[:, channels:] = low(dot_nn(steps, jnp.where(chosen, 1.0, 0.0).astype(jnp.bfloat16)))
    mine = out_ref[pl.ds(pl.multiple_of(index * HEADDIM, HEADDIM), HEADDIM), :]
    gate_out_ref[:HEADDIM, local_di:] = low(mine[:, : D // 2])
    gate_out_ref[HEADDIM:, local_di:] = low(mine[:, D // 2 :])


def update_kernel(groups, places_ref, *refs):
    gate_out_blocks = refs[:groups]
    rest_blocks = refs[groups : 2 * groups]
    (
        in_ref,
        in_first_ref,
        in_second_ref,
        out_ref,
        out_first_ref,
        out_second_ref,
        in_first_new_ref,
        in_second_new_ref,
        in_new_ref,
        out_first_new_ref,
        out_second_new_ref,
        out_new_ref,
        gate_out,
        rest,
    ) = refs[2 * groups :]
    chunk = pl.program_id(0)

    @pl.when(chunk == 0)
    def _():
        for number in range(groups):
            gate_out[places_ref[number]] = gate_out_blocks[number][...]
            rest[places_ref[number]] = rest_blocks[number][...]

    rows = in_ref.shape[0]
    here = pl.ds(pl.multiple_of(chunk * rows, rows), rows)
    lanes = 2 * HEADDIM
    local_di = gate_out.shape[2] // 2
    channels = local_di + 2 * STATE
    first = first_lanes((rows, lanes))

    def step_in(span, grad):
        first_new, second_new, new = adamw_step(
            in_ref[:, span],
            in_first_ref[:, span],
            in_second_ref[:, span],
            grad,
            matrix_rate,
            matrix_decay,
        )
        in_first_new_ref[:, span] = first_new
        in_second_new_ref[:, span] = second_new
        in_new_ref[:, span] = new

    for base, source in ((0, gate_out), (DI, rest)):
        for tile in range(DI // lanes):
            head, group = 2 * tile // groups, 2 * tile % groups
            start = head // 2 * lanes
            left = source[group, here, start : start + lanes].astype(jnp.float32)
            right = source[group + 1, here, start : start + lanes].astype(jnp.float32)
            if head % 2 == 0:
                right = pltpu.roll(right, HEADDIM, 1)
            else:
                left = pltpu.roll(left, HEADDIM, 1)
            step_in(
                slice(base + tile * lanes, base + (tile + 1) * lanes),
                jnp.where(first, left, right),
            )
    both = rest[0, here, local_di:channels].astype(jnp.float32)
    steps = jnp.zeros((rows, lanes), jnp.float32)
    source_lane = lax.broadcasted_iota(jnp.int32, (lanes, lanes), 0)
    target_lane = lax.broadcasted_iota(jnp.int32, (lanes, lanes), 1)
    for group in range(groups):
        if group > 0:
            both = both + rest[group, here, local_di:channels].astype(jnp.float32)
        chosen = (target_lane == groups * source_lane + group) & (target_lane < HEADS)
        spread = jnp.where(chosen, 1.0, 0.0).astype(jnp.bfloat16)
        steps = steps + dot_nn(rest[group, here, channels:], spread)
    step_in(slice(2 * DI, 2 * DI + 2 * STATE), both)
    step_in(slice(DI + CONVCH, DI + CONVCH + HEADS), steps[:, :HEADS])
    packed = gate_out[chunk, :, local_di:].astype(jnp.float32)
    for half in range(2):
        span = slice(half * D // 2, (half + 1) * D // 2)
        first_new, second_new, new = adamw_step(
            out_ref[:, span],
            out_first_ref[:, span],
            out_second_ref[:, span],
            packed[half * HEADDIM : (half + 1) * HEADDIM, :],
            matrix_rate,
            matrix_decay,
        )
        out_first_new_ref[:, span] = first_new
        out_second_new_ref[:, span] = second_new
        out_new_ref[:, span] = new


def kernel_params():
    return pltpu.CompilerParams(
        dimension_semantics=("arbitrary",), vmem_limit_bytes=56 * 1024 * 1024
    )


def cost(flops, moved, transcendentals):
    return pl.CostEstimate(flops=flops, bytes_accessed=moved, transcendentals=transcendentals)


def after(kernel, inputs, arrived):
    def run(*refs):
        kernel(*refs[:inputs], *refs[inputs + arrived :])

    return run


def corner(array):
    return pl.BlockSpec((min(16, array.shape[0]), 128), lambda *_: (0, 0))


def fixed(shape):
    return pl.BlockSpec(shape, lambda *_: (0,) * len(shape))


def rows_of(extent, first=0):
    return pl.BlockSpec((BLOCK, extent), lambda q, *_: (q + first, 0))


def struct(shape, dtype=jnp.float32):
    return jax.ShapeDtypeStruct(shape, dtype)


def call(kernel, places, inputs, in_specs, outputs, out_specs, scratch, grid, arrived, price, name):
    return pl.pallas_call(
        after(kernel, 1 + len(inputs), len(arrived)),
        grid_spec=pltpu.PrefetchScalarGridSpec(
            num_scalar_prefetch=1,
            grid=(grid,),
            in_specs=list(in_specs) + [corner(array) for array in arrived],
            out_specs=out_specs,
            scratch_shapes=scratch,
        ),
        out_shape=outputs,
        compiler_params=kernel_params(),
        cost_estimate=cost(*price),
        name=name,
    )(jnp.stack(places).astype(jnp.int32), *inputs, *arrived)


def run_prepare(index, in_weight, out_weight, lanes):
    rows = in_weight.shape[0]
    local_di = DI // 4
    rest = local_di + 2 * STATE + lanes
    return call(
        prepare_kernel,
        [index],
        [in_weight, out_weight],
        [fixed(in_weight.shape), fixed(out_weight.shape)],
        [struct((rows, rest), jnp.bfloat16), struct((rows, 2 * local_di), jnp.bfloat16)],
        [fixed((rows, rest)), fixed((rows, 2 * local_di))],
        [],
        1,
        [],
        (100_000_000, 4_000_000, 0),
        "prepare",
    )


def run_forward(hidden, rest, gain_one, conv, heads_vectors, expand):
    hidden_places, hidden_blocks = hidden
    rest_places, rest_blocks = rest
    length = hidden_blocks[0].shape[0] * len(hidden_blocks)
    chunks = length // BLOCK
    lanes, local_di = expand.shape
    rest_extent = rest_blocks[0].shape[1]
    channels = rest_extent - lanes
    vectors = [gain_one, *conv, *heads_vectors, expand]
    inputs = [*hidden_blocks, *rest_blocks, *vectors]
    return call(
        lambda *refs: forward_kernel(len(hidden_blocks), len(rest_blocks), *refs),
        hidden_places + rest_places,
        inputs,
        [fixed(array.shape) for array in inputs],
        [
            struct((length, D), jnp.bfloat16),
            struct((D, rest_extent), jnp.bfloat16),
            struct((length, D), jnp.bfloat16),
            struct((D, length), jnp.bfloat16),
            struct((length, channels)),
            struct((length, channels)),
            struct((length, lanes)),
            struct((length, local_di)),
            struct((length, local_di), jnp.bfloat16),
            struct((chunks, STATE, local_di)),
        ],
        [
            fixed((length, D)),
            fixed((D, rest_extent)),
            rows_of(D),
            pl.BlockSpec((D, BLOCK), lambda q, *_: (0, q)),
            rows_of(channels),
            rows_of(channels),
            rows_of(lanes),
            rows_of(local_di),
            rows_of(local_di),
            pl.BlockSpec((1, STATE, local_di), lambda q, *_: (q, 0, 0)),
        ],
        [
            pltpu.VMEM((8 + BLOCK, channels), jnp.float32),
            pltpu.VMEM((STATE, local_di), jnp.float32),
        ],
        chunks,
        [],
        (6_000_000_000, 30_000_000, 8_000_000),
        "forward",
    )


def run_gate(cot, gate_out, normed, scanned, gain_two):
    cot_places, cot_blocks = cot
    gate_out_places, gate_out_blocks = gate_out
    length, local_di = scanned.shape
    whole_blocks = [*cot_blocks, *gate_out_blocks]
    gate_out_shape = (D, gate_out_blocks[0].shape[1])
    return call(
        lambda *refs: gate_kernel(len(cot_blocks), len(gate_out_blocks), *refs),
        cot_places + gate_out_places,
        [*whole_blocks, normed, scanned, gain_two],
        [fixed(array.shape) for array in whole_blocks]
        + [rows_of(D), rows_of(local_di), fixed((1, local_di))],
        [
            struct((length, D), jnp.bfloat16),
            struct(gate_out_shape, jnp.bfloat16),
            struct((length, local_di)),
            struct((length, local_di)),
            struct((8, length)),
        ],
        [
            fixed((length, D)),
            fixed(gate_out_shape),
            rows_of(local_di),
            rows_of(local_di),
            pl.BlockSpec((8, BLOCK), lambda q, *_: (0, q)),
        ],
        [],
        length // BLOCK,
        [],
        (2_500_000_000, 12_000_000, 1_000_000),
        "gate",
    )


def run_middle(
    parity, gate_places, out_places, scanned, gating, d_gnorm, cot, normed_t, columns, gate_out, gain
):
    length, local_di = scanned.shape
    half = D // 2
    gate_shape = (D // len(gate_places), local_di)
    out_shape = (2 * local_di // len(out_places), half)
    shapes = [gate_shape] * len(gate_places) + [out_shape] * len(out_places)
    return call(
        lambda *refs: middle_kernel(len(gate_places), len(out_places), *refs),
        [parity] + gate_places + out_places,
        [scanned, gating, d_gnorm, cot, normed_t, *columns, gate_out, gain],
        [
            rows_of(local_di),
            rows_of(local_di),
            rows_of(local_di),
            rows_of(D),
            pl.BlockSpec((D, BLOCK), lambda q, *_: (0, q)),
            rows_of(1),
            rows_of(1),
            pl.BlockSpec((2 * local_di, half), lambda q, *_: (0, local_di // half)),
            fixed((1, local_di)),
        ],
        [
            struct((length // 2, D), jnp.bfloat16),
            struct((length // 2, D), jnp.bfloat16),
            struct((length, local_di), jnp.bfloat16),
            struct((length, local_di), jnp.bfloat16),
            struct((1, local_di)),
        ]
        + [struct(shape, jnp.bfloat16) for shape in shapes],
        [
            fixed((length // 2, D)),
            fixed((length // 2, D)),
            rows_of(local_di),
            rows_of(local_di),
            fixed((1, local_di)),
        ]
        + [fixed(shape) for shape in shapes],
        [
            pltpu.VMEM((local_di, half), jnp.float32),
            pltpu.VMEM((local_di, half), jnp.float32),
            pltpu.VMEM((D, local_di), jnp.float32),
        ],
        length // BLOCK,
        [],
        (4_000_000_000, 15_000_000, 500_000),
        "middle",
    )


def run_backward(
    conv_in, conv_pre, dt_raw, y, states, d_scanned, kernel, heads_vectors, expand
):
    length, local_di = y.shape
    chunks = length // BLOCK
    channels = conv_in.shape[1]
    lanes = expand.shape[0]
    shape = jax.ShapeDtypeStruct
    f32, bf16 = jnp.float32, jnp.bfloat16

    def back(extent):
        return wide_back(extent, chunks)

    return pl.pallas_call(
        backward_kernel,
        grid=(chunks,),
        in_specs=[
            back(channels),
            back(channels),
            back(lanes),
            back(local_di),
            pl.BlockSpec((1, STATE, local_di), lambda q: (chunks - 1 - q, 0, 0)),
            back(local_di),
            whole(WIDTH, channels),
            whole(1, lanes),
            whole(1, lanes),
            whole(1, local_di),
            whole(lanes, local_di),
        ],
        out_specs=[
            back(channels + lanes),
            whole(WIDTH, channels),
            whole(1, channels),
            whole(1, local_di),
            whole(2, lanes),
        ],
        out_shape=[
            shape((length, channels + lanes), bf16),
            shape((WIDTH, channels), f32),
            shape((1, channels), f32),
            shape((1, local_di), f32),
            shape((2, lanes), f32),
        ],
        scratch_shapes=[
            pltpu.VMEM((BLOCK + 8, channels), f32),
            pltpu.VMEM((STATE, local_di), f32),
            pltpu.VMEM((STATE, local_di), f32),
        ],
        compiler_params=kernel_params(),
        cost_estimate=cost(14_000_000_000, 40_000_000, 10_000_000),
        name="backward",
    )(conv_in, conv_pre, dt_raw, y, states, d_scanned, kernel, *heads_vectors, expand)


def run_rest(places, normed_t, d_rest, arrived):
    rest = d_rest.shape[1]
    shape = (D // len(places), rest)
    return call(
        rest_kernel,
        places,
        [normed_t, d_rest],
        [fixed(normed_t.shape), fixed(d_rest.shape)],
        [struct(shape, jnp.bfloat16)] * len(places),
        [fixed(shape)] * len(places),
        [],
        1,
        arrived,
        (2_000_000_000, 6_000_000, 0),
        "rest",
    )


def run_normed(half, parity, hidden, d_gating, d_rest, gate_out, rest_weight, before, arrived):
    length, local_di = d_gating.shape
    rest = d_rest.shape[1]
    return call(
        normed_kernel,
        [parity],
        [hidden, d_gating, d_rest, gate_out, rest_weight, before],
        [
            rows_of(D, 2 * half),
            rows_of(local_di, 2 * half),
            rows_of(rest, 2 * half),
            fixed((D, local_di)),
            fixed((D, rest)),
            fixed((1, D)),
        ],
        [
            struct((BLOCK, D), jnp.bfloat16),
            struct((BLOCK, D), jnp.bfloat16),
            struct((1, D)),
        ],
        [fixed((BLOCK, D)), fixed((BLOCK, D)), fixed((1, D))],
        [],
        2,
        arrived,
        (1_500_000_000, 6_000_000, 1000),
        "normed",
    )


def run_update(places, gate_out_blocks, rest_blocks, in_arrays, out_arrays):
    groups = len(places)
    blocks = [*gate_out_blocks, *rest_blocks]
    rows_in = in_arrays[0].shape[0] // groups
    rows_out = out_arrays[0].shape[0] // groups
    arrays = [*in_arrays, *out_arrays]
    specs = [
        pl.BlockSpec((rows, array.shape[1]), lambda q, *_: (q, 0))
        for rows, array in zip([rows_in] * 3 + [rows_out] * 3, arrays)
    ]
    return call(
        lambda *refs: update_kernel(groups, *refs),
        places,
        [*blocks, *arrays],
        [fixed(array.shape) for array in blocks] + specs,
        [struct(array.shape) for array in arrays],
        specs,
        [
            pltpu.VMEM((groups,) + gate_out_blocks[0].shape, jnp.bfloat16),
            pltpu.VMEM((groups,) + rest_blocks[0].shape, jnp.bfloat16),
        ],
        groups,
        [],
        (20_000_000, 22_000_000, 1_000_000),
        "update",
    )


def adamw_step(weight, first, second, grad, rate, decay):
    first_new = beta_one * first + (1.0 - beta_one) * grad
    second_new = beta_two * second + (1.0 - beta_two) * grad * grad
    fix_one = 1.0 - beta_one**STEP
    fix_two = 1.0 - beta_two**STEP
    normalized = first_new / fix_one / (jnp.sqrt(second_new / fix_two) + adam_eps)
    return (first_new, second_new, weight - rate * (normalized + decay * weight))


def pick_heads(values, axis, width, index, groups):
    shape = values.shape
    split = shape[:axis] + (HEADS // groups, groups, width) + shape[axis + 1 :]
    taken = lax.dynamic_index_in_dim(values.reshape(split), index, axis + 1, keepdims=False)
    return taken.reshape(shape[:axis] + (HEADS // groups * width,) + shape[axis + 1 :])


def merge_heads(stacked, axis, width):
    groups = stacked.shape[0]
    shape = stacked.shape[1:]
    split = (groups,) + shape[:axis] + (HEADS // groups, width) + shape[axis + 1 :]
    moved = jnp.moveaxis(stacked.reshape(split), 0, axis + 1)
    return moved.reshape(shape[:axis] + (HEADS * width,) + shape[axis + 1 :])


def swap(values, axis, mask):
    route = [(i, i ^ mask) for i in range(lax.axis_size(axis))]
    return lax.ppermute(values, axis, route)


def seq_blocks(rows, far=None):
    index = lax.axis_index("seq")
    far = swap(rows, "seq", 2) if far is None else far
    blocks = [rows, swap(rows, "seq", 1), far, swap(far, "seq", 1)]
    return [index ^ mask for mask in range(4)], blocks


def ring_step(held):
    count = lax.axis_size("wshard")
    return lax.ppermute(held, "wshard", [(i, (i + 2) % count) for i in range(count)])


def ring_blocks(rows):
    count = lax.axis_size("wshard")
    index = lax.axis_index("wshard")
    places, blocks = [], []
    for step in range(count // 2):
        source = (index + count - 2 * step) % count
        places = places + [source, source ^ 1]
        blocks = blocks + [rows, swap(rows, "wshard", 1)]
        if step < count // 2 - 1:
            rows = ring_step(rows)
    return places, blocks


def add_kernel(places_ref, *refs):
    total = refs[0][...].astype(jnp.float32)
    for ref in refs[1:-1]:
        total = total + ref[...].astype(jnp.float32)
    refs[-1][...] = total.astype(refs[-1].dtype)


def add(terms, arrived):
    spec = fixed(terms[0].shape)
    return call(
        add_kernel,
        [jnp.int32(0)],
        terms,
        [spec] * len(terms),
        struct(terms[0].shape, terms[0].dtype),
        spec,
        [],
        1,
        arrived,
        (200_000, 900_000, 0),
        "add",
    )


def take_block(values, index, rows):
    return lax.dynamic_slice_in_dim(values, index * rows, rows, 0)


def pack_out(rows):
    split = rows.reshape(-1, HEADDIM, 2, rows.shape[1] // 2)
    return jnp.swapaxes(split, 1, 2).reshape(2 * rows.shape[0], rows.shape[1] // 2)


def unpack_out(packed):
    split = packed.reshape(-1, 2, HEADDIM, packed.shape[1])
    return jnp.swapaxes(split, 1, 2).reshape(packed.shape[0] // 2, 2 * packed.shape[1])


def gather_out(out_low, seq_index, groups):
    rows = out_low.shape[0]
    if rows % (groups * HEADDIM) == 0:
        mine = pick_rows(out_low, seq_index, groups)
        return lax.all_gather(mine, "wshard", axis=0, tiled=True)
    whole = lax.all_gather(out_low, "wshard", axis=0, tiled=True)
    return pick_heads(whole, 0, HEADDIM, seq_index, groups)


def pick_rows(values, seq_index, groups):
    rows = values.shape[0]
    split = values.reshape(rows // (groups * HEADDIM), groups, HEADDIM, values.shape[1])
    return lax.dynamic_index_in_dim(split, seq_index, 1, keepdims=False).reshape(
        rows // groups, values.shape[1]
    )


def sum_out_grad(grad, rows, seq_index, groups):
    grad = grad.astype(jnp.bfloat16)
    if rows % (groups * HEADDIM) == 0:
        mine = lax.psum_scatter(grad, "wshard", scatter_dimension=0, tiled=True)
        every = lax.all_gather(mine, "seq", axis=0, tiled=False)
        split = every.reshape(groups, rows // (groups * HEADDIM), HEADDIM, grad.shape[1])
        return jnp.moveaxis(split, 0, 1).reshape(rows, grad.shape[1]).astype(jnp.float32)
    blocks = grad.reshape(HEADS // groups, 1, HEADDIM, grad.shape[1])
    here = (jnp.arange(groups) == seq_index)[None, :, None, None]
    spread = jnp.where(here, blocks, jnp.zeros((), jnp.bfloat16)).reshape(DI, grad.shape[1])
    mine = lax.psum_scatter(spread, "wshard", scatter_dimension=0, tiled=True)
    return lax.psum(mine.astype(jnp.float32), "seq")


def shards(
    block_in,
    cotangent,
    in_weight,
    in_first,
    in_second,
    out_weight,
    out_first,
    out_second,
    vec_weight,
    vec_first,
    vec_second,
):
    rows_here = block_in.shape[1]
    groups = lax.axis_size("seq")
    seq_index = lax.axis_index("seq")
    local_heads = HEADS // groups
    local_di = DI // groups
    hidden_rows = block_in.reshape(rows_here, D)
    cot_rows = cotangent.reshape(rows_here, D)
    gain_one, gain_two, kernel, conv_bias, a_log, dt_bias, d_skip = split_vector(vec_weight)

    def heads_of(values, axis, width):
        return pick_heads(values, axis, width, seq_index, groups)

    lanes = 128
    channels = local_di + 2 * STATE
    shard_index = lax.axis_index("wshard")
    rings = lax.axis_size("wshard") == 8
    near = seq_index % 2
    far = seq_index // 2
    if rings:
        y, z = shard_index % 2, shard_index // 2
        rest_mine, gate_out_mine = run_prepare(seq_index, in_weight, out_weight, lanes)
        rest = ring_blocks(rest_mine)
        hidden = seq_blocks(hidden_rows)
        gate_out = ring_blocks(gate_out_mine)
        cot = seq_blocks(cot_rows)
        gate_places = [z ^ mask for mask in range(4)]
        out_places = [y, 1 - y]
        rest_places = [
            (shard_index + 8 - 2 * step) % 8 ^ other for step in range(1, 5) for other in (0, 1)
        ]
    else:
        in_low = low(in_weight)
        steps_mine = heads_of(in_low[:, DI + CONVCH :], 1, 1)
        rest_mine = jnp.concatenate(
            [
                heads_of(in_low[:, DI : 2 * DI], 1, HEADDIM),
                in_low[:, 2 * DI : 2 * DI + 2 * STATE],
                jnp.pad(steps_mine, ((0, 0), (0, lanes - local_heads))),
            ],
            1,
        )
        gate_mine = heads_of(in_low[:, :DI], 1, HEADDIM)
        origin = [jnp.int32(0)]
        rest = (origin, [lax.all_gather(rest_mine, "wshard", axis=0, tiled=True)])
        hidden = (origin, [lax.all_gather(hidden_rows, "seq", axis=0, tiled=True)])
        cot = (origin, [lax.all_gather(cot_rows, "seq", axis=0, tiled=True)])
        gate_mine = lax.all_gather(gate_mine, "wshard", axis=0, tiled=True)
        out_mine = pack_out(gather_out(low(out_weight), seq_index, groups))
        gate_out = (origin, [jnp.concatenate([gate_mine, out_mine], 1)])
        gate_places, out_places, rest_places = origin, origin, origin
    my_gain_two = heads_of(gain_two, 0, HEADDIM)[None, :]
    my_kernel = jnp.concatenate([heads_of(kernel[:, :DI], 1, HEADDIM), kernel[:, DI:]], 1)
    my_bias = jnp.concatenate([heads_of(conv_bias[:DI], 0, HEADDIM), conv_bias[DI:]], 0)

    def on_lanes(values):
        return jnp.pad(values, (0, lanes - local_heads))[None, :]

    heads_vectors = (
        on_lanes(heads_of(a_log, 0, 1)),
        on_lanes(heads_of(dt_bias, 0, 1)),
        jnp.repeat(heads_of(d_skip, 0, 1), HEADDIM)[None, :],
    )
    expand = (
        jnp.arange(lanes)[:, None] == jnp.arange(local_di)[None, :] // HEADDIM
    ).astype(jnp.float32)
    (
        hidden_low,
        rest_weight,
        normed_low,
        normed_t,
        conv_in,
        conv_pre,
        dt_raw,
        y_part,
        scanned,
        states,
    ) = run_forward(
        hidden, rest, gain_one[None, :], (my_kernel, my_bias[None, :]), heads_vectors, expand
    )
    cot_low, gate_out_weight, gating, d_gnorm, sums = run_gate(
        cot, gate_out, normed_low, scanned, my_gain_two
    )
    sums = sums[:2]
    for mask in (1, 2):
        sums = sums + swap(sums, "seq", mask)
    sums = sums / DI
    scale = lax.rsqrt(sums[0] + norm_eps)
    slope = scale * scale * sums[1]
    middle = run_middle(
        near,
        gate_places,
        out_places,
        scanned,
        gating,
        d_gnorm,
        cot_low,
        normed_t,
        (scale[:, None], slope[:, None]),
        gate_out_weight,
        my_gain_two,
    )
    block_mine, block_send, d_gating, d_scanned, d_gain_two = middle[:5]
    gate_grads = middle[5 : 5 + len(gate_places)]
    out_grads = middle[5 + len(gate_places) :]
    block_arrived = swap(block_send, "seq", 1)
    early = [block_arrived]
    if rings:
        gate_pieces = [swap(gate_grads[mask], "wshard", 2 * mask) for mask in range(1, 4)]
        out_arrived = swap(out_grads[1], "wshard", 1)
        early = early + gate_pieces + [out_arrived]
    d_rest, d_kernel, d_conv_bias, d_skip_wide, d_head = run_backward(
        conv_in,
        conv_pre,
        dt_raw,
        y_part,
        states,
        d_scanned,
        my_kernel,
        heads_vectors,
        expand,
    )
    rest_grads = run_rest(rest_places, normed_t, d_rest, early)

    def sum_of(one, two):
        return low(one.astype(jnp.float32) + two.astype(jnp.float32))

    block_sum = sum_of(block_mine, block_arrived)
    block_far = swap(take_block(block_sum, 1 - far, rows_here), "seq", 2)
    before_first, before_second = [rest_grads[0]], []
    if rings:
        rest_arrived = swap(rest_grads[1], "wshard", 1)
        gate_paired = add([gate_grads[0]] + gate_pieces, [rest_grads[0]])
        out_paired = add([out_grads[0], out_arrived], [rest_grads[0]])
        held = add([rest_grads[0], rest_arrived], [gate_paired, out_paired])
        ring_arrived = ring_step(held)
        rows_shard = in_weight.shape[0]
        out_pieces = [
            swap(take_block(out_paired, z ^ mask, rows_shard), "wshard", 2 * mask)
            for mask in range(1, 4)
        ]
        before_first = [held]
        before_second = [ring_arrived, block_far] + out_pieces
    mine_one, send_one, d_gain_one = run_normed(
        0,
        near,
        hidden_low,
        d_gating,
        d_rest,
        gate_out_weight,
        rest_weight,
        jnp.zeros((1, D), jnp.float32),
        before_first,
    )
    arrived_one = swap(send_one, "seq", 1)
    mine_two, send_two, d_gain_one = run_normed(
        1,
        near,
        hidden_low,
        d_gating,
        d_rest,
        gate_out_weight,
        rest_weight,
        d_gain_one,
        before_second,
    )
    arrived_two = swap(send_two, "seq", 1)
    normed_one = mine_one.astype(jnp.float32) + arrived_one.astype(jnp.float32)
    normed_two = mine_two.astype(jnp.float32) + arrived_two.astype(jnp.float32)
    normed_far = swap(low(jnp.where(far == 0, normed_two, normed_one)), "seq", 2)
    normed_here = jnp.where(far == 0, normed_one, normed_two)
    shared = jnp.concatenate(
        [d_gain_one[0], d_kernel[:, local_di:].reshape(-1), d_conv_bias[0, local_di:]]
    )
    d_skip_part = jnp.sum(d_skip_wide.reshape(local_heads, HEADDIM), axis=1)
    apart = jnp.concatenate(
        [
            d_gain_two[0],
            d_kernel[:, :local_di].reshape(-1),
            d_conv_bias[0, :local_di],
            d_head[:, :local_heads].reshape(-1),
            d_skip_part,
        ]
    )
    vec_part = jnp.concatenate([shared, apart])[None]
    if rings:
        gate_arrived = swap(take_block(gate_paired, 1 - y, rows_shard), "wshard", 1)
        rest_arrived = swap(rest_grads[3], "wshard", 1)
        held = add(
            [rest_grads[2], rest_arrived, ring_arrived],
            [gate_arrived, arrived_one, arrived_two],
        )
        ring_arrived = ring_step(held)
        rest_arrived = swap(rest_grads[5], "wshard", 1)
        vec_arrived = swap(vec_part, "wshard", 1)
        gate_part = add([take_block(gate_paired, y, rows_shard), gate_arrived], [held])
        out_part = add([take_block(out_paired, z, rows_shard)] + out_pieces, [held])
        gate_out_part = jnp.concatenate([gate_part, out_part], 1)
        held = add([rest_grads[4], rest_arrived, ring_arrived], [vec_arrived])
        ring_arrived = ring_step(held)
        rest_arrived = swap(rest_grads[7], "wshard", 1)
        vec_part = add([vec_part, vec_arrived], [held])
        vec_arrived = swap(vec_part, "wshard", 2)
        gate_out_far = swap(gate_out_part, "seq", 2)
        rest_part = add(
            [rest_grads[6], rest_arrived, ring_arrived],
            [vec_arrived, normed_far, gate_out_far],
        )
        vec_part = add([vec_part, vec_arrived], [rest_part])
        vec_part = vec_part + swap(vec_part, "wshard", 4)
        vec_places, vec_blocks = seq_blocks(vec_part)
        every = jnp.zeros((groups, vec_part.shape[1]), jnp.float32)
        for spot, block in zip(vec_places, vec_blocks):
            every = lax.dynamic_update_slice_in_dim(every, block, spot, 0)
    else:
        vec_part = lax.psum(vec_part, "wshard")
        every = lax.all_gather(vec_part, "seq", axis=0, tiled=True)
    block_here = take_block(block_sum, far, rows_here).astype(jnp.float32)
    block_out = hidden_rows.astype(jnp.float32) + (block_here + block_far.astype(jnp.float32))
    d_normed = normed_here + normed_far.astype(jnp.float32)
    own_hidden = hidden_rows.astype(jnp.float32)
    own_scale = lax.rsqrt(jnp.mean(own_hidden * own_hidden, axis=-1, keepdims=True) + norm_eps)
    own_unit = own_hidden * own_scale
    d_own = d_normed * gain_one[None, :]
    d_hidden = own_scale * (
        d_own - own_unit * jnp.mean(d_own * own_unit, axis=-1, keepdims=True)
    )
    block_grad = cot_rows.astype(jnp.float32) + d_hidden
    shared, every = (
        jnp.sum(every[:, : shared.shape[0]], axis=0),
        every[:, shared.shape[0] :],
    )
    kernel_end = local_di * (1 + WIDTH)
    heads_at = kernel_end + local_di
    both_kernel = D + 2 * STATE * WIDTH
    vec_total = jnp.concatenate(
        [
            shared[:D],
            merge_heads(every[:, :local_di], 0, HEADDIM),
            jnp.concatenate(
                [
                    merge_heads(
                        every[:, local_di:kernel_end].reshape(groups, WIDTH, local_di), 1, HEADDIM
                    ),
                    shared[D:both_kernel].reshape(WIDTH, 2 * STATE),
                ],
                1,
            ).reshape(-1),
            merge_heads(every[:, kernel_end:heads_at], 0, HEADDIM),
            shared[both_kernel:],
            merge_heads(every[:, heads_at : heads_at + local_heads], 0, 1),
            merge_heads(every[:, heads_at + local_heads : heads_at + 2 * local_heads], 0, 1),
            merge_heads(every[:, heads_at + 2 * local_heads :], 0, 1),
        ]
    )
    vec_first_new, vec_second_new, vec_weight_new = adamw_step(
        vec_weight, vec_first, vec_second, vec_total, vector_rate, 0.0
    )
    if rings:
        rest_spots, rest_blocks = seq_blocks(rest_part)
        _, gate_out_blocks = seq_blocks(gate_out_part, gate_out_far)
        (
            in_first_new,
            in_second_new,
            in_weight_new,
            out_first_new,
            out_second_new,
            out_weight_new,
        ) = run_update(
            rest_spots,
            gate_out_blocks,
            rest_blocks,
            (in_weight, in_first, in_second),
            (out_weight, out_first, out_second),
        )
    else:
        rest_part = lax.psum_scatter(rest_grads[0], "wshard", scatter_dimension=0, tiled=True)
        gate_part = lax.psum_scatter(gate_grads[0], "wshard", scatter_dimension=0, tiled=True)
        gate_every = lax.all_gather(gate_part, "seq", axis=0, tiled=False).astype(jnp.float32)
        rest_every = lax.all_gather(rest_part, "seq", axis=0, tiled=False).astype(jnp.float32)
        out_total = sum_out_grad(
            unpack_out(out_grads[0]), out_weight.shape[0], seq_index, groups
        )
        in_total = jnp.concatenate(
            [
                merge_heads(gate_every, 1, HEADDIM),
                merge_heads(rest_every[:, :, :local_di], 1, HEADDIM),
                jnp.sum(rest_every[:, :, local_di:channels], axis=0),
                merge_heads(rest_every[:, :, channels : channels + local_heads], 1, 1),
            ],
            1,
        )
        in_first_new, in_second_new, in_weight_new = adamw_step(
            in_weight, in_first, in_second, in_total, matrix_rate, matrix_decay
        )
        out_first_new, out_second_new, out_weight_new = adamw_step(
            out_weight, out_first, out_second, out_total, matrix_rate, matrix_decay
        )
    return (
        block_out.reshape(1, rows_here, D),
        block_grad.reshape(1, rows_here, D),
        in_first_new,
        in_second_new,
        in_weight_new,
        out_first_new,
        out_second_new,
        out_weight_new,
        vec_first_new,
        vec_second_new,
        vec_weight_new,
    )


def solution(mesh):
    return jax.shard_map(
        shards,
        mesh=mesh,
        in_specs=(
            P("wshard", "seq", None),
            P("wshard", "seq", None),
            P("wshard", None),
            P("wshard", None),
            P("wshard", None),
            P("wshard", None),
            P("wshard", None),
            P("wshard", None),
            P(),
            P(),
            P(),
        ),
        out_specs=(
            P("wshard", "seq", None),
            P("wshard", "seq", None),
            P("wshard", None),
            P("wshard", None),
            P("wshard", None),
            P("wshard", None),
            P("wshard", None),
            P("wshard", None),
            P(),
            P(),
            P(),
        ),
        check_vma=False,
    )
```

```python
import jax
import jax.numpy as jnp
from jax import lax
from jax.experimental import pallas as pl
from jax.experimental.pallas import tpu as pltpu
from jax.sharding import PartitionSpec as P

D = 1024
HEADS = 32
HEADDIM = 64
STATE = 128
WIDTH = 4
BLOCK = 256
STEP = 10
DI = 2048
CONVCH = 2304


precise = lax.Precision.HIGHEST
norm_eps = 1e-05
beta_one = 0.9
beta_two = 0.95
adam_eps = 1e-08
matrix_rate = 0.05
matrix_decay = 0.1
vector_rate = 0.5


def rms_scale(values):
    return values * lax.rsqrt(jnp.mean(values * values, axis=-1, keepdims=True) + norm_eps)


def split_vector(vector):
    extents = [D, DI, WIDTH * CONVCH, CONVCH, HEADS, HEADS, HEADS]
    pieces = []
    offset = 0
    for extent in extents:
        pieces.append(vector[offset : offset + extent])
        offset = offset + extent
    pieces[2] = pieces[2].reshape(WIDTH, CONVCH)
    return pieces


def dot_nt(left, right, precision=None):
    return lax.dot_general(
        left,
        right,
        (((1,), (1,)), ((), ())),
        precision=precision,
        preferred_element_type=jnp.float32,
    )


def dot_tn(left, right):
    return lax.dot_general(
        left, right, (((0,), (0,)), ((), ())), preferred_element_type=jnp.float32
    )


def dot_nn(left, right, precision=None):
    return jnp.dot(left, right, precision=precision, preferred_element_type=jnp.float32)


def sigmoid(values):
    return 1.0 / (1.0 + jnp.exp(-values))


def low(values):
    return values.astype(jnp.bfloat16)


def lower_mask():
    rows = lax.broadcasted_iota(jnp.int32, (BLOCK, BLOCK), 0)
    return rows >= lax.broadcasted_iota(jnp.int32, (BLOCK, BLOCK), 1)


def decay_sums(dt_raw, dt_bias, a_log, expand):
    shifted = dt_raw + dt_bias
    step = jnp.maximum(shifted, 0.0) + jnp.log1p(jnp.exp(-jnp.abs(shifted)))
    log_decay = -jnp.exp(a_log) * step
    ones = jnp.where(lower_mask(), 1.0, 0.0)
    running = dot_nn(ones, log_decay, precise)
    step_wide = dot_nn(step, expand, precise)
    running_wide = dot_nn(running, expand, precise)
    return shifted, step, log_decay, running, step_wide, running_wide


def place_rows(result_ref, place, block):
    rows = block.shape[0]
    result_ref[pl.ds(pl.multiple_of(place * rows, rows), rows), :] = block


def place_columns(result_ref, place, block):
    rows, columns = block.shape
    start = pl.multiple_of(place * columns, columns)
    result_ref[:rows, pl.ds(start, columns)] = block


def forward_kernel(both_count, rest_count, places_ref, *refs):
    both_blocks = refs[:both_count]
    rest_blocks = refs[both_count : both_count + rest_count]
    (
        gain_one_ref,
        conv_ref,
        bias_ref,
        a_log_ref,
        dt_bias_ref,
        skip_ref,
        expand_ref,
        hidden_ref,
        cot_ref,
        rest_ref,
        normed_ref,
        conv_in_ref,
        conv_pre_ref,
        dt_ref,
        y_ref,
        scanned_ref,
        state_ref,
        ext,
        state,
    ) = refs[both_count + rest_count :]
    local_di = y_ref.shape[1]
    heads = local_di // HEADDIM
    channels = conv_in_ref.shape[1]

    @pl.when(pl.program_id(0) == 0)
    def _():
        ext[0:8, :] = jnp.zeros((8, ext.shape[1]), jnp.float32)
        state[...] = jnp.zeros_like(state)
        for number, block in enumerate(both_blocks):
            half = block.shape[0] // 2
            place_rows(hidden_ref, places_ref[number], block[:half, :])
            place_rows(cot_ref, places_ref[number], block[half:, :])
        rest_ref[channels:, :] = jnp.zeros_like(rest_ref[channels:, :])
        for number, block in enumerate(rest_blocks):
            place_columns(rest_ref, places_ref[both_count + number], block[...])

    chunk = pl.ds(pl.multiple_of(pl.program_id(0) * BLOCK, BLOCK), BLOCK)
    hidden = hidden_ref[chunk, :].astype(jnp.float32)
    normed = low(rms_scale(hidden) * gain_one_ref[...])
    normed_ref[...] = normed
    conv_in = dot_nt(normed, rest_ref[:channels, :])
    conv_in_ref[...] = conv_in
    ext[8 : 8 + BLOCK, :] = conv_in
    conv_pre = bias_ref[...] + conv_ref[WIDTH - 1 : WIDTH, :] * conv_in
    for tap in range(WIDTH - 1):
        first = 8 - WIDTH + 1 + tap
        conv_pre = conv_pre + conv_ref[tap : tap + 1, :] * ext[first : first + BLOCK, :]
    conv_pre_ref[...] = conv_pre
    ext[8 - WIDTH + 1 : 8, :] = ext[8 + BLOCK - WIDTH + 1 : 8 + BLOCK, :]
    conv_low = low(conv_pre * sigmoid(conv_pre))
    inner = conv_low[:, :local_di]
    b_rows = conv_low[:, local_di : local_di + STATE]
    c_rows = conv_low[:, local_di + STATE :]
    dt_raw = low(dot_nt(normed, rest_ref[channels:, :])).astype(jnp.float32)
    dt_ref[...] = dt_raw

    _, _, _, running, step_wide, running_wide = decay_sums(
        dt_raw, dt_bias_ref[...], a_log_ref[...], expand_ref[...]
    )
    running_t = running.T
    b_t = low(b_rows.astype(jnp.float32).T)
    scores = dot_nn(c_rows, b_t)
    mask = lower_mask()
    inner_wide = inner.astype(jnp.float32)
    stepped = step_wide * inner_wide
    stepped_low = low(stepped)
    first_half = lax.broadcasted_iota(jnp.int32, (BLOCK, 2 * HEADDIM), 1) < HEADDIM
    zero = jnp.zeros((), jnp.bfloat16)
    state_ref[...] = state[...].reshape(state_ref.shape)
    held = state[...]
    carried = jnp.exp(running_wide) * dot_nn(c_rows, low(held))
    for pair in range(heads // 2):
        span = slice(pair * 2 * HEADDIM, (pair + 1) * 2 * HEADDIM)
        both = stepped_low[:, span]
        total = carried[:, span]
        for half in range(2):
            head = 2 * pair + half
            differ = running[:, head : head + 1] - running_t[head : head + 1, :]
            mixed = low(jnp.exp(jnp.where(mask, differ, -jnp.inf)) * scores)
            mine = jnp.where(first_half if half == 0 else ~first_half, both, zero)
            total = total + dot_nn(mixed, mine)
        y_ref[:, span] = total
    last = running_wide[BLOCK - 1 : BLOCK, :]
    to_end = jnp.exp(last - running_wide)
    state[...] = jnp.exp(last) * held + dot_nn(b_t, low(to_end * stepped))
    scanned_ref[...] = low(y_ref[...] + skip_ref[...] * inner_wide)


def gate_kernel(count, places_ref, *refs):
    blocks = refs[:count]
    (
        cot_ref,
        normed_ref,
        scanned_ref,
        gain_two_ref,
        gate_ref,
        out_ref,
        gating_ref,
        d_gnorm_ref,
        sums_ref,
    ) = refs[count:]
    local_di = gating_ref.shape[1]

    @pl.when(pl.program_id(0) == 0)
    def _():
        if count == 2:
            gate_ref[...] = blocks[0][...]
            out_ref[...] = blocks[1][...]
        else:
            for number, block in enumerate(blocks):
                spot = places_ref[number]
                place_columns(gate_ref, spot, block[:local_di, :])
                for tile in range(D // block.shape[1]):
                    first = local_di + tile * HEADDIM
                    columns = slice(tile * block.shape[1], (tile + 1) * block.shape[1])
                    place_rows(out_ref.at[:, columns], spot, block[first : first + HEADDIM, :])

    gating = dot_nt(normed_ref[...], gate_ref[...])
    gating_ref[...] = gating
    d_gnorm = dot_nt(cot_ref[...], out_ref[...])
    d_gnorm_ref[...] = d_gnorm
    gated = scanned_ref[...].astype(jnp.float32) * (gating * sigmoid(gating))
    ones = jnp.ones((8, local_di), jnp.float32)
    squares = dot_nt(ones, gated * gated, precise)
    products = dot_nt(ones, d_gnorm * gain_two_ref[...] * gated, precise)
    sums_ref[...] = jnp.where(
        lax.broadcasted_iota(jnp.int32, squares.shape, 0) == 0, squares, products
    )


def keep_chunk(value, here, number, mine_ref, send_ref):
    rows = pl.ds(pl.multiple_of(number * BLOCK, BLOCK), BLOCK)

    @pl.when(here)
    def _():
        mine_ref[rows, :] = value

    @pl.when(jnp.logical_not(here))
    def _():
        send_ref[rows, :] = value


def middle_kernel(gate_count, out_count, places_ref, *refs):
    (
        scanned_ref,
        gating_ref,
        d_gnorm_ref,
        cot_ref,
        normed_ref,
        sums_one_ref,
        sums_two_ref,
        sums_three_ref,
        sums_four_ref,
        out_ref,
        gain_two_ref,
        mine_ref,
        send_ref,
        d_gating_ref,
        d_scanned_ref,
        d_gain_two_ref,
    ) = refs[:16]
    gate_refs = refs[16 : 16 + gate_count]
    out_refs = refs[16 + gate_count : 16 + gate_count + out_count]
    out_sum, gate_sum = refs[16 + gate_count + out_count :]
    chunk = pl.program_id(0)

    @pl.when(chunk == 0)
    def _():
        out_sum[...] = jnp.zeros_like(out_sum)
        gate_sum[...] = jnp.zeros_like(gate_sum)
        d_gain_two_ref[...] = jnp.zeros_like(d_gain_two_ref)

    sums = (sums_one_ref[...] + sums_two_ref[...]) + (sums_three_ref[...] + sums_four_ref[...])
    sums = (sums / DI).T
    scale = lax.rsqrt(sums[:, 0:1] + norm_eps)
    slope = scale * scale * sums[:, 1:2]
    gating = gating_ref[...]
    open_part = sigmoid(gating)
    gate = gating * open_part
    scanned = scanned_ref[...].astype(jnp.float32)
    unit = scanned * gate * scale
    d_gnorm = d_gnorm_ref[...]
    gain_two = gain_two_ref[...]
    gnorm = low(unit * gain_two)
    block_part = low(dot_nn(gnorm, out_ref[...]))
    keep_chunk(block_part, chunk % 2 == places_ref[0], chunk // 2, mine_ref, send_ref)
    out_sum[...] += dot_tn(gnorm, cot_ref[...])
    d_gain_two_ref[...] += jnp.sum(d_gnorm * unit, axis=0, keepdims=True)
    d_gated = scale * (d_gnorm * gain_two) - unit * slope
    d_gating = low(d_gated * scanned * (open_part * (1.0 + gating * (1.0 - open_part))))
    d_gating_ref[...] = d_gating
    d_scanned_ref[...] = low(d_gated * gate)
    gate_sum[...] += dot_tn(d_gating, normed_ref[...])

    @pl.when(chunk == pl.num_programs(0) - 1)
    def _():
        for number, gate_ref in enumerate(gate_refs):
            columns = gate_ref.shape[1]
            start = pl.multiple_of(places_ref[1 + number] * columns, columns)
            gate_ref[...] = low(gate_sum[:, pl.ds(start, columns)])
        for number, grad_ref in enumerate(out_refs):
            columns = grad_ref.shape[1]
            first = places_ref[1 + gate_count + number]
            for step in range(out_sum.shape[0] // HEADDIM // out_count):
                head = first + step * out_count
                rows = pl.ds(pl.multiple_of(head * HEADDIM, HEADDIM), HEADDIM)
                for tile in range(D // columns):
                    base = (step * (D // columns) + tile) * HEADDIM
                    grad_ref[base : base + HEADDIM, :] = low(
                        out_sum[rows, tile * columns : (tile + 1) * columns]
                    )


def backward_kernel(
    grad_count,
    places_ref,
    normed_ref,
    conv_in_ref,
    conv_pre_ref,
    dt_ref,
    y_ref,
    state_ref,
    d_scanned_ref,
    conv_ref,
    a_log_ref,
    dt_bias_ref,
    skip_ref,
    expand_ref,
    d_rest_ref,
    d_kernel_ref,
    d_conv_bias_ref,
    d_skip_ref,
    d_head_ref,
    *refs,
):
    grad_refs = refs[:grad_count]
    ext, d_state, later_state, rest_sum = refs[grad_count:]
    local_di = y_ref.shape[1]
    heads = local_di // HEADDIM
    chunk = pl.program_id(0)

    @pl.when(chunk == 0)
    def _():
        ext[BLOCK : BLOCK + 8, :] = jnp.zeros((8, ext.shape[1]), jnp.float32)
        d_state[...] = jnp.zeros_like(d_state)
        later_state[...] = jnp.zeros_like(later_state)
        rest_sum[...] = jnp.zeros_like(rest_sum)
        d_kernel_ref[...] = jnp.zeros_like(d_kernel_ref)
        d_conv_bias_ref[...] = jnp.zeros_like(d_conv_bias_ref)
        d_skip_ref[...] = jnp.zeros_like(d_skip_ref)
        d_head_ref[...] = jnp.zeros_like(d_head_ref)

    expand = expand_ref[...]
    conv_pre = conv_pre_ref[...]
    open_part = sigmoid(conv_pre)
    conv_low = low(conv_pre * open_part)
    inner = conv_low[:, :local_di].astype(jnp.float32)
    b_rows = conv_low[:, local_di : local_di + STATE]
    c_rows = conv_low[:, local_di + STATE :]
    a_log = a_log_ref[...]
    shifted, _, log_decay, running, step_wide, running_wide = decay_sums(
        dt_ref[...], dt_bias_ref[...], a_log, expand
    )
    running_t = running.T
    b_t = low(b_rows.astype(jnp.float32).T)
    c_t = low(c_rows.astype(jnp.float32).T)
    scores = dot_nn(c_rows, b_t)
    scores_t = dot_nn(b_rows, c_t)
    mask = lower_mask()
    rows = lax.broadcasted_iota(jnp.int32, (BLOCK, BLOCK), 0)
    mask_t = rows <= lax.broadcasted_iota(jnp.int32, (BLOCK, BLOCK), 1)
    d_y_low = d_scanned_ref[...]
    d_y = d_y_low.astype(jnp.float32)
    stepped_low = low(step_wide * inner)
    stepped = stepped_low.astype(jnp.float32)
    last = running_wide[BLOCK - 1 : BLOCK, :]
    to_end = jnp.exp(last - running_wide)
    d_later = d_state[...]
    d_later_low = low(d_later)
    held = state_ref[...].reshape(d_state.shape)
    decayed_dy = low(jnp.exp(running_wide) * d_y)
    d_c = dot_nt(decayed_dy, low(held))
    d_b = dot_nt(low(to_end * stepped), d_later_low)
    d_stepped = to_end * dot_nn(b_rows, d_later_low)
    cross = jnp.sum(later_state[...] * d_later, axis=0, keepdims=True)
    d_state[...] = jnp.exp(last) * d_later + dot_nn(c_t, decayed_dy)
    later_state[...] = held
    first_half = lax.broadcasted_iota(jnp.int32, (BLOCK, 2 * HEADDIM), 1) < HEADDIM
    zero = jnp.zeros((), jnp.bfloat16)
    d_scores = jnp.zeros((BLOCK, BLOCK), jnp.float32)
    pieces = []
    for pair in range(heads // 2):
        span = slice(pair * 2 * HEADDIM, (pair + 1) * 2 * HEADDIM)
        total = d_stepped[:, span]
        for half in range(2):
            head = 2 * pair + half
            mine = jnp.where(first_half if half == 0 else ~first_half, d_y_low[:, span], zero)
            column = running[:, head : head + 1]
            row = running_t[head : head + 1, :]
            decay = jnp.exp(jnp.where(mask, column - row, -jnp.inf))
            decay_t = jnp.exp(jnp.where(mask_t, row - column, -jnp.inf))
            d_scores = d_scores + dot_nt(mine, stepped_low[:, span]) * decay
            total = total + dot_nn(low(decay_t * scores_t), mine)
        pieces.append(total)
    d_stepped = jnp.concatenate(pieces, 1)
    d_scores_low = low(d_scores)
    d_c = d_c + dot_nn(d_scores_low, b_rows)
    d_b = d_b + dot_nn(low(d_scores.T), c_rows)
    d_inner = step_wide * d_stepped + skip_ref[...] * d_y
    d_running = dot_nt(d_y * y_ref[...] - d_stepped * stepped, expand, precise)
    upper = jnp.where(mask_t, 1.0, 0.0)
    d_log = dot_nn(upper, d_running, precise) + dot_nt(cross, expand, precise)
    d_step = dot_nt(d_stepped * inner, expand, precise) - jnp.exp(a_log) * d_log
    d_dt = d_step * sigmoid(shifted)
    d_head_ref[0:1, :] += jnp.sum(d_log * log_decay, axis=0, keepdims=True)
    d_head_ref[1:2, :] += jnp.sum(d_dt, axis=0, keepdims=True)
    d_skip_ref[...] += jnp.sum(d_y * inner, axis=0, keepdims=True)

    d_conv_out = jnp.concatenate([d_inner, d_b, d_c], 1)
    d_pre = d_conv_out * (open_part * (1.0 + conv_pre * (1.0 - open_part)))
    ext[0:BLOCK, :] = d_pre
    d_conv_bias_ref[...] += jnp.sum(d_pre, axis=0, keepdims=True)
    conv_in = conv_in_ref[...]
    d_conv_in = jnp.zeros_like(conv_in)
    for tap in range(WIDTH):
        moved = ext[WIDTH - 1 - tap : WIDTH - 1 - tap + BLOCK, :]
        d_conv_in = d_conv_in + conv_ref[tap : tap + 1, :] * moved
        d_kernel_ref[tap : tap + 1, :] += jnp.sum(moved * conv_in, axis=0, keepdims=True)
    ext[BLOCK : BLOCK + 8, :] = ext[0:8, :]
    d_rest = jnp.concatenate([low(d_conv_in), low(d_dt)], 1)
    d_rest_ref[...] = d_rest
    rest_sum[...] += dot_tn(d_rest, normed_ref[...])

    @pl.when(chunk == pl.num_programs(0) - 1)
    def _():
        for number, grad_ref in enumerate(grad_refs):
            rows, columns = grad_ref.shape
            start = pl.multiple_of(places_ref[number] * columns, columns)
            grad_ref[...] = low(rest_sum[:rows, pl.ds(start, columns)])


def sum_of(*refs):
    total = refs[0][...].astype(jnp.float32)
    for ref in refs[1:]:
        total = total + ref[...].astype(jnp.float32)
    return total


def pair_kernel(places_ref, *refs):
    gate, out, block = refs[:4], refs[4:6], refs[6:8]
    gate_keep_ref, gate_send_ref, block_keep_ref, block_send_ref = refs[8:12]
    out_refs = refs[12:]
    paired = sum_of(*gate)
    columns = gate_keep_ref.shape[1]
    even = places_ref[0] == 0
    first, second = low(paired[:, :columns]), low(paired[:, columns:])
    gate_keep_ref[...] = jnp.where(even, first, second)
    gate_send_ref[...] = jnp.where(even, second, first)
    rows = block_keep_ref.shape[0]
    for ref, place in ((block_keep_ref, places_ref[1]), (block_send_ref, 1 - places_ref[1])):
        here = pl.ds(pl.multiple_of(place * rows, rows), rows)
        ref[...] = low(sum_of(block[0].at[here, :], block[1].at[here, :]))
    for number, ref in enumerate(out_refs):
        rows = ref.shape[0]
        start = pl.multiple_of(places_ref[2 + number] * rows, rows)
        here = pl.ds(start, rows)
        ref[...] = low(sum_of(out[0].at[here, :], out[1].at[here, :]))


def normed_kernel(
    places_ref,
    hidden_ref,
    d_gating_ref,
    d_rest_ref,
    gate_weight_ref,
    rest_weight_ref,
    mine_ref,
    send_ref,
    d_gain_one_ref,
):
    chunk = pl.program_id(0)

    @pl.when(chunk == 0)
    def _():
        d_gain_one_ref[...] = jnp.zeros_like(d_gain_one_ref)

    d_normed = dot_nn(d_gating_ref[...], gate_weight_ref[...])
    d_normed = d_normed + dot_nn(d_rest_ref[...], rest_weight_ref[...])
    keep_chunk(low(d_normed), chunk % 2 == places_ref[0], chunk // 2, mine_ref, send_ref)
    unit = rms_scale(hidden_ref[...].astype(jnp.float32))
    d_gain_one_ref[...] += jnp.sum(d_normed * unit, axis=0, keepdims=True)


def prepare_kernel(places_ref, in_ref, out_ref, hidden_ref, cot_ref, rest_ref, gate_out_ref, both_ref):
    index = places_ref[0]
    local_di = gate_out_ref.shape[0] // 2
    groups = DI // local_di
    for head in range(HEADS // groups):
        rows = slice(head * HEADDIM, (head + 1) * HEADDIM)
        for base, result_ref in ((0, gate_out_ref), (DI, rest_ref)):
            start = pl.multiple_of(base + (groups * head + index) * HEADDIM, HEADDIM)
            result_ref[rows, :] = low(in_ref[pl.ds(start, HEADDIM), :])
    channels = local_di + 2 * STATE
    rest_ref[local_di:channels, :] = low(in_ref[2 * DI : 2 * DI + 2 * STATE, :])
    rows = rest_ref.shape[0] - channels
    target = lax.broadcasted_iota(jnp.int32, (rows, HEADS), 0)
    source = lax.broadcasted_iota(jnp.int32, (rows, HEADS), 1)
    chosen = (source == groups * target + index) & (target < HEADS // groups)
    steps = low(in_ref[DI + CONVCH :, :])
    rest_ref[channels:, :] = low(dot_nn(jnp.where(chosen, 1.0, 0.0).astype(jnp.bfloat16), steps))
    mine = pl.ds(pl.multiple_of(index * HEADDIM, HEADDIM), HEADDIM)
    columns = gate_out_ref.shape[1]
    for tile in range(D // columns):
        first = local_di + tile * HEADDIM
        gate_out_ref[first : first + HEADDIM, :] = low(
            out_ref[mine, tile * columns : (tile + 1) * columns]
        )
    half = hidden_ref.shape[0]
    both_ref[:half, :] = hidden_ref[...]
    both_ref[half:, :] = cot_ref[...]


def update_kernel(groups, places_ref, *refs):
    gate_out_blocks = refs[:groups]
    rest_blocks = refs[groups : 2 * groups]
    in_refs = refs[2 * groups : 2 * groups + 3]
    out_refs = refs[2 * groups + 3 : 2 * groups + 6]
    in_new_refs = refs[2 * groups + 6 : 2 * groups + 9]
    out_new_refs = refs[2 * groups + 9 : 2 * groups + 12]
    gate_out, rest = refs[2 * groups + 12 :]
    chunk = pl.program_id(0)
    local_di = gate_out.shape[1] // 2
    channels = local_di + 2 * STATE
    parts = DI // in_refs[0].shape[0]

    @pl.when(chunk == 0)
    def _():
        for number in range(groups):
            gate_out[places_ref[number]] = gate_out_blocks[number][...]
            rest[places_ref[number]] = rest_blocks[number][...]

    def step(old_refs, new_refs, rows, columns, grad):
        results = adamw_step(
            *[ref[rows, columns] for ref in old_refs], grad, matrix_rate, matrix_decay
        )
        for ref, result in zip(new_refs, results):
            ref[rows, columns] = result

    def step_heads(source, part):
        heads = local_di // HEADDIM // parts
        for head in range(heads):
            start = pl.multiple_of((part * heads + head) * HEADDIM, HEADDIM)
            for group in range(groups):
                first = (head * groups + group) * HEADDIM
                grad = source[group, pl.ds(start, HEADDIM), :].astype(jnp.float32)
                step(in_refs, in_new_refs, slice(first, first + HEADDIM), slice(None), grad)

    @pl.when(chunk < parts)
    def _():
        step_heads(gate_out, chunk)

    @pl.when((chunk >= parts) & (chunk < 2 * parts))
    def _():
        step_heads(rest, chunk - parts)

    @pl.when(chunk == 2 * parts)
    def _():
        both = rest[0, local_di:channels, :].astype(jnp.float32)
        rows = rest.shape[1] - channels
        steps = jnp.zeros((HEADS, rest.shape[2]), jnp.float32)
        target = lax.broadcasted_iota(jnp.int32, (HEADS, rows), 0)
        source = lax.broadcasted_iota(jnp.int32, (HEADS, rows), 1)
        for group in range(groups):
            if group > 0:
                both = both + rest[group, local_di:channels, :].astype(jnp.float32)
            chosen = jnp.where(target == groups * source + group, 1.0, 0.0).astype(jnp.bfloat16)
            steps = steps + dot_nn(chosen, rest[group, channels:, :])
        step(in_refs, in_new_refs, slice(0, 2 * STATE), slice(None), both)
        step(in_refs, in_new_refs, slice(2 * STATE, 2 * STATE + HEADS), slice(None), steps)

    @pl.when(chunk < groups)
    def _():
        columns = gate_out.shape[2]
        for tile in range(D // columns):
            first = local_di + tile * HEADDIM
            grad = gate_out[chunk, first : first + HEADDIM, :].astype(jnp.float32)
            span = slice(tile * columns, (tile + 1) * columns)
            step(out_refs, out_new_refs, slice(None), span, grad)


def kernel_params():
    return pltpu.CompilerParams(
        dimension_semantics=("arbitrary",), vmem_limit_bytes=56 * 1024 * 1024
    )


def cost(flops, moved, transcendentals):
    return pl.CostEstimate(flops=flops, bytes_accessed=moved, transcendentals=transcendentals)


def after(kernel, inputs, arrived):
    def run(*refs):
        kernel(*refs[:inputs], *refs[inputs + arrived :])

    return run


def corner(array):
    return pl.BlockSpec((min(16, array.shape[0]), 128), lambda *_: (0, 0))


def fixed(shape):
    return pl.BlockSpec(shape, lambda *_: (0,) * len(shape))


def rows_of(extent, first=0):
    return pl.BlockSpec((BLOCK, extent), lambda q, *_: (q + first, 0))


def struct(shape, dtype=jnp.float32):
    return jax.ShapeDtypeStruct(shape, dtype)


def call(kernel, places, inputs, in_specs, outputs, out_specs, scratch, grid, arrived, price, name):
    return pl.pallas_call(
        after(kernel, 1 + len(inputs), len(arrived)),
        grid_spec=pltpu.PrefetchScalarGridSpec(
            num_scalar_prefetch=1,
            grid=(grid,),
            in_specs=list(in_specs) + [corner(array) for array in arrived],
            out_specs=out_specs,
            scratch_shapes=scratch,
        ),
        out_shape=outputs,
        compiler_params=kernel_params(),
        cost_estimate=cost(*price),
        name=name,
    )(jnp.stack(places).astype(jnp.int32), *inputs, *arrived)


def run_prepare(index, in_t, out_weight, hidden, cot):
    columns = in_t.shape[1]
    local_di = DI // 4
    shapes = [
        (local_di + 2 * STATE + 16, columns),
        (2 * local_di, columns),
        (2 * hidden.shape[0], D),
    ]
    inputs = [in_t, out_weight, hidden, cot]
    return call(
        prepare_kernel,
        [index],
        inputs,
        [fixed(array.shape) for array in inputs],
        [struct(shape, jnp.bfloat16) for shape in shapes],
        [fixed(shape) for shape in shapes],
        [],
        1,
        [],
        (100_000_000, 4_000_000, 0),
        "prepare",
    )


def run_forward(both, rest, gain_one, conv, heads_vectors, expand):
    both_places, both_blocks = both
    rest_places, rest_blocks = rest
    length = both_blocks[0].shape[0] // 2 * len(both_blocks)
    chunks = length // BLOCK
    lanes, local_di = expand.shape
    channels = local_di + 2 * STATE
    vectors = [gain_one, *conv, *heads_vectors, expand]
    inputs = [*both_blocks, *rest_blocks, *vectors]
    return call(
        lambda *refs: forward_kernel(len(both_blocks), len(rest_blocks), *refs),
        both_places + rest_places,
        inputs,
        [fixed(array.shape) for array in inputs],
        [
            struct((length, D), jnp.bfloat16),
            struct((length, D), jnp.bfloat16),
            struct((channels + lanes, D), jnp.bfloat16),
            struct((length, D), jnp.bfloat16),
            struct((length, channels)),
            struct((length, channels)),
            struct((length, lanes)),
            struct((length, local_di)),
            struct((length, local_di), jnp.bfloat16),
            struct((chunks, STATE, local_di)),
        ],
        [
            fixed((length, D)),
            fixed((length, D)),
            fixed((channels + lanes, D)),
            rows_of(D),
            rows_of(channels),
            rows_of(channels),
            rows_of(lanes),
            rows_of(local_di),
            rows_of(local_di),
            pl.BlockSpec((1, STATE, local_di), lambda q, *_: (q, 0, 0)),
        ],
        [
            pltpu.VMEM((8 + BLOCK, channels), jnp.float32),
            pltpu.VMEM((STATE, local_di), jnp.float32),
        ],
        chunks,
        [],
        (6_000_000_000, 30_000_000, 8_000_000),
        "forward",
    )


def run_gate(gate_out, cot, normed, scanned, gain_two):
    places, blocks = gate_out
    length, local_di = scanned.shape
    return call(
        lambda *refs: gate_kernel(len(blocks), *refs),
        places,
        [*blocks, cot, normed, scanned, gain_two],
        [fixed(array.shape) for array in blocks]
        + [rows_of(D), rows_of(D), rows_of(local_di), fixed((1, local_di))],
        [
            struct((local_di, D), jnp.bfloat16),
            struct((local_di, D), jnp.bfloat16),
            struct((length, local_di)),
            struct((length, local_di)),
            struct((8, length)),
        ],
        [
            fixed((local_di, D)),
            fixed((local_di, D)),
            rows_of(local_di),
            rows_of(local_di),
            pl.BlockSpec((8, BLOCK), lambda q, *_: (0, q)),
        ],
        [],
        length // BLOCK,
        [],
        (2_500_000_000, 12_000_000, 1_000_000),
        "gate",
    )


def run_middle(parity, gate_places, out_places, scanned, gating, d_gnorm, cot, normed, sums, out, gain):
    length, local_di = scanned.shape
    gate_shape = (local_di, D // len(gate_places))
    out_shape = (local_di, D) if len(out_places) == 1 else (local_di * D // 256, 128)
    shapes = [gate_shape] * len(gate_places) + [out_shape] * len(out_places)
    return call(
        lambda *refs: middle_kernel(len(gate_places), len(out_places), *refs),
        [parity] + gate_places + out_places,
        [scanned, gating, d_gnorm, cot, normed, *sums, out, gain],
        [
            rows_of(local_di),
            rows_of(local_di),
            rows_of(local_di),
            rows_of(D),
            rows_of(D),
        ]
        + [pl.BlockSpec((8, BLOCK), lambda q, *_: (0, q))] * 4
        + [fixed((local_di, D)), fixed((1, local_di))],
        [
            struct((length // 2, D), jnp.bfloat16),
            struct((length // 2, D), jnp.bfloat16),
            struct((length, local_di), jnp.bfloat16),
            struct((length, local_di), jnp.bfloat16),
            struct((1, local_di)),
        ]
        + [struct(shape, jnp.bfloat16) for shape in shapes],
        [
            fixed((length // 2, D)),
            fixed((length // 2, D)),
            rows_of(local_di),
            rows_of(local_di),
            fixed((1, local_di)),
        ]
        + [fixed(shape) for shape in shapes],
        [pltpu.VMEM((local_di, D), jnp.float32), pltpu.VMEM((local_di, D), jnp.float32)],
        length // BLOCK,
        [],
        (4_000_000_000, 15_000_000, 500_000),
        "middle",
    )


def run_backward(
    places, normed, conv_in, conv_pre, dt_raw, y, states, d_scanned, kernel, heads_vectors, expand
):
    length, local_di = y.shape
    chunks = length // BLOCK
    channels = conv_in.shape[1]
    lanes = expand.shape[0]
    grad = (channels + 16, D // len(places))

    def back(extent):
        return pl.BlockSpec((BLOCK, extent), lambda q, *_: (chunks - 1 - q, 0))

    return call(
        lambda *refs: backward_kernel(len(places), *refs),
        places,
        [normed, conv_in, conv_pre, dt_raw, y, states, d_scanned, kernel, *heads_vectors, expand],
        [
            back(D),
            back(channels),
            back(channels),
            back(lanes),
            back(local_di),
            pl.BlockSpec((1, STATE, local_di), lambda q, *_: (chunks - 1 - q, 0, 0)),
            back(local_di),
            fixed((WIDTH, channels)),
            fixed((1, lanes)),
            fixed((1, lanes)),
            fixed((1, local_di)),
            fixed((lanes, local_di)),
        ],
        [
            struct((length, channels + lanes), jnp.bfloat16),
            struct((WIDTH, channels)),
            struct((1, channels)),
            struct((1, local_di)),
            struct((2, lanes)),
        ]
        + [struct(grad, jnp.bfloat16)] * len(places),
        [
            back(channels + lanes),
            fixed((WIDTH, channels)),
            fixed((1, channels)),
            fixed((1, local_di)),
            fixed((2, lanes)),
        ]
        + [fixed(grad)] * len(places),
        [
            pltpu.VMEM((BLOCK + 8, channels), jnp.float32),
            pltpu.VMEM((STATE, local_di), jnp.float32),
            pltpu.VMEM((STATE, local_di), jnp.float32),
            pltpu.VMEM((channels + lanes, D), jnp.float32),
        ],
        chunks,
        [],
        (14_000_000_000, 40_000_000, 10_000_000),
        "backward",
    )


def run_pair(y, far, out_places, gate, out, block):
    columns = gate[0].shape[1] // 2
    shapes = [
        (gate[0].shape[0], columns),
        (gate[0].shape[0], columns),
        (block[0].shape[0] // 2, D),
        (block[0].shape[0] // 2, D),
    ] + [(out[0].shape[0] // len(out_places), out[0].shape[1])] * len(out_places)
    inputs = [*gate, *out, *block]
    return call(
        pair_kernel,
        [y, far] + out_places,
        inputs,
        [fixed(array.shape) for array in inputs],
        [struct(shape, jnp.bfloat16) for shape in shapes],
        [fixed(shape) for shape in shapes],
        [],
        1,
        [],
        (3_000_000, 7_000_000, 0),
        "pair",
    )


def run_normed(parity, hidden, d_gating, d_rest, gate_weight, rest_weight, arrived):
    length, local_di = d_gating.shape
    rest = d_rest.shape[1]
    return call(
        normed_kernel,
        [parity],
        [hidden, d_gating, d_rest, gate_weight, rest_weight],
        [
            rows_of(D),
            rows_of(local_di),
            rows_of(rest),
            fixed((local_di, D)),
            fixed((rest, D)),
        ],
        [
            struct((length // 2, D), jnp.bfloat16),
            struct((length // 2, D), jnp.bfloat16),
            struct((1, D)),
        ],
        [fixed((length // 2, D)), fixed((length // 2, D)), fixed((1, D))],
        [],
        length // BLOCK,
        arrived,
        (3_000_000_000, 9_000_000, 1000),
        "normed",
    )


def run_update(places, gate_out_blocks, rest_blocks, in_arrays, out_arrays):
    groups = len(places)
    blocks = [*gate_out_blocks, *rest_blocks]
    rows_in = DI // 4
    rows_out = out_arrays[0].shape[0] // groups
    arrays = [*in_arrays, *out_arrays]
    in_spec = pl.BlockSpec((rows_in, in_arrays[0].shape[1]), lambda q, *_: (q, 0))
    out_spec = pl.BlockSpec((rows_out, D), lambda q, *_: (jnp.minimum(q, groups - 1), 0))
    specs = [in_spec] * 3 + [out_spec] * 3
    return call(
        lambda *refs: update_kernel(groups, *refs),
        places,
        [*blocks, *arrays],
        [fixed(array.shape) for array in blocks] + specs,
        [struct(array.shape) for array in arrays],
        specs,
        [
            pltpu.VMEM((groups,) + gate_out_blocks[0].shape, jnp.bfloat16),
            pltpu.VMEM((groups,) + rest_blocks[0].shape, jnp.bfloat16),
        ],
        2 * (DI // rows_in) + 1,
        [],
        (20_000_000, 22_000_000, 1_000_000),
        "update",
    )


def adamw_step(weight, first, second, grad, rate, decay):
    first_new = beta_one * first + (1.0 - beta_one) * grad
    second_new = beta_two * second + (1.0 - beta_two) * grad * grad
    fix_one = 1.0 - beta_one**STEP
    fix_two = 1.0 - beta_two**STEP
    normalized = first_new / fix_one / (jnp.sqrt(second_new / fix_two) + adam_eps)
    return (first_new, second_new, weight - rate * (normalized + decay * weight))


def pick_heads(values, axis, width, index, groups):
    shape = values.shape
    split = shape[:axis] + (HEADS // groups, groups, width) + shape[axis + 1 :]
    taken = lax.dynamic_index_in_dim(values.reshape(split), index, axis + 1, keepdims=False)
    return taken.reshape(shape[:axis] + (HEADS // groups * width,) + shape[axis + 1 :])


def merge_heads(stacked, axis, width):
    groups = stacked.shape[0]
    shape = stacked.shape[1:]
    split = (groups,) + shape[:axis] + (HEADS // groups, width) + shape[axis + 1 :]
    moved = jnp.moveaxis(stacked.reshape(split), 0, axis + 1)
    return moved.reshape(shape[:axis] + (HEADS * width,) + shape[axis + 1 :])


def swap(values, axis, mask):
    route = [(i, i ^ mask) for i in range(lax.axis_size(axis))]
    return lax.ppermute(values, axis, route)


def seq_blocks(rows, far=None):
    index = lax.axis_index("seq")
    far = swap(rows, "seq", 2) if far is None else far
    blocks = [rows, swap(rows, "seq", 1), far, swap(far, "seq", 1)]
    return [index ^ mask for mask in range(4)], blocks


def ring_step(held):
    count = lax.axis_size("wshard")
    return lax.ppermute(held, "wshard", [(i, (i + 2) % count) for i in range(count)])


def ring_blocks(rows):
    count = lax.axis_size("wshard")
    index = lax.axis_index("wshard")
    places, blocks = [], []
    for step in range(count // 2):
        source = (index + count - 2 * step) % count
        places = places + [source, source ^ 1]
        blocks = blocks + [rows, swap(rows, "wshard", 1)]
        if step < count // 2 - 1:
            rows = ring_step(rows)
    return places, blocks


def add_kernel(counts, places_ref, *refs):
    terms, results = refs[: sum(counts)], refs[sum(counts) :]
    first = 0
    for count, result in zip(counts, results):
        total = sum_of(*terms[first : first + count])
        result[...] = total.astype(result.dtype)
        first = first + count


def add(groups, arrived):
    terms = [term for group in groups for term in group]
    return call(
        lambda *refs: add_kernel([len(group) for group in groups], *refs),
        [jnp.int32(0)],
        terms,
        [fixed(term.shape) for term in terms],
        [struct(group[0].shape, group[0].dtype) for group in groups],
        [fixed(group[0].shape) for group in groups],
        [],
        1,
        arrived,
        (200_000, 900_000, 0),
        "add",
    )


def take_block(values, index, rows):
    return lax.dynamic_slice_in_dim(values, index * rows, rows, 0)


def gather_out(out_low, seq_index, groups):
    rows = out_low.shape[0]
    if rows % (groups * HEADDIM) == 0:
        mine = pick_rows(out_low, seq_index, groups)
        return lax.all_gather(mine, "wshard", axis=0, tiled=True)
    whole = lax.all_gather(out_low, "wshard", axis=0, tiled=True)
    return pick_heads(whole, 0, HEADDIM, seq_index, groups)


def pick_rows(values, seq_index, groups):
    rows = values.shape[0]
    split = values.reshape(rows // (groups * HEADDIM), groups, HEADDIM, values.shape[1])
    return lax.dynamic_index_in_dim(split, seq_index, 1, keepdims=False).reshape(
        rows // groups, values.shape[1]
    )


def sum_out_grad(grad, rows, seq_index, groups):
    grad = grad.astype(jnp.bfloat16)
    if rows % (groups * HEADDIM) == 0:
        mine = lax.psum_scatter(grad, "wshard", scatter_dimension=0, tiled=True)
        every = lax.all_gather(mine, "seq", axis=0, tiled=False)
        split = every.reshape(groups, rows // (groups * HEADDIM), HEADDIM, grad.shape[1])
        return jnp.moveaxis(split, 0, 1).reshape(rows, grad.shape[1]).astype(jnp.float32)
    blocks = grad.reshape(HEADS // groups, 1, HEADDIM, grad.shape[1])
    here = (jnp.arange(groups) == seq_index)[None, :, None, None]
    spread = jnp.where(here, blocks, jnp.zeros((), jnp.bfloat16)).reshape(DI, grad.shape[1])
    mine = lax.psum_scatter(spread, "wshard", scatter_dimension=0, tiled=True)
    return lax.psum(mine.astype(jnp.float32), "seq")


def shards(
    block_in,
    cotangent,
    in_weight,
    in_first,
    in_second,
    out_weight,
    out_first,
    out_second,
    vec_weight,
    vec_first,
    vec_second,
):
    rows_here = block_in.shape[1]
    groups = lax.axis_size("seq")
    seq_index = lax.axis_index("seq")
    local_heads = HEADS // groups
    local_di = DI // groups
    hidden_rows = block_in.reshape(rows_here, D)
    cot_rows = cotangent.reshape(rows_here, D)
    gain_one, gain_two, kernel, conv_bias, a_log, dt_bias, d_skip = split_vector(vec_weight)

    def heads_of(values, axis, width):
        return pick_heads(values, axis, width, seq_index, groups)

    lanes = 128
    channels = local_di + 2 * STATE
    shard_index = lax.axis_index("wshard")
    rings = lax.axis_size("wshard") == 8
    near = seq_index % 2
    far = seq_index // 2
    if rings:
        y, z = shard_index % 2, shard_index // 2
        rest_mine, gate_out_mine, both_mine = run_prepare(
            seq_index, in_weight.T, out_weight, hidden_rows, cot_rows
        )
        rest = ring_blocks(rest_mine)
        both = seq_blocks(both_mine)
        gate_out = ring_blocks(gate_out_mine)
        gate_places = [z ^ mask for mask in range(4)]
        out_places = [y, 1 - y]
        rest_places = [
            (shard_index + 8 - 2 * step) % 8 ^ other for step in range(1, 5) for other in (0, 1)
        ]
    else:
        in_low = low(in_weight)
        steps_mine = heads_of(in_low[:, DI + CONVCH :], 1, 1)
        rest_mine = jnp.concatenate(
            [
                heads_of(in_low[:, DI : 2 * DI], 1, HEADDIM),
                in_low[:, 2 * DI : 2 * DI + 2 * STATE],
                jnp.pad(steps_mine, ((0, 0), (0, 16 - local_heads))),
            ],
            1,
        )
        gate_mine = heads_of(in_low[:, :DI], 1, HEADDIM)
        origin = [jnp.int32(0)]
        rest = (origin, [lax.all_gather(rest_mine, "wshard", axis=0, tiled=True).T])
        hidden_low = lax.all_gather(hidden_rows, "seq", axis=0, tiled=True)
        cot_low = lax.all_gather(cot_rows, "seq", axis=0, tiled=True)
        both = (origin, [jnp.concatenate([hidden_low, cot_low], 0)])
        gate_mine = lax.all_gather(gate_mine, "wshard", axis=0, tiled=True).T
        gate_out = (origin, [gate_mine, gather_out(low(out_weight), seq_index, groups)])
        gate_places, out_places, rest_places = origin, origin, origin
    my_gain_two = heads_of(gain_two, 0, HEADDIM)[None, :]
    my_kernel = jnp.concatenate([heads_of(kernel[:, :DI], 1, HEADDIM), kernel[:, DI:]], 1)
    my_bias = jnp.concatenate([heads_of(conv_bias[:DI], 0, HEADDIM), conv_bias[DI:]], 0)

    def on_lanes(values):
        return jnp.pad(values, (0, lanes - local_heads))[None, :]

    heads_vectors = (
        on_lanes(heads_of(a_log, 0, 1)),
        on_lanes(heads_of(dt_bias, 0, 1)),
        jnp.repeat(heads_of(d_skip, 0, 1), HEADDIM)[None, :],
    )
    expand = (
        jnp.arange(lanes)[:, None] == jnp.arange(local_di)[None, :] // HEADDIM
    ).astype(jnp.float32)
    (
        hidden_low,
        cot_low,
        rest_weight,
        normed_low,
        conv_in,
        conv_pre,
        dt_raw,
        y_part,
        scanned,
        states,
    ) = run_forward(
        both, rest, gain_one[None, :], (my_kernel, my_bias[None, :]), heads_vectors, expand
    )
    gate_weight, out_low, gating, d_gnorm, sums = run_gate(
        gate_out, cot_low, normed_low, scanned, my_gain_two
    )
    middle = run_middle(
        near,
        gate_places,
        out_places,
        scanned,
        gating,
        d_gnorm,
        cot_low,
        normed_low,
        [sums] + [swap(sums, "seq", mask) for mask in range(1, 4)],
        out_low,
        my_gain_two,
    )
    block_mine, block_send, d_gating, d_scanned, d_gain_two = middle[:5]
    gate_grads = middle[5 : 5 + len(gate_places)]
    out_grads = middle[5 + len(gate_places) :]
    block_arrived = swap(block_send, "seq", 1)
    if rings:
        gate_pieces = [swap(gate_grads[mask], "wshard", 2 * mask) for mask in range(1, 4)]
        out_arrived = swap(out_grads[1], "wshard", 1)
    backward = run_backward(
        rest_places,
        normed_low,
        conv_in,
        conv_pre,
        dt_raw,
        y_part,
        states,
        d_scanned,
        my_kernel,
        heads_vectors,
        expand,
    )
    d_rest, d_kernel, d_conv_bias, d_skip_wide, d_head = backward[:5]
    rest_grads = backward[5:]
    before_normed = []
    if rings:
        rest_arrived = swap(rest_grads[1], "wshard", 1)
        gate_keep, gate_send, block_keep, block_send, *out_sums = run_pair(
            y,
            far,
            gate_places,
            [gate_grads[0]] + gate_pieces,
            [out_grads[0], out_arrived],
            [block_mine, block_arrived],
        )
        gate_arrived = swap(gate_send, "wshard", 1)
        out_pieces = [swap(out_sums[mask], "wshard", 2 * mask) for mask in range(1, 4)]
        before_normed = [gate_keep]
    else:
        block_sum = low(block_mine.astype(jnp.float32) + block_arrived.astype(jnp.float32))
        block_keep = take_block(block_sum, far, rows_here)
        block_send = take_block(block_sum, 1 - far, rows_here)
    block_far = swap(block_send, "seq", 2)
    normed_mine, normed_send, d_gain_one = run_normed(
        near, hidden_low, d_gating, d_rest, gate_weight, rest_weight, before_normed
    )
    normed_arrived = swap(normed_send, "seq", 1)
    normed_sum = normed_mine.astype(jnp.float32) + normed_arrived.astype(jnp.float32)
    normed_far = swap(low(take_block(normed_sum, 1 - far, rows_here)), "seq", 2)
    shared = jnp.concatenate(
        [d_gain_one[0], d_kernel[:, local_di:].reshape(-1), d_conv_bias[0, local_di:]]
    )
    d_skip_part = jnp.sum(d_skip_wide.reshape(local_heads, HEADDIM), axis=1)
    apart = jnp.concatenate(
        [
            d_gain_two[0],
            d_kernel[:, :local_di].reshape(-1),
            d_conv_bias[0, :local_di],
            d_head[:, :local_heads].reshape(-1),
            d_skip_part,
        ]
    )
    vec_part = jnp.concatenate([shared, apart])[None]
    if rings:
        (held,) = add(
            [[rest_grads[0], rest_arrived]], [d_gain_one, gate_arrived, block_far] + out_pieces
        )
        vec_arrived = swap(vec_part, "wshard", 1)
        held, gate_part, out_part, vec_part = add(
            [
                [rest_grads[2], swap(rest_grads[3], "wshard", 1), ring_step(held)],
                [gate_keep, gate_arrived],
                [out_sums[0]] + out_pieces,
                [vec_part, vec_arrived],
            ],
            [normed_arrived],
        )
        gate_out_part = jnp.concatenate([gate_part, out_part], 0)
        gate_out_far = swap(gate_out_part, "seq", 2)
        held, vec_part = add(
            [
                [rest_grads[4], swap(rest_grads[5], "wshard", 1), ring_step(held)],
                [vec_part, swap(vec_part, "wshard", 2)],
            ],
            [gate_out_far],
        )
        rest_part, vec_part = add(
            [
                [rest_grads[6], swap(rest_grads[7], "wshard", 1), ring_step(held)],
                [vec_part, swap(vec_part, "wshard", 4)],
            ],
            [normed_far],
        )
        vec_places, vec_blocks = seq_blocks(vec_part)
        every = jnp.zeros((groups, vec_part.shape[1]), jnp.float32)
        for spot, block in zip(vec_places, vec_blocks):
            every = lax.dynamic_update_slice_in_dim(every, block, spot, 0)
    else:
        vec_part = lax.psum(vec_part, "wshard")
        every = lax.all_gather(vec_part, "seq", axis=0, tiled=True)
    block_here = block_keep.astype(jnp.float32) + block_far.astype(jnp.float32)
    block_out = hidden_rows.astype(jnp.float32) + block_here
    d_normed = take_block(normed_sum, far, rows_here) + normed_far.astype(jnp.float32)
    own_hidden = hidden_rows.astype(jnp.float32)
    own_scale = lax.rsqrt(jnp.mean(own_hidden * own_hidden, axis=-1, keepdims=True) + norm_eps)
    own_unit = own_hidden * own_scale
    d_own = d_normed * gain_one[None, :]
    d_hidden = own_scale * (
        d_own - own_unit * jnp.mean(d_own * own_unit, axis=-1, keepdims=True)
    )
    block_grad = cot_rows.astype(jnp.float32) + d_hidden
    shared, every = (
        jnp.sum(every[:, : shared.shape[0]], axis=0),
        every[:, shared.shape[0] :],
    )
    kernel_end = local_di * (1 + WIDTH)
    heads_at = kernel_end + local_di
    both_kernel = D + 2 * STATE * WIDTH
    vec_total = jnp.concatenate(
        [
            shared[:D],
            merge_heads(every[:, :local_di], 0, HEADDIM),
            jnp.concatenate(
                [
                    merge_heads(
                        every[:, local_di:kernel_end].reshape(groups, WIDTH, local_di), 1, HEADDIM
                    ),
                    shared[D:both_kernel].reshape(WIDTH, 2 * STATE),
                ],
                1,
            ).reshape(-1),
            merge_heads(every[:, kernel_end:heads_at], 0, HEADDIM),
            shared[both_kernel:],
            merge_heads(every[:, heads_at : heads_at + local_heads], 0, 1),
            merge_heads(every[:, heads_at + local_heads : heads_at + 2 * local_heads], 0, 1),
            merge_heads(every[:, heads_at + 2 * local_heads :], 0, 1),
        ]
    )
    vec_first_new, vec_second_new, vec_weight_new = adamw_step(
        vec_weight, vec_first, vec_second, vec_total, vector_rate, 0.0
    )
    if rings:
        rest_spots, rest_blocks = seq_blocks(rest_part)
        _, gate_out_blocks = seq_blocks(gate_out_part, gate_out_far)
        updated = run_update(
            rest_spots,
            gate_out_blocks,
            rest_blocks,
            (in_weight.T, in_first.T, in_second.T),
            (out_weight, out_first, out_second),
        )
        in_first_new, in_second_new, in_weight_new = [array.T for array in updated[:3]]
        out_first_new, out_second_new, out_weight_new = updated[3:]
    else:
        rest_part = lax.psum_scatter(rest_grads[0].T, "wshard", scatter_dimension=0, tiled=True)
        gate_part = lax.psum_scatter(gate_grads[0].T, "wshard", scatter_dimension=0, tiled=True)
        gate_every = lax.all_gather(gate_part, "seq", axis=0, tiled=False).astype(jnp.float32)
        rest_every = lax.all_gather(rest_part, "seq", axis=0, tiled=False).astype(jnp.float32)
        out_total = sum_out_grad(out_grads[0], out_weight.shape[0], seq_index, groups)
        in_total = jnp.concatenate(
            [
                merge_heads(gate_every, 1, HEADDIM),
                merge_heads(rest_every[:, :, :local_di], 1, HEADDIM),
                jnp.sum(rest_every[:, :, local_di:channels], axis=0),
                merge_heads(rest_every[:, :, channels : channels + local_heads], 1, 1),
            ],
            1,
        )
        in_first_new, in_second_new, in_weight_new = adamw_step(
            in_weight, in_first, in_second, in_total, matrix_rate, matrix_decay
        )
        out_first_new, out_second_new, out_weight_new = adamw_step(
            out_weight, out_first, out_second, out_total, matrix_rate, matrix_decay
        )
    return (
        block_out.reshape(1, rows_here, D),
        block_grad.reshape(1, rows_here, D),
        in_first_new,
        in_second_new,
        in_weight_new,
        out_first_new,
        out_second_new,
        out_weight_new,
        vec_first_new,
        vec_second_new,
        vec_weight_new,
    )


def solution(mesh):
    return jax.shard_map(
        shards,
        mesh=mesh,
        in_specs=(
            P("wshard", "seq", None),
            P("wshard", "seq", None),
            P("wshard", None),
            P("wshard", None),
            P("wshard", None),
            P("wshard", None),
            P("wshard", None),
            P("wshard", None),
            P(),
            P(),
            P(),
        ),
        out_specs=(
            P("wshard", "seq", None),
            P("wshard", "seq", None),
            P("wshard", None),
            P("wshard", None),
            P("wshard", None),
            P("wshard", None),
            P("wshard", None),
            P("wshard", None),
            P(),
            P(),
            P(),
        ),
        check_vma=False,
    )
```

```python
import jax
import jax.numpy as jnp
from jax import lax
from jax.experimental import pallas as pl
from jax.experimental.pallas import tpu as pltpu
from jax.sharding import PartitionSpec as P

D = 1024
HEADS = 32
HEADDIM = 64
STATE = 128
WIDTH = 4
BLOCK = 256
STEP = 10
DI = 2048
CONVCH = 2304


precise = lax.Precision.HIGHEST
norm_eps = 1e-05
beta_one = 0.9
beta_two = 0.95
adam_eps = 1e-08
matrix_rate = 0.05
matrix_decay = 0.1
vector_rate = 0.5


def rms_scale(values):
    return values * lax.rsqrt(jnp.mean(values * values, axis=-1, keepdims=True) + norm_eps)


def split_vector(vector):
    extents = [D, DI, WIDTH * CONVCH, CONVCH, HEADS, HEADS, HEADS]
    pieces = []
    offset = 0
    for extent in extents:
        pieces.append(vector[offset : offset + extent])
        offset = offset + extent
    pieces[2] = pieces[2].reshape(WIDTH, CONVCH)
    return pieces


def dot_nt(left, right, precision=None):
    return lax.dot_general(
        left,
        right,
        (((1,), (1,)), ((), ())),
        precision=precision,
        preferred_element_type=jnp.float32,
    )


def dot_tn(left, right):
    return lax.dot_general(
        left, right, (((0,), (0,)), ((), ())), preferred_element_type=jnp.float32
    )


def dot_nn(left, right, precision=None):
    return jnp.dot(left, right, precision=precision, preferred_element_type=jnp.float32)


def sigmoid(values):
    return 1.0 / (1.0 + jnp.exp(-values))


def low(values):
    return values.astype(jnp.bfloat16)


def lower_mask():
    rows = lax.broadcasted_iota(jnp.int32, (BLOCK, BLOCK), 0)
    return rows >= lax.broadcasted_iota(jnp.int32, (BLOCK, BLOCK), 1)


def decay_sums(dt_raw, dt_bias, a_log, expand):
    shifted = dt_raw + dt_bias
    step = jnp.maximum(shifted, 0.0) + jnp.log1p(jnp.exp(-jnp.abs(shifted)))
    log_decay = -jnp.exp(a_log) * step
    ones = jnp.where(lower_mask(), 1.0, 0.0)
    running = dot_nn(ones, log_decay, precise)
    step_wide = dot_nn(step, expand, precise)
    running_wide = dot_nn(running, expand, precise)
    return shifted, step, log_decay, running, step_wide, running_wide


def place_rows(result_ref, place, block):
    rows = block.shape[0]
    result_ref[pl.ds(pl.multiple_of(place * rows, rows), rows), :] = block


def place_columns(result_ref, place, block):
    rows, columns = block.shape
    start = pl.multiple_of(place * columns, columns)
    result_ref[:rows, pl.ds(start, columns)] = block


def forward_kernel(rest_count, places_ref, *refs):
    rest_blocks = refs[:rest_count]
    (
        hidden_ref,
        gain_one_ref,
        conv_ref,
        bias_ref,
        a_log_ref,
        dt_bias_ref,
        skip_ref,
        expand_ref,
        rest_ref,
        normed_ref,
        conv_in_ref,
        conv_pre_ref,
        dt_ref,
        y_ref,
        scanned_ref,
        state_ref,
        ext,
        state,
    ) = refs[rest_count:]
    local_di = y_ref.shape[1]
    heads = local_di // HEADDIM
    channels = conv_in_ref.shape[1]

    @pl.when(pl.program_id(0) == 0)
    def _():
        ext[0:8, :] = jnp.zeros((8, ext.shape[1]), jnp.float32)
        state[...] = jnp.zeros_like(state)
        rest_ref[channels:, :] = jnp.zeros_like(rest_ref[channels:, :])
        for number, block in enumerate(rest_blocks):
            place_columns(rest_ref, places_ref[number], block[...])

    hidden = hidden_ref[...].astype(jnp.float32)
    normed = low(rms_scale(hidden) * gain_one_ref[...])
    normed_ref[...] = normed
    conv_in = dot_nt(normed, rest_ref[:channels, :])
    conv_in_ref[...] = conv_in
    ext[8 : 8 + BLOCK, :] = conv_in
    conv_pre = bias_ref[...] + conv_ref[WIDTH - 1 : WIDTH, :] * conv_in
    for tap in range(WIDTH - 1):
        first = 8 - WIDTH + 1 + tap
        conv_pre = conv_pre + conv_ref[tap : tap + 1, :] * ext[first : first + BLOCK, :]
    conv_pre_ref[...] = conv_pre
    ext[8 - WIDTH + 1 : 8, :] = ext[8 + BLOCK - WIDTH + 1 : 8 + BLOCK, :]
    conv_low = low(conv_pre * sigmoid(conv_pre))
    inner = conv_low[:, :local_di]
    b_rows = conv_low[:, local_di : local_di + STATE]
    c_rows = conv_low[:, local_di + STATE :]
    dt_raw = low(dot_nt(normed, rest_ref[channels:, :])).astype(jnp.float32)
    dt_ref[...] = dt_raw

    _, _, _, running, step_wide, running_wide = decay_sums(
        dt_raw, dt_bias_ref[...], a_log_ref[...], expand_ref[...]
    )
    running_t = running.T
    b_t = low(b_rows.astype(jnp.float32).T)
    scores = dot_nn(c_rows, b_t)
    mask = lower_mask()
    inner_wide = inner.astype(jnp.float32)
    stepped = step_wide * inner_wide
    stepped_low = low(stepped)
    first_half = lax.broadcasted_iota(jnp.int32, (BLOCK, 2 * HEADDIM), 1) < HEADDIM
    zero = jnp.zeros((), jnp.bfloat16)
    state_ref[...] = state[...].reshape(state_ref.shape)
    held = state[...]
    carried = jnp.exp(running_wide) * dot_nn(c_rows, low(held))
    for pair in range(heads // 2):
        span = slice(pair * 2 * HEADDIM, (pair + 1) * 2 * HEADDIM)
        both = stepped_low[:, span]
        total = carried[:, span]
        for half in range(2):
            head = 2 * pair + half
            differ = running[:, head : head + 1] - running_t[head : head + 1, :]
            mixed = low(jnp.exp(jnp.where(mask, differ, -jnp.inf)) * scores)
            mine = jnp.where(first_half if half == 0 else ~first_half, both, zero)
            total = total + dot_nn(mixed, mine)
        y_ref[:, span] = total
    last = running_wide[BLOCK - 1 : BLOCK, :]
    to_end = jnp.exp(last - running_wide)
    state[...] = jnp.exp(last) * held + dot_nn(b_t, low(to_end * stepped))
    scanned_ref[...] = low(y_ref[...] + skip_ref[...] * inner_wide)


def gate_kernel(count, places_ref, *refs):
    blocks = refs[:count]
    (
        cot_ref,
        normed_ref,
        scanned_ref,
        gain_two_ref,
        gate_ref,
        out_ref,
        gating_ref,
        d_gnorm_ref,
        sums_ref,
    ) = refs[count:]
    local_di = gating_ref.shape[1]

    @pl.when(pl.program_id(0) == 0)
    def _():
        if count == 2:
            gate_ref[...] = blocks[0][...]
            out_ref[...] = blocks[1][...]
        else:
            for number, block in enumerate(blocks):
                spot = places_ref[number]
                place_columns(gate_ref, spot, block[:local_di, :])
                for tile in range(D // block.shape[1]):
                    first = local_di + tile * HEADDIM
                    columns = slice(tile * block.shape[1], (tile + 1) * block.shape[1])
                    place_rows(out_ref.at[:, columns], spot, block[first : first + HEADDIM, :])

    gating = dot_nt(normed_ref[...], gate_ref[...])
    gating_ref[...] = gating
    d_gnorm = dot_nt(cot_ref[...], out_ref[...])
    d_gnorm_ref[...] = d_gnorm
    gated = scanned_ref[...].astype(jnp.float32) * (gating * sigmoid(gating))
    ones = jnp.ones((8, local_di), jnp.float32)
    squares = dot_nt(ones, gated * gated, precise)
    products = dot_nt(ones, d_gnorm * gain_two_ref[...] * gated, precise)
    sums_ref[...] = jnp.where(
        lax.broadcasted_iota(jnp.int32, squares.shape, 0) == 0, squares, products
    )


def keep_chunk(value, here, number, mine_ref, send_ref):
    rows = pl.ds(pl.multiple_of(number * BLOCK, BLOCK), BLOCK)

    @pl.when(here)
    def _():
        mine_ref[rows, :] = value

    @pl.when(jnp.logical_not(here))
    def _():
        send_ref[rows, :] = value


def middle_kernel(gate_count, out_count, places_ref, *refs):
    (
        scanned_ref,
        gating_ref,
        d_gnorm_ref,
        cot_ref,
        normed_ref,
        sums_one_ref,
        sums_two_ref,
        sums_three_ref,
        sums_four_ref,
        out_ref,
        gain_two_ref,
        mine_ref,
        send_ref,
        d_gating_ref,
        d_scanned_ref,
        d_gain_two_ref,
    ) = refs[:16]
    gate_refs = refs[16 : 16 + gate_count]
    out_refs = refs[16 + gate_count : 16 + gate_count + out_count]
    out_sum, gate_sum = refs[16 + gate_count + out_count :]
    chunk = pl.program_id(0)

    @pl.when(chunk == 0)
    def _():
        out_sum[...] = jnp.zeros_like(out_sum)
        gate_sum[...] = jnp.zeros_like(gate_sum)
        d_gain_two_ref[...] = jnp.zeros_like(d_gain_two_ref)

    sums = (sums_one_ref[...] + sums_two_ref[...]) + (sums_three_ref[...] + sums_four_ref[...])
    sums = (sums / DI).T
    scale = lax.rsqrt(sums[:, 0:1] + norm_eps)
    slope = scale * scale * sums[:, 1:2]
    gating = gating_ref[...]
    open_part = sigmoid(gating)
    gate = gating * open_part
    scanned = scanned_ref[...].astype(jnp.float32)
    unit = scanned * gate * scale
    d_gnorm = d_gnorm_ref[...]
    gain_two = gain_two_ref[...]
    gnorm = low(unit * gain_two)
    block_part = low(dot_nn(gnorm, out_ref[...]))
    keep_chunk(block_part, chunk % 2 == places_ref[0], chunk // 2, mine_ref, send_ref)
    out_sum[...] += dot_tn(gnorm, cot_ref[...])
    d_gain_two_ref[...] += jnp.sum(d_gnorm * unit, axis=0, keepdims=True)
    d_gated = scale * (d_gnorm * gain_two) - unit * slope
    d_gating = low(d_gated * scanned * (open_part * (1.0 + gating * (1.0 - open_part))))
    d_gating_ref[...] = d_gating
    d_scanned_ref[...] = low(d_gated * gate)
    gate_sum[...] += dot_tn(d_gating, normed_ref[...])

    @pl.when(chunk == pl.num_programs(0) - 1)
    def _():
        for number, gate_ref in enumerate(gate_refs):
            columns = gate_ref.shape[1]
            start = pl.multiple_of(places_ref[1 + number] * columns, columns)
            gate_ref[...] = low(gate_sum[:, pl.ds(start, columns)])
        for number, grad_ref in enumerate(out_refs):
            columns = grad_ref.shape[1]
            first = places_ref[1 + gate_count + number]
            for step in range(out_sum.shape[0] // HEADDIM // out_count):
                head = first + step * out_count
                rows = pl.ds(pl.multiple_of(head * HEADDIM, HEADDIM), HEADDIM)
                for tile in range(D // columns):
                    base = (step * (D // columns) + tile) * HEADDIM
                    grad_ref[base : base + HEADDIM, :] = low(
                        out_sum[rows, tile * columns : (tile + 1) * columns]
                    )


def backward_kernel(
    grad_count,
    places_ref,
    normed_ref,
    conv_in_ref,
    conv_pre_ref,
    dt_ref,
    y_ref,
    state_ref,
    d_scanned_ref,
    conv_ref,
    a_log_ref,
    dt_bias_ref,
    skip_ref,
    expand_ref,
    d_rest_ref,
    d_kernel_ref,
    d_conv_bias_ref,
    d_skip_ref,
    d_head_ref,
    *refs,
):
    grad_refs = refs[:grad_count]
    ext, d_state, later_state, rest_sum = refs[grad_count:]
    local_di = y_ref.shape[1]
    heads = local_di // HEADDIM
    chunk = pl.program_id(0)

    @pl.when(chunk == 0)
    def _():
        ext[BLOCK : BLOCK + 8, :] = jnp.zeros((8, ext.shape[1]), jnp.float32)
        d_state[...] = jnp.zeros_like(d_state)
        later_state[...] = jnp.zeros_like(later_state)
        rest_sum[...] = jnp.zeros_like(rest_sum)
        d_kernel_ref[...] = jnp.zeros_like(d_kernel_ref)
        d_conv_bias_ref[...] = jnp.zeros_like(d_conv_bias_ref)
        d_skip_ref[...] = jnp.zeros_like(d_skip_ref)
        d_head_ref[...] = jnp.zeros_like(d_head_ref)

    expand = expand_ref[...]
    conv_pre = conv_pre_ref[...]
    open_part = sigmoid(conv_pre)
    conv_low = low(conv_pre * open_part)
    inner = conv_low[:, :local_di].astype(jnp.float32)
    b_rows = conv_low[:, local_di : local_di + STATE]
    c_rows = conv_low[:, local_di + STATE :]
    a_log = a_log_ref[...]
    shifted, _, log_decay, running, step_wide, running_wide = decay_sums(
        dt_ref[...], dt_bias_ref[...], a_log, expand
    )
    running_t = running.T
    b_t = low(b_rows.astype(jnp.float32).T)
    c_t = low(c_rows.astype(jnp.float32).T)
    scores = dot_nn(c_rows, b_t)
    scores_t = dot_nn(b_rows, c_t)
    mask = lower_mask()
    rows = lax.broadcasted_iota(jnp.int32, (BLOCK, BLOCK), 0)
    mask_t = rows <= lax.broadcasted_iota(jnp.int32, (BLOCK, BLOCK), 1)
    d_y_low = d_scanned_ref[...]
    d_y = d_y_low.astype(jnp.float32)
    stepped_low = low(step_wide * inner)
    stepped = stepped_low.astype(jnp.float32)
    last = running_wide[BLOCK - 1 : BLOCK, :]
    to_end = jnp.exp(last - running_wide)
    d_later = d_state[...]
    d_later_low = low(d_later)
    held = state_ref[...].reshape(d_state.shape)
    decayed_dy = low(jnp.exp(running_wide) * d_y)
    d_c = dot_nt(decayed_dy, low(held))
    d_b = dot_nt(low(to_end * stepped), d_later_low)
    d_stepped = to_end * dot_nn(b_rows, d_later_low)
    cross = jnp.sum(later_state[...] * d_later, axis=0, keepdims=True)
    d_state[...] = jnp.exp(last) * d_later + dot_nn(c_t, decayed_dy)
    later_state[...] = held
    first_half = lax.broadcasted_iota(jnp.int32, (BLOCK, 2 * HEADDIM), 1) < HEADDIM
    zero = jnp.zeros((), jnp.bfloat16)
    d_scores = jnp.zeros((BLOCK, BLOCK), jnp.float32)
    pieces = []
    for pair in range(heads // 2):
        span = slice(pair * 2 * HEADDIM, (pair + 1) * 2 * HEADDIM)
        total = d_stepped[:, span]
        for half in range(2):
            head = 2 * pair + half
            mine = jnp.where(first_half if half == 0 else ~first_half, d_y_low[:, span], zero)
            column = running[:, head : head + 1]
            row = running_t[head : head + 1, :]
            decay = jnp.exp(jnp.where(mask, column - row, -jnp.inf))
            decay_t = jnp.exp(jnp.where(mask_t, row - column, -jnp.inf))
            d_scores = d_scores + dot_nt(mine, stepped_low[:, span]) * decay
            total = total + dot_nn(low(decay_t * scores_t), mine)
        pieces.append(total)
    d_stepped = jnp.concatenate(pieces, 1)
    d_scores_low = low(d_scores)
    d_c = d_c + dot_nn(d_scores_low, b_rows)
    d_b = d_b + dot_nn(low(d_scores.T), c_rows)
    d_inner = step_wide * d_stepped + skip_ref[...] * d_y
    d_running = dot_nt(d_y * y_ref[...] - d_stepped * stepped, expand, precise)
    upper = jnp.where(mask_t, 1.0, 0.0)
    d_log = dot_nn(upper, d_running, precise) + dot_nt(cross, expand, precise)
    d_step = dot_nt(d_stepped * inner, expand, precise) - jnp.exp(a_log) * d_log
    d_dt = d_step * sigmoid(shifted)
    d_head_ref[0:1, :] += jnp.sum(d_log * log_decay, axis=0, keepdims=True)
    d_head_ref[1:2, :] += jnp.sum(d_dt, axis=0, keepdims=True)
    d_skip_ref[...] += jnp.sum(d_y * inner, axis=0, keepdims=True)

    d_conv_out = jnp.concatenate([d_inner, d_b, d_c], 1)
    d_pre = d_conv_out * (open_part * (1.0 + conv_pre * (1.0 - open_part)))
    ext[0:BLOCK, :] = d_pre
    d_conv_bias_ref[...] += jnp.sum(d_pre, axis=0, keepdims=True)
    conv_in = conv_in_ref[...]
    d_conv_in = jnp.zeros_like(conv_in)
    for tap in range(WIDTH):
        moved = ext[WIDTH - 1 - tap : WIDTH - 1 - tap + BLOCK, :]
        d_conv_in = d_conv_in + conv_ref[tap : tap + 1, :] * moved
        d_kernel_ref[tap : tap + 1, :] += jnp.sum(moved * conv_in, axis=0, keepdims=True)
    ext[BLOCK : BLOCK + 8, :] = ext[0:8, :]
    d_rest = jnp.concatenate([low(d_conv_in), low(d_dt)], 1)
    d_rest_ref[...] = d_rest
    rest_sum[...] += dot_tn(d_rest, normed_ref[...])

    @pl.when(chunk == pl.num_programs(0) - 1)
    def _():
        for number, grad_ref in enumerate(grad_refs):
            columns = grad_ref.shape[1]
            blocks = rest_sum.shape[1] // columns // grad_count
            rows = grad_ref.shape[0] // blocks
            for step in range(blocks):
                place = places_ref[number] + step * grad_count
                start = pl.multiple_of(place * columns, columns)
                grad_ref[step * rows : (step + 1) * rows, :] = low(
                    rest_sum[:rows, pl.ds(start, columns)]
                )


def sum_of(*refs):
    total = refs[0][...].astype(jnp.float32)
    for ref in refs[1:]:
        total = total + ref[...].astype(jnp.float32)
    return total


def pair_kernel(places_ref, *refs):
    gate, out, block = refs[:4], refs[4:6], refs[6:8]
    gate_keep_ref, gate_send_ref, block_keep_ref, block_send_ref = refs[8:12]
    out_refs = refs[12:]
    paired = sum_of(*gate)
    columns = gate_keep_ref.shape[1]
    even = places_ref[0] == 0
    first, second = low(paired[:, :columns]), low(paired[:, columns:])
    gate_keep_ref[...] = jnp.where(even, first, second)
    gate_send_ref[...] = jnp.where(even, second, first)
    rows = block_keep_ref.shape[0]
    for ref, place in ((block_keep_ref, places_ref[1]), (block_send_ref, 1 - places_ref[1])):
        here = pl.ds(pl.multiple_of(place * rows, rows), rows)
        ref[...] = low(sum_of(block[0].at[here, :], block[1].at[here, :]))
    for number, ref in enumerate(out_refs):
        rows = ref.shape[0]
        start = pl.multiple_of(places_ref[2 + number] * rows, rows)
        here = pl.ds(start, rows)
        ref[...] = low(sum_of(out[0].at[here, :], out[1].at[here, :]))


def rest_pair_kernel(places_ref, mine_ref, arrived_ref, *rest_refs):
    for number, ref in enumerate(rest_refs):
        rows = ref.shape[0]
        here = pl.ds(pl.multiple_of(places_ref[number] * rows, rows), rows)
        ref[...] = low(sum_of(mine_ref.at[here, :], arrived_ref.at[here, :]))


def join_kernel(places_ref, *refs):
    joined_ref, vec_ref = refs[-2:]
    rows = refs[0].shape[0]
    joined_ref[:rows, :] = low(sum_of(*refs[:2]))
    joined_ref[rows:, :] = low(sum_of(*refs[2:6]))
    vec_ref[...] = refs[6][...] + refs[7][...]


def final_kernel(places_ref, *refs):
    rest_ref, vec_ref = refs[6:]
    rest_ref[...] = low(sum_of(*refs[:4]))
    vec_ref[...] = refs[4][...] + refs[5][...]


def normed_kernel(
    places_ref,
    hidden_ref,
    d_gating_ref,
    d_rest_ref,
    gate_weight_ref,
    rest_weight_ref,
    mine_ref,
    send_ref,
    d_gain_one_ref,
):
    chunk = pl.program_id(0)

    @pl.when(chunk == 0)
    def _():
        d_gain_one_ref[...] = jnp.zeros_like(d_gain_one_ref)

    d_normed = dot_nn(d_gating_ref[...], gate_weight_ref[...])
    d_normed = d_normed + dot_nn(d_rest_ref[...], rest_weight_ref[...])
    keep_chunk(low(d_normed), chunk % 2 == places_ref[0], chunk // 2, mine_ref, send_ref)
    unit = rms_scale(hidden_ref[...].astype(jnp.float32))
    d_gain_one_ref[...] += jnp.sum(d_normed * unit, axis=0, keepdims=True)


def prepare_kernel(places_ref, in_ref, out_ref, rest_ref, gate_out_ref):
    index = places_ref[0]
    local_di = gate_out_ref.shape[0] // 2
    groups = DI // local_di
    for head in range(HEADS // groups):
        rows = slice(head * HEADDIM, (head + 1) * HEADDIM)
        for base, result_ref in ((0, gate_out_ref), (DI, rest_ref)):
            start = pl.multiple_of(base + (groups * head + index) * HEADDIM, HEADDIM)
            result_ref[rows, :] = low(in_ref[pl.ds(start, HEADDIM), :])
    channels = local_di + 2 * STATE
    rest_ref[local_di:channels, :] = low(in_ref[2 * DI : 2 * DI + 2 * STATE, :])
    rows = rest_ref.shape[0] - channels
    target = lax.broadcasted_iota(jnp.int32, (rows, HEADS), 0)
    source = lax.broadcasted_iota(jnp.int32, (rows, HEADS), 1)
    chosen = (source == groups * target + index) & (target < HEADS // groups)
    steps = low(in_ref[DI + CONVCH :, :])
    rest_ref[channels:, :] = low(dot_nn(jnp.where(chosen, 1.0, 0.0).astype(jnp.bfloat16), steps))
    mine = pl.ds(pl.multiple_of(index * HEADDIM, HEADDIM), HEADDIM)
    columns = gate_out_ref.shape[1]
    for tile in range(D // columns):
        first = local_di + tile * HEADDIM
        gate_out_ref[first : first + HEADDIM, :] = low(
            out_ref[mine, tile * columns : (tile + 1) * columns]
        )


def adamw_store(old_refs, new_refs, rows, columns, grad):
    results = adamw_step(*[ref[rows, columns] for ref in old_refs], grad, matrix_rate, matrix_decay)
    for ref, result in zip(new_refs, results):
        ref[rows, columns] = result


def update_heads(old_refs, new_refs, source, part):
    groups = source.shape[0]
    heads = old_refs[0].shape[0] // HEADDIM // groups
    for head in range(heads):
        start = pl.multiple_of((part * heads + head) * HEADDIM, HEADDIM)
        for group in range(groups):
            first = (head * groups + group) * HEADDIM
            grad = source[group, pl.ds(start, HEADDIM), :].astype(jnp.float32)
            adamw_store(old_refs, new_refs, slice(first, first + HEADDIM), slice(None), grad)


def update_gate_kernel(groups, places_ref, *refs):
    blocks, in_refs, out_refs = refs[:groups], refs[groups : groups + 3], refs[groups + 3 : groups + 6]
    in_new_refs, out_new_refs = refs[groups + 6 : groups + 9], refs[groups + 9 : groups + 12]
    (gate_out,) = refs[groups + 12 :]
    chunk = pl.program_id(0)

    @pl.when(chunk == 0)
    def _():
        for number in range(groups):
            gate_out[places_ref[number]] = blocks[number][...]

    update_heads(in_refs, in_new_refs, gate_out, chunk)
    local_di = gate_out.shape[1] // 2
    columns = gate_out.shape[2]
    for tile in range(D // columns):
        first = local_di + tile * HEADDIM
        grad = gate_out[chunk, first : first + HEADDIM, :].astype(jnp.float32)
        span = slice(tile * columns, (tile + 1) * columns)
        adamw_store(out_refs, out_new_refs, slice(None), span, grad)


def update_rest_kernel(groups, places_ref, *refs):
    blocks, in_refs = refs[:groups], refs[groups : groups + 3]
    in_new_refs, (rest,) = refs[groups + 6 : groups + 9], refs[groups + 9 :]
    chunk = pl.program_id(0)

    @pl.when(chunk == 0)
    def _():
        for number in range(groups):
            rest[places_ref[number]] = blocks[number][...]

    @pl.when(chunk < pl.num_programs(0) - 1)
    def _():
        update_heads(in_refs, in_new_refs, rest, chunk)

    @pl.when(chunk == pl.num_programs(0) - 1)
    def _():
        local_di = DI // groups
        channels = local_di + 2 * STATE
        both = rest[0, local_di:channels, :].astype(jnp.float32)
        rows = rest.shape[1] - channels
        steps = jnp.zeros((HEADS, rest.shape[2]), jnp.float32)
        target = lax.broadcasted_iota(jnp.int32, (HEADS, rows), 0)
        source = lax.broadcasted_iota(jnp.int32, (HEADS, rows), 1)
        for group in range(groups):
            if group > 0:
                both = both + rest[group, local_di:channels, :].astype(jnp.float32)
            chosen = jnp.where(target == groups * source + group, 1.0, 0.0).astype(jnp.bfloat16)
            steps = steps + dot_nn(chosen, rest[group, channels:, :])
        after_both = slice(2 * STATE, 2 * STATE + HEADS)
        adamw_store(in_refs, in_new_refs, slice(0, 2 * STATE), slice(None), both)
        adamw_store(in_refs, in_new_refs, after_both, slice(None), steps)


def kernel_params():
    return pltpu.CompilerParams(
        dimension_semantics=("arbitrary",), vmem_limit_bytes=56 * 1024 * 1024
    )


def cost(flops, moved, transcendentals):
    return pl.CostEstimate(flops=flops, bytes_accessed=moved, transcendentals=transcendentals)


def after(kernel, inputs, arrived):
    def run(*refs):
        kernel(*refs[:inputs], *refs[inputs + arrived :])

    return run


def corner(array):
    return pl.BlockSpec((min(16, array.shape[0]), 128), lambda *_: (0, 0))


def fixed(shape):
    return pl.BlockSpec(shape, lambda *_: (0,) * len(shape))


def rows_of(extent, first=0):
    return pl.BlockSpec((BLOCK, extent), lambda q, *_: (q + first, 0))


def struct(shape, dtype=jnp.float32):
    return jax.ShapeDtypeStruct(shape, dtype)


def call(
    kernel, places, inputs, in_specs, outputs, out_specs, scratch, grid, arrived, price, name, same=()
):
    return pl.pallas_call(
        after(kernel, 1 + len(inputs), len(arrived)),
        grid_spec=pltpu.PrefetchScalarGridSpec(
            num_scalar_prefetch=1,
            grid=(grid,),
            in_specs=list(in_specs) + [corner(array) for array in arrived],
            out_specs=out_specs,
            scratch_shapes=scratch,
        ),
        out_shape=outputs,
        input_output_aliases=dict(same),
        compiler_params=kernel_params(),
        cost_estimate=cost(*price),
        name=name,
    )(jnp.stack(places).astype(jnp.int32), *inputs, *arrived)


def run_prepare(index, in_t, out_weight):
    columns = in_t.shape[1]
    local_di = DI // 4
    shapes = [
        (local_di + 2 * STATE + 16, columns),
        (2 * local_di, columns),
    ]
    inputs = [in_t, out_weight]
    return call(
        prepare_kernel,
        [index],
        inputs,
        [fixed(array.shape) for array in inputs],
        [struct(shape, jnp.bfloat16) for shape in shapes],
        [fixed(shape) for shape in shapes],
        [],
        1,
        [],
        (100_000_000, 4_000_000, 0),
        "prepare",
    )


def run_forward(hidden, rest, gain_one, conv, heads_vectors, expand):
    places, blocks = rest
    length = hidden.shape[0]
    chunks = length // BLOCK
    lanes, local_di = expand.shape
    channels = local_di + 2 * STATE
    vectors = [gain_one, *conv, *heads_vectors, expand]
    return call(
        lambda *refs: forward_kernel(len(blocks), *refs),
        places,
        [*blocks, hidden, *vectors],
        [fixed(array.shape) for array in blocks]
        + [rows_of(D)]
        + [fixed(array.shape) for array in vectors],
        [
            struct((channels + lanes, D), jnp.bfloat16),
            struct((length, D), jnp.bfloat16),
            struct((length, channels)),
            struct((length, channels)),
            struct((length, lanes)),
            struct((length, local_di)),
            struct((length, local_di), jnp.bfloat16),
            struct((chunks, STATE, local_di)),
        ],
        [
            fixed((channels + lanes, D)),
            rows_of(D),
            rows_of(channels),
            rows_of(channels),
            rows_of(lanes),
            rows_of(local_di),
            rows_of(local_di),
            pl.BlockSpec((1, STATE, local_di), lambda q, *_: (q, 0, 0)),
        ],
        [
            pltpu.VMEM((8 + BLOCK, channels), jnp.float32),
            pltpu.VMEM((STATE, local_di), jnp.float32),
        ],
        chunks,
        [],
        (6_000_000_000, 30_000_000, 8_000_000),
        "forward",
    )


def run_gate(gate_out, cot, normed, scanned, gain_two):
    places, blocks = gate_out
    length, local_di = scanned.shape
    return call(
        lambda *refs: gate_kernel(len(blocks), *refs),
        places,
        [*blocks, cot, normed, scanned, gain_two],
        [fixed(array.shape) for array in blocks]
        + [rows_of(D), rows_of(D), rows_of(local_di), fixed((1, local_di))],
        [
            struct((local_di, D), jnp.bfloat16),
            struct((local_di, D), jnp.bfloat16),
            struct((length, local_di)),
            struct((length, local_di)),
            struct((8, length)),
        ],
        [
            fixed((local_di, D)),
            fixed((local_di, D)),
            rows_of(local_di),
            rows_of(local_di),
            pl.BlockSpec((8, BLOCK), lambda q, *_: (0, q)),
        ],
        [],
        length // BLOCK,
        [],
        (2_500_000_000, 12_000_000, 1_000_000),
        "gate",
    )


def run_middle(parity, gate_places, out_places, scanned, gating, d_gnorm, cot, normed, sums, out, gain):
    length, local_di = scanned.shape
    gate_shape = (local_di, D // len(gate_places))
    out_shape = (local_di, D) if len(out_places) == 1 else (local_di * D // 256, 128)
    shapes = [gate_shape] * len(gate_places) + [out_shape] * len(out_places)
    return call(
        lambda *refs: middle_kernel(len(gate_places), len(out_places), *refs),
        [parity] + gate_places + out_places,
        [scanned, gating, d_gnorm, cot, normed, *sums, out, gain],
        [
            rows_of(local_di),
            rows_of(local_di),
            rows_of(local_di),
            rows_of(D),
            rows_of(D),
        ]
        + [pl.BlockSpec((8, BLOCK), lambda q, *_: (0, q))] * 4
        + [fixed((local_di, D)), fixed((1, local_di))],
        [
            struct((length // 2, D), jnp.bfloat16),
            struct((length // 2, D), jnp.bfloat16),
            struct((length, local_di), jnp.bfloat16),
            struct((length, local_di), jnp.bfloat16),
            struct((1, local_di)),
        ]
        + [struct(shape, jnp.bfloat16) for shape in shapes],
        [
            fixed((length // 2, D)),
            fixed((length // 2, D)),
            rows_of(local_di),
            rows_of(local_di),
            fixed((1, local_di)),
        ]
        + [fixed(shape) for shape in shapes],
        [pltpu.VMEM((local_di, D), jnp.float32), pltpu.VMEM((local_di, D), jnp.float32)],
        length // BLOCK,
        [],
        (4_000_000_000, 15_000_000, 500_000),
        "middle",
    )


def run_backward(
    places, normed, conv_in, conv_pre, dt_raw, y, states, d_scanned, kernel, heads_vectors, expand
):
    length, local_di = y.shape
    chunks = length // BLOCK
    channels = conv_in.shape[1]
    lanes = expand.shape[0]
    grad = (channels + 16, D) if len(places) == 1 else ((channels + 16) * D // 256, 128)

    def back(extent):
        return pl.BlockSpec((BLOCK, extent), lambda q, *_: (chunks - 1 - q, 0))

    return call(
        lambda *refs: backward_kernel(len(places), *refs),
        places,
        [normed, conv_in, conv_pre, dt_raw, y, states, d_scanned, kernel, *heads_vectors, expand],
        [
            back(D),
            back(channels),
            back(channels),
            back(lanes),
            back(local_di),
            pl.BlockSpec((1, STATE, local_di), lambda q, *_: (chunks - 1 - q, 0, 0)),
            back(local_di),
            fixed((WIDTH, channels)),
            fixed((1, lanes)),
            fixed((1, lanes)),
            fixed((1, local_di)),
            fixed((lanes, local_di)),
        ],
        [
            struct((length, channels + lanes), jnp.bfloat16),
            struct((WIDTH, channels)),
            struct((1, channels)),
            struct((1, local_di)),
            struct((2, lanes)),
        ]
        + [struct(grad, jnp.bfloat16)] * len(places),
        [
            back(channels + lanes),
            fixed((WIDTH, channels)),
            fixed((1, channels)),
            fixed((1, local_di)),
            fixed((2, lanes)),
        ]
        + [fixed(grad)] * len(places),
        [
            pltpu.VMEM((BLOCK + 8, channels), jnp.float32),
            pltpu.VMEM((STATE, local_di), jnp.float32),
            pltpu.VMEM((STATE, local_di), jnp.float32),
            pltpu.VMEM((channels + lanes, D), jnp.float32),
        ],
        chunks,
        [],
        (14_000_000_000, 40_000_000, 10_000_000),
        "backward",
    )


def run_pair(y, far, out_places, gate, out, block):
    columns = gate[0].shape[1] // 2
    shapes = [
        (gate[0].shape[0], columns),
        (gate[0].shape[0], columns),
        (block[0].shape[0] // 2, D),
        (block[0].shape[0] // 2, D),
    ] + [(out[0].shape[0] // len(out_places), out[0].shape[1])] * len(out_places)
    inputs = [*gate, *out, *block]
    return call(
        pair_kernel,
        [y, far] + out_places,
        inputs,
        [fixed(array.shape) for array in inputs],
        [struct(shape, jnp.bfloat16) for shape in shapes],
        [fixed(shape) for shape in shapes],
        [],
        1,
        [],
        (3_000_000, 7_000_000, 0),
        "pair",
    )


def run_normed(parity, hidden, d_gating, d_rest, gate_weight, rest_weight, arrived):
    length, local_di = d_gating.shape
    rest = d_rest.shape[1]
    return call(
        normed_kernel,
        [parity],
        [hidden, d_gating, d_rest, gate_weight, rest_weight],
        [
            rows_of(D),
            rows_of(local_di),
            rows_of(rest),
            fixed((local_di, D)),
            fixed((rest, D)),
        ],
        [
            struct((length // 2, D), jnp.bfloat16),
            struct((length // 2, D), jnp.bfloat16),
            struct((1, D)),
        ],
        [fixed((length // 2, D)), fixed((length // 2, D)), fixed((1, D))],
        [],
        length // BLOCK,
        arrived,
        (3_000_000_000, 9_000_000, 1000),
        "normed",
    )


def run_rest_pair(places, mine, arrived, there):
    rest = (mine.shape[0] // len(places), mine.shape[1])
    shapes = [struct(rest, jnp.bfloat16)] * len(places)
    inputs = [mine, arrived]
    return call(
        rest_pair_kernel,
        places,
        inputs,
        [fixed(array.shape) for array in inputs],
        shapes,
        [fixed(shape.shape) for shape in shapes],
        [],
        1,
        there,
        (2_000_000, 3_000_000, 0),
        "rest_pair",
    )


def run_join(gate, out, vec, there):
    inputs = [*gate, *out, *vec]
    shape = (gate[0].shape[0] + out[0].shape[0], gate[0].shape[1])
    return call(
        join_kernel,
        [jnp.int32(0)],
        inputs,
        [fixed(array.shape) for array in inputs],
        [struct(shape, jnp.bfloat16), struct(vec[0].shape)],
        [fixed(shape), fixed(vec[0].shape)],
        [],
        1,
        there,
        (500_000, 1_000_000, 0),
        "join",
    )


def run_final(rest, vec, there):
    inputs = [*rest, *vec]
    return call(
        final_kernel,
        [jnp.int32(0)],
        inputs,
        [fixed(array.shape) for array in inputs],
        [struct(rest[0].shape, jnp.bfloat16), struct(vec[0].shape)],
        [fixed(rest[0].shape), fixed(vec[0].shape)],
        [],
        1,
        there,
        (500_000, 1_000_000, 0),
        "final",
    )


def run_update_gate(places, blocks, in_arrays, out_arrays, there):
    groups = len(places)
    rows_out = out_arrays[0].shape[0] // groups
    arrays = [*in_arrays, *out_arrays]
    in_spec = pl.BlockSpec((DI // groups, in_arrays[0].shape[1]), lambda q, *_: (q, 0))
    out_spec = pl.BlockSpec((rows_out, D), lambda q, *_: (q, 0))
    specs = [in_spec] * 3 + [out_spec] * 3
    return call(
        lambda *refs: update_gate_kernel(groups, *refs),
        places,
        [*blocks, *arrays],
        [fixed(array.shape) for array in blocks] + specs,
        [struct(array.shape) for array in arrays],
        specs,
        [pltpu.VMEM((groups,) + blocks[0].shape, jnp.bfloat16)],
        groups,
        there,
        (10_000_000, 13_000_000, 500_000),
        "update_gate",
    )


def run_update_rest(places, blocks, in_arrays, so_far):
    groups = len(places)
    spec = pl.BlockSpec((DI // groups, in_arrays[0].shape[1]), lambda q, *_: (q + groups, 0))
    return call(
        lambda *refs: update_rest_kernel(groups, *refs),
        places,
        [*blocks, *in_arrays, *so_far],
        [fixed(array.shape) for array in blocks]
        + [spec] * 3
        + [pl.BlockSpec(memory_space=pl.ANY)] * 3,
        [struct(array.shape) for array in in_arrays],
        [spec] * 3,
        [pltpu.VMEM((groups,) + blocks[0].shape, jnp.bfloat16)],
        groups + 1,
        [],
        (10_000_000, 8_000_000, 500_000),
        "update_rest",
        [(1 + groups + 3 + number, number) for number in range(3)],
    )


def adamw_step(weight, first, second, grad, rate, decay):
    first_new = beta_one * first + (1.0 - beta_one) * grad
    second_new = beta_two * second + (1.0 - beta_two) * grad * grad
    fix_one = 1.0 - beta_one**STEP
    fix_two = 1.0 - beta_two**STEP
    normalized = first_new / fix_one / (jnp.sqrt(second_new / fix_two) + adam_eps)
    return (first_new, second_new, weight - rate * (normalized + decay * weight))


def pick_heads(values, axis, width, index, groups):
    shape = values.shape
    split = shape[:axis] + (HEADS // groups, groups, width) + shape[axis + 1 :]
    taken = lax.dynamic_index_in_dim(values.reshape(split), index, axis + 1, keepdims=False)
    return taken.reshape(shape[:axis] + (HEADS // groups * width,) + shape[axis + 1 :])


def merge_heads(stacked, axis, width):
    groups = stacked.shape[0]
    shape = stacked.shape[1:]
    split = (groups,) + shape[:axis] + (HEADS // groups, width) + shape[axis + 1 :]
    moved = jnp.moveaxis(stacked.reshape(split), 0, axis + 1)
    return moved.reshape(shape[:axis] + (HEADS * width,) + shape[axis + 1 :])


def swap(values, axis, mask):
    route = [(i, i ^ mask) for i in range(lax.axis_size(axis))]
    return lax.ppermute(values, axis, route)


def seq_blocks(rows, far=None):
    index = lax.axis_index("seq")
    far = swap(rows, "seq", 2) if far is None else far
    blocks = [rows, swap(rows, "seq", 1), far, swap(far, "seq", 1)]
    return [index ^ mask for mask in range(4)], blocks


def ring_step(held):
    count = lax.axis_size("wshard")
    return lax.ppermute(held, "wshard", [(i, (i + 2) % count) for i in range(count)])


def ring_blocks(rows):
    count = lax.axis_size("wshard")
    index = lax.axis_index("wshard")
    places, blocks = [], []
    for step in range(count // 2):
        source = (index + count - 2 * step) % count
        places = places + [source, source ^ 1]
        blocks = blocks + [rows, swap(rows, "wshard", 1)]
        if step < count // 2 - 1:
            rows = ring_step(rows)
    return places, blocks


def take_block(values, index, rows):
    return lax.dynamic_slice_in_dim(values, index * rows, rows, 0)


def gather_out(out_low, seq_index, groups):
    rows = out_low.shape[0]
    if rows % (groups * HEADDIM) == 0:
        mine = pick_rows(out_low, seq_index, groups)
        return lax.all_gather(mine, "wshard", axis=0, tiled=True)
    whole = lax.all_gather(out_low, "wshard", axis=0, tiled=True)
    return pick_heads(whole, 0, HEADDIM, seq_index, groups)


def pick_rows(values, seq_index, groups):
    rows = values.shape[0]
    split = values.reshape(rows // (groups * HEADDIM), groups, HEADDIM, values.shape[1])
    return lax.dynamic_index_in_dim(split, seq_index, 1, keepdims=False).reshape(
        rows // groups, values.shape[1]
    )


def sum_out_grad(grad, rows, seq_index, groups):
    grad = grad.astype(jnp.bfloat16)
    if rows % (groups * HEADDIM) == 0:
        mine = lax.psum_scatter(grad, "wshard", scatter_dimension=0, tiled=True)
        every = lax.all_gather(mine, "seq", axis=0, tiled=False)
        split = every.reshape(groups, rows // (groups * HEADDIM), HEADDIM, grad.shape[1])
        return jnp.moveaxis(split, 0, 1).reshape(rows, grad.shape[1]).astype(jnp.float32)
    blocks = grad.reshape(HEADS // groups, 1, HEADDIM, grad.shape[1])
    here = (jnp.arange(groups) == seq_index)[None, :, None, None]
    spread = jnp.where(here, blocks, jnp.zeros((), jnp.bfloat16)).reshape(DI, grad.shape[1])
    mine = lax.psum_scatter(spread, "wshard", scatter_dimension=0, tiled=True)
    return lax.psum(mine.astype(jnp.float32), "seq")


def shards(
    block_in,
    cotangent,
    in_weight,
    in_first,
    in_second,
    out_weight,
    out_first,
    out_second,
    vec_weight,
    vec_first,
    vec_second,
):
    rows_here = block_in.shape[1]
    groups = lax.axis_size("seq")
    seq_index = lax.axis_index("seq")
    local_heads = HEADS // groups
    local_di = DI // groups
    hidden_rows = block_in.reshape(rows_here, D)
    cot_rows = cotangent.reshape(rows_here, D)
    gain_one, gain_two, kernel, conv_bias, a_log, dt_bias, d_skip = split_vector(vec_weight)

    def heads_of(values, axis, width):
        return pick_heads(values, axis, width, seq_index, groups)

    lanes = 128
    channels = local_di + 2 * STATE
    shard_index = lax.axis_index("wshard")
    rings = lax.axis_size("wshard") == 8
    near = seq_index % 2
    far = seq_index // 2
    if rings:
        y, z = shard_index % 2, shard_index // 2
        rest_mine, gate_out_mine = run_prepare(seq_index, in_weight.T, out_weight)
        rest = ring_blocks(rest_mine)
        gate_out = ring_blocks(gate_out_mine)
        gate_places = [z ^ mask for mask in range(4)]
        out_places = [y, 1 - y]
    else:
        in_low = low(in_weight)
        steps_mine = heads_of(in_low[:, DI + CONVCH :], 1, 1)
        rest_mine = jnp.concatenate(
            [
                heads_of(in_low[:, DI : 2 * DI], 1, HEADDIM),
                in_low[:, 2 * DI : 2 * DI + 2 * STATE],
                jnp.pad(steps_mine, ((0, 0), (0, 16 - local_heads))),
            ],
            1,
        )
        gate_mine = heads_of(in_low[:, :DI], 1, HEADDIM)
        origin = [jnp.int32(0)]
        rest = (origin, [lax.all_gather(rest_mine, "wshard", axis=0, tiled=True).T])
        gate_mine = lax.all_gather(gate_mine, "wshard", axis=0, tiled=True).T
        gate_out = (origin, [gate_mine, gather_out(low(out_weight), seq_index, groups)])
        gate_places, out_places = origin, origin
    hidden_low = lax.all_gather(hidden_rows, "seq", axis=0, tiled=True)
    cot_low = lax.all_gather(cot_rows, "seq", axis=0, tiled=True)
    my_gain_two = heads_of(gain_two, 0, HEADDIM)[None, :]
    my_kernel = jnp.concatenate([heads_of(kernel[:, :DI], 1, HEADDIM), kernel[:, DI:]], 1)
    my_bias = jnp.concatenate([heads_of(conv_bias[:DI], 0, HEADDIM), conv_bias[DI:]], 0)

    def on_lanes(values):
        return jnp.pad(values, (0, lanes - local_heads))[None, :]

    heads_vectors = (
        on_lanes(heads_of(a_log, 0, 1)),
        on_lanes(heads_of(dt_bias, 0, 1)),
        jnp.repeat(heads_of(d_skip, 0, 1), HEADDIM)[None, :],
    )
    expand = (
        jnp.arange(lanes)[:, None] == jnp.arange(local_di)[None, :] // HEADDIM
    ).astype(jnp.float32)
    (
        rest_weight,
        normed_low,
        conv_in,
        conv_pre,
        dt_raw,
        y_part,
        scanned,
        states,
    ) = run_forward(
        hidden_low, rest, gain_one[None, :], (my_kernel, my_bias[None, :]), heads_vectors, expand
    )
    gate_weight, out_low, gating, d_gnorm, sums = run_gate(
        gate_out, cot_low, normed_low, scanned, my_gain_two
    )
    middle = run_middle(
        near,
        gate_places,
        out_places,
        scanned,
        gating,
        d_gnorm,
        cot_low,
        normed_low,
        [sums] + [swap(sums, "seq", mask) for mask in range(1, 4)],
        out_low,
        my_gain_two,
    )
    block_mine, block_send, d_gating, d_scanned, d_gain_two = middle[:5]
    gate_grads = middle[5 : 5 + len(gate_places)]
    out_grads = middle[5 + len(gate_places) :]
    block_arrived = swap(block_send, "seq", 1)
    if rings:
        gate_pieces = [swap(gate_grads[mask], "wshard", 2 * mask) for mask in range(1, 4)]
        out_arrived = swap(out_grads[1], "wshard", 1)
    backward = run_backward(
        out_places,
        normed_low,
        conv_in,
        conv_pre,
        dt_raw,
        y_part,
        states,
        d_scanned,
        my_kernel,
        heads_vectors,
        expand,
    )
    d_rest, d_kernel, d_conv_bias, d_skip_wide, d_head = backward[:5]
    rest_grads = backward[5:]
    before_normed = []
    if rings:
        rest_arrived = swap(rest_grads[1], "wshard", 1)
        gate_keep, gate_send, block_keep, block_send, *out_sums = run_pair(
            y,
            far,
            gate_places,
            [gate_grads[0]] + gate_pieces,
            [out_grads[0], out_arrived],
            [block_mine, block_arrived],
        )
        gate_arrived = swap(gate_send, "wshard", 1)
        out_pieces = [swap(out_sums[mask], "wshard", 2 * mask) for mask in range(1, 4)]
        before_normed = [gate_keep]
    else:
        block_sum = low(block_mine.astype(jnp.float32) + block_arrived.astype(jnp.float32))
        block_keep = take_block(block_sum, far, rows_here)
        block_send = take_block(block_sum, 1 - far, rows_here)
    block_far = swap(block_send, "seq", 2)
    normed_mine, normed_send, d_gain_one = run_normed(
        near, hidden_low, d_gating, d_rest, gate_weight, rest_weight, before_normed
    )
    normed_arrived = swap(normed_send, "seq", 1)
    normed_sum = normed_mine.astype(jnp.float32) + normed_arrived.astype(jnp.float32)
    normed_far = swap(low(take_block(normed_sum, 1 - far, rows_here)), "seq", 2)
    shared = jnp.concatenate(
        [d_gain_one[0], d_kernel[:, local_di:].reshape(-1), d_conv_bias[0, local_di:]]
    )
    d_skip_part = jnp.sum(d_skip_wide.reshape(local_heads, HEADDIM), axis=1)
    apart = jnp.concatenate(
        [
            d_gain_two[0],
            d_kernel[:, :local_di].reshape(-1),
            d_conv_bias[0, :local_di],
            d_head[:, :local_heads].reshape(-1),
            d_skip_part,
        ]
    )
    vec_part = jnp.concatenate([shared, apart])[None]
    if rings:
        rest_sums = run_rest_pair(
            gate_places, rest_grads[0], rest_arrived, [d_gain_one, block_far] + out_pieces
        )
        rest_pieces = [swap(rest_sums[mask], "wshard", 2 * mask) for mask in range(1, 4)]
        gate_out_part, vec_part = run_join(
            [gate_keep, gate_arrived],
            [out_sums[0]] + out_pieces,
            [vec_part, swap(vec_part, "wshard", 1)],
            [rest_sums[0]],
        )
        vec_arrived = swap(vec_part, "wshard", 2)
        spots, gate_out_blocks = seq_blocks(gate_out_part)
        in_arrays = (in_weight.T, in_first.T, in_second.T)
        updated = run_update_gate(
            spots,
            gate_out_blocks,
            in_arrays,
            (out_weight, out_first, out_second),
            [vec_arrived],
        )
        out_first_new, out_second_new, out_weight_new = updated[3:]
        vec_part = vec_part + vec_arrived
        rest_part, vec_part = run_final(
            [rest_sums[0]] + rest_pieces,
            [vec_part, swap(vec_part, "wshard", 4)],
            [out_first_new],
        )
        vec_places, vec_blocks = seq_blocks(vec_part)
        every = jnp.zeros((groups, vec_part.shape[1]), jnp.float32)
        for spot, block in zip(vec_places, vec_blocks):
            every = lax.dynamic_update_slice_in_dim(every, block, spot, 0)
    else:
        vec_part = lax.psum(vec_part, "wshard")
        every = lax.all_gather(vec_part, "seq", axis=0, tiled=True)
    block_here = block_keep.astype(jnp.float32) + block_far.astype(jnp.float32)
    block_out = hidden_rows.astype(jnp.float32) + block_here
    d_normed = take_block(normed_sum, far, rows_here) + normed_far.astype(jnp.float32)
    own_hidden = hidden_rows.astype(jnp.float32)
    own_scale = lax.rsqrt(jnp.mean(own_hidden * own_hidden, axis=-1, keepdims=True) + norm_eps)
    own_unit = own_hidden * own_scale
    d_own = d_normed * gain_one[None, :]
    d_hidden = own_scale * (
        d_own - own_unit * jnp.mean(d_own * own_unit, axis=-1, keepdims=True)
    )
    block_grad = cot_rows.astype(jnp.float32) + d_hidden
    shared, every = (
        jnp.sum(every[:, : shared.shape[0]], axis=0),
        every[:, shared.shape[0] :],
    )
    kernel_end = local_di * (1 + WIDTH)
    heads_at = kernel_end + local_di
    both_kernel = D + 2 * STATE * WIDTH
    vec_total = jnp.concatenate(
        [
            shared[:D],
            merge_heads(every[:, :local_di], 0, HEADDIM),
            jnp.concatenate(
                [
                    merge_heads(
                        every[:, local_di:kernel_end].reshape(groups, WIDTH, local_di), 1, HEADDIM
                    ),
                    shared[D:both_kernel].reshape(WIDTH, 2 * STATE),
                ],
                1,
            ).reshape(-1),
            merge_heads(every[:, kernel_end:heads_at], 0, HEADDIM),
            shared[both_kernel:],
            merge_heads(every[:, heads_at : heads_at + local_heads], 0, 1),
            merge_heads(every[:, heads_at + local_heads : heads_at + 2 * local_heads], 0, 1),
            merge_heads(every[:, heads_at + 2 * local_heads :], 0, 1),
        ]
    )
    vec_first_new, vec_second_new, vec_weight_new = adamw_step(
        vec_weight, vec_first, vec_second, vec_total, vector_rate, 0.0
    )
    if rings:
        spots, rest_blocks = seq_blocks(rest_part)
        updated = run_update_rest(spots, rest_blocks, in_arrays, updated[:3])
        in_first_new, in_second_new, in_weight_new = [array.T for array in updated]
    else:
        rest_part = lax.psum_scatter(rest_grads[0].T, "wshard", scatter_dimension=0, tiled=True)
        gate_part = lax.psum_scatter(gate_grads[0].T, "wshard", scatter_dimension=0, tiled=True)
        gate_every = lax.all_gather(gate_part, "seq", axis=0, tiled=False).astype(jnp.float32)
        rest_every = lax.all_gather(rest_part, "seq", axis=0, tiled=False).astype(jnp.float32)
        out_total = sum_out_grad(out_grads[0], out_weight.shape[0], seq_index, groups)
        in_total = jnp.concatenate(
            [
                merge_heads(gate_every, 1, HEADDIM),
                merge_heads(rest_every[:, :, :local_di], 1, HEADDIM),
                jnp.sum(rest_every[:, :, local_di:channels], axis=0),
                merge_heads(rest_every[:, :, channels : channels + local_heads], 1, 1),
            ],
            1,
        )
        in_first_new, in_second_new, in_weight_new = adamw_step(
            in_weight, in_first, in_second, in_total, matrix_rate, matrix_decay
        )
        out_first_new, out_second_new, out_weight_new = adamw_step(
            out_weight, out_first, out_second, out_total, matrix_rate, matrix_decay
        )
    return (
        block_out.reshape(1, rows_here, D),
        block_grad.reshape(1, rows_here, D),
        in_first_new,
        in_second_new,
        in_weight_new,
        out_first_new,
        out_second_new,
        out_weight_new,
        vec_first_new,
        vec_second_new,
        vec_weight_new,
    )


def solution(mesh):
    return jax.shard_map(
        shards,
        mesh=mesh,
        in_specs=(
            P("wshard", "seq", None),
            P("wshard", "seq", None),
            P("wshard", None),
            P("wshard", None),
            P("wshard", None),
            P("wshard", None),
            P("wshard", None),
            P("wshard", None),
            P(),
            P(),
            P(),
        ),
        out_specs=(
            P("wshard", "seq", None),
            P("wshard", "seq", None),
            P("wshard", None),
            P("wshard", None),
            P("wshard", None),
            P("wshard", None),
            P("wshard", None),
            P("wshard", None),
            P(),
            P(),
            P(),
        ),
        check_vma=False,
    )
```

```python
import jax
import jax.numpy as jnp
from jax import lax
from jax.experimental import pallas as pl
from jax.experimental.pallas import tpu as pltpu
from jax.sharding import PartitionSpec as P

D = 1024
HEADS = 32
HEADDIM = 64
STATE = 128
WIDTH = 4
BLOCK = 256
STEP = 10
DI = 2048
CONVCH = 2304


precise = lax.Precision.HIGHEST
norm_eps = 1e-05
beta_one = 0.9
beta_two = 0.95
adam_eps = 1e-08
matrix_rate = 0.05
matrix_decay = 0.1
vector_rate = 0.5


def rms_scale(values):
    return values * lax.rsqrt(jnp.mean(values * values, axis=-1, keepdims=True) + norm_eps)


def split_vector(vector):
    extents = [D, DI, WIDTH * CONVCH, CONVCH, HEADS, HEADS, HEADS]
    pieces = []
    offset = 0
    for extent in extents:
        pieces.append(vector[offset : offset + extent])
        offset = offset + extent
    pieces[2] = pieces[2].reshape(WIDTH, CONVCH)
    return pieces


def dot_nt(left, right, precision=None):
    return lax.dot_general(
        left,
        right,
        (((1,), (1,)), ((), ())),
        precision=precision,
        preferred_element_type=jnp.float32,
    )


def dot_tn(left, right):
    return lax.dot_general(
        left, right, (((0,), (0,)), ((), ())), preferred_element_type=jnp.float32
    )


def dot_nn(left, right, precision=None):
    return jnp.dot(left, right, precision=precision, preferred_element_type=jnp.float32)


def sigmoid(values):
    return 1.0 / (1.0 + jnp.exp(-values))


def low(values):
    return values.astype(jnp.bfloat16)


def lower_mask():
    rows = lax.broadcasted_iota(jnp.int32, (BLOCK, BLOCK), 0)
    return rows >= lax.broadcasted_iota(jnp.int32, (BLOCK, BLOCK), 1)


def decay_sums(dt_raw, dt_bias, a_log, expand):
    shifted = dt_raw + dt_bias
    step = jnp.maximum(shifted, 0.0) + jnp.log1p(jnp.exp(-jnp.abs(shifted)))
    log_decay = -jnp.exp(a_log) * step
    ones = jnp.where(lower_mask(), 1.0, 0.0)
    running = dot_nn(ones, log_decay, precise)
    step_wide = dot_nn(step, expand, precise)
    running_wide = dot_nn(running, expand, precise)
    return shifted, step, log_decay, running, step_wide, running_wide


def place_rows(result_ref, place, block):
    rows = block.shape[0]
    result_ref[pl.ds(pl.multiple_of(place * rows, rows), rows), :] = block


def place_columns(result_ref, place, block):
    rows, columns = block.shape
    start = pl.multiple_of(place * columns, columns)
    result_ref[:rows, pl.ds(start, columns)] = block


def forward_kernel(rest_count, places_ref, *refs):
    rest_blocks = refs[:rest_count]
    (
        hidden_ref,
        gain_one_ref,
        conv_ref,
        bias_ref,
        a_log_ref,
        dt_bias_ref,
        skip_ref,
        expand_ref,
        rest_ref,
        normed_ref,
        conv_in_ref,
        conv_pre_ref,
        dt_ref,
        y_ref,
        scanned_ref,
        state_ref,
        ext,
        state,
    ) = refs[rest_count:]
    local_di = y_ref.shape[1]
    heads = local_di // HEADDIM
    channels = conv_in_ref.shape[1]

    @pl.when(pl.program_id(0) == 0)
    def _():
        ext[0:8, :] = jnp.zeros((8, ext.shape[1]), jnp.float32)
        state[...] = jnp.zeros_like(state)
        rest_ref[channels:, :] = jnp.zeros_like(rest_ref[channels:, :])
        for number, block in enumerate(rest_blocks):
            place_columns(rest_ref, places_ref[number], block[...])

    hidden = hidden_ref[...].astype(jnp.float32)
    normed = low(rms_scale(hidden) * gain_one_ref[...])
    normed_ref[...] = normed
    conv_in = dot_nt(normed, rest_ref[:channels, :])
    conv_in_ref[...] = conv_in
    ext[8 : 8 + BLOCK, :] = conv_in
    conv_pre = bias_ref[...] + conv_ref[WIDTH - 1 : WIDTH, :] * conv_in
    for tap in range(WIDTH - 1):
        first = 8 - WIDTH + 1 + tap
        conv_pre = conv_pre + conv_ref[tap : tap + 1, :] * ext[first : first + BLOCK, :]
    conv_pre_ref[...] = conv_pre
    ext[8 - WIDTH + 1 : 8, :] = ext[8 + BLOCK - WIDTH + 1 : 8 + BLOCK, :]
    conv_low = low(conv_pre * sigmoid(conv_pre))
    inner = conv_low[:, :local_di]
    b_rows = conv_low[:, local_di : local_di + STATE]
    c_rows = conv_low[:, local_di + STATE :]
    dt_raw = low(dot_nt(normed, rest_ref[channels:, :])).astype(jnp.float32)
    dt_ref[...] = dt_raw

    _, _, _, running, step_wide, running_wide = decay_sums(
        dt_raw, dt_bias_ref[...], a_log_ref[...], expand_ref[...]
    )
    running_t = running.T
    b_t = low(b_rows.astype(jnp.float32).T)
    scores = dot_nn(c_rows, b_t)
    mask = lower_mask()
    inner_wide = inner.astype(jnp.float32)
    stepped = step_wide * inner_wide
    stepped_low = low(stepped)
    first_half = lax.broadcasted_iota(jnp.int32, (BLOCK, 2 * HEADDIM), 1) < HEADDIM
    zero = jnp.zeros((), jnp.bfloat16)
    state_ref[...] = state[...].reshape(state_ref.shape)
    held = state[...]
    carried = jnp.exp(running_wide) * dot_nn(c_rows, low(held))
    for pair in range(heads // 2):
        span = slice(pair * 2 * HEADDIM, (pair + 1) * 2 * HEADDIM)
        both = stepped_low[:, span]
        total = carried[:, span]
        for half in range(2):
            head = 2 * pair + half
            differ = running[:, head : head + 1] - running_t[head : head + 1, :]
            mixed = low(jnp.exp(jnp.where(mask, differ, -jnp.inf)) * scores)
            mine = jnp.where(first_half if half == 0 else ~first_half, both, zero)
            total = total + dot_nn(mixed, mine)
        y_ref[:, span] = total
    last = running_wide[BLOCK - 1 : BLOCK, :]
    to_end = jnp.exp(last - running_wide)
    state[...] = jnp.exp(last) * held + dot_nn(b_t, low(to_end * stepped))
    scanned_ref[...] = low(y_ref[...] + skip_ref[...] * inner_wide)


def gate_kernel(count, places_ref, *refs):
    blocks = refs[:count]
    (
        cot_ref,
        normed_ref,
        scanned_ref,
        gain_two_ref,
        gate_ref,
        out_ref,
        gating_ref,
        d_gnorm_ref,
        sums_ref,
    ) = refs[count:]
    local_di = gating_ref.shape[1]

    @pl.when(pl.program_id(0) == 0)
    def _():
        if count == 2:
            gate_ref[...] = blocks[0][...]
            out_ref[...] = blocks[1][...]
            return
        number = 0
        for block in blocks:
            columns = block.shape[1]
            for base in range(0, block.shape[0], 2 * local_di):
                spot = places_ref[number]
                number = number + 1
                place_columns(gate_ref, spot, block[base : base + local_di, :])
                for tile in range(D // columns):
                    first = base + local_di + tile * HEADDIM
                    span = slice(tile * columns, (tile + 1) * columns)
                    place_rows(out_ref.at[:, span], spot, block[first : first + HEADDIM, :])

    gating = dot_nt(normed_ref[...], gate_ref[...])
    gating_ref[...] = gating
    d_gnorm = dot_nt(cot_ref[...], out_ref[...])
    d_gnorm_ref[...] = d_gnorm
    gated = scanned_ref[...].astype(jnp.float32) * (gating * sigmoid(gating))
    ones = jnp.ones((8, local_di), jnp.float32)
    squares = dot_nt(ones, gated * gated, precise)
    products = dot_nt(ones, d_gnorm * gain_two_ref[...] * gated, precise)
    sums_ref[...] = jnp.where(
        lax.broadcasted_iota(jnp.int32, squares.shape, 0) == 0, squares, products
    )


def middle_kernel(gate_count, out_count, places_ref, *refs):
    (
        scanned_ref,
        gating_ref,
        d_gnorm_ref,
        cot_ref,
        normed_ref,
        sums_one_ref,
        sums_two_ref,
        sums_three_ref,
        sums_four_ref,
        out_ref,
        gain_two_ref,
        block_ref,
        d_gating_ref,
        d_scanned_ref,
        d_gain_two_ref,
    ) = refs[:15]
    gate_refs = refs[15 : 15 + gate_count]
    out_refs = refs[15 + gate_count : 15 + gate_count + out_count]
    out_sum, gate_sum = refs[15 + gate_count + out_count :]
    chunk = pl.program_id(0)

    @pl.when(chunk == 0)
    def _():
        out_sum[...] = jnp.zeros_like(out_sum)
        gate_sum[...] = jnp.zeros_like(gate_sum)
        d_gain_two_ref[...] = jnp.zeros_like(d_gain_two_ref)

    sums = (sums_one_ref[...] + sums_two_ref[...]) + (sums_three_ref[...] + sums_four_ref[...])
    sums = (sums / DI).T
    scale = lax.rsqrt(sums[:, 0:1] + norm_eps)
    slope = scale * scale * sums[:, 1:2]
    gating = gating_ref[...]
    open_part = sigmoid(gating)
    gate = gating * open_part
    scanned = scanned_ref[...].astype(jnp.float32)
    unit = scanned * gate * scale
    d_gnorm = d_gnorm_ref[...]
    gain_two = gain_two_ref[...]
    gnorm = low(unit * gain_two)
    block_ref[...] = low(dot_nn(gnorm, out_ref[...]))
    out_sum[...] += dot_tn(gnorm, cot_ref[...])
    d_gain_two_ref[...] += jnp.sum(d_gnorm * unit, axis=0, keepdims=True)
    d_gated = scale * (d_gnorm * gain_two) - unit * slope
    d_gating = low(d_gated * scanned * (open_part * (1.0 + gating * (1.0 - open_part))))
    d_gating_ref[...] = d_gating
    d_scanned_ref[...] = low(d_gated * gate)
    gate_sum[...] += dot_tn(d_gating, normed_ref[...])

    @pl.when(chunk == pl.num_programs(0) - 1)
    def _():
        for number, gate_ref in enumerate(gate_refs):
            columns = gate_ref.shape[1]
            start = pl.multiple_of(places_ref[number] * columns, columns)
            gate_ref[...] = low(gate_sum[:, pl.ds(start, columns)])
        for number, grad_ref in enumerate(out_refs):
            columns = grad_ref.shape[1]
            first = places_ref[gate_count + number]
            for step in range(out_sum.shape[0] // HEADDIM // out_count):
                head = first + step * out_count
                rows = pl.ds(pl.multiple_of(head * HEADDIM, HEADDIM), HEADDIM)
                for tile in range(D // columns):
                    base = (step * (D // columns) + tile) * HEADDIM
                    grad_ref[base : base + HEADDIM, :] = low(
                        out_sum[rows, tile * columns : (tile + 1) * columns]
                    )


def backward_kernel(
    grad_count,
    places_ref,
    normed_ref,
    conv_in_ref,
    conv_pre_ref,
    dt_ref,
    y_ref,
    state_ref,
    d_scanned_ref,
    conv_ref,
    a_log_ref,
    dt_bias_ref,
    skip_ref,
    expand_ref,
    d_rest_ref,
    d_kernel_ref,
    d_conv_bias_ref,
    d_skip_ref,
    d_head_ref,
    *refs,
):
    grad_refs = refs[:grad_count]
    ext, d_state, later_state, rest_sum = refs[grad_count:]
    local_di = y_ref.shape[1]
    heads = local_di // HEADDIM
    chunk = pl.program_id(0)

    @pl.when(chunk == 0)
    def _():
        ext[BLOCK : BLOCK + 8, :] = jnp.zeros((8, ext.shape[1]), jnp.float32)
        d_state[...] = jnp.zeros_like(d_state)
        later_state[...] = jnp.zeros_like(later_state)
        rest_sum[...] = jnp.zeros_like(rest_sum)
        d_kernel_ref[...] = jnp.zeros_like(d_kernel_ref)
        d_conv_bias_ref[...] = jnp.zeros_like(d_conv_bias_ref)
        d_skip_ref[...] = jnp.zeros_like(d_skip_ref)
        d_head_ref[...] = jnp.zeros_like(d_head_ref)

    expand = expand_ref[...]
    conv_pre = conv_pre_ref[...]
    open_part = sigmoid(conv_pre)
    conv_low = low(conv_pre * open_part)
    inner = conv_low[:, :local_di].astype(jnp.float32)
    b_rows = conv_low[:, local_di : local_di + STATE]
    c_rows = conv_low[:, local_di + STATE :]
    a_log = a_log_ref[...]
    shifted, _, log_decay, running, step_wide, running_wide = decay_sums(
        dt_ref[...], dt_bias_ref[...], a_log, expand
    )
    running_t = running.T
    b_t = low(b_rows.astype(jnp.float32).T)
    c_t = low(c_rows.astype(jnp.float32).T)
    scores = dot_nn(c_rows, b_t)
    scores_t = dot_nn(b_rows, c_t)
    mask = lower_mask()
    rows = lax.broadcasted_iota(jnp.int32, (BLOCK, BLOCK), 0)
    mask_t = rows <= lax.broadcasted_iota(jnp.int32, (BLOCK, BLOCK), 1)
    d_y_low = d_scanned_ref[...]
    d_y = d_y_low.astype(jnp.float32)
    stepped_low = low(step_wide * inner)
    stepped = stepped_low.astype(jnp.float32)
    last = running_wide[BLOCK - 1 : BLOCK, :]
    to_end = jnp.exp(last - running_wide)
    d_later = d_state[...]
    d_later_low = low(d_later)
    held = state_ref[...].reshape(d_state.shape)
    decayed_dy = low(jnp.exp(running_wide) * d_y)
    d_c = dot_nt(decayed_dy, low(held))
    d_b = dot_nt(low(to_end * stepped), d_later_low)
    d_stepped = to_end * dot_nn(b_rows, d_later_low)
    cross = jnp.sum(later_state[...] * d_later, axis=0, keepdims=True)
    d_state[...] = jnp.exp(last) * d_later + dot_nn(c_t, decayed_dy)
    later_state[...] = held
    first_half = lax.broadcasted_iota(jnp.int32, (BLOCK, 2 * HEADDIM), 1) < HEADDIM
    zero = jnp.zeros((), jnp.bfloat16)
    d_scores = jnp.zeros((BLOCK, BLOCK), jnp.float32)
    pieces = []
    for pair in range(heads // 2):
        span = slice(pair * 2 * HEADDIM, (pair + 1) * 2 * HEADDIM)
        total = d_stepped[:, span]
        for half in range(2):
            head = 2 * pair + half
            mine = jnp.where(first_half if half == 0 else ~first_half, d_y_low[:, span], zero)
            column = running[:, head : head + 1]
            row = running_t[head : head + 1, :]
            decay = jnp.exp(jnp.where(mask, column - row, -jnp.inf))
            decay_t = jnp.exp(jnp.where(mask_t, row - column, -jnp.inf))
            d_scores = d_scores + dot_nt(mine, stepped_low[:, span]) * decay
            total = total + dot_nn(low(decay_t * scores_t), mine)
        pieces.append(total)
    d_stepped = jnp.concatenate(pieces, 1)
    d_scores_low = low(d_scores)
    d_c = d_c + dot_nn(d_scores_low, b_rows)
    d_b = d_b + dot_nn(low(d_scores.T), c_rows)
    d_inner = step_wide * d_stepped + skip_ref[...] * d_y
    d_running = dot_nt(d_y * y_ref[...] - d_stepped * stepped, expand, precise)
    upper = jnp.where(mask_t, 1.0, 0.0)
    d_log = dot_nn(upper, d_running, precise) + dot_nt(cross, expand, precise)
    d_step = dot_nt(d_stepped * inner, expand, precise) - jnp.exp(a_log) * d_log
    d_dt = d_step * sigmoid(shifted)
    d_head_ref[0:1, :] += jnp.sum(d_log * log_decay, axis=0, keepdims=True)
    d_head_ref[1:2, :] += jnp.sum(d_dt, axis=0, keepdims=True)
    d_skip_ref[...] += jnp.sum(d_y * inner, axis=0, keepdims=True)

    d_conv_out = jnp.concatenate([d_inner, d_b, d_c], 1)
    d_pre = d_conv_out * (open_part * (1.0 + conv_pre * (1.0 - open_part)))
    ext[0:BLOCK, :] = d_pre
    d_conv_bias_ref[...] += jnp.sum(d_pre, axis=0, keepdims=True)
    conv_in = conv_in_ref[...]
    d_conv_in = jnp.zeros_like(conv_in)
    for tap in range(WIDTH):
        moved = ext[WIDTH - 1 - tap : WIDTH - 1 - tap + BLOCK, :]
        d_conv_in = d_conv_in + conv_ref[tap : tap + 1, :] * moved
        d_kernel_ref[tap : tap + 1, :] += jnp.sum(moved * conv_in, axis=0, keepdims=True)
    ext[BLOCK : BLOCK + 8, :] = ext[0:8, :]
    d_rest = jnp.concatenate([low(d_conv_in), low(d_dt)], 1)
    d_rest_ref[...] = d_rest
    rest_sum[...] += dot_tn(d_rest, normed_ref[...])

    @pl.when(chunk == pl.num_programs(0) - 1)
    def _():
        for number, grad_ref in enumerate(grad_refs):
            columns = grad_ref.shape[1]
            blocks = rest_sum.shape[1] // columns // grad_count
            rows = grad_ref.shape[0] // blocks
            for step in range(blocks):
                place = places_ref[number] + step * grad_count
                start = pl.multiple_of(place * columns, columns)
                grad_ref[step * rows : (step + 1) * rows, :] = low(
                    rest_sum[:rows, pl.ds(start, columns)]
                )


def sum_of(*refs):
    total = refs[0][...].astype(jnp.float32)
    for ref in refs[1:]:
        total = total + ref[...].astype(jnp.float32)
    return total


def pair_kernel(places_ref, *refs):
    gate, out = refs[:4], refs[4:6]
    gate_keep_ref, gate_send_ref = refs[7:9]
    out_refs = refs[9:-1]
    paired = sum_of(*gate)
    columns = gate_keep_ref.shape[1]
    even = places_ref[0] == 0
    first, second = low(paired[:, :columns]), low(paired[:, columns:])
    gate_keep_ref[...] = jnp.where(even, first, second)
    gate_send_ref[...] = jnp.where(even, second, first)
    for number, ref in enumerate(out_refs):
        rows = ref.shape[0]
        start = pl.multiple_of(places_ref[1 + number] * rows, rows)
        here = pl.ds(start, rows)
        ref[...] = low(sum_of(out[0].at[here, :], out[1].at[here, :]))


def rest_pair_kernel(places_ref, mine_ref, arrived_ref, *rest_refs):
    for number, ref in enumerate(rest_refs):
        rows = ref.shape[0]
        here = pl.ds(pl.multiple_of(places_ref[number] * rows, rows), rows)
        ref[...] = low(sum_of(mine_ref.at[here, :], arrived_ref.at[here, :]))


def join_kernel(places_ref, *refs):
    joined_ref = refs[-1]
    rows = refs[0].shape[0]
    joined_ref[:rows, :] = low(sum_of(*refs[:2]))
    joined_ref[rows:, :] = low(sum_of(*refs[2:6]))


def final_kernel(places_ref, *refs):
    refs[-2][...] = low(sum_of(*refs[:4]))


def vec_kernel(places_ref, *refs):
    refs[-1][...] = (refs[0][...] + refs[1][...]) + (refs[2][...] + refs[3][...])


def normed_kernel(
    places_ref,
    hidden_ref,
    d_gating_ref,
    d_rest_ref,
    gate_weight_ref,
    rest_weight_ref,
    d_normed_ref,
    d_gain_one_ref,
):
    chunk = pl.program_id(0)

    @pl.when(chunk == 0)
    def _():
        d_gain_one_ref[...] = jnp.zeros_like(d_gain_one_ref)

    d_normed = dot_nn(d_gating_ref[...], gate_weight_ref[...])
    d_normed = d_normed + dot_nn(d_rest_ref[...], rest_weight_ref[...])
    d_normed_ref[...] = low(d_normed)
    unit = rms_scale(hidden_ref[...].astype(jnp.float32))
    d_gain_one_ref[...] += jnp.sum(d_normed * unit, axis=0, keepdims=True)


def prepare_kernel(places_ref, in_ref, out_ref, rest_ref, gate_out_ref):
    index = places_ref[0]
    local_di = gate_out_ref.shape[0] // 2
    groups = DI // local_di
    for head in range(HEADS // groups):
        rows = slice(head * HEADDIM, (head + 1) * HEADDIM)
        for base, result_ref in ((0, gate_out_ref), (DI, rest_ref)):
            start = pl.multiple_of(base + (groups * head + index) * HEADDIM, HEADDIM)
            result_ref[rows, :] = low(in_ref[pl.ds(start, HEADDIM), :])
    channels = local_di + 2 * STATE
    rest_ref[local_di:channels, :] = low(in_ref[2 * DI : 2 * DI + 2 * STATE, :])
    rows = rest_ref.shape[0] - channels
    target = lax.broadcasted_iota(jnp.int32, (rows, HEADS), 0)
    source = lax.broadcasted_iota(jnp.int32, (rows, HEADS), 1)
    chosen = (source == groups * target + index) & (target < HEADS // groups)
    steps = low(in_ref[DI + CONVCH :, :])
    rest_ref[channels:, :] = low(dot_nn(jnp.where(chosen, 1.0, 0.0).astype(jnp.bfloat16), steps))
    mine = pl.ds(pl.multiple_of(index * HEADDIM, HEADDIM), HEADDIM)
    columns = gate_out_ref.shape[1]
    for tile in range(D // columns):
        first = local_di + tile * HEADDIM
        gate_out_ref[first : first + HEADDIM, :] = low(
            out_ref[mine, tile * columns : (tile + 1) * columns]
        )


def adamw_store(old_refs, new_refs, rows, columns, grad):
    results = adamw_step(*[ref[rows, columns] for ref in old_refs], grad, matrix_rate, matrix_decay)
    for ref, result in zip(new_refs, results):
        ref[rows, columns] = result


def update_heads(old_refs, new_refs, source, part):
    groups = source.shape[0]
    heads = old_refs[0].shape[0] // HEADDIM // groups
    for head in range(heads):
        start = pl.multiple_of((part * heads + head) * HEADDIM, HEADDIM)
        for group in range(groups):
            first = (head * groups + group) * HEADDIM
            grad = source[group, pl.ds(start, HEADDIM), :].astype(jnp.float32)
            adamw_store(old_refs, new_refs, slice(first, first + HEADDIM), slice(None), grad)


def update_gate_kernel(groups, places_ref, *refs):
    blocks, in_refs, out_refs = refs[:groups], refs[groups : groups + 3], refs[groups + 3 : groups + 6]
    in_new_refs, out_new_refs = refs[groups + 6 : groups + 9], refs[groups + 9 : groups + 12]
    (gate_out,) = refs[groups + 12 :]
    chunk = pl.program_id(0)

    @pl.when(chunk == 0)
    def _():
        for number in range(groups):
            gate_out[places_ref[number]] = blocks[number][...]

    update_heads(in_refs, in_new_refs, gate_out, chunk)
    local_di = gate_out.shape[1] // 2
    columns = gate_out.shape[2]
    for tile in range(D // columns):
        first = local_di + tile * HEADDIM
        grad = gate_out[chunk, first : first + HEADDIM, :].astype(jnp.float32)
        span = slice(tile * columns, (tile + 1) * columns)
        adamw_store(out_refs, out_new_refs, slice(None), span, grad)


def update_rest_kernel(groups, places_ref, *refs):
    blocks, in_refs = refs[:groups], refs[groups : groups + 3]
    in_new_refs, (rest,) = refs[groups + 6 : groups + 9], refs[groups + 9 :]
    chunk = pl.program_id(0)

    @pl.when(chunk == 0)
    def _():
        for number in range(groups):
            rest[places_ref[number]] = blocks[number][...]

    @pl.when(chunk < pl.num_programs(0) - 1)
    def _():
        update_heads(in_refs, in_new_refs, rest, chunk)

    @pl.when(chunk == pl.num_programs(0) - 1)
    def _():
        local_di = DI // groups
        channels = local_di + 2 * STATE
        both = rest[0, local_di:channels, :].astype(jnp.float32)
        rows = rest.shape[1] - channels
        steps = jnp.zeros((HEADS, rest.shape[2]), jnp.float32)
        target = lax.broadcasted_iota(jnp.int32, (HEADS, rows), 0)
        source = lax.broadcasted_iota(jnp.int32, (HEADS, rows), 1)
        for group in range(groups):
            if group > 0:
                both = both + rest[group, local_di:channels, :].astype(jnp.float32)
            chosen = jnp.where(target == groups * source + group, 1.0, 0.0).astype(jnp.bfloat16)
            steps = steps + dot_nn(chosen, rest[group, channels:, :])
        after_both = slice(2 * STATE, 2 * STATE + HEADS)
        adamw_store(in_refs, in_new_refs, slice(0, 2 * STATE), slice(None), both)
        adamw_store(in_refs, in_new_refs, after_both, slice(None), steps)


def kernel_params():
    return pltpu.CompilerParams(
        dimension_semantics=("arbitrary",), vmem_limit_bytes=56 * 1024 * 1024
    )


def cost(flops, moved, transcendentals):
    return pl.CostEstimate(flops=flops, bytes_accessed=moved, transcendentals=transcendentals)


def after(kernel, inputs, arrived):
    def run(*refs):
        kernel(*refs[:inputs], *refs[inputs + arrived :])

    return run


def corner(array):
    return pl.BlockSpec((min(16, array.shape[0]), 128), lambda *_: (0, 0))


def fixed(shape):
    return pl.BlockSpec(shape, lambda *_: (0,) * len(shape))


def rows_of(extent, first=0):
    return pl.BlockSpec((BLOCK, extent), lambda q, *_: (q + first, 0))


def struct(shape, dtype=jnp.float32):
    return jax.ShapeDtypeStruct(shape, dtype)


def call(
    kernel, places, inputs, in_specs, outputs, out_specs, scratch, grid, arrived, price, name, same=()
):
    return pl.pallas_call(
        after(kernel, 1 + len(inputs), len(arrived)),
        grid_spec=pltpu.PrefetchScalarGridSpec(
            num_scalar_prefetch=1,
            grid=(grid,),
            in_specs=list(in_specs) + [corner(array) for array in arrived],
            out_specs=out_specs,
            scratch_shapes=scratch,
        ),
        out_shape=outputs,
        input_output_aliases=dict(same),
        compiler_params=kernel_params(),
        cost_estimate=cost(*price),
        name=name,
    )(jnp.stack(places).astype(jnp.int32), *inputs, *arrived)


def run_prepare(index, in_t, out_weight):
    columns = in_t.shape[1]
    local_di = DI // 4
    shapes = [
        (local_di + 2 * STATE + 16, columns),
        (2 * local_di, columns),
    ]
    inputs = [in_t, out_weight]
    return call(
        prepare_kernel,
        [index],
        inputs,
        [fixed(array.shape) for array in inputs],
        [struct(shape, jnp.bfloat16) for shape in shapes],
        [fixed(shape) for shape in shapes],
        [],
        1,
        [],
        (100_000_000, 4_000_000, 0),
        "prepare",
    )


def run_forward(hidden, rest, gain_one, conv, heads_vectors, expand):
    places, blocks = rest
    length = hidden.shape[0]
    chunks = length // BLOCK
    lanes, local_di = expand.shape
    channels = local_di + 2 * STATE
    vectors = [gain_one, *conv, *heads_vectors, expand]
    return call(
        lambda *refs: forward_kernel(len(blocks), *refs),
        places,
        [*blocks, hidden, *vectors],
        [fixed(array.shape) for array in blocks]
        + [rows_of(D)]
        + [fixed(array.shape) for array in vectors],
        [
            struct((channels + lanes, D), jnp.bfloat16),
            struct((length, D), jnp.bfloat16),
            struct((length, channels)),
            struct((length, channels)),
            struct((length, lanes)),
            struct((length, local_di)),
            struct((length, local_di), jnp.bfloat16),
            struct((chunks, STATE, local_di)),
        ],
        [
            fixed((channels + lanes, D)),
            rows_of(D),
            rows_of(channels),
            rows_of(channels),
            rows_of(lanes),
            rows_of(local_di),
            rows_of(local_di),
            pl.BlockSpec((1, STATE, local_di), lambda q, *_: (q, 0, 0)),
        ],
        [
            pltpu.VMEM((8 + BLOCK, channels), jnp.float32),
            pltpu.VMEM((STATE, local_di), jnp.float32),
        ],
        chunks,
        [],
        (6_000_000_000, 30_000_000, 8_000_000),
        "forward",
    )


def run_gate(gate_out, cot, normed, scanned, gain_two):
    places, blocks = gate_out
    length, local_di = scanned.shape
    return call(
        lambda *refs: gate_kernel(len(blocks), *refs),
        places,
        [*blocks, cot, normed, scanned, gain_two],
        [fixed(array.shape) for array in blocks]
        + [rows_of(D), rows_of(D), rows_of(local_di), fixed((1, local_di))],
        [
            struct((local_di, D), jnp.bfloat16),
            struct((local_di, D), jnp.bfloat16),
            struct((length, local_di)),
            struct((length, local_di)),
            struct((8, length)),
        ],
        [
            fixed((local_di, D)),
            fixed((local_di, D)),
            rows_of(local_di),
            rows_of(local_di),
            pl.BlockSpec((8, BLOCK), lambda q, *_: (0, q)),
        ],
        [],
        length // BLOCK,
        [],
        (2_500_000_000, 12_000_000, 1_000_000),
        "gate",
    )


def run_middle(gate_places, out_places, scanned, gating, d_gnorm, cot, normed, sums, out, gain):
    length, local_di = scanned.shape
    gate_shape = (local_di, D // len(gate_places))
    out_shape = (local_di, D) if len(out_places) == 1 else (local_di * D // 256, 128)
    shapes = [gate_shape] * len(gate_places) + [out_shape] * len(out_places)
    return call(
        lambda *refs: middle_kernel(len(gate_places), len(out_places), *refs),
        gate_places + out_places,
        [scanned, gating, d_gnorm, cot, normed, *sums, out, gain],
        [
            rows_of(local_di),
            rows_of(local_di),
            rows_of(local_di),
            rows_of(D),
            rows_of(D),
        ]
        + [pl.BlockSpec((8, BLOCK), lambda q, *_: (0, q))] * 4
        + [fixed((local_di, D)), fixed((1, local_di))],
        [
            struct((length, D), jnp.bfloat16),
            struct((length, local_di), jnp.bfloat16),
            struct((length, local_di), jnp.bfloat16),
            struct((1, local_di)),
        ]
        + [struct(shape, jnp.bfloat16) for shape in shapes],
        [
            rows_of(D),
            rows_of(local_di),
            rows_of(local_di),
            fixed((1, local_di)),
        ]
        + [fixed(shape) for shape in shapes],
        [pltpu.VMEM((local_di, D), jnp.float32), pltpu.VMEM((local_di, D), jnp.float32)],
        length // BLOCK,
        [],
        (4_000_000_000, 15_000_000, 500_000),
        "middle",
    )


def run_backward(
    places, normed, conv_in, conv_pre, dt_raw, y, states, d_scanned, kernel, heads_vectors, expand
):
    length, local_di = y.shape
    chunks = length // BLOCK
    channels = conv_in.shape[1]
    lanes = expand.shape[0]
    grad = (channels + 16, D) if len(places) == 1 else ((channels + 16) * D // 256, 128)

    def back(extent):
        return pl.BlockSpec((BLOCK, extent), lambda q, *_: (chunks - 1 - q, 0))

    return call(
        lambda *refs: backward_kernel(len(places), *refs),
        places,
        [normed, conv_in, conv_pre, dt_raw, y, states, d_scanned, kernel, *heads_vectors, expand],
        [
            back(D),
            back(channels),
            back(channels),
            back(lanes),
            back(local_di),
            pl.BlockSpec((1, STATE, local_di), lambda q, *_: (chunks - 1 - q, 0, 0)),
            back(local_di),
            fixed((WIDTH, channels)),
            fixed((1, lanes)),
            fixed((1, lanes)),
            fixed((1, local_di)),
            fixed((lanes, local_di)),
        ],
        [
            struct((length, channels + lanes), jnp.bfloat16),
            struct((WIDTH, channels)),
            struct((1, channels)),
            struct((1, local_di)),
            struct((2, lanes)),
        ]
        + [struct(grad, jnp.bfloat16)] * len(places),
        [
            back(channels + lanes),
            fixed((WIDTH, channels)),
            fixed((1, channels)),
            fixed((1, local_di)),
            fixed((2, lanes)),
        ]
        + [fixed(grad)] * len(places),
        [
            pltpu.VMEM((BLOCK + 8, channels), jnp.float32),
            pltpu.VMEM((STATE, local_di), jnp.float32),
            pltpu.VMEM((STATE, local_di), jnp.float32),
            pltpu.VMEM((channels + lanes, D), jnp.float32),
        ],
        chunks,
        [],
        (14_000_000_000, 40_000_000, 10_000_000),
        "backward",
    )


def run_pair(y, out_places, gate, out, through):
    columns = gate[0].shape[1] // 2
    shapes = [
        (gate[0].shape[0], columns),
        (gate[0].shape[0], columns),
    ] + [(out[0].shape[0] // len(out_places), out[0].shape[1])] * len(out_places)
    inputs = [*gate, *out]
    untouched = pl.BlockSpec(memory_space=pl.ANY)
    return call(
        pair_kernel,
        [y] + out_places,
        [*inputs, through],
        [fixed(array.shape) for array in inputs] + [untouched],
        [struct(shape, jnp.bfloat16) for shape in shapes] + [struct(through.shape, through.dtype)],
        [fixed(shape) for shape in shapes] + [untouched],
        [],
        1,
        [],
        (3_000_000, 7_000_000, 0),
        "pair",
        [(1 + len(inputs), len(shapes))],
    )


def run_normed(hidden, d_gating, d_rest, gate_weight, rest_weight, arrived):
    length, local_di = d_gating.shape
    rest = d_rest.shape[1]
    return call(
        normed_kernel,
        [jnp.int32(0)],
        [hidden, d_gating, d_rest, gate_weight, rest_weight],
        [
            rows_of(D),
            rows_of(local_di),
            rows_of(rest),
            fixed((local_di, D)),
            fixed((rest, D)),
        ],
        [
            struct((length, D), jnp.bfloat16),
            struct((1, D)),
        ],
        [rows_of(D), fixed((1, D))],
        [],
        length // BLOCK,
        arrived,
        (3_000_000_000, 9_000_000, 1000),
        "normed",
    )


def run_rest_pair(places, mine, arrived, there):
    rest = (mine.shape[0] // len(places), mine.shape[1])
    shapes = [struct(rest, jnp.bfloat16)] * len(places)
    inputs = [mine, arrived]
    return call(
        rest_pair_kernel,
        places,
        inputs,
        [fixed(array.shape) for array in inputs],
        shapes,
        [fixed(shape.shape) for shape in shapes],
        [],
        1,
        there,
        (2_000_000, 3_000_000, 0),
        "rest_pair",
    )


def run_join(gate, out, there):
    inputs = [*gate, *out]
    shape = (gate[0].shape[0] + out[0].shape[0], gate[0].shape[1])
    return call(
        join_kernel,
        [jnp.int32(0)],
        inputs,
        [fixed(array.shape) for array in inputs],
        struct(shape, jnp.bfloat16),
        fixed(shape),
        [],
        1,
        there,
        (500_000, 1_000_000, 0),
        "join",
    )


def run_final(rest, through, there):
    untouched = pl.BlockSpec(memory_space=pl.ANY)
    return call(
        final_kernel,
        [jnp.int32(0)],
        [*rest, through],
        [fixed(array.shape) for array in rest] + [untouched],
        [struct(rest[0].shape, jnp.bfloat16), struct(through.shape, through.dtype)],
        [fixed(rest[0].shape), untouched],
        [],
        1,
        there,
        (500_000, 1_000_000, 0),
        "final",
        [(1 + len(rest), 1)],
    )


def run_vec(terms):
    return call(
        vec_kernel,
        [jnp.int32(0)],
        terms,
        [fixed(array.shape) for array in terms],
        struct(terms[0].shape),
        fixed(terms[0].shape),
        [],
        1,
        [],
        (20_000, 100_000, 0),
        "vec",
    )


def run_update_gate(places, blocks, in_arrays, out_arrays, there):
    groups = len(places)
    rows_out = out_arrays[0].shape[0] // groups
    arrays = [*in_arrays, *out_arrays]
    in_spec = pl.BlockSpec((DI // groups, in_arrays[0].shape[1]), lambda q, *_: (q, 0))
    out_spec = pl.BlockSpec((rows_out, D), lambda q, *_: (q, 0))
    specs = [in_spec] * 3 + [out_spec] * 3
    return call(
        lambda *refs: update_gate_kernel(groups, *refs),
        places,
        [*blocks, *arrays],
        [fixed(array.shape) for array in blocks] + specs,
        [struct(array.shape) for array in arrays],
        specs,
        [pltpu.VMEM((groups,) + blocks[0].shape, jnp.bfloat16)],
        groups,
        there,
        (10_000_000, 13_000_000, 500_000),
        "update_gate",
    )


def run_update_rest(places, blocks, in_arrays, so_far):
    groups = len(places)
    spec = pl.BlockSpec((DI // groups, in_arrays[0].shape[1]), lambda q, *_: (q + groups, 0))
    return call(
        lambda *refs: update_rest_kernel(groups, *refs),
        places,
        [*blocks, *in_arrays, *so_far],
        [fixed(array.shape) for array in blocks]
        + [spec] * 3
        + [pl.BlockSpec(memory_space=pl.ANY)] * 3,
        [struct(array.shape) for array in in_arrays],
        [spec] * 3,
        [pltpu.VMEM((groups,) + blocks[0].shape, jnp.bfloat16)],
        groups + 1,
        [],
        (10_000_000, 8_000_000, 500_000),
        "update_rest",
        [(1 + groups + 3 + number, number) for number in range(3)],
    )


def adamw_step(weight, first, second, grad, rate, decay):
    first_new = beta_one * first + (1.0 - beta_one) * grad
    second_new = beta_two * second + (1.0 - beta_two) * grad * grad
    fix_one = 1.0 - beta_one**STEP
    fix_two = 1.0 - beta_two**STEP
    normalized = first_new / fix_one / (jnp.sqrt(second_new / fix_two) + adam_eps)
    return (first_new, second_new, weight - rate * (normalized + decay * weight))


def pick_heads(values, axis, width, index, groups):
    shape = values.shape
    split = shape[:axis] + (HEADS // groups, groups, width) + shape[axis + 1 :]
    taken = lax.dynamic_index_in_dim(values.reshape(split), index, axis + 1, keepdims=False)
    return taken.reshape(shape[:axis] + (HEADS // groups * width,) + shape[axis + 1 :])


def merge_heads(stacked, axis, width):
    groups = stacked.shape[0]
    shape = stacked.shape[1:]
    split = (groups,) + shape[:axis] + (HEADS // groups, width) + shape[axis + 1 :]
    moved = jnp.moveaxis(stacked.reshape(split), 0, axis + 1)
    return moved.reshape(shape[:axis] + (HEADS * width,) + shape[axis + 1 :])


def swap(values, axis, mask):
    route = [(i, i ^ mask) for i in range(lax.axis_size(axis))]
    return lax.ppermute(values, axis, route)


def seq_blocks(rows, far=None):
    index = lax.axis_index("seq")
    far = swap(rows, "seq", 2) if far is None else far
    blocks = [rows, swap(rows, "seq", 1), far, swap(far, "seq", 1)]
    return [index ^ mask for mask in range(4)], blocks


def ring_step(held):
    count = lax.axis_size("wshard")
    return lax.ppermute(held, "wshard", [(i, (i + 2) % count) for i in range(count)])


def ring_blocks(rows):
    count = lax.axis_size("wshard")
    index = lax.axis_index("wshard")
    places, blocks = [], []
    for step in range(count // 2):
        source = (index + count - 2 * step) % count
        places = places + [source, source ^ 1]
        blocks = blocks + [rows, swap(rows, "wshard", 1)]
        if step < count // 2 - 1:
            rows = ring_step(rows)
    return places, blocks


def ring_pairs(rows):
    count = lax.axis_size("wshard")
    index = lax.axis_index("wshard")
    places = [(index + count - 2 * step) % count for step in range(count // 2)]
    blocks = [rows]
    for _ in range(count // 2 - 1):
        blocks = blocks + [ring_step(blocks[-1])]
    swapped = [
        swap(jnp.concatenate(blocks[first : first + 2], 0), "wshard", 1)
        for first in range(0, count // 2, 2)
    ]
    return places + [place ^ 1 for place in places], blocks + swapped


def take_block(values, index, rows):
    return lax.dynamic_slice_in_dim(values, index * rows, rows, 0)


def gather_out(out_low, seq_index, groups):
    rows = out_low.shape[0]
    if rows % (groups * HEADDIM) == 0:
        mine = pick_rows(out_low, seq_index, groups)
        return lax.all_gather(mine, "wshard", axis=0, tiled=True)
    whole = lax.all_gather(out_low, "wshard", axis=0, tiled=True)
    return pick_heads(whole, 0, HEADDIM, seq_index, groups)


def pick_rows(values, seq_index, groups):
    rows = values.shape[0]
    split = values.reshape(rows // (groups * HEADDIM), groups, HEADDIM, values.shape[1])
    return lax.dynamic_index_in_dim(split, seq_index, 1, keepdims=False).reshape(
        rows // groups, values.shape[1]
    )


def sum_out_grad(grad, rows, seq_index, groups):
    grad = grad.astype(jnp.bfloat16)
    if rows % (groups * HEADDIM) == 0:
        mine = lax.psum_scatter(grad, "wshard", scatter_dimension=0, tiled=True)
        every = lax.all_gather(mine, "seq", axis=0, tiled=False)
        split = every.reshape(groups, rows // (groups * HEADDIM), HEADDIM, grad.shape[1])
        return jnp.moveaxis(split, 0, 1).reshape(rows, grad.shape[1]).astype(jnp.float32)
    blocks = grad.reshape(HEADS // groups, 1, HEADDIM, grad.shape[1])
    here = (jnp.arange(groups) == seq_index)[None, :, None, None]
    spread = jnp.where(here, blocks, jnp.zeros((), jnp.bfloat16)).reshape(DI, grad.shape[1])
    mine = lax.psum_scatter(spread, "wshard", scatter_dimension=0, tiled=True)
    return lax.psum(mine.astype(jnp.float32), "seq")


def shards(
    block_in,
    cotangent,
    in_weight,
    in_first,
    in_second,
    out_weight,
    out_first,
    out_second,
    vec_weight,
    vec_first,
    vec_second,
):
    rows_here = block_in.shape[1]
    groups = lax.axis_size("seq")
    seq_index = lax.axis_index("seq")
    local_heads = HEADS // groups
    local_di = DI // groups
    hidden_rows = block_in.reshape(rows_here, D)
    cot_rows = cotangent.reshape(rows_here, D)
    gain_one, gain_two, kernel, conv_bias, a_log, dt_bias, d_skip = split_vector(vec_weight)

    def heads_of(values, axis, width):
        return pick_heads(values, axis, width, seq_index, groups)

    lanes = 128
    channels = local_di + 2 * STATE
    shard_index = lax.axis_index("wshard")
    rings = lax.axis_size("wshard") == 8
    if rings:
        y, z = shard_index % 2, shard_index // 2
        rest_mine, gate_out_mine = run_prepare(seq_index, in_weight.T, out_weight)
        rest = ring_blocks(rest_mine)
        gate_out = ring_pairs(gate_out_mine)
        gate_places = [z ^ mask for mask in range(4)]
        out_places = [y, 1 - y]
    else:
        in_low = low(in_weight)
        steps_mine = heads_of(in_low[:, DI + CONVCH :], 1, 1)
        rest_mine = jnp.concatenate(
            [
                heads_of(in_low[:, DI : 2 * DI], 1, HEADDIM),
                in_low[:, 2 * DI : 2 * DI + 2 * STATE],
                jnp.pad(steps_mine, ((0, 0), (0, 16 - local_heads))),
            ],
            1,
        )
        gate_mine = heads_of(in_low[:, :DI], 1, HEADDIM)
        origin = [jnp.int32(0)]
        rest = (origin, [lax.all_gather(rest_mine, "wshard", axis=0, tiled=True).T])
        gate_mine = lax.all_gather(gate_mine, "wshard", axis=0, tiled=True).T
        gate_out = (origin, [gate_mine, gather_out(low(out_weight), seq_index, groups)])
        gate_places, out_places = origin, origin
    hidden_low = lax.all_gather(hidden_rows, "seq", axis=0, tiled=True)
    cot_low = lax.all_gather(cot_rows, "seq", axis=0, tiled=True)
    my_gain_two = heads_of(gain_two, 0, HEADDIM)[None, :]
    my_kernel = jnp.concatenate([heads_of(kernel[:, :DI], 1, HEADDIM), kernel[:, DI:]], 1)
    my_bias = jnp.concatenate([heads_of(conv_bias[:DI], 0, HEADDIM), conv_bias[DI:]], 0)

    def on_lanes(values):
        return jnp.pad(values, (0, lanes - local_heads))[None, :]

    heads_vectors = (
        on_lanes(heads_of(a_log, 0, 1)),
        on_lanes(heads_of(dt_bias, 0, 1)),
        jnp.repeat(heads_of(d_skip, 0, 1), HEADDIM)[None, :],
    )
    expand = (
        jnp.arange(lanes)[:, None] == jnp.arange(local_di)[None, :] // HEADDIM
    ).astype(jnp.float32)
    (
        rest_weight,
        normed_low,
        conv_in,
        conv_pre,
        dt_raw,
        y_part,
        scanned,
        states,
    ) = run_forward(
        hidden_low, rest, gain_one[None, :], (my_kernel, my_bias[None, :]), heads_vectors, expand
    )
    gate_weight, out_low, gating, d_gnorm, sums = run_gate(
        gate_out, cot_low, normed_low, scanned, my_gain_two
    )
    middle = run_middle(
        gate_places,
        out_places,
        scanned,
        gating,
        d_gnorm,
        cot_low,
        normed_low,
        [sums] + [swap(sums, "seq", mask) for mask in range(1, 4)],
        out_low,
        my_gain_two,
    )
    block_part, d_gating, d_scanned, d_gain_two = middle[:4]
    gate_grads = middle[4 : 4 + len(gate_places)]
    out_grads = middle[4 + len(gate_places) :]
    block_rows = lax.psum_scatter(block_part, "seq", scatter_dimension=0, tiled=True)
    if rings:
        gate_pieces = [swap(gate_grads[mask], "wshard", 2 * mask) for mask in range(1, 4)]
        out_arrived = swap(out_grads[1], "wshard", 1)
    backward = run_backward(
        out_places,
        normed_low,
        conv_in,
        conv_pre,
        dt_raw,
        y_part,
        states,
        d_scanned,
        my_kernel,
        heads_vectors,
        expand,
    )
    d_rest, d_kernel, d_conv_bias, d_skip_wide, d_head = backward[:5]
    rest_grads = backward[5:]
    before_normed = []
    if rings:
        gate_keep, gate_send, *out_sums, rest_send = run_pair(
            y,
            gate_places,
            [gate_grads[0]] + gate_pieces,
            [out_grads[0], out_arrived],
            rest_grads[1],
        )
        rest_arrived = swap(rest_send, "wshard", 1)
        gate_arrived = swap(gate_send, "wshard", 1)
        out_pieces = [swap(out_sums[mask], "wshard", 2 * mask) for mask in range(1, 4)]
        before_normed = [gate_keep]
    d_normed_part, d_gain_one = run_normed(
        hidden_low, d_gating, d_rest, gate_weight, rest_weight, before_normed
    )
    d_normed = lax.psum_scatter(d_normed_part, "seq", scatter_dimension=0, tiled=True)
    shared = jnp.concatenate(
        [d_gain_one[0], d_kernel[:, local_di:].reshape(-1), d_conv_bias[0, local_di:]]
    )
    d_skip_part = jnp.sum(d_skip_wide.reshape(local_heads, HEADDIM), axis=1)
    apart = jnp.concatenate(
        [
            d_gain_two[0],
            d_kernel[:, :local_di].reshape(-1),
            d_conv_bias[0, :local_di],
            d_head[:, :local_heads].reshape(-1),
            d_skip_part,
        ]
    )
    vec_part = jnp.concatenate([shared, apart])[None]
    if rings:
        gate_out_part = run_join(
            [gate_keep, gate_arrived], [out_sums[0]] + out_pieces, [d_gain_one]
        )
        gate_out_far = swap(gate_out_part, "seq", 2)
        gate_out_near = swap(gate_out_part, "seq", 1)
        rest_sums = run_rest_pair(
            gate_places,
            rest_grads[0],
            rest_arrived,
            [gate_out_far, gate_out_near, block_rows],
        )
        rest_pieces = [swap(rest_sums[mask], "wshard", 2 * mask) for mask in range(1, 4)]
        spots = [seq_index ^ mask for mask in range(4)]
        gate_out_blocks = [
            gate_out_part, gate_out_near, gate_out_far, swap(gate_out_far, "seq", 1)
        ]
        in_arrays = (in_weight.T, in_first.T, in_second.T)
        updated = run_update_gate(
            spots, gate_out_blocks, in_arrays, (out_weight, out_first, out_second), []
        )
        out_first_new, out_second_new, out_weight_new = updated[3:]
        vec_part = vec_part + swap(vec_part, "wshard", 1)
        rest_part, vec_part = run_final(
            [rest_sums[0]] + rest_pieces, vec_part, [out_first_new]
        )
        vec_pieces = [swap(vec_part, "wshard", 2 * mask) for mask in range(1, 4)]
        vec_part = run_vec([vec_part] + vec_pieces)
        vec_places, vec_blocks = seq_blocks(vec_part)
        every = jnp.zeros((groups, vec_part.shape[1]), jnp.float32)
        for spot, block in zip(vec_places, vec_blocks):
            every = lax.dynamic_update_slice_in_dim(every, block, spot, 0)
    else:
        vec_part = lax.psum(vec_part, "wshard")
        every = lax.all_gather(vec_part, "seq", axis=0, tiled=True)
    block_out = hidden_rows.astype(jnp.float32) + block_rows.astype(jnp.float32)
    d_normed = d_normed.astype(jnp.float32)
    own_hidden = hidden_rows.astype(jnp.float32)
    own_scale = lax.rsqrt(jnp.mean(own_hidden * own_hidden, axis=-1, keepdims=True) + norm_eps)
    own_unit = own_hidden * own_scale
    d_own = d_normed * gain_one[None, :]
    d_hidden = own_scale * (
        d_own - own_unit * jnp.mean(d_own * own_unit, axis=-1, keepdims=True)
    )
    block_grad = cot_rows.astype(jnp.float32) + d_hidden
    shared, every = (
        jnp.sum(every[:, : shared.shape[0]], axis=0),
        every[:, shared.shape[0] :],
    )
    kernel_end = local_di * (1 + WIDTH)
    heads_at = kernel_end + local_di
    both_kernel = D + 2 * STATE * WIDTH
    vec_total = jnp.concatenate(
        [
            shared[:D],
            merge_heads(every[:, :local_di], 0, HEADDIM),
            jnp.concatenate(
                [
                    merge_heads(
                        every[:, local_di:kernel_end].reshape(groups, WIDTH, local_di), 1, HEADDIM
                    ),
                    shared[D:both_kernel].reshape(WIDTH, 2 * STATE),
                ],
                1,
            ).reshape(-1),
            merge_heads(every[:, kernel_end:heads_at], 0, HEADDIM),
            shared[both_kernel:],
            merge_heads(every[:, heads_at : heads_at + local_heads], 0, 1),
            merge_heads(every[:, heads_at + local_heads : heads_at + 2 * local_heads], 0, 1),
            merge_heads(every[:, heads_at + 2 * local_heads :], 0, 1),
        ]
    )
    vec_first_new, vec_second_new, vec_weight_new = adamw_step(
        vec_weight, vec_first, vec_second, vec_total, vector_rate, 0.0
    )
    if rings:
        spots, rest_blocks = seq_blocks(rest_part)
        updated = run_update_rest(spots, rest_blocks, in_arrays, updated[:3])
        in_first_new, in_second_new, in_weight_new = [array.T for array in updated]
    else:
        rest_part = lax.psum_scatter(rest_grads[0].T, "wshard", scatter_dimension=0, tiled=True)
        gate_part = lax.psum_scatter(gate_grads[0].T, "wshard", scatter_dimension=0, tiled=True)
        gate_every = lax.all_gather(gate_part, "seq", axis=0, tiled=False).astype(jnp.float32)
        rest_every = lax.all_gather(rest_part, "seq", axis=0, tiled=False).astype(jnp.float32)
        out_total = sum_out_grad(out_grads[0], out_weight.shape[0], seq_index, groups)
        in_total = jnp.concatenate(
            [
                merge_heads(gate_every, 1, HEADDIM),
                merge_heads(rest_every[:, :, :local_di], 1, HEADDIM),
                jnp.sum(rest_every[:, :, local_di:channels], axis=0),
                merge_heads(rest_every[:, :, channels : channels + local_heads], 1, 1),
            ],
            1,
        )
        in_first_new, in_second_new, in_weight_new = adamw_step(
            in_weight, in_first, in_second, in_total, matrix_rate, matrix_decay
        )
        out_first_new, out_second_new, out_weight_new = adamw_step(
            out_weight, out_first, out_second, out_total, matrix_rate, matrix_decay
        )
    return (
        block_out.reshape(1, rows_here, D),
        block_grad.reshape(1, rows_here, D),
        in_first_new,
        in_second_new,
        in_weight_new,
        out_first_new,
        out_second_new,
        out_weight_new,
        vec_first_new,
        vec_second_new,
        vec_weight_new,
    )


def solution(mesh):
    return jax.shard_map(
        shards,
        mesh=mesh,
        in_specs=(
            P("wshard", "seq", None),
            P("wshard", "seq", None),
            P("wshard", None),
            P("wshard", None),
            P("wshard", None),
            P("wshard", None),
            P("wshard", None),
            P("wshard", None),
            P(),
            P(),
            P(),
        ),
        out_specs=(
            P("wshard", "seq", None),
            P("wshard", "seq", None),
            P("wshard", None),
            P("wshard", None),
            P("wshard", None),
            P("wshard", None),
            P("wshard", None),
            P("wshard", None),
            P(),
            P(),
            P(),
        ),
        check_vma=False,
    )
```

```python
import jax
import jax.numpy as jnp
from jax import lax
from jax.experimental import pallas as pl
from jax.experimental.pallas import tpu as pltpu
from jax.sharding import PartitionSpec as P

D = 1024
HEADS = 32
HEADDIM = 64
STATE = 128
WIDTH = 4
BLOCK = 256
STEP = 10
DI = 2048
CONVCH = 2304


precise = lax.Precision.HIGHEST
norm_eps = 1e-05
beta_one = 0.9
beta_two = 0.95
adam_eps = 1e-08
matrix_rate = 0.05
matrix_decay = 0.1
vector_rate = 0.5


def rms_scale(values):
    return values * lax.rsqrt(jnp.mean(values * values, axis=-1, keepdims=True) + norm_eps)


def split_vector(vector):
    extents = [D, DI, WIDTH * CONVCH, CONVCH, HEADS, HEADS, HEADS]
    pieces = []
    offset = 0
    for extent in extents:
        pieces.append(vector[offset : offset + extent])
        offset = offset + extent
    pieces[2] = pieces[2].reshape(WIDTH, CONVCH)
    return pieces


def dot_nt(left, right, precision=None):
    return lax.dot_general(
        left,
        right,
        (((1,), (1,)), ((), ())),
        precision=precision,
        preferred_element_type=jnp.float32,
    )


def dot_tn(left, right):
    return lax.dot_general(
        left, right, (((0,), (0,)), ((), ())), preferred_element_type=jnp.float32
    )


def dot_nn(left, right, precision=None):
    return jnp.dot(left, right, precision=precision, preferred_element_type=jnp.float32)


def sigmoid(values):
    return 1.0 / (1.0 + jnp.exp(-values))


def low(values):
    return values.astype(jnp.bfloat16)


def lower_mask():
    rows = lax.broadcasted_iota(jnp.int32, (BLOCK, BLOCK), 0)
    return rows >= lax.broadcasted_iota(jnp.int32, (BLOCK, BLOCK), 1)


def decay_sums(dt_raw, dt_bias, a_log, expand):
    shifted = dt_raw + dt_bias
    step = jnp.maximum(shifted, 0.0) + jnp.log1p(jnp.exp(-jnp.abs(shifted)))
    log_decay = -jnp.exp(a_log) * step
    ones = jnp.where(lower_mask(), 1.0, 0.0)
    running = dot_nn(ones, log_decay, precise)
    step_wide = dot_nn(step, expand, precise)
    running_wide = dot_nn(running, expand, precise)
    return shifted, step, log_decay, running, step_wide, running_wide


def place_rows(result_ref, place, block):
    rows = block.shape[0]
    result_ref[pl.ds(pl.multiple_of(place * rows, rows), rows), :] = block


def place_columns(result_ref, place, block):
    rows, columns = block.shape
    start = pl.multiple_of(place * columns, columns)
    result_ref[:rows, pl.ds(start, columns)] = block


def forward_kernel(rest_count, places_ref, *refs):
    rest_blocks = refs[:rest_count]
    (
        hidden_ref,
        gain_one_ref,
        conv_ref,
        bias_ref,
        a_log_ref,
        dt_bias_ref,
        skip_ref,
        expand_ref,
        rest_ref,
        unit_ref,
        normed_ref,
        conv_in_ref,
        conv_pre_ref,
        dt_ref,
        y_ref,
        scanned_ref,
        state_ref,
        ext,
        state,
    ) = refs[rest_count:]
    local_di = y_ref.shape[1]
    heads = local_di // HEADDIM
    channels = conv_in_ref.shape[1]

    @pl.when(pl.program_id(0) == 0)
    def _():
        ext[0:8, :] = jnp.zeros((8, ext.shape[1]), jnp.float32)
        state[...] = jnp.zeros_like(state)
        rest_ref[channels:, :] = jnp.zeros_like(rest_ref[channels:, :])
        for number, block in enumerate(rest_blocks):
            place_columns(rest_ref, places_ref[number], block[...])

    hidden = hidden_ref[...].astype(jnp.float32)
    unit = rms_scale(hidden)
    unit_ref[...] = low(unit)
    normed = low(unit * gain_one_ref[...])
    normed_ref[...] = normed
    conv_in = dot_nt(normed, rest_ref[:channels, :])
    conv_in_ref[...] = conv_in
    ext[8 : 8 + BLOCK, :] = conv_in
    conv_pre = bias_ref[...] + conv_ref[WIDTH - 1 : WIDTH, :] * conv_in
    for tap in range(WIDTH - 1):
        first = 8 - WIDTH + 1 + tap
        conv_pre = conv_pre + conv_ref[tap : tap + 1, :] * ext[first : first + BLOCK, :]
    conv_pre_ref[...] = conv_pre
    ext[8 - WIDTH + 1 : 8, :] = ext[8 + BLOCK - WIDTH + 1 : 8 + BLOCK, :]
    conv_low = low(conv_pre * sigmoid(conv_pre))
    inner = conv_low[:, :local_di]
    b_rows = conv_low[:, local_di : local_di + STATE]
    c_rows = conv_low[:, local_di + STATE :]
    dt_raw = low(dot_nt(normed, rest_ref[channels:, :])).astype(jnp.float32)
    dt_ref[...] = dt_raw

    _, _, _, running, step_wide, running_wide = decay_sums(
        dt_raw, dt_bias_ref[...], a_log_ref[...], expand_ref[...]
    )
    running_t = running.T
    b_t = low(b_rows.astype(jnp.float32).T)
    scores = dot_nn(c_rows, b_t)
    mask = lower_mask()
    inner_wide = inner.astype(jnp.float32)
    stepped = step_wide * inner_wide
    stepped_low = low(stepped)
    first_half = lax.broadcasted_iota(jnp.int32, (BLOCK, 2 * HEADDIM), 1) < HEADDIM
    zero = jnp.zeros((), jnp.bfloat16)
    state_ref[...] = state[...].reshape(state_ref.shape)
    held = state[...]
    carried = jnp.exp(running_wide) * dot_nn(c_rows, low(held))
    for pair in range(heads // 2):
        span = slice(pair * 2 * HEADDIM, (pair + 1) * 2 * HEADDIM)
        both = stepped_low[:, span]
        total = carried[:, span]
        for half in range(2):
            head = 2 * pair + half
            differ = running[:, head : head + 1] - running_t[head : head + 1, :]
            mixed = low(jnp.exp(jnp.where(mask, differ, -jnp.inf)) * scores)
            mine = jnp.where(first_half if half == 0 else ~first_half, both, zero)
            total = total + dot_nn(mixed, mine)
        y_ref[:, span] = total
    last = running_wide[BLOCK - 1 : BLOCK, :]
    to_end = jnp.exp(last - running_wide)
    state[...] = jnp.exp(last) * held + dot_nn(b_t, low(to_end * stepped))
    scanned_ref[...] = low(y_ref[...] + skip_ref[...] * inner_wide)


def gate_kernel(count, places_ref, *refs):
    blocks = refs[:count]
    (
        cot_ref,
        normed_ref,
        scanned_ref,
        gain_two_ref,
        gate_ref,
        out_ref,
        gating_ref,
        d_gnorm_ref,
        sums_ref,
    ) = refs[count:]
    local_di = gating_ref.shape[1]

    @pl.when(pl.program_id(0) == 0)
    def _():
        if count == 2:
            gate_ref[...] = blocks[0][...]
            out_ref[...] = blocks[1][...]
            return
        number = 0
        for block in blocks:
            columns = block.shape[1]
            for base in range(0, block.shape[0], 2 * local_di):
                spot = places_ref[number]
                number = number + 1
                place_columns(gate_ref, spot, block[base : base + local_di, :])
                for tile in range(D // columns):
                    first = base + local_di + tile * HEADDIM
                    span = slice(tile * columns, (tile + 1) * columns)
                    place_rows(out_ref.at[:, span], spot, block[first : first + HEADDIM, :])

    gating = dot_nt(normed_ref[...], gate_ref[...])
    gating_ref[...] = gating
    d_gnorm = dot_nt(cot_ref[...], out_ref[...])
    d_gnorm_ref[...] = d_gnorm
    gated = scanned_ref[...].astype(jnp.float32) * (gating * sigmoid(gating))
    ones = jnp.ones((8, local_di), jnp.float32)
    squares = dot_nt(ones, gated * gated, precise)
    products = dot_nt(ones, d_gnorm * gain_two_ref[...] * gated, precise)
    sums_ref[...] = jnp.where(
        lax.broadcasted_iota(jnp.int32, squares.shape, 0) == 0, squares, products
    )


def middle_kernel(count, places_ref, *refs):
    (
        scanned_ref,
        gating_ref,
        d_gnorm_ref,
        cot_ref,
        unit_ref,
        sums_one_ref,
        sums_two_ref,
        sums_three_ref,
        sums_four_ref,
        out_ref,
        gain_two_ref,
        gain_one_ref,
        gate_weight_ref,
        block_ref,
        d_gating_ref,
        d_scanned_ref,
        d_gain_two_ref,
        d_gain_one_ref,
    ) = refs[:18]
    grad_refs = refs[18 : 18 + count]
    out_sum, gate_sum = refs[18 + count :]
    chunk = pl.program_id(0)

    @pl.when(chunk == 0)
    def _():
        out_sum[...] = jnp.zeros_like(out_sum)
        gate_sum[...] = jnp.zeros_like(gate_sum)
        d_gain_two_ref[...] = jnp.zeros_like(d_gain_two_ref)

    sums = (sums_one_ref[...] + sums_two_ref[...]) + (sums_three_ref[...] + sums_four_ref[...])
    sums = (sums / DI).T
    scale = lax.rsqrt(sums[:, 0:1] + norm_eps)
    slope = scale * scale * sums[:, 1:2]
    gating = gating_ref[...]
    open_part = sigmoid(gating)
    gate = gating * open_part
    scanned = scanned_ref[...].astype(jnp.float32)
    unit = scanned * gate * scale
    d_gnorm = d_gnorm_ref[...]
    gain_two = gain_two_ref[...]
    gnorm = low(unit * gain_two)
    block_ref[...] = low(dot_nn(gnorm, out_ref[...]))
    out_sum[...] += dot_tn(gnorm, cot_ref[...])
    d_gain_two_ref[...] += jnp.sum(d_gnorm * unit, axis=0, keepdims=True)
    d_gated = scale * (d_gnorm * gain_two) - unit * slope
    d_gating = low(d_gated * scanned * (open_part * (1.0 + gating * (1.0 - open_part))))
    d_gating_ref[...] = d_gating
    d_scanned_ref[...] = low(d_gated * gate)
    gate_sum[...] += dot_tn(d_gating, unit_ref[...])

    @pl.when(chunk == pl.num_programs(0) - 1)
    def _():
        weights = gate_weight_ref[...].astype(jnp.float32)
        d_gain_one_ref[...] = jnp.sum(gate_sum[...] * weights, axis=0, keepdims=True)
        gate_sum[...] = gate_sum[...] * gain_one_ref[...]
        local_di = gate_sum.shape[0]
        if grad_refs[0].shape == gate_sum.shape:
            grad_refs[0][...] = low(gate_sum[...])
            grad_refs[1][...] = low(out_sum[...])
            return
        for number, grad_ref in enumerate(grad_refs):
            columns = grad_ref.shape[1]
            for step in range(D // columns // count):
                place = places_ref[number] + step * count
                start = pl.multiple_of(place * columns, columns)
                base = step * 2 * local_di
                grad_ref[base : base + local_di, :] = low(gate_sum[:, pl.ds(start, columns)])
                rows = pl.ds(pl.multiple_of(place * HEADDIM, HEADDIM), HEADDIM)
                for tile in range(D // columns):
                    first = base + local_di + tile * HEADDIM
                    grad_ref[first : first + HEADDIM, :] = low(
                        out_sum[rows, tile * columns : (tile + 1) * columns]
                    )


def backward_kernel(
    grad_count,
    places_ref,
    unit_ref,
    conv_in_ref,
    conv_pre_ref,
    dt_ref,
    y_ref,
    state_ref,
    d_scanned_ref,
    conv_ref,
    a_log_ref,
    dt_bias_ref,
    skip_ref,
    expand_ref,
    gain_one_ref,
    rest_weight_ref,
    d_rest_ref,
    d_kernel_ref,
    d_conv_bias_ref,
    d_skip_ref,
    d_head_ref,
    d_gain_one_ref,
    *refs,
):
    grad_refs = refs[:grad_count]
    ext, d_state, later_state, rest_sum = refs[grad_count:]
    local_di = y_ref.shape[1]
    heads = local_di // HEADDIM
    chunk = pl.program_id(0)

    @pl.when(chunk == 0)
    def _():
        ext[BLOCK : BLOCK + 8, :] = jnp.zeros((8, ext.shape[1]), jnp.float32)
        d_state[...] = jnp.zeros_like(d_state)
        later_state[...] = jnp.zeros_like(later_state)
        rest_sum[...] = jnp.zeros_like(rest_sum)
        d_kernel_ref[...] = jnp.zeros_like(d_kernel_ref)
        d_conv_bias_ref[...] = jnp.zeros_like(d_conv_bias_ref)
        d_skip_ref[...] = jnp.zeros_like(d_skip_ref)
        d_head_ref[...] = jnp.zeros_like(d_head_ref)

    expand = expand_ref[...]
    conv_pre = conv_pre_ref[...]
    open_part = sigmoid(conv_pre)
    conv_low = low(conv_pre * open_part)
    inner = conv_low[:, :local_di].astype(jnp.float32)
    b_rows = conv_low[:, local_di : local_di + STATE]
    c_rows = conv_low[:, local_di + STATE :]
    a_log = a_log_ref[...]
    shifted, _, log_decay, running, step_wide, running_wide = decay_sums(
        dt_ref[...], dt_bias_ref[...], a_log, expand
    )
    running_t = running.T
    b_t = low(b_rows.astype(jnp.float32).T)
    c_t = low(c_rows.astype(jnp.float32).T)
    scores = dot_nn(c_rows, b_t)
    scores_t = dot_nn(b_rows, c_t)
    mask = lower_mask()
    rows = lax.broadcasted_iota(jnp.int32, (BLOCK, BLOCK), 0)
    mask_t = rows <= lax.broadcasted_iota(jnp.int32, (BLOCK, BLOCK), 1)
    d_y_low = d_scanned_ref[...]
    d_y = d_y_low.astype(jnp.float32)
    stepped_low = low(step_wide * inner)
    stepped = stepped_low.astype(jnp.float32)
    last = running_wide[BLOCK - 1 : BLOCK, :]
    to_end = jnp.exp(last - running_wide)
    d_later = d_state[...]
    d_later_low = low(d_later)
    held = state_ref[...].reshape(d_state.shape)
    decayed_dy = low(jnp.exp(running_wide) * d_y)
    d_c = dot_nt(decayed_dy, low(held))
    d_b = dot_nt(low(to_end * stepped), d_later_low)
    d_stepped = to_end * dot_nn(b_rows, d_later_low)
    cross = jnp.sum(later_state[...] * d_later, axis=0, keepdims=True)
    d_state[...] = jnp.exp(last) * d_later + dot_nn(c_t, decayed_dy)
    later_state[...] = held
    first_half = lax.broadcasted_iota(jnp.int32, (BLOCK, 2 * HEADDIM), 1) < HEADDIM
    zero = jnp.zeros((), jnp.bfloat16)
    d_scores = jnp.zeros((BLOCK, BLOCK), jnp.float32)
    pieces = []
    for pair in range(heads // 2):
        span = slice(pair * 2 * HEADDIM, (pair + 1) * 2 * HEADDIM)
        total = d_stepped[:, span]
        for half in range(2):
            head = 2 * pair + half
            mine = jnp.where(first_half if half == 0 else ~first_half, d_y_low[:, span], zero)
            column = running[:, head : head + 1]
            row = running_t[head : head + 1, :]
            decay = jnp.exp(jnp.where(mask, column - row, -jnp.inf))
            decay_t = jnp.exp(jnp.where(mask_t, row - column, -jnp.inf))
            d_scores = d_scores + dot_nt(mine, stepped_low[:, span]) * decay
            total = total + dot_nn(low(decay_t * scores_t), mine)
        pieces.append(total)
    d_stepped = jnp.concatenate(pieces, 1)
    d_scores_low = low(d_scores)
    d_c = d_c + dot_nn(d_scores_low, b_rows)
    d_b = d_b + dot_nn(low(d_scores.T), c_rows)
    d_inner = step_wide * d_stepped + skip_ref[...] * d_y
    d_running = dot_nt(d_y * y_ref[...] - d_stepped * stepped, expand, precise)
    upper = jnp.where(mask_t, 1.0, 0.0)
    d_log = dot_nn(upper, d_running, precise) + dot_nt(cross, expand, precise)
    d_step = dot_nt(d_stepped * inner, expand, precise) - jnp.exp(a_log) * d_log
    d_dt = d_step * sigmoid(shifted)
    d_head_ref[0:1, :] += jnp.sum(d_log * log_decay, axis=0, keepdims=True)
    d_head_ref[1:2, :] += jnp.sum(d_dt, axis=0, keepdims=True)
    d_skip_ref[...] += jnp.sum(d_y * inner, axis=0, keepdims=True)

    d_conv_out = jnp.concatenate([d_inner, d_b, d_c], 1)
    d_pre = d_conv_out * (open_part * (1.0 + conv_pre * (1.0 - open_part)))
    ext[0:BLOCK, :] = d_pre
    d_conv_bias_ref[...] += jnp.sum(d_pre, axis=0, keepdims=True)
    conv_in = conv_in_ref[...]
    d_conv_in = jnp.zeros_like(conv_in)
    for tap in range(WIDTH):
        moved = ext[WIDTH - 1 - tap : WIDTH - 1 - tap + BLOCK, :]
        d_conv_in = d_conv_in + conv_ref[tap : tap + 1, :] * moved
        d_kernel_ref[tap : tap + 1, :] += jnp.sum(moved * conv_in, axis=0, keepdims=True)
    ext[BLOCK : BLOCK + 8, :] = ext[0:8, :]
    d_rest = jnp.concatenate([low(d_conv_in), low(d_dt)], 1)
    d_rest_ref[...] = d_rest
    rest_sum[...] += dot_tn(d_rest, unit_ref[...])

    @pl.when(chunk == pl.num_programs(0) - 1)
    def _():
        weights = rest_weight_ref[...].astype(jnp.float32)
        d_gain_one_ref[...] = jnp.sum(rest_sum[...] * weights, axis=0, keepdims=True)
        rest_sum[...] = rest_sum[...] * gain_one_ref[...]
        for number, grad_ref in enumerate(grad_refs):
            columns = grad_ref.shape[1]
            blocks = rest_sum.shape[1] // columns // grad_count
            rows = grad_ref.shape[0] // blocks
            for step in range(blocks):
                place = places_ref[number] + step * grad_count
                start = pl.multiple_of(place * columns, columns)
                grad_ref[step * rows : (step + 1) * rows, :] = low(
                    rest_sum[:rows, pl.ds(start, columns)]
                )


def sum_of(*refs):
    total = refs[0][...].astype(jnp.float32)
    for ref in refs[1:]:
        total = total + ref[...].astype(jnp.float32)
    return total


def pair_kernel(count, places_ref, mine_ref, arrived_ref, *refs):
    for number, ref in enumerate(refs[count : len(refs) - count]):
        rows = ref.shape[0]
        here = pl.ds(pl.multiple_of(places_ref[number] * rows, rows), rows)
        ref[...] = low(sum_of(mine_ref.at[here, :], arrived_ref.at[here, :]))


def hold_kernel(places_ref, *refs):
    rows = refs[0].shape[0]
    for number, ref in enumerate(refs[:-1]):
        refs[-1][number * rows : (number + 1) * rows, :] = ref[...]


def final_kernel(places_ref, *refs):
    refs[-1][...] = low(sum_of(*refs[:-1]))


def normed_kernel(
    places_ref, d_gating_ref, d_rest_ref, gate_weight_ref, rest_weight_ref, mine_ref, send_ref
):
    chunk = pl.program_id(0)
    d_normed = dot_nn(d_gating_ref[...], gate_weight_ref[...])
    d_normed = low(d_normed + dot_nn(d_rest_ref[...], rest_weight_ref[...]))
    here = chunk % 2 == places_ref[0]
    rows = pl.ds(pl.multiple_of(chunk // 2 * BLOCK, BLOCK), BLOCK)

    @pl.when(here)
    def _():
        mine_ref[rows, :] = d_normed

    @pl.when(jnp.logical_not(here))
    def _():
        send_ref[rows, :] = d_normed


def prepare_kernel(places_ref, in_ref, out_ref, rest_ref, gate_out_ref):
    index = places_ref[0]
    local_di = gate_out_ref.shape[0] // 2
    groups = DI // local_di
    for head in range(HEADS // groups):
        rows = slice(head * HEADDIM, (head + 1) * HEADDIM)
        for base, result_ref in ((0, gate_out_ref), (DI, rest_ref)):
            start = pl.multiple_of(base + (groups * head + index) * HEADDIM, HEADDIM)
            result_ref[rows, :] = low(in_ref[pl.ds(start, HEADDIM), :])
    channels = local_di + 2 * STATE
    rest_ref[local_di:channels, :] = low(in_ref[2 * DI : 2 * DI + 2 * STATE, :])
    rows = rest_ref.shape[0] - channels
    target = lax.broadcasted_iota(jnp.int32, (rows, HEADS), 0)
    source = lax.broadcasted_iota(jnp.int32, (rows, HEADS), 1)
    chosen = (source == groups * target + index) & (target < HEADS // groups)
    steps = low(in_ref[DI + CONVCH :, :])
    rest_ref[channels:, :] = low(dot_nn(jnp.where(chosen, 1.0, 0.0).astype(jnp.bfloat16), steps))
    mine = pl.ds(pl.multiple_of(index * HEADDIM, HEADDIM), HEADDIM)
    columns = gate_out_ref.shape[1]
    for tile in range(D // columns):
        first = local_di + tile * HEADDIM
        gate_out_ref[first : first + HEADDIM, :] = low(
            out_ref[mine, tile * columns : (tile + 1) * columns]
        )


def adamw_store(old_refs, new_refs, rows, columns, grad):
    results = adamw_step(*[ref[rows, columns] for ref in old_refs], grad, matrix_rate, matrix_decay)
    for ref, result in zip(new_refs, results):
        ref[rows, columns] = result


def update_heads(old_refs, new_refs, source, part):
    groups = source.shape[0]
    heads = old_refs[0].shape[0] // HEADDIM // groups
    for head in range(heads):
        start = pl.multiple_of((part * heads + head) * HEADDIM, HEADDIM)
        for group in range(groups):
            first = (head * groups + group) * HEADDIM
            grad = source[group, pl.ds(start, HEADDIM), :].astype(jnp.float32)
            adamw_store(old_refs, new_refs, slice(first, first + HEADDIM), slice(None), grad)


def update_gate_kernel(groups, places_ref, *refs):
    blocks, in_refs, out_refs = refs[:groups], refs[groups : groups + 3], refs[groups + 3 : groups + 6]
    in_new_refs, out_new_refs = refs[groups + 6 : groups + 9], refs[groups + 9 : groups + 12]
    (gate_out,) = refs[groups + 12 :]
    chunk = pl.program_id(0)

    @pl.when(chunk == 0)
    def _():
        for number in range(groups):
            gate_out[places_ref[number]] = blocks[number][...]

    update_heads(in_refs, in_new_refs, gate_out, chunk)
    local_di = gate_out.shape[1] // 2
    columns = gate_out.shape[2]
    for tile in range(D // columns):
        first = local_di + tile * HEADDIM
        grad = gate_out[chunk, first : first + HEADDIM, :].astype(jnp.float32)
        span = slice(tile * columns, (tile + 1) * columns)
        adamw_store(out_refs, out_new_refs, slice(None), span, grad)


def update_rest_kernel(groups, places_ref, *refs):
    blocks, in_refs = refs[:groups], refs[groups : groups + 3]
    in_new_refs, (rest,) = refs[groups + 6 : groups + 9], refs[groups + 9 :]
    chunk = pl.program_id(0)

    @pl.when(chunk == 0)
    def _():
        for number in range(groups):
            rest[places_ref[number]] = blocks[number][...]

    @pl.when(chunk < pl.num_programs(0) - 1)
    def _():
        update_heads(in_refs, in_new_refs, rest, chunk)

    @pl.when(chunk == pl.num_programs(0) - 1)
    def _():
        local_di = DI // groups
        channels = local_di + 2 * STATE
        both = rest[0, local_di:channels, :].astype(jnp.float32)
        rows = rest.shape[1] - channels
        steps = jnp.zeros((HEADS, rest.shape[2]), jnp.float32)
        target = lax.broadcasted_iota(jnp.int32, (HEADS, rows), 0)
        source = lax.broadcasted_iota(jnp.int32, (HEADS, rows), 1)
        for group in range(groups):
            if group > 0:
                both = both + rest[group, local_di:channels, :].astype(jnp.float32)
            chosen = jnp.where(target == groups * source + group, 1.0, 0.0).astype(jnp.bfloat16)
            steps = steps + dot_nn(chosen, rest[group, channels:, :])
        after_both = slice(2 * STATE, 2 * STATE + HEADS)
        adamw_store(in_refs, in_new_refs, slice(0, 2 * STATE), slice(None), both)
        adamw_store(in_refs, in_new_refs, after_both, slice(None), steps)


def kernel_params():
    return pltpu.CompilerParams(
        dimension_semantics=("arbitrary",), vmem_limit_bytes=56 * 1024 * 1024
    )


def cost(flops, moved, transcendentals):
    return pl.CostEstimate(flops=flops, bytes_accessed=moved, transcendentals=transcendentals)


def after(kernel, inputs, arrived):
    def run(*refs):
        kernel(*refs[:inputs], *refs[inputs + arrived :])

    return run


def corner(array):
    return pl.BlockSpec((min(16, array.shape[0]), 128), lambda *_: (0, 0))


def fixed(shape):
    return pl.BlockSpec(shape, lambda *_: (0,) * len(shape))


def rows_of(extent, first=0):
    return pl.BlockSpec((BLOCK, extent), lambda q, *_: (q + first, 0))


def struct(shape, dtype=jnp.float32):
    return jax.ShapeDtypeStruct(shape, dtype)


def call(
    kernel, places, inputs, in_specs, outputs, out_specs, scratch, grid, arrived, price, name, same=()
):
    return pl.pallas_call(
        after(kernel, 1 + len(inputs), len(arrived)),
        grid_spec=pltpu.PrefetchScalarGridSpec(
            num_scalar_prefetch=1,
            grid=(grid,),
            in_specs=list(in_specs) + [corner(array) for array in arrived],
            out_specs=out_specs,
            scratch_shapes=scratch,
        ),
        out_shape=outputs,
        input_output_aliases=dict(same),
        compiler_params=kernel_params(),
        cost_estimate=cost(*price),
        name=name,
    )(jnp.stack(places).astype(jnp.int32), *inputs, *arrived)


def run_prepare(index, in_t, out_weight):
    columns = in_t.shape[1]
    local_di = DI // 4
    shapes = [
        (local_di + 2 * STATE + 16, columns),
        (2 * local_di, columns),
    ]
    inputs = [in_t, out_weight]
    return call(
        prepare_kernel,
        [index],
        inputs,
        [fixed(array.shape) for array in inputs],
        [struct(shape, jnp.bfloat16) for shape in shapes],
        [fixed(shape) for shape in shapes],
        [],
        1,
        [],
        (100_000_000, 4_000_000, 0),
        "prepare",
    )


def run_forward(hidden, rest, gain_one, conv, heads_vectors, expand):
    places, blocks = rest
    length = hidden.shape[0]
    chunks = length // BLOCK
    lanes, local_di = expand.shape
    channels = local_di + 2 * STATE
    vectors = [gain_one, *conv, *heads_vectors, expand]
    return call(
        lambda *refs: forward_kernel(len(blocks), *refs),
        places,
        [*blocks, hidden, *vectors],
        [fixed(array.shape) for array in blocks]
        + [rows_of(D)]
        + [fixed(array.shape) for array in vectors],
        [
            struct((channels + lanes, D), jnp.bfloat16),
            struct((length, D), jnp.bfloat16),
            struct((length, D), jnp.bfloat16),
            struct((length, channels)),
            struct((length, channels)),
            struct((length, lanes)),
            struct((length, local_di)),
            struct((length, local_di), jnp.bfloat16),
            struct((chunks, STATE, local_di)),
        ],
        [
            fixed((channels + lanes, D)),
            rows_of(D),
            rows_of(D),
            rows_of(channels),
            rows_of(channels),
            rows_of(lanes),
            rows_of(local_di),
            rows_of(local_di),
            pl.BlockSpec((1, STATE, local_di), lambda q, *_: (q, 0, 0)),
        ],
        [
            pltpu.VMEM((8 + BLOCK, channels), jnp.float32),
            pltpu.VMEM((STATE, local_di), jnp.float32),
        ],
        chunks,
        [],
        (6_000_000_000, 30_000_000, 8_000_000),
        "forward",
    )


def run_gate(gate_out, cot, normed, scanned, gain_two):
    places, blocks = gate_out
    length, local_di = scanned.shape
    return call(
        lambda *refs: gate_kernel(len(blocks), *refs),
        places,
        [*blocks, cot, normed, scanned, gain_two],
        [fixed(array.shape) for array in blocks]
        + [rows_of(D), rows_of(D), rows_of(local_di), fixed((1, local_di))],
        [
            struct((local_di, D), jnp.bfloat16),
            struct((local_di, D), jnp.bfloat16),
            struct((length, local_di)),
            struct((length, local_di)),
            struct((8, length)),
        ],
        [
            fixed((local_di, D)),
            fixed((local_di, D)),
            rows_of(local_di),
            rows_of(local_di),
            pl.BlockSpec((8, BLOCK), lambda q, *_: (0, q)),
        ],
        [],
        length // BLOCK,
        [],
        (2_500_000_000, 12_000_000, 1_000_000),
        "gate",
    )


def run_middle(
    places, scanned, gating, d_gnorm, cot, unit, sums, out, gain_two, gain_one, gate_weight
):
    length, local_di = scanned.shape
    shapes = [(local_di, D)] * 2
    if len(places) > 1:
        shapes = [(2 * local_di * D // 256, 128)] * 2
    return call(
        lambda *refs: middle_kernel(2, *refs),
        places,
        [scanned, gating, d_gnorm, cot, unit, *sums, out, gain_two, gain_one, gate_weight],
        [
            rows_of(local_di),
            rows_of(local_di),
            rows_of(local_di),
            rows_of(D),
            rows_of(D),
        ]
        + [pl.BlockSpec((8, BLOCK), lambda q, *_: (0, q))] * 4
        + [fixed((local_di, D)), fixed((1, local_di)), fixed((1, D)), fixed((local_di, D))],
        [
            struct((length, D), jnp.bfloat16),
            struct((length, local_di), jnp.bfloat16),
            struct((length, local_di), jnp.bfloat16),
            struct((1, local_di)),
            struct((1, D)),
        ]
        + [struct(shape, jnp.bfloat16) for shape in shapes],
        [
            rows_of(D),
            rows_of(local_di),
            rows_of(local_di),
            fixed((1, local_di)),
            fixed((1, D)),
        ]
        + [fixed(shape) for shape in shapes],
        [pltpu.VMEM((local_di, D), jnp.float32), pltpu.VMEM((local_di, D), jnp.float32)],
        length // BLOCK,
        [],
        (4_000_000_000, 15_000_000, 500_000),
        "middle",
    )


def run_backward(
    places,
    unit,
    conv_in,
    conv_pre,
    dt_raw,
    y,
    states,
    d_scanned,
    kernel,
    heads_vectors,
    expand,
    gain_one,
    rest_weight,
):
    length, local_di = y.shape
    chunks = length // BLOCK
    channels = conv_in.shape[1]
    lanes = expand.shape[0]
    grad = (channels + 16, D) if len(places) == 1 else ((channels + 16) * D // 256, 128)

    def back(extent):
        return pl.BlockSpec((BLOCK, extent), lambda q, *_: (chunks - 1 - q, 0))

    return call(
        lambda *refs: backward_kernel(len(places), *refs),
        places,
        [
            *[unit, conv_in, conv_pre, dt_raw, y, states, d_scanned, kernel],
            *[*heads_vectors, expand, gain_one, rest_weight],
        ],
        [
            back(D),
            back(channels),
            back(channels),
            back(lanes),
            back(local_di),
            pl.BlockSpec((1, STATE, local_di), lambda q, *_: (chunks - 1 - q, 0, 0)),
            back(local_di),
            fixed((WIDTH, channels)),
            fixed((1, lanes)),
            fixed((1, lanes)),
            fixed((1, local_di)),
            fixed((lanes, local_di)),
            fixed((1, D)),
            fixed((channels + lanes, D)),
        ],
        [
            struct((length, channels + lanes), jnp.bfloat16),
            struct((WIDTH, channels)),
            struct((1, channels)),
            struct((1, local_di)),
            struct((2, lanes)),
            struct((1, D)),
        ]
        + [struct(grad, jnp.bfloat16)] * len(places),
        [
            back(channels + lanes),
            fixed((WIDTH, channels)),
            fixed((1, channels)),
            fixed((1, local_di)),
            fixed((2, lanes)),
            fixed((1, D)),
        ]
        + [fixed(grad)] * len(places),
        [
            pltpu.VMEM((BLOCK + 8, channels), jnp.float32),
            pltpu.VMEM((STATE, local_di), jnp.float32),
            pltpu.VMEM((STATE, local_di), jnp.float32),
            pltpu.VMEM((channels + lanes, D), jnp.float32),
        ],
        chunks,
        [],
        (14_000_000_000, 40_000_000, 10_000_000),
        "backward",
    )


def run_normed(parity, d_gating, d_rest, gate_weight, rest_weight, arrived):
    length, local_di = d_gating.shape
    rest = d_rest.shape[1]
    return call(
        normed_kernel,
        [parity],
        [d_gating, d_rest, gate_weight, rest_weight],
        [rows_of(local_di), rows_of(rest), fixed((local_di, D)), fixed((rest, D))],
        [struct((length // 2, D), jnp.bfloat16)] * 2,
        [fixed((length // 2, D))] * 2,
        [],
        length // BLOCK,
        arrived,
        (3_000_000_000, 9_000_000, 1000),
        "normed",
    )


def run_pair(places, mine, arrived, through, there):
    block = (mine.shape[0] // len(places), mine.shape[1])
    untouched = [pl.BlockSpec(memory_space=pl.ANY)] * len(through)
    return call(
        lambda *refs: pair_kernel(len(through), *refs),
        places,
        [mine, arrived, *through],
        [fixed(mine.shape), fixed(arrived.shape)] + untouched,
        [struct(block, jnp.bfloat16)] * len(places)
        + [struct(array.shape, array.dtype) for array in through],
        [fixed(block)] * len(places) + untouched,
        [],
        1,
        there,
        (2_000_000, 3_000_000, 0),
        "pair",
        [(3 + number, len(places) + number) for number in range(len(through))],
    )


def run_hold(blocks, there):
    rows, columns = blocks[0].shape
    shape = (rows * len(blocks), columns)
    return call(
        hold_kernel,
        [jnp.int32(0)],
        blocks,
        [fixed(block.shape) for block in blocks],
        struct(shape, blocks[0].dtype),
        fixed(shape),
        [],
        1,
        there,
        (0, 2_000_000, 0),
        "hold",
    )


def run_final(terms, there):
    return call(
        final_kernel,
        [jnp.int32(0)],
        terms,
        [fixed(array.shape) for array in terms],
        struct(terms[0].shape, jnp.bfloat16),
        fixed(terms[0].shape),
        [],
        1,
        there,
        (500_000, 1_000_000, 0),
        "final",
    )


def run_update_gate(places, blocks, in_arrays, out_arrays, there):
    groups = len(places)
    rows_out = out_arrays[0].shape[0] // groups
    arrays = [*in_arrays, *out_arrays]
    in_spec = pl.BlockSpec((DI // groups, in_arrays[0].shape[1]), lambda q, *_: (q, 0))
    out_spec = pl.BlockSpec((rows_out, D), lambda q, *_: (q, 0))
    specs = [in_spec] * 3 + [out_spec] * 3
    return call(
        lambda *refs: update_gate_kernel(groups, *refs),
        places,
        [*blocks, *arrays],
        [fixed(array.shape) for array in blocks] + specs,
        [struct(array.shape) for array in arrays],
        specs,
        [pltpu.VMEM((groups,) + blocks[0].shape, jnp.bfloat16)],
        groups,
        there,
        (10_000_000, 13_000_000, 500_000),
        "update_gate",
    )


def run_update_rest(places, blocks, in_arrays, so_far):
    groups = len(places)
    spec = pl.BlockSpec((DI // groups, in_arrays[0].shape[1]), lambda q, *_: (q + groups, 0))
    return call(
        lambda *refs: update_rest_kernel(groups, *refs),
        places,
        [*blocks, *in_arrays, *so_far],
        [fixed(array.shape) for array in blocks]
        + [spec] * 3
        + [pl.BlockSpec(memory_space=pl.ANY)] * 3,
        [struct(array.shape) for array in in_arrays],
        [spec] * 3,
        [pltpu.VMEM((groups,) + blocks[0].shape, jnp.bfloat16)],
        groups + 1,
        [],
        (10_000_000, 8_000_000, 500_000),
        "update_rest",
        [(1 + groups + 3 + number, number) for number in range(3)],
    )


def adamw_step(weight, first, second, grad, rate, decay):
    first_new = beta_one * first + (1.0 - beta_one) * grad
    second_new = beta_two * second + (1.0 - beta_two) * grad * grad
    fix_one = 1.0 - beta_one**STEP
    fix_two = 1.0 - beta_two**STEP
    normalized = first_new / fix_one / (jnp.sqrt(second_new / fix_two) + adam_eps)
    return (first_new, second_new, weight - rate * (normalized + decay * weight))


def pick_heads(values, axis, width, index, groups):
    shape = values.shape
    split = shape[:axis] + (HEADS // groups, groups, width) + shape[axis + 1 :]
    taken = lax.dynamic_index_in_dim(values.reshape(split), index, axis + 1, keepdims=False)
    return taken.reshape(shape[:axis] + (HEADS // groups * width,) + shape[axis + 1 :])


def merge_heads(stacked, axis, width):
    groups = stacked.shape[0]
    shape = stacked.shape[1:]
    split = (groups,) + shape[:axis] + (HEADS // groups, width) + shape[axis + 1 :]
    moved = jnp.moveaxis(stacked.reshape(split), 0, axis + 1)
    return moved.reshape(shape[:axis] + (HEADS * width,) + shape[axis + 1 :])


def swap(values, axis, mask):
    route = [(i, i ^ mask) for i in range(lax.axis_size(axis))]
    return lax.ppermute(values, axis, route)


def seq_blocks(rows, far=None):
    index = lax.axis_index("seq")
    far = swap(rows, "seq", 2) if far is None else far
    blocks = [rows, swap(rows, "seq", 1), far, swap(far, "seq", 1)]
    return [index ^ mask for mask in range(4)], blocks


def ring_step(held):
    count = lax.axis_size("wshard")
    return lax.ppermute(held, "wshard", [(i, (i + 2) % count) for i in range(count)])


def ring_blocks(rows):
    count = lax.axis_size("wshard")
    index = lax.axis_index("wshard")
    places, blocks = [], []
    for step in range(count // 2):
        source = (index + count - 2 * step) % count
        places = places + [source, source ^ 1]
        blocks = blocks + [rows, swap(rows, "wshard", 1)]
        if step < count // 2 - 1:
            rows = ring_step(rows)
    return places, blocks


def ring_late(rows, arrived):
    count = lax.axis_size("wshard")
    index = lax.axis_index("wshard")
    places = [(index + count - 2 * step) % count for step in range(count // 2)]
    blocks = [rows]
    for _ in range(count // 2 - 1):
        blocks = blocks + [ring_step(blocks[-1])]
    swapped = swap(run_hold(blocks, arrived), "wshard", 1)
    return places + [place ^ 1 for place in places], blocks + [swapped]


def take_block(values, index, rows):
    return lax.dynamic_slice_in_dim(values, index * rows, rows, 0)


def gather_out(out_low, seq_index, groups):
    rows = out_low.shape[0]
    if rows % (groups * HEADDIM) == 0:
        mine = pick_rows(out_low, seq_index, groups)
        return lax.all_gather(mine, "wshard", axis=0, tiled=True)
    whole = lax.all_gather(out_low, "wshard", axis=0, tiled=True)
    return pick_heads(whole, 0, HEADDIM, seq_index, groups)


def pick_rows(values, seq_index, groups):
    rows = values.shape[0]
    split = values.reshape(rows // (groups * HEADDIM), groups, HEADDIM, values.shape[1])
    return lax.dynamic_index_in_dim(split, seq_index, 1, keepdims=False).reshape(
        rows // groups, values.shape[1]
    )


def sum_out_grad(grad, rows, seq_index, groups):
    grad = grad.astype(jnp.bfloat16)
    if rows % (groups * HEADDIM) == 0:
        mine = lax.psum_scatter(grad, "wshard", scatter_dimension=0, tiled=True)
        every = lax.all_gather(mine, "seq", axis=0, tiled=False)
        split = every.reshape(groups, rows // (groups * HEADDIM), HEADDIM, grad.shape[1])
        return jnp.moveaxis(split, 0, 1).reshape(rows, grad.shape[1]).astype(jnp.float32)
    blocks = grad.reshape(HEADS // groups, 1, HEADDIM, grad.shape[1])
    here = (jnp.arange(groups) == seq_index)[None, :, None, None]
    spread = jnp.where(here, blocks, jnp.zeros((), jnp.bfloat16)).reshape(DI, grad.shape[1])
    mine = lax.psum_scatter(spread, "wshard", scatter_dimension=0, tiled=True)
    return lax.psum(mine.astype(jnp.float32), "seq")


def shards(
    block_in,
    cotangent,
    in_weight,
    in_first,
    in_second,
    out_weight,
    out_first,
    out_second,
    vec_weight,
    vec_first,
    vec_second,
):
    rows_here = block_in.shape[1]
    groups = lax.axis_size("seq")
    seq_index = lax.axis_index("seq")
    local_heads = HEADS // groups
    local_di = DI // groups
    hidden_rows = block_in.reshape(rows_here, D)
    cot_rows = cotangent.reshape(rows_here, D)
    gain_one, gain_two, kernel, conv_bias, a_log, dt_bias, d_skip = split_vector(vec_weight)

    def heads_of(values, axis, width):
        return pick_heads(values, axis, width, seq_index, groups)

    lanes = 128
    channels = local_di + 2 * STATE
    shard_index = lax.axis_index("wshard")
    rings = lax.axis_size("wshard") == 8
    if rings:
        y, z = shard_index % 2, shard_index // 2
        rest_mine, gate_out_mine = run_prepare(seq_index, in_weight.T, out_weight)
        rest = ring_blocks(rest_mine)
        gate_out = ring_late(gate_out_mine, rest[1][1::2])
        gate_places = [z ^ mask for mask in range(4)]
        out_places = [y, 1 - y]
    else:
        in_low = low(in_weight)
        steps_mine = heads_of(in_low[:, DI + CONVCH :], 1, 1)
        rest_mine = jnp.concatenate(
            [
                heads_of(in_low[:, DI : 2 * DI], 1, HEADDIM),
                in_low[:, 2 * DI : 2 * DI + 2 * STATE],
                jnp.pad(steps_mine, ((0, 0), (0, 16 - local_heads))),
            ],
            1,
        )
        gate_mine = heads_of(in_low[:, :DI], 1, HEADDIM)
        origin = [jnp.int32(0)]
        rest = (origin, [lax.all_gather(rest_mine, "wshard", axis=0, tiled=True).T])
        gate_mine = lax.all_gather(gate_mine, "wshard", axis=0, tiled=True).T
        gate_out = (origin, [gate_mine, gather_out(low(out_weight), seq_index, groups)])
        out_places = origin
    hidden_low = lax.all_gather(hidden_rows, "seq", axis=0, tiled=True)
    cot_low = lax.all_gather(cot_rows, "seq", axis=0, tiled=True)
    my_gain_two = heads_of(gain_two, 0, HEADDIM)[None, :]
    my_kernel = jnp.concatenate([heads_of(kernel[:, :DI], 1, HEADDIM), kernel[:, DI:]], 1)
    my_bias = jnp.concatenate([heads_of(conv_bias[:DI], 0, HEADDIM), conv_bias[DI:]], 0)

    def on_lanes(values):
        return jnp.pad(values, (0, lanes - local_heads))[None, :]

    heads_vectors = (
        on_lanes(heads_of(a_log, 0, 1)),
        on_lanes(heads_of(dt_bias, 0, 1)),
        jnp.repeat(heads_of(d_skip, 0, 1), HEADDIM)[None, :],
    )
    expand = (
        jnp.arange(lanes)[:, None] == jnp.arange(local_di)[None, :] // HEADDIM
    ).astype(jnp.float32)
    (
        rest_weight,
        unit_low,
        normed_low,
        conv_in,
        conv_pre,
        dt_raw,
        y_part,
        scanned,
        states,
    ) = run_forward(
        hidden_low, rest, gain_one[None, :], (my_kernel, my_bias[None, :]), heads_vectors, expand
    )
    gate_weight, out_low, gating, d_gnorm, sums = run_gate(
        gate_out, cot_low, normed_low, scanned, my_gain_two
    )
    middle = run_middle(
        out_places,
        scanned,
        gating,
        d_gnorm,
        cot_low,
        unit_low,
        [sums] + [swap(sums, "seq", mask) for mask in range(1, 4)],
        out_low,
        my_gain_two,
        gain_one[None, :],
        gate_weight,
    )
    block_part, d_gating, d_scanned, d_gain_two, d_gain_gate, *gate_out_grads = middle
    block_rows = lax.psum_scatter(block_part, "seq", scatter_dimension=0, tiled=True)
    if rings:
        gate_out_arrived = swap(gate_out_grads[1], "wshard", 1)
    d_rest, d_kernel, d_conv_bias, d_skip_wide, d_head, d_gain_rest, *rest_grads = run_backward(
        out_places,
        unit_low,
        conv_in,
        conv_pre,
        dt_raw,
        y_part,
        states,
        d_scanned,
        my_kernel,
        heads_vectors,
        expand,
        gain_one[None, :],
        rest_weight,
    )
    d_gain_one = d_gain_gate[0] + d_gain_rest[0]
    shared = jnp.concatenate(
        [d_gain_one, d_kernel[:, local_di:].reshape(-1), d_conv_bias[0, local_di:]]
    )
    d_skip_part = jnp.sum(d_skip_wide.reshape(local_heads, HEADDIM), axis=1)
    apart = jnp.concatenate(
        [
            d_gain_two[0],
            d_kernel[:, :local_di].reshape(-1),
            d_conv_bias[0, :local_di],
            d_head[:, :local_heads].reshape(-1),
            d_skip_part,
        ]
    )
    vec_part = jnp.concatenate([shared, apart])[None]
    near, far = seq_index % 2, seq_index // 2
    if rings:
        *gate_out_sums, rest_send, vec_part = run_pair(
            gate_places,
            gate_out_grads[0],
            gate_out_arrived,
            [rest_grads[1], vec_part],
            [block_rows],
        )
        rest_arrived = swap(rest_send, "wshard", 1)
        gate_out_pieces = [
            swap(gate_out_sums[mask], "wshard", 2 * mask) for mask in range(1, 4)
        ]
        normed_mine, normed_send = run_normed(
            near, d_gating, d_rest, gate_weight, rest_weight, [gate_out_sums[0]]
        )
        vec_parts = lax.all_gather(vec_part, "wshard", axis=0, tiled=True)
        gate_out_part = run_final(
            [gate_out_sums[0]] + gate_out_pieces, [normed_mine, vec_parts]
        )
        vec_part = jnp.sum(vec_parts, axis=0, keepdims=True)
        every = lax.all_gather(vec_part, "seq", axis=0, tiled=True)
        gate_out_near = swap(gate_out_part, "seq", 1)
        rest_sums = run_pair(
            gate_places, rest_grads[0], rest_arrived, [], [gate_out_near]
        )
        rest_pieces = [swap(rest_sums[mask], "wshard", 2 * mask) for mask in range(1, 4)]
        gate_out_far = swap(gate_out_part, "seq", 2)
    else:
        vec_part = lax.psum(vec_part, "wshard")
        every = lax.all_gather(vec_part, "seq", axis=0, tiled=True)
        normed_mine, normed_send = run_normed(
            near, d_gating, d_rest, gate_weight, rest_weight, []
        )
    normed_arrived = swap(normed_send, "seq", 1)
    normed_sum = normed_mine.astype(jnp.float32) + normed_arrived.astype(jnp.float32)
    normed_far = swap(low(take_block(normed_sum, 1 - far, rows_here)), "seq", 2)
    if rings:
        spots = [seq_index ^ mask for mask in range(4)]
        gate_out_blocks = [gate_out_part, gate_out_near, gate_out_far]
        gate_out_blocks = gate_out_blocks + [swap(gate_out_far, "seq", 1)]
        in_arrays = (in_weight.T, in_first.T, in_second.T)
        updated = run_update_gate(
            spots,
            gate_out_blocks,
            in_arrays,
            (out_weight, out_first, out_second),
            [rest_sums[0]],
        )
        out_first_new, out_second_new, out_weight_new = updated[3:]
        rest_part = run_final([rest_sums[0]] + rest_pieces, [out_first_new, every])
    block_out = hidden_rows.astype(jnp.float32) + block_rows.astype(jnp.float32)
    d_normed = take_block(normed_sum, far, rows_here) + normed_far.astype(jnp.float32)
    own_hidden = hidden_rows.astype(jnp.float32)
    own_scale = lax.rsqrt(jnp.mean(own_hidden * own_hidden, axis=-1, keepdims=True) + norm_eps)
    own_unit = own_hidden * own_scale
    d_own = d_normed * gain_one[None, :]
    d_hidden = own_scale * (
        d_own - own_unit * jnp.mean(d_own * own_unit, axis=-1, keepdims=True)
    )
    block_grad = cot_rows.astype(jnp.float32) + d_hidden
    shared, every = (
        jnp.sum(every[:, : shared.shape[0]], axis=0),
        every[:, shared.shape[0] :],
    )
    kernel_end = local_di * (1 + WIDTH)
    heads_at = kernel_end + local_di
    both_kernel = D + 2 * STATE * WIDTH
    vec_total = jnp.concatenate(
        [
            shared[:D],
            merge_heads(every[:, :local_di], 0, HEADDIM),
            jnp.concatenate(
                [
                    merge_heads(
                        every[:, local_di:kernel_end].reshape(groups, WIDTH, local_di), 1, HEADDIM
                    ),
                    shared[D:both_kernel].reshape(WIDTH, 2 * STATE),
                ],
                1,
            ).reshape(-1),
            merge_heads(every[:, kernel_end:heads_at], 0, HEADDIM),
            shared[both_kernel:],
            merge_heads(every[:, heads_at : heads_at + local_heads], 0, 1),
            merge_heads(every[:, heads_at + local_heads : heads_at + 2 * local_heads], 0, 1),
            merge_heads(every[:, heads_at + 2 * local_heads :], 0, 1),
        ]
    )
    vec_first_new, vec_second_new, vec_weight_new = adamw_step(
        vec_weight, vec_first, vec_second, vec_total, vector_rate, 0.0
    )
    if rings:
        spots, rest_blocks = seq_blocks(rest_part)
        updated = run_update_rest(spots, rest_blocks, in_arrays, updated[:3])
        in_first_new, in_second_new, in_weight_new = [array.T for array in updated]
    else:
        rest_part = lax.psum_scatter(rest_grads[0].T, "wshard", scatter_dimension=0, tiled=True)
        gate_part = lax.psum_scatter(gate_out_grads[0].T, "wshard", scatter_dimension=0, tiled=True)
        gate_every = lax.all_gather(gate_part, "seq", axis=0, tiled=False).astype(jnp.float32)
        rest_every = lax.all_gather(rest_part, "seq", axis=0, tiled=False).astype(jnp.float32)
        out_total = sum_out_grad(gate_out_grads[1], out_weight.shape[0], seq_index, groups)
        in_total = jnp.concatenate(
            [
                merge_heads(gate_every, 1, HEADDIM),
                merge_heads(rest_every[:, :, :local_di], 1, HEADDIM),
                jnp.sum(rest_every[:, :, local_di:channels], axis=0),
                merge_heads(rest_every[:, :, channels : channels + local_heads], 1, 1),
            ],
            1,
        )
        in_first_new, in_second_new, in_weight_new = adamw_step(
            in_weight, in_first, in_second, in_total, matrix_rate, matrix_decay
        )
        out_first_new, out_second_new, out_weight_new = adamw_step(
            out_weight, out_first, out_second, out_total, matrix_rate, matrix_decay
        )
    return (
        block_out.reshape(1, rows_here, D),
        block_grad.reshape(1, rows_here, D),
        in_first_new,
        in_second_new,
        in_weight_new,
        out_first_new,
        out_second_new,
        out_weight_new,
        vec_first_new,
        vec_second_new,
        vec_weight_new,
    )


def solution(mesh):
    return jax.shard_map(
        shards,
        mesh=mesh,
        in_specs=(
            P("wshard", "seq", None),
            P("wshard", "seq", None),
            P("wshard", None),
            P("wshard", None),
            P("wshard", None),
            P("wshard", None),
            P("wshard", None),
            P("wshard", None),
            P(),
            P(),
            P(),
        ),
        out_specs=(
            P("wshard", "seq", None),
            P("wshard", "seq", None),
            P("wshard", None),
            P("wshard", None),
            P("wshard", None),
            P("wshard", None),
            P("wshard", None),
            P("wshard", None),
            P(),
            P(),
            P(),
        ),
        check_vma=False,
    )
```

```python
import jax
import jax.numpy as jnp
from jax import lax
from jax.experimental import pallas as pl
from jax.experimental.pallas import tpu as pltpu
from jax.sharding import PartitionSpec as P

D = 1024
HEADS = 32
HEADDIM = 64
STATE = 128
WIDTH = 4
BLOCK = 256
STEP = 10
DI = 2048
CONVCH = 2304
VEC_ROWS = 48


precise = lax.Precision.HIGHEST
norm_eps = 1e-05
beta_one = 0.9
beta_two = 0.95
adam_eps = 1e-08
matrix_rate = 0.05
matrix_decay = 0.1
vector_rate = 0.5


def rms_scale(values):
    return values * lax.rsqrt(jnp.mean(values * values, axis=-1, keepdims=True) + norm_eps)


def split_vector(vector):
    extents = [D, DI, WIDTH * CONVCH, CONVCH, HEADS, HEADS, HEADS]
    pieces = []
    offset = 0
    for extent in extents:
        pieces.append(vector[offset : offset + extent])
        offset = offset + extent
    pieces[2] = pieces[2].reshape(WIDTH, CONVCH)
    return pieces


def dot_nt(left, right, precision=None):
    return lax.dot_general(
        left,
        right,
        (((1,), (1,)), ((), ())),
        precision=precision,
        preferred_element_type=jnp.float32,
    )


def dot_tn(left, right):
    return lax.dot_general(
        left, right, (((0,), (0,)), ((), ())), preferred_element_type=jnp.float32
    )


def dot_nn(left, right, precision=None):
    return jnp.dot(left, right, precision=precision, preferred_element_type=jnp.float32)


def sigmoid(values):
    return 1.0 / (1.0 + jnp.exp(-values))


def low(values):
    return values.astype(jnp.bfloat16)


def lower_mask():
    rows = lax.broadcasted_iota(jnp.int32, (BLOCK, BLOCK), 0)
    return rows >= lax.broadcasted_iota(jnp.int32, (BLOCK, BLOCK), 1)


def decay_sums(dt_raw, dt_bias, a_log, expand):
    shifted = dt_raw + dt_bias
    step = jnp.maximum(shifted, 0.0) + jnp.log1p(jnp.exp(-jnp.abs(shifted)))
    log_decay = -jnp.exp(a_log) * step
    ones = jnp.where(lower_mask(), 1.0, 0.0)
    running = dot_nn(ones, log_decay, precise)
    step_wide = dot_nn(step, expand, precise)
    running_wide = dot_nn(running, expand, precise)
    return shifted, step, log_decay, running, step_wide, running_wide


def place_rows(result_ref, place, block):
    rows = block.shape[0]
    result_ref[pl.ds(pl.multiple_of(place * rows, rows), rows), :] = block


def place_columns(result_ref, place, block):
    rows, columns = block.shape
    start = pl.multiple_of(place * columns, columns)
    result_ref[:rows, pl.ds(start, columns)] = block


def forward_kernel(rest_count, places_ref, *refs):
    rest_blocks = refs[:rest_count]
    (
        hidden_ref,
        gain_one_ref,
        conv_ref,
        bias_ref,
        a_log_ref,
        dt_bias_ref,
        skip_ref,
        expand_ref,
        rest_ref,
        unit_ref,
        normed_ref,
        conv_in_ref,
        conv_pre_ref,
        dt_ref,
        y_ref,
        scanned_ref,
        state_ref,
        ext,
        state,
    ) = refs[rest_count:]
    local_di = y_ref.shape[1]
    heads = local_di // HEADDIM
    channels = conv_in_ref.shape[1]

    @pl.when(pl.program_id(0) == 0)
    def _():
        ext[0:8, :] = jnp.zeros((8, ext.shape[1]), jnp.float32)
        state[...] = jnp.zeros_like(state)
        rest_ref[channels:, :] = jnp.zeros_like(rest_ref[channels:, :])
        for number, block in enumerate(rest_blocks):
            place_columns(rest_ref, places_ref[number], block[...])

    hidden = hidden_ref[...].astype(jnp.float32)
    unit = rms_scale(hidden)
    unit_ref[...] = low(unit)
    normed = low(unit * gain_one_ref[...])
    normed_ref[...] = normed
    conv_in = dot_nt(normed, rest_ref[:channels, :])
    conv_in_ref[...] = conv_in
    ext[8 : 8 + BLOCK, :] = conv_in
    conv_pre = bias_ref[...] + conv_ref[WIDTH - 1 : WIDTH, :] * conv_in
    for tap in range(WIDTH - 1):
        first = 8 - WIDTH + 1 + tap
        conv_pre = conv_pre + conv_ref[tap : tap + 1, :] * ext[first : first + BLOCK, :]
    conv_pre_ref[...] = conv_pre
    ext[8 - WIDTH + 1 : 8, :] = ext[8 + BLOCK - WIDTH + 1 : 8 + BLOCK, :]
    conv_low = low(conv_pre * sigmoid(conv_pre))
    inner = conv_low[:, :local_di]
    b_rows = conv_low[:, local_di : local_di + STATE]
    c_rows = conv_low[:, local_di + STATE :]
    dt_raw = low(dot_nt(normed, rest_ref[channels:, :])).astype(jnp.float32)
    dt_ref[...] = dt_raw

    _, _, _, running, step_wide, running_wide = decay_sums(
        dt_raw, dt_bias_ref[...], a_log_ref[...], expand_ref[...]
    )
    running_t = running.T
    b_t = low(b_rows.astype(jnp.float32).T)
    scores = dot_nn(c_rows, b_t)
    mask = lower_mask()
    inner_wide = inner.astype(jnp.float32)
    stepped = step_wide * inner_wide
    stepped_low = low(stepped)
    first_half = lax.broadcasted_iota(jnp.int32, (BLOCK, 2 * HEADDIM), 1) < HEADDIM
    zero = jnp.zeros((), jnp.bfloat16)
    state_ref[...] = state[...].reshape(state_ref.shape)
    held = state[...]
    carried = jnp.exp(running_wide) * dot_nn(c_rows, low(held))
    for pair in range(heads // 2):
        span = slice(pair * 2 * HEADDIM, (pair + 1) * 2 * HEADDIM)
        both = stepped_low[:, span]
        total = carried[:, span]
        for half in range(2):
            head = 2 * pair + half
            differ = running[:, head : head + 1] - running_t[head : head + 1, :]
            mixed = low(jnp.exp(jnp.where(mask, differ, -jnp.inf)) * scores)
            mine = jnp.where(first_half if half == 0 else ~first_half, both, zero)
            total = total + dot_nn(mixed, mine)
        y_ref[:, span] = total
    last = running_wide[BLOCK - 1 : BLOCK, :]
    to_end = jnp.exp(last - running_wide)
    state[...] = jnp.exp(last) * held + dot_nn(b_t, low(to_end * stepped))
    scanned_ref[...] = low(y_ref[...] + skip_ref[...] * inner_wide)


def gate_kernel(count, places_ref, *refs):
    blocks = refs[:count]
    (
        cot_ref,
        normed_ref,
        scanned_ref,
        gain_two_ref,
        gate_ref,
        out_ref,
        gating_ref,
        d_gnorm_ref,
        sums_ref,
    ) = refs[count:]
    local_di = gating_ref.shape[1]

    @pl.when(pl.program_id(0) == 0)
    def _():
        if count == 2:
            gate_ref[...] = blocks[0][...]
            out_ref[...] = blocks[1][...]
            return
        number = 0
        for block in blocks:
            columns = block.shape[1]
            for base in range(0, block.shape[0], 2 * local_di):
                spot = places_ref[number]
                number = number + 1
                place_columns(gate_ref, spot, block[base : base + local_di, :])
                for tile in range(D // columns):
                    first = base + local_di + tile * HEADDIM
                    span = slice(tile * columns, (tile + 1) * columns)
                    place_rows(out_ref.at[:, span], spot, block[first : first + HEADDIM, :])

    gating = dot_nt(normed_ref[...], gate_ref[...])
    gating_ref[...] = gating
    d_gnorm = dot_nt(cot_ref[...], out_ref[...])
    d_gnorm_ref[...] = d_gnorm
    gated = scanned_ref[...].astype(jnp.float32) * (gating * sigmoid(gating))
    ones = jnp.ones((8, local_di), jnp.float32)
    squares = dot_nt(ones, gated * gated, precise)
    products = dot_nt(ones, d_gnorm * gain_two_ref[...] * gated, precise)
    sums_ref[...] = jnp.where(
        lax.broadcasted_iota(jnp.int32, squares.shape, 0) == 0, squares, products
    )


def middle_kernel(count, places_ref, *refs):
    (
        scanned_ref,
        gating_ref,
        d_gnorm_ref,
        cot_ref,
        unit_ref,
        sums_one_ref,
        sums_two_ref,
        sums_three_ref,
        sums_four_ref,
        out_ref,
        gain_two_ref,
        gain_one_ref,
        gate_weight_ref,
        block_ref,
        d_gating_ref,
        d_scanned_ref,
        d_gain_two_ref,
        d_gain_one_ref,
    ) = refs[:18]
    grad_refs = refs[18 : 18 + count]
    out_sum, gate_sum = refs[18 + count :]
    chunk = pl.program_id(0)

    @pl.when(chunk == 0)
    def _():
        out_sum[...] = jnp.zeros_like(out_sum)
        gate_sum[...] = jnp.zeros_like(gate_sum)
        d_gain_two_ref[...] = jnp.zeros_like(d_gain_two_ref)

    sums = (sums_one_ref[...] + sums_two_ref[...]) + (sums_three_ref[...] + sums_four_ref[...])
    sums = (sums / DI).T
    scale = lax.rsqrt(sums[:, 0:1] + norm_eps)
    slope = scale * scale * sums[:, 1:2]
    gating = gating_ref[...]
    open_part = sigmoid(gating)
    gate = gating * open_part
    scanned = scanned_ref[...].astype(jnp.float32)
    unit = scanned * gate * scale
    d_gnorm = d_gnorm_ref[...]
    gain_two = gain_two_ref[...]
    gnorm = low(unit * gain_two)
    block_ref[...] = low(dot_nn(gnorm, out_ref[...]))
    out_sum[...] += dot_tn(gnorm, cot_ref[...])
    d_gain_two_ref[...] += jnp.sum(d_gnorm * unit, axis=0, keepdims=True)
    d_gated = scale * (d_gnorm * gain_two) - unit * slope
    d_gating = low(d_gated * scanned * (open_part * (1.0 + gating * (1.0 - open_part))))
    d_gating_ref[...] = d_gating
    d_scanned_ref[...] = low(d_gated * gate)
    gate_sum[...] += dot_tn(d_gating, unit_ref[...])

    @pl.when(chunk == pl.num_programs(0) - 1)
    def _():
        weights = gate_weight_ref[...].astype(jnp.float32)
        d_gain_one_ref[...] = jnp.sum(gate_sum[...] * weights, axis=0, keepdims=True)
        gate_sum[...] = gate_sum[...] * gain_one_ref[...]
        local_di = gate_sum.shape[0]
        if grad_refs[0].shape == gate_sum.shape:
            grad_refs[0][...] = low(gate_sum[...])
            grad_refs[1][...] = low(out_sum[...])
            return
        for number, grad_ref in enumerate(grad_refs):
            columns = grad_ref.shape[1]
            for step in range(D // columns // count):
                place = places_ref[number] + step * count
                start = pl.multiple_of(place * columns, columns)
                base = step * 2 * local_di
                grad_ref[base : base + local_di, :] = low(gate_sum[:, pl.ds(start, columns)])
                rows = pl.ds(pl.multiple_of(place * HEADDIM, HEADDIM), HEADDIM)
                for tile in range(D // columns):
                    first = base + local_di + tile * HEADDIM
                    grad_ref[first : first + HEADDIM, :] = low(
                        out_sum[rows, tile * columns : (tile + 1) * columns]
                    )


def backward_kernel(
    grad_count,
    places_ref,
    unit_ref,
    conv_in_ref,
    conv_pre_ref,
    dt_ref,
    y_ref,
    state_ref,
    d_scanned_ref,
    conv_ref,
    a_log_ref,
    dt_bias_ref,
    skip_ref,
    expand_ref,
    gain_one_ref,
    rest_weight_ref,
    d_gain_gate_ref,
    d_gain_two_ref,
    d_rest_ref,
    vec_ref,
    *refs,
):
    grad_refs = refs[:grad_count]
    ext, d_state, later_state, rest_sum = refs[grad_count : grad_count + 4]
    d_kernel_ref, d_conv_bias_ref, d_skip_ref, d_head_ref = refs[grad_count + 4 :]
    local_di = y_ref.shape[1]
    heads = local_di // HEADDIM
    chunk = pl.program_id(0)

    @pl.when(chunk == 0)
    def _():
        ext[BLOCK : BLOCK + 8, :] = jnp.zeros((8, ext.shape[1]), jnp.float32)
        d_state[...] = jnp.zeros_like(d_state)
        later_state[...] = jnp.zeros_like(later_state)
        rest_sum[...] = jnp.zeros_like(rest_sum)
        d_kernel_ref[...] = jnp.zeros_like(d_kernel_ref)
        d_conv_bias_ref[...] = jnp.zeros_like(d_conv_bias_ref)
        d_skip_ref[...] = jnp.zeros_like(d_skip_ref)
        d_head_ref[...] = jnp.zeros_like(d_head_ref)

    expand = expand_ref[...]
    conv_pre = conv_pre_ref[...]
    open_part = sigmoid(conv_pre)
    conv_low = low(conv_pre * open_part)
    inner = conv_low[:, :local_di].astype(jnp.float32)
    b_rows = conv_low[:, local_di : local_di + STATE]
    c_rows = conv_low[:, local_di + STATE :]
    a_log = a_log_ref[...]
    shifted, _, log_decay, running, step_wide, running_wide = decay_sums(
        dt_ref[...], dt_bias_ref[...], a_log, expand
    )
    running_t = running.T
    b_t = low(b_rows.astype(jnp.float32).T)
    c_t = low(c_rows.astype(jnp.float32).T)
    scores = dot_nn(c_rows, b_t)
    scores_t = dot_nn(b_rows, c_t)
    mask = lower_mask()
    rows = lax.broadcasted_iota(jnp.int32, (BLOCK, BLOCK), 0)
    mask_t = rows <= lax.broadcasted_iota(jnp.int32, (BLOCK, BLOCK), 1)
    d_y_low = d_scanned_ref[...]
    d_y = d_y_low.astype(jnp.float32)
    stepped_low = low(step_wide * inner)
    stepped = stepped_low.astype(jnp.float32)
    last = running_wide[BLOCK - 1 : BLOCK, :]
    to_end = jnp.exp(last - running_wide)
    d_later = d_state[...]
    d_later_low = low(d_later)
    held = state_ref[...].reshape(d_state.shape)
    decayed_dy = low(jnp.exp(running_wide) * d_y)
    d_c = dot_nt(decayed_dy, low(held))
    d_b = dot_nt(low(to_end * stepped), d_later_low)
    d_stepped = to_end * dot_nn(b_rows, d_later_low)
    cross = jnp.sum(later_state[...] * d_later, axis=0, keepdims=True)
    d_state[...] = jnp.exp(last) * d_later + dot_nn(c_t, decayed_dy)
    later_state[...] = held
    first_half = lax.broadcasted_iota(jnp.int32, (BLOCK, 2 * HEADDIM), 1) < HEADDIM
    zero = jnp.zeros((), jnp.bfloat16)
    d_scores = jnp.zeros((BLOCK, BLOCK), jnp.float32)
    pieces = []
    for pair in range(heads // 2):
        span = slice(pair * 2 * HEADDIM, (pair + 1) * 2 * HEADDIM)
        total = d_stepped[:, span]
        for half in range(2):
            head = 2 * pair + half
            mine = jnp.where(first_half if half == 0 else ~first_half, d_y_low[:, span], zero)
            column = running[:, head : head + 1]
            row = running_t[head : head + 1, :]
            decay = jnp.exp(jnp.where(mask, column - row, -jnp.inf))
            decay_t = jnp.exp(jnp.where(mask_t, row - column, -jnp.inf))
            d_scores = d_scores + dot_nt(mine, stepped_low[:, span]) * decay
            total = total + dot_nn(low(decay_t * scores_t), mine)
        pieces.append(total)
    d_stepped = jnp.concatenate(pieces, 1)
    d_scores_low = low(d_scores)
    d_c = d_c + dot_nn(d_scores_low, b_rows)
    d_b = d_b + dot_nn(low(d_scores.T), c_rows)
    d_inner = step_wide * d_stepped + skip_ref[...] * d_y
    d_running = dot_nt(d_y * y_ref[...] - d_stepped * stepped, expand, precise)
    upper = jnp.where(mask_t, 1.0, 0.0)
    d_log = dot_nn(upper, d_running, precise) + dot_nt(cross, expand, precise)
    d_step = dot_nt(d_stepped * inner, expand, precise) - jnp.exp(a_log) * d_log
    d_dt = d_step * sigmoid(shifted)
    d_head_ref[0:1, :] += jnp.sum(d_log * log_decay, axis=0, keepdims=True)
    d_head_ref[1:2, :] += jnp.sum(d_dt, axis=0, keepdims=True)
    d_skip_ref[...] += jnp.sum(d_y * inner, axis=0, keepdims=True)

    d_conv_out = jnp.concatenate([d_inner, d_b, d_c], 1)
    d_pre = d_conv_out * (open_part * (1.0 + conv_pre * (1.0 - open_part)))
    ext[0:BLOCK, :] = d_pre
    d_conv_bias_ref[...] += jnp.sum(d_pre, axis=0, keepdims=True)
    conv_in = conv_in_ref[...]
    d_conv_in = jnp.zeros_like(conv_in)
    for tap in range(WIDTH):
        moved = ext[WIDTH - 1 - tap : WIDTH - 1 - tap + BLOCK, :]
        d_conv_in = d_conv_in + conv_ref[tap : tap + 1, :] * moved
        d_kernel_ref[tap : tap + 1, :] += jnp.sum(moved * conv_in, axis=0, keepdims=True)
    ext[BLOCK : BLOCK + 8, :] = ext[0:8, :]
    d_rest = jnp.concatenate([low(d_conv_in), low(d_dt)], 1)
    d_rest_ref[...] = d_rest
    rest_sum[...] += dot_tn(d_rest, unit_ref[...])

    @pl.when(chunk == pl.num_programs(0) - 1)
    def _():
        weights = rest_weight_ref[...].astype(jnp.float32)
        d_gain_one = jnp.sum(rest_sum[...] * weights, axis=0, keepdims=True)
        pieces = [d_gain_one + d_gain_gate_ref[...]]
        pieces = pieces + [d_kernel_ref[tap : tap + 1, :] for tap in range(WIDTH)]
        pieces = pieces + [d_conv_bias_ref[...], d_gain_two_ref[...], d_skip_ref[...]]
        pieces = pieces + [d_head_ref[0:1, :], d_head_ref[1:2, :]]
        row = 0
        for piece in pieces:
            for first in range(0, piece.shape[1], 128):
                vec_ref[row : row + 1, :] = piece[:, first : first + 128]
                row = row + 1
        rest_sum[...] = rest_sum[...] * gain_one_ref[...]
        for number, grad_ref in enumerate(grad_refs):
            columns = grad_ref.shape[1]
            blocks = rest_sum.shape[1] // columns // grad_count
            rows = grad_ref.shape[0] // blocks
            for step in range(blocks):
                place = places_ref[number] + step * grad_count
                start = pl.multiple_of(place * columns, columns)
                grad_ref[step * rows : (step + 1) * rows, :] = low(
                    rest_sum[:rows, pl.ds(start, columns)]
                )


def sum_of(*refs):
    total = refs[0][...].astype(jnp.float32)
    for ref in refs[1:]:
        total = total + ref[...].astype(jnp.float32)
    return total


def pair_kernel(count, extra, places_ref, mine_ref, arrived_ref, *refs):
    for ref in refs[extra + count : len(refs) - count]:
        if extra:
            ref[ref.shape[0] - VEC_ROWS :, :] = low(refs[0][...])
    for number, ref in enumerate(refs[extra + count : len(refs) - count]):
        rows = ref.shape[0] - extra * VEC_ROWS
        here = pl.ds(pl.multiple_of(places_ref[number] * rows, rows), rows)
        ref[:rows, :] = low(sum_of(mine_ref.at[here, :], arrived_ref.at[here, :]))


def hold_kernel(places_ref, *refs):
    rows = refs[0].shape[0]
    for number, ref in enumerate(refs[:-1]):
        refs[-1][number * rows : (number + 1) * rows, :] = ref[...]


def final_kernel(count, places_ref, one_ref, two_ref, three_ref, four_ref, *refs):
    refs[count][...] = low(sum_of(one_ref, two_ref) + sum_of(three_ref, four_ref))


def normed_kernel(
    places_ref, d_gating_ref, d_rest_ref, gate_weight_ref, rest_weight_ref, mine_ref, send_ref
):
    chunk = pl.program_id(0)
    d_normed = dot_nn(d_gating_ref[...], gate_weight_ref[...])
    d_normed = low(d_normed + dot_nn(d_rest_ref[...], rest_weight_ref[...]))
    here = chunk % 2 == places_ref[0]
    rows = pl.ds(pl.multiple_of(chunk // 2 * BLOCK, BLOCK), BLOCK)

    @pl.when(here)
    def _():
        mine_ref[rows, :] = d_normed

    @pl.when(jnp.logical_not(here))
    def _():
        send_ref[rows, :] = d_normed


def prepare_kernel(places_ref, in_ref, out_ref, rest_ref, gate_out_ref):
    index = places_ref[0]
    local_di = gate_out_ref.shape[0] // 2
    groups = DI // local_di
    for head in range(HEADS // groups):
        rows = slice(head * HEADDIM, (head + 1) * HEADDIM)
        for base, result_ref in ((0, gate_out_ref), (DI, rest_ref)):
            start = pl.multiple_of(base + (groups * head + index) * HEADDIM, HEADDIM)
            result_ref[rows, :] = low(in_ref[pl.ds(start, HEADDIM), :])
    channels = local_di + 2 * STATE
    rest_ref[local_di:channels, :] = low(in_ref[2 * DI : 2 * DI + 2 * STATE, :])
    rows = rest_ref.shape[0] - channels
    target = lax.broadcasted_iota(jnp.int32, (rows, HEADS), 0)
    source = lax.broadcasted_iota(jnp.int32, (rows, HEADS), 1)
    chosen = (source == groups * target + index) & (target < HEADS // groups)
    steps = low(in_ref[DI + CONVCH :, :])
    rest_ref[channels:, :] = low(dot_nn(jnp.where(chosen, 1.0, 0.0).astype(jnp.bfloat16), steps))
    mine = pl.ds(pl.multiple_of(index * HEADDIM, HEADDIM), HEADDIM)
    columns = gate_out_ref.shape[1]
    for tile in range(D // columns):
        first = local_di + tile * HEADDIM
        gate_out_ref[first : first + HEADDIM, :] = low(
            out_ref[mine, tile * columns : (tile + 1) * columns]
        )


def adamw_store(old_refs, new_refs, rows, columns, grad):
    results = adamw_step(*[ref[rows, columns] for ref in old_refs], grad, matrix_rate, matrix_decay)
    for ref, result in zip(new_refs, results):
        ref[rows, columns] = result


def update_heads(old_refs, new_refs, source, part):
    groups = source.shape[0]
    heads = old_refs[0].shape[0] // HEADDIM // groups
    for head in range(heads):
        start = pl.multiple_of((part * heads + head) * HEADDIM, HEADDIM)
        for group in range(groups):
            first = (head * groups + group) * HEADDIM
            grad = source[group, pl.ds(start, HEADDIM), :].astype(jnp.float32)
            adamw_store(old_refs, new_refs, slice(first, first + HEADDIM), slice(None), grad)


def update_gate_kernel(groups, places_ref, *refs):
    blocks, in_refs, out_refs = refs[:groups], refs[groups : groups + 3], refs[groups + 3 : groups + 6]
    in_new_refs, out_new_refs = refs[groups + 6 : groups + 9], refs[groups + 9 : groups + 12]
    every_ref, gate_out = refs[groups + 12 :]
    chunk = pl.program_id(0)

    @pl.when(chunk == 0)
    def _():
        for number in range(groups):
            gate_out[places_ref[number]] = blocks[number][...]

    local_di = (gate_out.shape[1] - VEC_ROWS) // 2
    every_ref[...] = gate_out[:, 2 * local_di :, :]
    update_heads(in_refs, in_new_refs, gate_out, chunk)
    columns = gate_out.shape[2]
    for tile in range(D // columns):
        first = local_di + tile * HEADDIM
        grad = gate_out[chunk, first : first + HEADDIM, :].astype(jnp.float32)
        span = slice(tile * columns, (tile + 1) * columns)
        adamw_store(out_refs, out_new_refs, slice(None), span, grad)


def update_rest_kernel(groups, places_ref, *refs):
    blocks, in_refs = refs[:groups], refs[groups : groups + 3]
    in_new_refs, (rest,) = refs[groups + 6 : groups + 9], refs[groups + 9 :]
    chunk = pl.program_id(0)

    @pl.when(chunk == 0)
    def _():
        for number in range(groups):
            rest[places_ref[number]] = blocks[number][...]

    @pl.when(chunk < pl.num_programs(0) - 1)
    def _():
        update_heads(in_refs, in_new_refs, rest, chunk)

    @pl.when(chunk == pl.num_programs(0) - 1)
    def _():
        local_di = DI // groups
        channels = local_di + 2 * STATE
        both = rest[0, local_di:channels, :].astype(jnp.float32)
        rows = rest.shape[1] - channels
        steps = jnp.zeros((HEADS, rest.shape[2]), jnp.float32)
        target = lax.broadcasted_iota(jnp.int32, (HEADS, rows), 0)
        source = lax.broadcasted_iota(jnp.int32, (HEADS, rows), 1)
        for group in range(groups):
            if group > 0:
                both = both + rest[group, local_di:channels, :].astype(jnp.float32)
            chosen = jnp.where(target == groups * source + group, 1.0, 0.0).astype(jnp.bfloat16)
            steps = steps + dot_nn(chosen, rest[group, channels:, :])
        after_both = slice(2 * STATE, 2 * STATE + HEADS)
        adamw_store(in_refs, in_new_refs, slice(0, 2 * STATE), slice(None), both)
        adamw_store(in_refs, in_new_refs, after_both, slice(None), steps)


def kernel_params():
    return pltpu.CompilerParams(
        dimension_semantics=("arbitrary",), vmem_limit_bytes=56 * 1024 * 1024
    )


def cost(flops, moved, transcendentals):
    return pl.CostEstimate(flops=flops, bytes_accessed=moved, transcendentals=transcendentals)


def after(kernel, inputs, arrived):
    def run(*refs):
        kernel(*refs[:inputs], *refs[inputs + arrived :])

    return run


def corner(array):
    return pl.BlockSpec((min(16, array.shape[0]), 128), lambda *_: (0, 0))


def fixed(shape):
    return pl.BlockSpec(shape, lambda *_: (0,) * len(shape))


def rows_of(extent, first=0):
    return pl.BlockSpec((BLOCK, extent), lambda q, *_: (q + first, 0))


def struct(shape, dtype=jnp.float32):
    return jax.ShapeDtypeStruct(shape, dtype)


def call(
    kernel, places, inputs, in_specs, outputs, out_specs, scratch, grid, arrived, price, name, same=()
):
    return pl.pallas_call(
        after(kernel, 1 + len(inputs), len(arrived)),
        grid_spec=pltpu.PrefetchScalarGridSpec(
            num_scalar_prefetch=1,
            grid=(grid,),
            in_specs=list(in_specs) + [corner(array) for array in arrived],
            out_specs=out_specs,
            scratch_shapes=scratch,
        ),
        out_shape=outputs,
        input_output_aliases=dict(same),
        compiler_params=kernel_params(),
        cost_estimate=cost(*price),
        name=name,
    )(jnp.stack(places).astype(jnp.int32), *inputs, *arrived)


def run_prepare(index, in_t, out_weight):
    columns = in_t.shape[1]
    local_di = DI // 4
    shapes = [
        (local_di + 2 * STATE + 16, columns),
        (2 * local_di, columns),
    ]
    inputs = [in_t, out_weight]
    return call(
        prepare_kernel,
        [index],
        inputs,
        [fixed(array.shape) for array in inputs],
        [struct(shape, jnp.bfloat16) for shape in shapes],
        [fixed(shape) for shape in shapes],
        [],
        1,
        [],
        (100_000_000, 4_000_000, 0),
        "prepare",
    )


def run_forward(hidden, rest, gain_one, conv, heads_vectors, expand):
    places, blocks = rest
    length = hidden.shape[0]
    chunks = length // BLOCK
    lanes, local_di = expand.shape
    channels = local_di + 2 * STATE
    vectors = [gain_one, *conv, *heads_vectors, expand]
    return call(
        lambda *refs: forward_kernel(len(blocks), *refs),
        places,
        [*blocks, hidden, *vectors],
        [fixed(array.shape) for array in blocks]
        + [rows_of(D)]
        + [fixed(array.shape) for array in vectors],
        [
            struct((channels + lanes, D), jnp.bfloat16),
            struct((length, D), jnp.bfloat16),
            struct((length, D), jnp.bfloat16),
            struct((length, channels)),
            struct((length, channels)),
            struct((length, lanes)),
            struct((length, local_di)),
            struct((length, local_di), jnp.bfloat16),
            struct((chunks, STATE, local_di)),
        ],
        [
            fixed((channels + lanes, D)),
            rows_of(D),
            rows_of(D),
            rows_of(channels),
            rows_of(channels),
            rows_of(lanes),
            rows_of(local_di),
            rows_of(local_di),
            pl.BlockSpec((1, STATE, local_di), lambda q, *_: (q, 0, 0)),
        ],
        [
            pltpu.VMEM((8 + BLOCK, channels), jnp.float32),
            pltpu.VMEM((STATE, local_di), jnp.float32),
        ],
        chunks,
        [],
        (6_000_000_000, 30_000_000, 8_000_000),
        "forward",
    )


def run_gate(gate_out, cot, normed, scanned, gain_two):
    places, blocks = gate_out
    length, local_di = scanned.shape
    return call(
        lambda *refs: gate_kernel(len(blocks), *refs),
        places,
        [*blocks, cot, normed, scanned, gain_two],
        [fixed(array.shape) for array in blocks]
        + [rows_of(D), rows_of(D), rows_of(local_di), fixed((1, local_di))],
        [
            struct((local_di, D), jnp.bfloat16),
            struct((local_di, D), jnp.bfloat16),
            struct((length, local_di)),
            struct((length, local_di)),
            struct((8, length)),
        ],
        [
            fixed((local_di, D)),
            fixed((local_di, D)),
            rows_of(local_di),
            rows_of(local_di),
            pl.BlockSpec((8, BLOCK), lambda q, *_: (0, q)),
        ],
        [],
        length // BLOCK,
        [],
        (2_500_000_000, 12_000_000, 1_000_000),
        "gate",
    )


def run_middle(
    places, scanned, gating, d_gnorm, cot, unit, sums, out, gain_two, gain_one, gate_weight
):
    length, local_di = scanned.shape
    shapes = [(local_di, D)] * 2
    if len(places) > 1:
        shapes = [(2 * local_di * D // 256, 128)] * 2
    return call(
        lambda *refs: middle_kernel(2, *refs),
        places,
        [scanned, gating, d_gnorm, cot, unit, *sums, out, gain_two, gain_one, gate_weight],
        [
            rows_of(local_di),
            rows_of(local_di),
            rows_of(local_di),
            rows_of(D),
            rows_of(D),
        ]
        + [pl.BlockSpec((8, BLOCK), lambda q, *_: (0, q))] * 4
        + [fixed((local_di, D)), fixed((1, local_di)), fixed((1, D)), fixed((local_di, D))],
        [
            struct((length, D), jnp.bfloat16),
            struct((length, local_di), jnp.bfloat16),
            struct((length, local_di), jnp.bfloat16),
            struct((1, local_di)),
            struct((1, D)),
        ]
        + [struct(shape, jnp.bfloat16) for shape in shapes],
        [
            rows_of(D),
            rows_of(local_di),
            rows_of(local_di),
            fixed((1, local_di)),
            fixed((1, D)),
        ]
        + [fixed(shape) for shape in shapes],
        [pltpu.VMEM((local_di, D), jnp.float32), pltpu.VMEM((local_di, D), jnp.float32)],
        length // BLOCK,
        [],
        (4_000_000_000, 15_000_000, 500_000),
        "middle",
    )


def run_backward(
    places,
    unit,
    conv_in,
    conv_pre,
    dt_raw,
    y,
    states,
    d_scanned,
    kernel,
    heads_vectors,
    expand,
    gain_one,
    rest_weight,
    d_gain_gate,
    d_gain_two,
):
    length, local_di = y.shape
    chunks = length // BLOCK
    channels = conv_in.shape[1]
    lanes = expand.shape[0]
    grad = (channels + 16, D) if len(places) == 1 else ((channels + 16) * D // 256, 128)

    def back(extent):
        return pl.BlockSpec((BLOCK, extent), lambda q, *_: (chunks - 1 - q, 0))

    return call(
        lambda *refs: backward_kernel(len(places), *refs),
        places,
        [
            *[unit, conv_in, conv_pre, dt_raw, y, states, d_scanned, kernel],
            *[*heads_vectors, expand, gain_one, rest_weight, d_gain_gate, d_gain_two],
        ],
        [
            back(D),
            back(channels),
            back(channels),
            back(lanes),
            back(local_di),
            pl.BlockSpec((1, STATE, local_di), lambda q, *_: (chunks - 1 - q, 0, 0)),
            back(local_di),
            fixed((WIDTH, channels)),
            fixed((1, lanes)),
            fixed((1, lanes)),
            fixed((1, local_di)),
            fixed((lanes, local_di)),
            fixed((1, D)),
            fixed((channels + lanes, D)),
            fixed((1, D)),
            fixed((1, local_di)),
        ],
        [
            struct((length, channels + lanes), jnp.bfloat16),
            struct((VEC_ROWS, 128)),
        ]
        + [struct(grad, jnp.bfloat16)] * len(places),
        [
            back(channels + lanes),
            fixed((VEC_ROWS, 128)),
        ]
        + [fixed(grad)] * len(places),
        [
            pltpu.VMEM((BLOCK + 8, channels), jnp.float32),
            pltpu.VMEM((STATE, local_di), jnp.float32),
            pltpu.VMEM((STATE, local_di), jnp.float32),
            pltpu.VMEM((channels + lanes, D), jnp.float32),
            pltpu.VMEM((WIDTH, channels), jnp.float32),
            pltpu.VMEM((1, channels), jnp.float32),
            pltpu.VMEM((1, local_di), jnp.float32),
            pltpu.VMEM((2, lanes), jnp.float32),
        ],
        chunks,
        [],
        (14_000_000_000, 40_000_000, 10_000_000),
        "backward",
    )


def run_normed(parity, d_gating, d_rest, gate_weight, rest_weight, arrived):
    length, local_di = d_gating.shape
    rest = d_rest.shape[1]
    return call(
        normed_kernel,
        [parity],
        [d_gating, d_rest, gate_weight, rest_weight],
        [rows_of(local_di), rows_of(rest), fixed((local_di, D)), fixed((rest, D))],
        [struct((length // 2, D), jnp.bfloat16)] * 2,
        [fixed((length // 2, D))] * 2,
        [],
        length // BLOCK,
        arrived,
        (3_000_000_000, 9_000_000, 1000),
        "normed",
    )


def run_pair(places, mine, arrived, extra, through, there):
    rows = mine.shape[0] // len(places) + len(extra) * VEC_ROWS
    block = (rows, mine.shape[1])
    inputs = [mine, arrived, *extra]
    untouched = [pl.BlockSpec(memory_space=pl.ANY)] * len(through)
    return call(
        lambda *refs: pair_kernel(len(through), len(extra), *refs),
        places,
        [*inputs, *through],
        [fixed(array.shape) for array in inputs] + untouched,
        [struct(block, jnp.bfloat16)] * len(places)
        + [struct(array.shape, array.dtype) for array in through],
        [fixed(block)] * len(places) + untouched,
        [],
        1,
        there,
        (2_000_000, 3_000_000, 0),
        "pair",
        [(1 + len(inputs) + number, len(places) + number) for number in range(len(through))],
    )


def run_hold(blocks, there):
    rows, columns = blocks[0].shape
    shape = (rows * len(blocks), columns)
    return call(
        hold_kernel,
        [jnp.int32(0)],
        blocks,
        [fixed(block.shape) for block in blocks],
        struct(shape, blocks[0].dtype),
        fixed(shape),
        [],
        1,
        there,
        (0, 2_000_000, 0),
        "hold",
    )


def run_final(terms, through, there):
    untouched = [pl.BlockSpec(memory_space=pl.ANY)] * len(through)
    return call(
        lambda *refs: final_kernel(len(through), *refs),
        [jnp.int32(0)],
        [*terms, *through],
        [fixed(array.shape) for array in terms] + untouched,
        [struct(terms[0].shape, jnp.bfloat16)]
        + [struct(array.shape, array.dtype) for array in through],
        [fixed(terms[0].shape)] + untouched,
        [],
        1,
        there,
        (500_000, 1_000_000, 0),
        "final",
        [(1 + len(terms) + number, 1 + number) for number in range(len(through))],
    )


def run_update_gate(places, blocks, in_arrays, out_arrays, there):
    groups = len(places)
    rows_out = out_arrays[0].shape[0] // groups
    arrays = [*in_arrays, *out_arrays]
    in_spec = pl.BlockSpec((DI // groups, in_arrays[0].shape[1]), lambda q, *_: (q, 0))
    out_spec = pl.BlockSpec((rows_out, D), lambda q, *_: (q, 0))
    specs = [in_spec] * 3 + [out_spec] * 3
    return call(
        lambda *refs: update_gate_kernel(groups, *refs),
        places,
        [*blocks, *arrays],
        [fixed(array.shape) for array in blocks] + specs,
        [struct(array.shape) for array in arrays]
        + [struct((groups, VEC_ROWS, 128), jnp.bfloat16)],
        specs + [fixed((groups, VEC_ROWS, 128))],
        [pltpu.VMEM((groups,) + blocks[0].shape, jnp.bfloat16)],
        groups,
        there,
        (10_000_000, 13_000_000, 500_000),
        "update_gate",
    )


def run_update_rest(places, blocks, in_arrays, so_far):
    groups = len(places)
    spec = pl.BlockSpec((DI // groups, in_arrays[0].shape[1]), lambda q, *_: (q + groups, 0))
    return call(
        lambda *refs: update_rest_kernel(groups, *refs),
        places,
        [*blocks, *in_arrays, *so_far],
        [fixed(array.shape) for array in blocks]
        + [spec] * 3
        + [pl.BlockSpec(memory_space=pl.ANY)] * 3,
        [struct(array.shape) for array in in_arrays],
        [spec] * 3,
        [pltpu.VMEM((groups,) + blocks[0].shape, jnp.bfloat16)],
        groups + 1,
        [],
        (10_000_000, 8_000_000, 500_000),
        "update_rest",
        [(1 + groups + 3 + number, number) for number in range(3)],
    )


def adamw_step(weight, first, second, grad, rate, decay):
    first_new = beta_one * first + (1.0 - beta_one) * grad
    second_new = beta_two * second + (1.0 - beta_two) * grad * grad
    fix_one = 1.0 - beta_one**STEP
    fix_two = 1.0 - beta_two**STEP
    normalized = first_new / fix_one / (jnp.sqrt(second_new / fix_two) + adam_eps)
    return (first_new, second_new, weight - rate * (normalized + decay * weight))


def pick_heads(values, axis, width, index, groups):
    shape = values.shape
    split = shape[:axis] + (HEADS // groups, groups, width) + shape[axis + 1 :]
    taken = lax.dynamic_index_in_dim(values.reshape(split), index, axis + 1, keepdims=False)
    return taken.reshape(shape[:axis] + (HEADS // groups * width,) + shape[axis + 1 :])


def merge_heads(stacked, axis, width):
    groups = stacked.shape[0]
    shape = stacked.shape[1:]
    split = (groups,) + shape[:axis] + (HEADS // groups, width) + shape[axis + 1 :]
    moved = jnp.moveaxis(stacked.reshape(split), 0, axis + 1)
    return moved.reshape(shape[:axis] + (HEADS * width,) + shape[axis + 1 :])


def swap(values, axis, mask):
    route = [(i, i ^ mask) for i in range(lax.axis_size(axis))]
    return lax.ppermute(values, axis, route)


def seq_blocks(rows, far=None):
    index = lax.axis_index("seq")
    far = swap(rows, "seq", 2) if far is None else far
    blocks = [rows, swap(rows, "seq", 1), far, swap(far, "seq", 1)]
    return [index ^ mask for mask in range(4)], blocks


def ring_step(held):
    count = lax.axis_size("wshard")
    return lax.ppermute(held, "wshard", [(i, (i + 2) % count) for i in range(count)])


def ring_blocks(rows):
    count = lax.axis_size("wshard")
    index = lax.axis_index("wshard")
    places, blocks = [], []
    for step in range(count // 2):
        source = (index + count - 2 * step) % count
        places = places + [source, source ^ 1]
        blocks = blocks + [rows, swap(rows, "wshard", 1)]
        if step < count // 2 - 1:
            rows = ring_step(rows)
    return places, blocks


def ring_late(rows, arrived):
    count = lax.axis_size("wshard")
    index = lax.axis_index("wshard")
    places = [(index + count - 2 * step) % count for step in range(count // 2)]
    blocks = [rows]
    for _ in range(count // 2 - 1):
        blocks = blocks + [ring_step(blocks[-1])]
    swapped = swap(run_hold(blocks, arrived), "wshard", 1)
    return places + [place ^ 1 for place in places], blocks + [swapped]


def take_block(values, index, rows):
    return lax.dynamic_slice_in_dim(values, index * rows, rows, 0)


def gather_out(out_low, seq_index, groups):
    rows = out_low.shape[0]
    if rows % (groups * HEADDIM) == 0:
        mine = pick_rows(out_low, seq_index, groups)
        return lax.all_gather(mine, "wshard", axis=0, tiled=True)
    whole = lax.all_gather(out_low, "wshard", axis=0, tiled=True)
    return pick_heads(whole, 0, HEADDIM, seq_index, groups)


def pick_rows(values, seq_index, groups):
    rows = values.shape[0]
    split = values.reshape(rows // (groups * HEADDIM), groups, HEADDIM, values.shape[1])
    return lax.dynamic_index_in_dim(split, seq_index, 1, keepdims=False).reshape(
        rows // groups, values.shape[1]
    )


def sum_out_grad(grad, rows, seq_index, groups):
    grad = grad.astype(jnp.bfloat16)
    if rows % (groups * HEADDIM) == 0:
        mine = lax.psum_scatter(grad, "wshard", scatter_dimension=0, tiled=True)
        every = lax.all_gather(mine, "seq", axis=0, tiled=False)
        split = every.reshape(groups, rows // (groups * HEADDIM), HEADDIM, grad.shape[1])
        return jnp.moveaxis(split, 0, 1).reshape(rows, grad.shape[1]).astype(jnp.float32)
    blocks = grad.reshape(HEADS // groups, 1, HEADDIM, grad.shape[1])
    here = (jnp.arange(groups) == seq_index)[None, :, None, None]
    spread = jnp.where(here, blocks, jnp.zeros((), jnp.bfloat16)).reshape(DI, grad.shape[1])
    mine = lax.psum_scatter(spread, "wshard", scatter_dimension=0, tiled=True)
    return lax.psum(mine.astype(jnp.float32), "seq")


def shards(
    block_in,
    cotangent,
    in_weight,
    in_first,
    in_second,
    out_weight,
    out_first,
    out_second,
    vec_weight,
    vec_first,
    vec_second,
):
    rows_here = block_in.shape[1]
    groups = lax.axis_size("seq")
    seq_index = lax.axis_index("seq")
    local_heads = HEADS // groups
    local_di = DI // groups
    hidden_rows = block_in.reshape(rows_here, D)
    cot_rows = cotangent.reshape(rows_here, D)
    gain_one, gain_two, kernel, conv_bias, a_log, dt_bias, d_skip = split_vector(vec_weight)

    def heads_of(values, axis, width):
        return pick_heads(values, axis, width, seq_index, groups)

    lanes = 128
    channels = local_di + 2 * STATE
    shard_index = lax.axis_index("wshard")
    rings = lax.axis_size("wshard") == 8
    if rings:
        y, z = shard_index % 2, shard_index // 2
        rest_mine, gate_out_mine = run_prepare(seq_index, in_weight.T, out_weight)
        rest = ring_blocks(rest_mine)
        gate_out_late = gate_out_mine
        gate_places = [z ^ mask for mask in range(4)]
        out_places = [y, 1 - y]
    else:
        in_low = low(in_weight)
        steps_mine = heads_of(in_low[:, DI + CONVCH :], 1, 1)
        rest_mine = jnp.concatenate(
            [
                heads_of(in_low[:, DI : 2 * DI], 1, HEADDIM),
                in_low[:, 2 * DI : 2 * DI + 2 * STATE],
                jnp.pad(steps_mine, ((0, 0), (0, 16 - local_heads))),
            ],
            1,
        )
        gate_mine = heads_of(in_low[:, :DI], 1, HEADDIM)
        origin = [jnp.int32(0)]
        rest = (origin, [lax.all_gather(rest_mine, "wshard", axis=0, tiled=True).T])
        gate_mine = lax.all_gather(gate_mine, "wshard", axis=0, tiled=True).T
        gate_out = (origin, [gate_mine, gather_out(low(out_weight), seq_index, groups)])
        out_places = origin
    hidden_low = lax.all_gather(hidden_rows, "seq", axis=0, tiled=True)
    cot_low = lax.all_gather(cot_rows, "seq", axis=0, tiled=True)
    my_gain_two = heads_of(gain_two, 0, HEADDIM)[None, :]
    my_kernel = jnp.concatenate([heads_of(kernel[:, :DI], 1, HEADDIM), kernel[:, DI:]], 1)
    my_bias = jnp.concatenate([heads_of(conv_bias[:DI], 0, HEADDIM), conv_bias[DI:]], 0)

    def on_lanes(values):
        return jnp.pad(values, (0, lanes - local_heads))[None, :]

    heads_vectors = (
        on_lanes(heads_of(a_log, 0, 1)),
        on_lanes(heads_of(dt_bias, 0, 1)),
        jnp.repeat(heads_of(d_skip, 0, 1), HEADDIM)[None, :],
    )
    expand = (
        jnp.arange(lanes)[:, None] == jnp.arange(local_di)[None, :] // HEADDIM
    ).astype(jnp.float32)
    if rings:
        gate_out = ring_late(
            gate_out_late,
            rest[1][1::2] + [my_kernel, my_bias[None, :], *heads_vectors, expand],
        )
    (
        rest_weight,
        unit_low,
        normed_low,
        conv_in,
        conv_pre,
        dt_raw,
        y_part,
        scanned,
        states,
    ) = run_forward(
        hidden_low, rest, gain_one[None, :], (my_kernel, my_bias[None, :]), heads_vectors, expand
    )
    gate_weight, out_low, gating, d_gnorm, sums = run_gate(
        gate_out, cot_low, normed_low, scanned, my_gain_two
    )
    middle = run_middle(
        out_places,
        scanned,
        gating,
        d_gnorm,
        cot_low,
        unit_low,
        [sums] + [swap(sums, "seq", mask) for mask in range(1, 4)],
        out_low,
        my_gain_two,
        gain_one[None, :],
        gate_weight,
    )
    block_part, d_gating, d_scanned, d_gain_two, d_gain_gate, *gate_out_grads = middle
    block_rows = lax.psum_scatter(block_part, "seq", scatter_dimension=0, tiled=True)
    if rings:
        gate_out_arrived = swap(gate_out_grads[1], "wshard", 1)
    d_rest, vec_rows, *rest_grads = run_backward(
        out_places,
        unit_low,
        conv_in,
        conv_pre,
        dt_raw,
        y_part,
        states,
        d_scanned,
        my_kernel,
        heads_vectors,
        expand,
        gain_one[None, :],
        rest_weight,
        d_gain_gate,
        d_gain_two,
    )
    near, far = seq_index % 2, seq_index // 2
    if rings:
        *gate_out_sums, rest_send = run_pair(
            gate_places,
            gate_out_grads[0],
            gate_out_arrived,
            [vec_rows],
            [rest_grads[1]],
            [block_rows],
        )
        rest_arrived = swap(rest_send, "wshard", 1)
        gate_out_pieces = [
            swap(gate_out_sums[mask], "wshard", 2 * mask) for mask in range(1, 4)
        ]
        normed_mine, normed_send = run_normed(
            near, d_gating, d_rest, gate_weight, rest_weight, [gate_out_sums[0]]
        )
        gate_out_part, normed_send = run_final(
            [gate_out_sums[0]] + gate_out_pieces, [normed_send], []
        )
        gate_out_near = swap(gate_out_part, "seq", 1)
        rest_sums = run_pair(
            gate_places, rest_grads[0], rest_arrived, [], [], [gate_out_near]
        )
        rest_pieces = [swap(rest_sums[mask], "wshard", 2 * mask) for mask in range(1, 4)]
        gate_out_far = swap(gate_out_part, "seq", 2)
    else:
        every = lax.all_gather(lax.psum(vec_rows, "wshard"), "seq", axis=0, tiled=False)
        normed_mine, normed_send = run_normed(
            near, d_gating, d_rest, gate_weight, rest_weight, []
        )
    normed_arrived = swap(normed_send, "seq", 1)
    normed_sum = normed_mine.astype(jnp.float32) + normed_arrived.astype(jnp.float32)
    normed_far = swap(low(take_block(normed_sum, 1 - far, rows_here)), "seq", 2)
    if rings:
        spots = [seq_index ^ mask for mask in range(4)]
        gate_out_blocks = [gate_out_part, gate_out_near, gate_out_far]
        gate_out_blocks = gate_out_blocks + [swap(gate_out_far, "seq", 1)]
        in_arrays = (in_weight.T, in_first.T, in_second.T)
        updated = run_update_gate(
            spots,
            gate_out_blocks,
            in_arrays,
            (out_weight, out_first, out_second),
            [rest_sums[0]],
        )
        out_first_new, out_second_new, out_weight_new, every = updated[3:]
        rest_part, every = run_final([rest_sums[0]] + rest_pieces, [every], [])
        every_there = swap(every, "wshard", 1)
        every = every.astype(jnp.float32) + every_there.astype(jnp.float32)
    block_out = hidden_rows.astype(jnp.float32) + block_rows.astype(jnp.float32)
    d_normed = take_block(normed_sum, far, rows_here) + normed_far.astype(jnp.float32)
    own_hidden = hidden_rows.astype(jnp.float32)
    own_scale = lax.rsqrt(jnp.mean(own_hidden * own_hidden, axis=-1, keepdims=True) + norm_eps)
    own_unit = own_hidden * own_scale
    d_own = d_normed * gain_one[None, :]
    d_hidden = own_scale * (
        d_own - own_unit * jnp.mean(d_own * own_unit, axis=-1, keepdims=True)
    )
    block_grad = cot_rows.astype(jnp.float32) + d_hidden
    if rings:
        spots, rest_blocks = seq_blocks(rest_part)
        updated = run_update_rest(spots, rest_blocks, in_arrays, updated[:3])
        in_first_new, in_second_new, in_weight_new = [array.T for array in updated]
    else:
        rest_part = lax.psum_scatter(rest_grads[0].T, "wshard", scatter_dimension=0, tiled=True)
        gate_part = lax.psum_scatter(gate_out_grads[0].T, "wshard", scatter_dimension=0, tiled=True)
        gate_every = lax.all_gather(gate_part, "seq", axis=0, tiled=False).astype(jnp.float32)
        rest_every = lax.all_gather(rest_part, "seq", axis=0, tiled=False).astype(jnp.float32)
        out_total = sum_out_grad(gate_out_grads[1], out_weight.shape[0], seq_index, groups)
        in_total = jnp.concatenate(
            [
                merge_heads(gate_every, 1, HEADDIM),
                merge_heads(rest_every[:, :, :local_di], 1, HEADDIM),
                jnp.sum(rest_every[:, :, local_di:channels], axis=0),
                merge_heads(rest_every[:, :, channels : channels + local_heads], 1, 1),
            ],
            1,
        )
        in_first_new, in_second_new, in_weight_new = adamw_step(
            in_weight, in_first, in_second, in_total, matrix_rate, matrix_decay
        )
        out_first_new, out_second_new, out_weight_new = adamw_step(
            out_weight, out_first, out_second, out_total, matrix_rate, matrix_decay
        )
    every = every.reshape(groups, VEC_ROWS * 128)
    cuts = [0, D]
    for extent in (WIDTH * channels, channels, local_di, local_di, lanes, lanes):
        cuts.append(cuts[-1] + extent)
    parts = [every[:, cuts[number] : cuts[number + 1]] for number in range(7)]
    kernel_every = parts[1].reshape(groups, WIDTH, channels)
    kernel_total = jnp.concatenate(
        [
            merge_heads(kernel_every[:, :, :local_di], 1, HEADDIM),
            jnp.sum(kernel_every[:, :, local_di:], axis=0),
        ],
        1,
    )
    skip_every = jnp.sum(parts[4].reshape(groups, local_heads, HEADDIM), axis=2)
    vec_total = jnp.concatenate(
        [
            jnp.sum(parts[0], axis=0),
            merge_heads(parts[3], 0, HEADDIM),
            kernel_total.reshape(-1),
            merge_heads(parts[2][:, :local_di], 0, HEADDIM),
            jnp.sum(parts[2][:, local_di:], axis=0),
            merge_heads(parts[5][:, :local_heads], 0, 1),
            merge_heads(parts[6][:, :local_heads], 0, 1),
            merge_heads(skip_every, 0, 1),
        ]
    )
    vec_first_new, vec_second_new, vec_weight_new = adamw_step(
        vec_weight, vec_first, vec_second, vec_total, vector_rate, 0.0
    )
    return (
        block_out.reshape(1, rows_here, D),
        block_grad.reshape(1, rows_here, D),
        in_first_new,
        in_second_new,
        in_weight_new,
        out_first_new,
        out_second_new,
        out_weight_new,
        vec_first_new,
        vec_second_new,
        vec_weight_new,
    )


def solution(mesh):
    return jax.shard_map(
        shards,
        mesh=mesh,
        in_specs=(
            P("wshard", "seq", None),
            P("wshard", "seq", None),
            P("wshard", None),
            P("wshard", None),
            P("wshard", None),
            P("wshard", None),
            P("wshard", None),
            P("wshard", None),
            P(),
            P(),
            P(),
        ),
        out_specs=(
            P("wshard", "seq", None),
            P("wshard", "seq", None),
            P("wshard", None),
            P("wshard", None),
            P("wshard", None),
            P("wshard", None),
            P("wshard", None),
            P("wshard", None),
            P(),
            P(),
            P(),
        ),
        check_vma=False,
    )
```

```python
import jax
import jax.numpy as jnp
from jax import lax
from jax.experimental import pallas as pl
from jax.experimental.pallas import tpu as pltpu
from jax.sharding import PartitionSpec as P

D = 1024
HEADS = 32
HEADDIM = 64
STATE = 128
WIDTH = 4
BLOCK = 256
STEP = 10
DI = 2048
CONVCH = 2304
VEC_ROWS = 48


norm_eps = 1e-05
beta_one = 0.9
beta_two = 0.95
adam_eps = 1e-08
matrix_rate = 0.05
matrix_decay = 0.1
vector_rate = 0.5


def rms_scale(values):
    return values * lax.rsqrt(jnp.mean(values * values, axis=-1, keepdims=True) + norm_eps)


def split_vector(vector):
    extents = [D, DI, WIDTH * CONVCH, CONVCH, HEADS, HEADS, HEADS]
    pieces = []
    offset = 0
    for extent in extents:
        pieces.append(vector[offset : offset + extent])
        offset = offset + extent
    pieces[2] = pieces[2].reshape(WIDTH, CONVCH)
    return pieces


def dot_nt(left, right, precision=None):
    return lax.dot_general(
        left,
        right,
        (((1,), (1,)), ((), ())),
        precision=precision,
        preferred_element_type=jnp.float32,
    )


def dot_tn(left, right):
    return lax.dot_general(
        left, right, (((0,), (0,)), ((), ())), preferred_element_type=jnp.float32
    )


def dot_nn(left, right, precision=None):
    return jnp.dot(left, right, precision=precision, preferred_element_type=jnp.float32)


def terms_of(values, count):
    terms = []
    for _ in range(count):
        terms.append(values.astype(jnp.bfloat16))
        values = values - terms[-1].astype(jnp.float32)
    return terms


def sum_terms(product, values, count):
    total = None
    for term in terms_of(values, count):
        total = product(term) if total is None else total + product(term)
    return total


def sigmoid(values):
    return 1.0 / (1.0 + jnp.exp(-values))


def low(values):
    return values.astype(jnp.bfloat16)


def lower_mask():
    rows = lax.broadcasted_iota(jnp.int32, (BLOCK, BLOCK), 0)
    return rows >= lax.broadcasted_iota(jnp.int32, (BLOCK, BLOCK), 1)


def decay_sums(dt_raw, dt_bias, a_log, expand):
    shifted = dt_raw + dt_bias
    step = jnp.maximum(shifted, 0.0) + jnp.log1p(jnp.exp(-jnp.abs(shifted)))
    log_decay = -jnp.exp(a_log) * step
    ones = low(jnp.where(lower_mask(), 1.0, 0.0))
    running = sum_terms(lambda term: dot_nn(ones, term), log_decay, 3)
    step_wide = sum_terms(lambda term: dot_nn(term, expand), step, 2)
    running_wide = sum_terms(lambda term: dot_nn(term, expand), running, 3)
    return shifted, step, log_decay, running, step_wide, running_wide


def place_rows(result_ref, place, block):
    rows = block.shape[0]
    result_ref[pl.ds(pl.multiple_of(place * rows, rows), rows), :] = block


def place_columns(result_ref, place, block):
    rows, columns = block.shape
    start = pl.multiple_of(place * columns, columns)
    result_ref[:rows, pl.ds(start, columns)] = block


def forward_kernel(rest_count, places_ref, *refs):
    rest_blocks = refs[:rest_count]
    (
        hidden_ref,
        gain_one_ref,
        conv_ref,
        bias_ref,
        a_log_ref,
        dt_bias_ref,
        skip_ref,
        expand_ref,
        rest_ref,
        unit_ref,
        normed_ref,
        conv_in_ref,
        conv_pre_ref,
        dt_ref,
        y_ref,
        scanned_ref,
        state_ref,
        ext,
        state,
    ) = refs[rest_count:]
    local_di = y_ref.shape[1]
    heads = local_di // HEADDIM
    channels = conv_in_ref.shape[1]

    @pl.when(pl.program_id(0) == 0)
    def _():
        ext[0:8, :] = jnp.zeros((8, ext.shape[1]), jnp.float32)
        state[...] = jnp.zeros_like(state)
        rest_ref[channels:, :] = jnp.zeros_like(rest_ref[channels:, :])
        for number, block in enumerate(rest_blocks):
            place_columns(rest_ref, places_ref[number], block[...])

    hidden = hidden_ref[...].astype(jnp.float32)
    unit = rms_scale(hidden)
    unit_ref[...] = low(unit)
    normed = low(unit * gain_one_ref[...])
    normed_ref[...] = normed
    conv_in = dot_nt(normed, rest_ref[:channels, :])
    conv_in_ref[...] = conv_in
    ext[8 : 8 + BLOCK, :] = conv_in
    conv_pre = bias_ref[...] + conv_ref[WIDTH - 1 : WIDTH, :] * conv_in
    for tap in range(WIDTH - 1):
        first = 8 - WIDTH + 1 + tap
        conv_pre = conv_pre + conv_ref[tap : tap + 1, :] * ext[first : first + BLOCK, :]
    conv_pre_ref[...] = conv_pre
    ext[8 - WIDTH + 1 : 8, :] = ext[8 + BLOCK - WIDTH + 1 : 8 + BLOCK, :]
    conv_low = low(conv_pre * sigmoid(conv_pre))
    inner = conv_low[:, :local_di]
    b_rows = conv_low[:, local_di : local_di + STATE]
    c_rows = conv_low[:, local_di + STATE :]
    dt_raw = low(dot_nt(normed, rest_ref[channels:, :])).astype(jnp.float32)
    dt_ref[...] = dt_raw

    _, _, _, running, step_wide, running_wide = decay_sums(
        dt_raw, dt_bias_ref[...], a_log_ref[...], expand_ref[...]
    )
    running_t = running.T
    b_t = low(b_rows.astype(jnp.float32).T)
    scores = dot_nn(c_rows, b_t)
    mask = lower_mask()
    inner_wide = inner.astype(jnp.float32)
    stepped = step_wide * inner_wide
    stepped_low = low(stepped)
    first_half = lax.broadcasted_iota(jnp.int32, (BLOCK, 2 * HEADDIM), 1) < HEADDIM
    zero = jnp.zeros((), jnp.bfloat16)
    state_ref[...] = state[...].reshape(state_ref.shape)
    held = state[...]
    carried = jnp.exp(running_wide) * dot_nn(c_rows, low(held))
    for pair in range(heads // 2):
        span = slice(pair * 2 * HEADDIM, (pair + 1) * 2 * HEADDIM)
        both = stepped_low[:, span]
        total = carried[:, span]
        for half in range(2):
            head = 2 * pair + half
            differ = running[:, head : head + 1] - running_t[head : head + 1, :]
            mixed = low(jnp.exp(jnp.where(mask, differ, -jnp.inf)) * scores)
            mine = jnp.where(first_half if half == 0 else ~first_half, both, zero)
            total = total + dot_nn(mixed, mine)
        y_ref[:, span] = total
    last = running_wide[BLOCK - 1 : BLOCK, :]
    to_end = jnp.exp(last - running_wide)
    state[...] = jnp.exp(last) * held + dot_nn(b_t, low(to_end * stepped))
    scanned_ref[...] = low(y_ref[...] + skip_ref[...] * inner_wide)


def gate_kernel(count, places_ref, *refs):
    blocks = refs[:count]
    (
        cot_ref,
        normed_ref,
        scanned_ref,
        gain_two_ref,
        gate_ref,
        out_ref,
        gating_ref,
        d_gnorm_ref,
        sums_ref,
    ) = refs[count:]
    local_di = gating_ref.shape[1]

    @pl.when(pl.program_id(0) == 0)
    def _():
        if count == 2:
            gate_ref[...] = blocks[0][...]
            out_ref[...] = blocks[1][...]
            return
        number = 0
        for block in blocks:
            columns = block.shape[1]
            for base in range(0, block.shape[0], 2 * local_di):
                spot = places_ref[number]
                number = number + 1
                place_columns(gate_ref, spot, block[base : base + local_di, :])
                for tile in range(D // columns):
                    first = base + local_di + tile * HEADDIM
                    span = slice(tile * columns, (tile + 1) * columns)
                    place_rows(out_ref.at[:, span], spot, block[first : first + HEADDIM, :])

    gating = dot_nt(normed_ref[...], gate_ref[...])
    gating_ref[...] = gating
    d_gnorm = dot_nt(cot_ref[...], out_ref[...])
    d_gnorm_ref[...] = d_gnorm
    gated = scanned_ref[...].astype(jnp.float32) * (gating * sigmoid(gating))
    ones = jnp.ones((8, local_di), jnp.bfloat16)
    squares = sum_terms(lambda term: dot_nt(ones, term), gated * gated, 2)
    products = d_gnorm * gain_two_ref[...] * gated
    products = sum_terms(lambda term: dot_nt(ones, term), products, 2)
    sums_ref[...] = jnp.where(
        lax.broadcasted_iota(jnp.int32, squares.shape, 0) == 0, squares, products
    )


def middle_kernel(count, places_ref, *refs):
    (
        scanned_ref,
        gating_ref,
        d_gnorm_ref,
        cot_ref,
        unit_ref,
        sums_one_ref,
        sums_two_ref,
        sums_three_ref,
        sums_four_ref,
        out_ref,
        gain_two_ref,
        gain_one_ref,
        gate_weight_ref,
        block_ref,
        d_gating_ref,
        d_scanned_ref,
        d_gain_two_ref,
        d_gain_one_ref,
    ) = refs[:18]
    grad_refs = refs[18 : 18 + count]
    out_sum, gate_sum = refs[18 + count :]
    chunk = pl.program_id(0)

    @pl.when(chunk == 0)
    def _():
        out_sum[...] = jnp.zeros_like(out_sum)
        gate_sum[...] = jnp.zeros_like(gate_sum)
        d_gain_two_ref[...] = jnp.zeros_like(d_gain_two_ref)

    sums = (sums_one_ref[...] + sums_two_ref[...]) + (sums_three_ref[...] + sums_four_ref[...])
    sums = (sums / DI).T
    scale = lax.rsqrt(sums[:, 0:1] + norm_eps)
    slope = scale * scale * sums[:, 1:2]
    gating = gating_ref[...]
    open_part = sigmoid(gating)
    gate = gating * open_part
    scanned = scanned_ref[...].astype(jnp.float32)
    unit = scanned * gate * scale
    d_gnorm = d_gnorm_ref[...]
    gain_two = gain_two_ref[...]
    gnorm = low(unit * gain_two)
    block_ref[...] = low(dot_nn(gnorm, out_ref[...]))
    out_sum[...] += dot_tn(gnorm, cot_ref[...])
    d_gain_two_ref[...] += jnp.sum(d_gnorm * unit, axis=0, keepdims=True)
    d_gated = scale * (d_gnorm * gain_two) - unit * slope
    d_gating = low(d_gated * scanned * (open_part * (1.0 + gating * (1.0 - open_part))))
    d_gating_ref[...] = d_gating
    d_scanned_ref[...] = low(d_gated * gate)
    gate_sum[...] += dot_tn(d_gating, unit_ref[...])

    @pl.when(chunk == pl.num_programs(0) - 1)
    def _():
        weights = gate_weight_ref[...].astype(jnp.float32)
        d_gain_one_ref[...] = jnp.sum(gate_sum[...] * weights, axis=0, keepdims=True)
        gate_sum[...] = gate_sum[...] * gain_one_ref[...]
        local_di = gate_sum.shape[0]
        if grad_refs[0].shape == gate_sum.shape:
            grad_refs[0][...] = low(gate_sum[...])
            grad_refs[1][...] = low(out_sum[...])
            return
        for number, grad_ref in enumerate(grad_refs):
            columns = grad_ref.shape[1]
            for step in range(D // columns // count):
                place = places_ref[number] + step * count
                start = pl.multiple_of(place * columns, columns)
                base = step * 2 * local_di
                grad_ref[base : base + local_di, :] = low(gate_sum[:, pl.ds(start, columns)])
                rows = pl.ds(pl.multiple_of(place * HEADDIM, HEADDIM), HEADDIM)
                for tile in range(D // columns):
                    first = base + local_di + tile * HEADDIM
                    grad_ref[first : first + HEADDIM, :] = low(
                        out_sum[rows, tile * columns : (tile + 1) * columns]
                    )


def backward_kernel(
    grad_count,
    places_ref,
    unit_ref,
    conv_in_ref,
    conv_pre_ref,
    dt_ref,
    y_ref,
    state_ref,
    d_scanned_ref,
    conv_ref,
    a_log_ref,
    dt_bias_ref,
    skip_ref,
    expand_ref,
    gain_one_ref,
    rest_weight_ref,
    d_gain_gate_ref,
    d_gain_two_ref,
    d_rest_ref,
    vec_ref,
    *refs,
):
    grad_refs = refs[:grad_count]
    ext, d_state, later_state, rest_sum = refs[grad_count : grad_count + 4]
    d_kernel_ref, d_conv_bias_ref, d_skip_ref, d_head_ref = refs[grad_count + 4 :]
    local_di = y_ref.shape[1]
    heads = local_di // HEADDIM
    chunk = pl.program_id(0)

    @pl.when(chunk == 0)
    def _():
        ext[BLOCK : BLOCK + 8, :] = jnp.zeros((8, ext.shape[1]), jnp.float32)
        d_state[...] = jnp.zeros_like(d_state)
        later_state[...] = jnp.zeros_like(later_state)
        rest_sum[...] = jnp.zeros_like(rest_sum)
        d_kernel_ref[...] = jnp.zeros_like(d_kernel_ref)
        d_conv_bias_ref[...] = jnp.zeros_like(d_conv_bias_ref)
        d_skip_ref[...] = jnp.zeros_like(d_skip_ref)
        d_head_ref[...] = jnp.zeros_like(d_head_ref)

    expand = expand_ref[...]
    conv_pre = conv_pre_ref[...]
    open_part = sigmoid(conv_pre)
    conv_low = low(conv_pre * open_part)
    inner = conv_low[:, :local_di].astype(jnp.float32)
    b_rows = conv_low[:, local_di : local_di + STATE]
    c_rows = conv_low[:, local_di + STATE :]
    a_log = a_log_ref[...]
    shifted, _, log_decay, running, step_wide, running_wide = decay_sums(
        dt_ref[...], dt_bias_ref[...], a_log, expand
    )
    running_t = running.T
    b_t = low(b_rows.astype(jnp.float32).T)
    c_t = low(c_rows.astype(jnp.float32).T)
    scores = dot_nn(c_rows, b_t)
    scores_t = dot_nn(b_rows, c_t)
    mask = lower_mask()
    rows = lax.broadcasted_iota(jnp.int32, (BLOCK, BLOCK), 0)
    mask_t = rows <= lax.broadcasted_iota(jnp.int32, (BLOCK, BLOCK), 1)
    d_y_low = d_scanned_ref[...]
    d_y = d_y_low.astype(jnp.float32)
    stepped_low = low(step_wide * inner)
    stepped = stepped_low.astype(jnp.float32)
    last = running_wide[BLOCK - 1 : BLOCK, :]
    to_end = jnp.exp(last - running_wide)
    d_later = d_state[...]
    d_later_low = low(d_later)
    held = state_ref[...].reshape(d_state.shape)
    decayed_dy = low(jnp.exp(running_wide) * d_y)
    d_c = dot_nt(decayed_dy, low(held))
    d_b = dot_nt(low(to_end * stepped), d_later_low)
    d_stepped = to_end * dot_nn(b_rows, d_later_low)
    cross = jnp.sum(later_state[...] * d_later, axis=0, keepdims=True)
    d_state[...] = jnp.exp(last) * d_later + dot_nn(c_t, decayed_dy)
    later_state[...] = held
    first_half = lax.broadcasted_iota(jnp.int32, (BLOCK, 2 * HEADDIM), 1) < HEADDIM
    zero = jnp.zeros((), jnp.bfloat16)
    d_scores = jnp.zeros((BLOCK, BLOCK), jnp.float32)
    pieces = []
    for pair in range(heads // 2):
        span = slice(pair * 2 * HEADDIM, (pair + 1) * 2 * HEADDIM)
        total = d_stepped[:, span]
        for half in range(2):
            head = 2 * pair + half
            mine = jnp.where(first_half if half == 0 else ~first_half, d_y_low[:, span], zero)
            column = running[:, head : head + 1]
            row = running_t[head : head + 1, :]
            decay = jnp.exp(jnp.where(mask, column - row, -jnp.inf))
            decay_t = jnp.exp(jnp.where(mask_t, row - column, -jnp.inf))
            d_scores = d_scores + dot_nt(mine, stepped_low[:, span]) * decay
            total = total + dot_nn(low(decay_t * scores_t), mine)
        pieces.append(total)
    d_stepped = jnp.concatenate(pieces, 1)
    d_scores_low = low(d_scores)
    d_c = d_c + dot_nn(d_scores_low, b_rows)
    d_b = d_b + dot_nn(low(d_scores.T), c_rows)
    d_inner = step_wide * d_stepped + skip_ref[...] * d_y
    d_running = d_y * y_ref[...] - d_stepped * stepped
    d_running = sum_terms(lambda term: dot_nt(term, expand), d_running, 2)
    upper = low(jnp.where(mask_t, 1.0, 0.0))
    d_log = sum_terms(lambda term: dot_nn(upper, term), d_running, 3)
    d_log = d_log + sum_terms(lambda term: dot_nt(term, expand), cross, 3)
    d_step = sum_terms(lambda term: dot_nt(term, expand), d_stepped * inner, 2)
    d_step = d_step - jnp.exp(a_log) * d_log
    d_dt = d_step * sigmoid(shifted)
    d_head_ref[0:1, :] += jnp.sum(d_log * log_decay, axis=0, keepdims=True)
    d_head_ref[1:2, :] += jnp.sum(d_dt, axis=0, keepdims=True)
    d_skip_ref[...] += jnp.sum(d_y * inner, axis=0, keepdims=True)

    d_conv_out = jnp.concatenate([d_inner, d_b, d_c], 1)
    d_pre = d_conv_out * (open_part * (1.0 + conv_pre * (1.0 - open_part)))
    ext[0:BLOCK, :] = d_pre
    d_conv_bias_ref[...] += jnp.sum(d_pre, axis=0, keepdims=True)
    conv_in = conv_in_ref[...]
    d_conv_in = jnp.zeros_like(conv_in)
    for tap in range(WIDTH):
        moved = ext[WIDTH - 1 - tap : WIDTH - 1 - tap + BLOCK, :]
        d_conv_in = d_conv_in + conv_ref[tap : tap + 1, :] * moved
        d_kernel_ref[tap : tap + 1, :] += jnp.sum(moved * conv_in, axis=0, keepdims=True)
    ext[BLOCK : BLOCK + 8, :] = ext[0:8, :]
    d_rest = jnp.concatenate([low(d_conv_in), low(d_dt)], 1)
    d_rest_ref[...] = d_rest
    rest_sum[...] += dot_tn(d_rest, unit_ref[...])

    @pl.when(chunk == pl.num_programs(0) - 1)
    def _():
        weights = rest_weight_ref[...].astype(jnp.float32)
        d_gain_one = jnp.sum(rest_sum[...] * weights, axis=0, keepdims=True)
        pieces = [d_gain_one + d_gain_gate_ref[...]]
        pieces = pieces + [d_kernel_ref[tap : tap + 1, :] for tap in range(WIDTH)]
        pieces = pieces + [d_conv_bias_ref[...], d_gain_two_ref[...], d_skip_ref[...]]
        pieces = pieces + [d_head_ref[0:1, :], d_head_ref[1:2, :]]
        row = 0
        for piece in pieces:
            for first in range(0, piece.shape[1], 128):
                vec_ref[row : row + 1, :] = piece[:, first : first + 128]
                row = row + 1
        rest_sum[...] = rest_sum[...] * gain_one_ref[...]
        for number, grad_ref in enumerate(grad_refs):
            columns = grad_ref.shape[1]
            blocks = rest_sum.shape[1] // columns // grad_count
            rows = grad_ref.shape[0] // blocks
            for step in range(blocks):
                place = places_ref[number] + step * grad_count
                start = pl.multiple_of(place * columns, columns)
                grad_ref[step * rows : (step + 1) * rows, :] = low(
                    rest_sum[:rows, pl.ds(start, columns)]
                )


def sum_of(*refs):
    total = refs[0][...].astype(jnp.float32)
    for ref in refs[1:]:
        total = total + ref[...].astype(jnp.float32)
    return total


def pair_kernel(count, extra, places_ref, mine_ref, arrived_ref, *refs):
    for ref in refs[extra + count : len(refs) - count]:
        if extra:
            ref[ref.shape[0] - VEC_ROWS :, :] = low(refs[0][...])
    for number, ref in enumerate(refs[extra + count : len(refs) - count]):
        rows = ref.shape[0] - extra * VEC_ROWS
        here = pl.ds(pl.multiple_of(places_ref[number] * rows, rows), rows)
        ref[:rows, :] = low(sum_of(mine_ref.at[here, :], arrived_ref.at[here, :]))


def hold_kernel(places_ref, *refs):
    rows = refs[0].shape[0]
    for number, ref in enumerate(refs[:-1]):
        refs[-1][number * rows : (number + 1) * rows, :] = ref[...]


def final_kernel(count, places_ref, one_ref, two_ref, three_ref, four_ref, *refs):
    refs[count][...] = low(sum_of(one_ref, two_ref) + sum_of(three_ref, four_ref))


def normed_kernel(
    places_ref, d_gating_ref, d_rest_ref, gate_weight_ref, rest_weight_ref, mine_ref, send_ref
):
    chunk = pl.program_id(0)
    d_normed = dot_nn(d_gating_ref[...], gate_weight_ref[...])
    d_normed = low(d_normed + dot_nn(d_rest_ref[...], rest_weight_ref[...]))
    here = chunk % 2 == places_ref[0]
    rows = pl.ds(pl.multiple_of(chunk // 2 * BLOCK, BLOCK), BLOCK)

    @pl.when(here)
    def _():
        mine_ref[rows, :] = d_normed

    @pl.when(jnp.logical_not(here))
    def _():
        send_ref[rows, :] = d_normed


def prepare_kernel(places_ref, in_ref, out_ref, rest_ref, gate_out_ref):
    index = places_ref[0]
    local_di = gate_out_ref.shape[0] // 2
    groups = DI // local_di
    for head in range(HEADS // groups):
        rows = slice(head * HEADDIM, (head + 1) * HEADDIM)
        for base, result_ref in ((0, gate_out_ref), (DI, rest_ref)):
            start = pl.multiple_of(base + (groups * head + index) * HEADDIM, HEADDIM)
            result_ref[rows, :] = low(in_ref[pl.ds(start, HEADDIM), :])
    channels = local_di + 2 * STATE
    rest_ref[local_di:channels, :] = low(in_ref[2 * DI : 2 * DI + 2 * STATE, :])
    rows = rest_ref.shape[0] - channels
    target = lax.broadcasted_iota(jnp.int32, (rows, HEADS), 0)
    source = lax.broadcasted_iota(jnp.int32, (rows, HEADS), 1)
    chosen = (source == groups * target + index) & (target < HEADS // groups)
    steps = low(in_ref[DI + CONVCH :, :])
    rest_ref[channels:, :] = low(dot_nn(jnp.where(chosen, 1.0, 0.0).astype(jnp.bfloat16), steps))
    mine = pl.ds(pl.multiple_of(index * HEADDIM, HEADDIM), HEADDIM)
    columns = gate_out_ref.shape[1]
    for tile in range(D // columns):
        first = local_di + tile * HEADDIM
        gate_out_ref[first : first + HEADDIM, :] = low(
            out_ref[mine, tile * columns : (tile + 1) * columns]
        )


def adamw_store(old_refs, new_refs, rows, columns, grad):
    results = adamw_step(*[ref[rows, columns] for ref in old_refs], grad, matrix_rate, matrix_decay)
    for ref, result in zip(new_refs, results):
        ref[rows, columns] = result


def update_heads(old_refs, new_refs, source, part):
    groups = source.shape[0]
    heads = old_refs[0].shape[0] // HEADDIM // groups
    for head in range(heads):
        start = pl.multiple_of((part * heads + head) * HEADDIM, HEADDIM)
        for group in range(groups):
            first = (head * groups + group) * HEADDIM
            grad = source[group, pl.ds(start, HEADDIM), :].astype(jnp.float32)
            adamw_store(old_refs, new_refs, slice(first, first + HEADDIM), slice(None), grad)


def update_gate_kernel(groups, places_ref, *refs):
    blocks, in_refs, out_refs = refs[:groups], refs[groups : groups + 3], refs[groups + 3 : groups + 6]
    in_new_refs, out_new_refs = refs[groups + 6 : groups + 9], refs[groups + 9 : groups + 12]
    every_ref, gate_out = refs[groups + 12 :]
    chunk = pl.program_id(0)

    @pl.when(chunk == 0)
    def _():
        for number in range(groups):
            gate_out[places_ref[number]] = blocks[number][...]

    local_di = (gate_out.shape[1] - VEC_ROWS) // 2
    every_ref[...] = gate_out[:, 2 * local_di :, :]
    update_heads(in_refs, in_new_refs, gate_out, chunk)
    columns = gate_out.shape[2]
    for tile in range(D // columns):
        first = local_di + tile * HEADDIM
        grad = gate_out[chunk, first : first + HEADDIM, :].astype(jnp.float32)
        span = slice(tile * columns, (tile + 1) * columns)
        adamw_store(out_refs, out_new_refs, slice(None), span, grad)


def update_rest_kernel(groups, places_ref, *refs):
    blocks, in_refs = refs[:groups], refs[groups : groups + 3]
    in_new_refs, (rest,) = refs[groups + 6 : groups + 9], refs[groups + 9 :]
    chunk = pl.program_id(0)

    @pl.when(chunk == 0)
    def _():
        for number in range(groups):
            rest[places_ref[number]] = blocks[number][...]

    @pl.when(chunk < pl.num_programs(0) - 1)
    def _():
        update_heads(in_refs, in_new_refs, rest, chunk)

    @pl.when(chunk == pl.num_programs(0) - 1)
    def _():
        local_di = DI // groups
        channels = local_di + 2 * STATE
        both = rest[0, local_di:channels, :].astype(jnp.float32)
        rows = rest.shape[1] - channels
        steps = jnp.zeros((HEADS, rest.shape[2]), jnp.float32)
        target = lax.broadcasted_iota(jnp.int32, (HEADS, rows), 0)
        source = lax.broadcasted_iota(jnp.int32, (HEADS, rows), 1)
        for group in range(groups):
            if group > 0:
                both = both + rest[group, local_di:channels, :].astype(jnp.float32)
            chosen = jnp.where(target == groups * source + group, 1.0, 0.0).astype(jnp.bfloat16)
            steps = steps + dot_nn(chosen, rest[group, channels:, :])
        after_both = slice(2 * STATE, 2 * STATE + HEADS)
        adamw_store(in_refs, in_new_refs, slice(0, 2 * STATE), slice(None), both)
        adamw_store(in_refs, in_new_refs, after_both, slice(None), steps)


def kernel_params():
    return pltpu.CompilerParams(
        dimension_semantics=("arbitrary",), vmem_limit_bytes=56 * 1024 * 1024
    )


def cost(flops, moved, transcendentals):
    return pl.CostEstimate(flops=flops, bytes_accessed=moved, transcendentals=transcendentals)


def after(kernel, inputs, arrived):
    def run(*refs):
        kernel(*refs[:inputs], *refs[inputs + arrived :])

    return run


def corner(array):
    return pl.BlockSpec((min(16, array.shape[0]), 128), lambda *_: (0, 0))


def fixed(shape):
    return pl.BlockSpec(shape, lambda *_: (0,) * len(shape))


def rows_of(extent, first=0):
    return pl.BlockSpec((BLOCK, extent), lambda q, *_: (q + first, 0))


def struct(shape, dtype=jnp.float32):
    return jax.ShapeDtypeStruct(shape, dtype)


def call(
    kernel, places, inputs, in_specs, outputs, out_specs, scratch, grid, arrived, price, name, same=()
):
    return pl.pallas_call(
        after(kernel, 1 + len(inputs), len(arrived)),
        grid_spec=pltpu.PrefetchScalarGridSpec(
            num_scalar_prefetch=1,
            grid=(grid,),
            in_specs=list(in_specs) + [corner(array) for array in arrived],
            out_specs=out_specs,
            scratch_shapes=scratch,
        ),
        out_shape=outputs,
        input_output_aliases=dict(same),
        compiler_params=kernel_params(),
        cost_estimate=cost(*price),
        name=name,
    )(jnp.stack(places).astype(jnp.int32), *inputs, *arrived)


def run_prepare(index, in_t, out_weight):
    columns = in_t.shape[1]
    local_di = DI // 4
    shapes = [
        (local_di + 2 * STATE + 16, columns),
        (2 * local_di, columns),
    ]
    inputs = [in_t, out_weight]
    return call(
        prepare_kernel,
        [index],
        inputs,
        [fixed(array.shape) for array in inputs],
        [struct(shape, jnp.bfloat16) for shape in shapes],
        [fixed(shape) for shape in shapes],
        [],
        1,
        [],
        (100_000_000, 4_000_000, 0),
        "prepare",
    )


def run_forward(hidden, rest, gain_one, conv, heads_vectors, expand):
    places, blocks = rest
    length = hidden.shape[0]
    chunks = length // BLOCK
    lanes, local_di = expand.shape
    channels = local_di + 2 * STATE
    vectors = [gain_one, *conv, *heads_vectors, expand]
    return call(
        lambda *refs: forward_kernel(len(blocks), *refs),
        places,
        [*blocks, hidden, *vectors],
        [fixed(array.shape) for array in blocks]
        + [rows_of(D)]
        + [fixed(array.shape) for array in vectors],
        [
            struct((channels + lanes, D), jnp.bfloat16),
            struct((length, D), jnp.bfloat16),
            struct((length, D), jnp.bfloat16),
            struct((length, channels)),
            struct((length, channels)),
            struct((length, lanes)),
            struct((length, local_di)),
            struct((length, local_di), jnp.bfloat16),
            struct((chunks, STATE, local_di)),
        ],
        [
            fixed((channels + lanes, D)),
            rows_of(D),
            rows_of(D),
            rows_of(channels),
            rows_of(channels),
            rows_of(lanes),
            rows_of(local_di),
            rows_of(local_di),
            pl.BlockSpec((1, STATE, local_di), lambda q, *_: (q, 0, 0)),
        ],
        [
            pltpu.VMEM((8 + BLOCK, channels), jnp.float32),
            pltpu.VMEM((STATE, local_di), jnp.float32),
        ],
        chunks,
        [],
        (6_000_000_000, 30_000_000, 8_000_000),
        "forward",
    )


def run_gate(gate_out, cot, normed, scanned, gain_two):
    places, blocks = gate_out
    length, local_di = scanned.shape
    return call(
        lambda *refs: gate_kernel(len(blocks), *refs),
        places,
        [*blocks, cot, normed, scanned, gain_two],
        [fixed(array.shape) for array in blocks]
        + [rows_of(D), rows_of(D), rows_of(local_di), fixed((1, local_di))],
        [
            struct((local_di, D), jnp.bfloat16),
            struct((local_di, D), jnp.bfloat16),
            struct((length, local_di)),
            struct((length, local_di)),
            struct((8, length)),
        ],
        [
            fixed((local_di, D)),
            fixed((local_di, D)),
            rows_of(local_di),
            rows_of(local_di),
            pl.BlockSpec((8, BLOCK), lambda q, *_: (0, q)),
        ],
        [],
        length // BLOCK,
        [],
        (2_500_000_000, 12_000_000, 1_000_000),
        "gate",
    )


def run_middle(
    places, scanned, gating, d_gnorm, cot, unit, sums, out, gain_two, gain_one, gate_weight
):
    length, local_di = scanned.shape
    shapes = [(local_di, D)] * 2
    if len(places) > 1:
        shapes = [(2 * local_di * D // 256, 128)] * 2
    return call(
        lambda *refs: middle_kernel(2, *refs),
        places,
        [scanned, gating, d_gnorm, cot, unit, *sums, out, gain_two, gain_one, gate_weight],
        [
            rows_of(local_di),
            rows_of(local_di),
            rows_of(local_di),
            rows_of(D),
            rows_of(D),
        ]
        + [pl.BlockSpec((8, BLOCK), lambda q, *_: (0, q))] * 4
        + [fixed((local_di, D)), fixed((1, local_di)), fixed((1, D)), fixed((local_di, D))],
        [
            struct((length, D), jnp.bfloat16),
            struct((length, local_di), jnp.bfloat16),
            struct((length, local_di), jnp.bfloat16),
            struct((1, local_di)),
            struct((1, D)),
        ]
        + [struct(shape, jnp.bfloat16) for shape in shapes],
        [
            rows_of(D),
            rows_of(local_di),
            rows_of(local_di),
            fixed((1, local_di)),
            fixed((1, D)),
        ]
        + [fixed(shape) for shape in shapes],
        [pltpu.VMEM((local_di, D), jnp.float32), pltpu.VMEM((local_di, D), jnp.float32)],
        length // BLOCK,
        [],
        (4_000_000_000, 15_000_000, 500_000),
        "middle",
    )


def run_backward(
    places,
    unit,
    conv_in,
    conv_pre,
    dt_raw,
    y,
    states,
    d_scanned,
    kernel,
    heads_vectors,
    expand,
    gain_one,
    rest_weight,
    d_gain_gate,
    d_gain_two,
):
    length, local_di = y.shape
    chunks = length // BLOCK
    channels = conv_in.shape[1]
    lanes = expand.shape[0]
    grad = (channels + 16, D) if len(places) == 1 else ((channels + 16) * D // 256, 128)

    def back(extent):
        return pl.BlockSpec((BLOCK, extent), lambda q, *_: (chunks - 1 - q, 0))

    return call(
        lambda *refs: backward_kernel(len(places), *refs),
        places,
        [
            *[unit, conv_in, conv_pre, dt_raw, y, states, d_scanned, kernel],
            *[*heads_vectors, expand, gain_one, rest_weight, d_gain_gate, d_gain_two],
        ],
        [
            back(D),
            back(channels),
            back(channels),
            back(lanes),
            back(local_di),
            pl.BlockSpec((1, STATE, local_di), lambda q, *_: (chunks - 1 - q, 0, 0)),
            back(local_di),
            fixed((WIDTH, channels)),
            fixed((1, lanes)),
            fixed((1, lanes)),
            fixed((1, local_di)),
            fixed((lanes, local_di)),
            fixed((1, D)),
            fixed((channels + lanes, D)),
            fixed((1, D)),
            fixed((1, local_di)),
        ],
        [
            struct((length, channels + lanes), jnp.bfloat16),
            struct((VEC_ROWS, 128)),
        ]
        + [struct(grad, jnp.bfloat16)] * len(places),
        [
            back(channels + lanes),
            fixed((VEC_ROWS, 128)),
        ]
        + [fixed(grad)] * len(places),
        [
            pltpu.VMEM((BLOCK + 8, channels), jnp.float32),
            pltpu.VMEM((STATE, local_di), jnp.float32),
            pltpu.VMEM((STATE, local_di), jnp.float32),
            pltpu.VMEM((channels + lanes, D), jnp.float32),
            pltpu.VMEM((WIDTH, channels), jnp.float32),
            pltpu.VMEM((1, channels), jnp.float32),
            pltpu.VMEM((1, local_di), jnp.float32),
            pltpu.VMEM((2, lanes), jnp.float32),
        ],
        chunks,
        [],
        (14_000_000_000, 40_000_000, 10_000_000),
        "backward",
    )


def run_normed(parity, d_gating, d_rest, gate_weight, rest_weight, arrived):
    length, local_di = d_gating.shape
    rest = d_rest.shape[1]
    return call(
        normed_kernel,
        [parity],
        [d_gating, d_rest, gate_weight, rest_weight],
        [rows_of(local_di), rows_of(rest), fixed((local_di, D)), fixed((rest, D))],
        [struct((length // 2, D), jnp.bfloat16)] * 2,
        [fixed((length // 2, D))] * 2,
        [],
        length // BLOCK,
        arrived,
        (3_000_000_000, 9_000_000, 1000),
        "normed",
    )


def run_pair(places, mine, arrived, extra, through, there):
    rows = mine.shape[0] // len(places) + len(extra) * VEC_ROWS
    block = (rows, mine.shape[1])
    inputs = [mine, arrived, *extra]
    untouched = [pl.BlockSpec(memory_space=pl.ANY)] * len(through)
    return call(
        lambda *refs: pair_kernel(len(through), len(extra), *refs),
        places,
        [*inputs, *through],
        [fixed(array.shape) for array in inputs] + untouched,
        [struct(block, jnp.bfloat16)] * len(places)
        + [struct(array.shape, array.dtype) for array in through],
        [fixed(block)] * len(places) + untouched,
        [],
        1,
        there,
        (2_000_000, 3_000_000, 0),
        "pair",
        [(1 + len(inputs) + number, len(places) + number) for number in range(len(through))],
    )


def run_hold(places, blocks, there):
    rows, columns = blocks[0].shape
    shape = (rows * len(blocks), columns)
    return call(
        hold_kernel,
        places,
        blocks,
        [fixed(block.shape) for block in blocks],
        struct(shape, blocks[0].dtype),
        fixed(shape),
        [],
        1,
        there,
        (0, 2_000_000, 0),
        "hold",
    )


def run_final(terms, through, there):
    untouched = [pl.BlockSpec(memory_space=pl.ANY)] * len(through)
    return call(
        lambda *refs: final_kernel(len(through), *refs),
        [jnp.int32(0)],
        [*terms, *through],
        [fixed(array.shape) for array in terms] + untouched,
        [struct(terms[0].shape, jnp.bfloat16)]
        + [struct(array.shape, array.dtype) for array in through],
        [fixed(terms[0].shape)] + untouched,
        [],
        1,
        there,
        (500_000, 1_000_000, 0),
        "final",
        [(1 + len(terms) + number, 1 + number) for number in range(len(through))],
    )


def run_update_gate(places, blocks, in_arrays, out_arrays, there):
    groups = len(places)
    rows_out = out_arrays[0].shape[0] // groups
    arrays = [*in_arrays, *out_arrays]
    in_spec = pl.BlockSpec((DI // groups, in_arrays[0].shape[1]), lambda q, *_: (q, 0))
    out_spec = pl.BlockSpec((rows_out, D), lambda q, *_: (q, 0))
    specs = [in_spec] * 3 + [out_spec] * 3
    return call(
        lambda *refs: update_gate_kernel(groups, *refs),
        places,
        [*blocks, *arrays],
        [fixed(array.shape) for array in blocks] + specs,
        [struct(array.shape) for array in arrays]
        + [struct((groups, VEC_ROWS, 128), jnp.bfloat16)],
        specs + [fixed((groups, VEC_ROWS, 128))],
        [pltpu.VMEM((groups,) + blocks[0].shape, jnp.bfloat16)],
        groups,
        there,
        (10_000_000, 13_000_000, 500_000),
        "update_gate",
    )


def run_update_rest(places, blocks, in_arrays, so_far):
    groups = len(places)
    spec = pl.BlockSpec((DI // groups, in_arrays[0].shape[1]), lambda q, *_: (q + groups, 0))
    return call(
        lambda *refs: update_rest_kernel(groups, *refs),
        places,
        [*blocks, *in_arrays, *so_far],
        [fixed(array.shape) for array in blocks]
        + [spec] * 3
        + [pl.BlockSpec(memory_space=pl.ANY)] * 3,
        [struct(array.shape) for array in in_arrays],
        [spec] * 3,
        [pltpu.VMEM((groups,) + blocks[0].shape, jnp.bfloat16)],
        groups + 1,
        [],
        (10_000_000, 8_000_000, 500_000),
        "update_rest",
        [(1 + groups + 3 + number, number) for number in range(3)],
    )


def adamw_step(weight, first, second, grad, rate, decay):
    first_new = beta_one * first + (1.0 - beta_one) * grad
    second_new = beta_two * second + (1.0 - beta_two) * grad * grad
    fix_one = 1.0 - beta_one**STEP
    fix_two = 1.0 - beta_two**STEP
    normalized = first_new / fix_one / (jnp.sqrt(second_new / fix_two) + adam_eps)
    return (first_new, second_new, weight - rate * (normalized + decay * weight))


def pick_heads(values, axis, width, index, groups):
    shape = values.shape
    split = shape[:axis] + (HEADS // groups, groups, width) + shape[axis + 1 :]
    taken = lax.dynamic_index_in_dim(values.reshape(split), index, axis + 1, keepdims=False)
    return taken.reshape(shape[:axis] + (HEADS // groups * width,) + shape[axis + 1 :])


def merge_heads(stacked, axis, width):
    groups = stacked.shape[0]
    shape = stacked.shape[1:]
    split = (groups,) + shape[:axis] + (HEADS // groups, width) + shape[axis + 1 :]
    moved = jnp.moveaxis(stacked.reshape(split), 0, axis + 1)
    return moved.reshape(shape[:axis] + (HEADS * width,) + shape[axis + 1 :])


def swap(values, axis, mask):
    route = [(i, i ^ mask) for i in range(lax.axis_size(axis))]
    return lax.ppermute(values, axis, route)


def seq_blocks(rows, far=None):
    index = lax.axis_index("seq")
    far = swap(rows, "seq", 2) if far is None else far
    blocks = [rows, swap(rows, "seq", 1), far, swap(far, "seq", 1)]
    return [index ^ mask for mask in range(4)], blocks


def ring_step(held):
    count = lax.axis_size("wshard")
    return lax.ppermute(held, "wshard", [(i, (i + 2) % count) for i in range(count)])


def ring_blocks(rows):
    count = lax.axis_size("wshard")
    index = lax.axis_index("wshard")
    places, blocks = [], []
    for step in range(count // 2):
        source = (index + count - 2 * step) % count
        places = places + [source, source ^ 1]
        blocks = blocks + [rows, swap(rows, "wshard", 1)]
        if step < count // 2 - 1:
            rows = ring_step(rows)
    return places, blocks


def ring_late(hold_places, rows, arrived):
    count = lax.axis_size("wshard")
    index = lax.axis_index("wshard")
    places = [(index + count - 2 * step) % count for step in range(count // 2)]
    blocks = [rows]
    for _ in range(count // 2 - 1):
        blocks = blocks + [ring_step(blocks[-1])]
    swapped = swap(run_hold(hold_places, blocks, arrived), "wshard", 1)
    return places + [place ^ 1 for place in places], blocks + [swapped]


def take_block(values, index, rows):
    return lax.dynamic_slice_in_dim(values, index * rows, rows, 0)


def gather_out(out_low, seq_index, groups):
    rows = out_low.shape[0]
    if rows % (groups * HEADDIM) == 0:
        mine = pick_rows(out_low, seq_index, groups)
        return lax.all_gather(mine, "wshard", axis=0, tiled=True)
    whole = lax.all_gather(out_low, "wshard", axis=0, tiled=True)
    return pick_heads(whole, 0, HEADDIM, seq_index, groups)


def pick_rows(values, seq_index, groups):
    rows = values.shape[0]
    split = values.reshape(rows // (groups * HEADDIM), groups, HEADDIM, values.shape[1])
    return lax.dynamic_index_in_dim(split, seq_index, 1, keepdims=False).reshape(
        rows // groups, values.shape[1]
    )


def sum_out_grad(grad, rows, seq_index, groups):
    grad = grad.astype(jnp.bfloat16)
    if rows % (groups * HEADDIM) == 0:
        mine = lax.psum_scatter(grad, "wshard", scatter_dimension=0, tiled=True)
        every = lax.all_gather(mine, "seq", axis=0, tiled=False)
        split = every.reshape(groups, rows // (groups * HEADDIM), HEADDIM, grad.shape[1])
        return jnp.moveaxis(split, 0, 1).reshape(rows, grad.shape[1]).astype(jnp.float32)
    blocks = grad.reshape(HEADS // groups, 1, HEADDIM, grad.shape[1])
    here = (jnp.arange(groups) == seq_index)[None, :, None, None]
    spread = jnp.where(here, blocks, jnp.zeros((), jnp.bfloat16)).reshape(DI, grad.shape[1])
    mine = lax.psum_scatter(spread, "wshard", scatter_dimension=0, tiled=True)
    return lax.psum(mine.astype(jnp.float32), "seq")


def shards(
    block_in,
    cotangent,
    in_weight,
    in_first,
    in_second,
    out_weight,
    out_first,
    out_second,
    vec_weight,
    vec_first,
    vec_second,
):
    rows_here = block_in.shape[1]
    groups = lax.axis_size("seq")
    seq_index = lax.axis_index("seq")
    local_heads = HEADS // groups
    local_di = DI // groups
    hidden_rows = block_in.reshape(rows_here, D)
    cot_rows = cotangent.reshape(rows_here, D)
    gain_one, gain_two, kernel, conv_bias, a_log, dt_bias, d_skip = split_vector(vec_weight)

    def heads_of(values, axis, width):
        return pick_heads(values, axis, width, seq_index, groups)

    lanes = 128
    channels = local_di + 2 * STATE
    shard_index = lax.axis_index("wshard")
    rings = lax.axis_size("wshard") == 8
    if rings:
        y, z = shard_index % 2, shard_index // 2
        rest_mine, gate_out_mine = run_prepare(seq_index, in_weight.T, out_weight)
        rest = ring_blocks(rest_mine)
        gate_out_late = gate_out_mine
        gate_places = [z ^ mask for mask in range(4)]
        out_places = [y, 1 - y]
    else:
        in_low = low(in_weight)
        steps_mine = heads_of(in_low[:, DI + CONVCH :], 1, 1)
        rest_mine = jnp.concatenate(
            [
                heads_of(in_low[:, DI : 2 * DI], 1, HEADDIM),
                in_low[:, 2 * DI : 2 * DI + 2 * STATE],
                jnp.pad(steps_mine, ((0, 0), (0, 16 - local_heads))),
            ],
            1,
        )
        gate_mine = heads_of(in_low[:, :DI], 1, HEADDIM)
        origin = [jnp.int32(0)]
        rest = (origin, [lax.all_gather(rest_mine, "wshard", axis=0, tiled=True).T])
        gate_mine = lax.all_gather(gate_mine, "wshard", axis=0, tiled=True).T
        gate_out = (origin, [gate_mine, gather_out(low(out_weight), seq_index, groups)])
        out_places = origin
    hidden_low = lax.all_gather(hidden_rows, "seq", axis=0, tiled=True)
    cot_low = lax.all_gather(cot_rows, "seq", axis=0, tiled=True)
    my_gain_two = heads_of(gain_two, 0, HEADDIM)[None, :]
    my_kernel = jnp.concatenate([heads_of(kernel[:, :DI], 1, HEADDIM), kernel[:, DI:]], 1)
    my_bias = jnp.concatenate([heads_of(conv_bias[:DI], 0, HEADDIM), conv_bias[DI:]], 0)

    def on_lanes(values):
        return jnp.pad(values, (0, lanes - local_heads))[None, :]

    heads_vectors = (
        on_lanes(heads_of(a_log, 0, 1)),
        on_lanes(heads_of(dt_bias, 0, 1)),
        jnp.repeat(heads_of(d_skip, 0, 1), HEADDIM)[None, :],
    )
    expand = (
        jnp.arange(lanes)[:, None] == jnp.arange(local_di)[None, :] // HEADDIM
    ).astype(jnp.bfloat16)
    if rings:
        gate_out = ring_late(
            rest[0],
            gate_out_late,
            rest[1][1::2] + [my_kernel, my_bias[None, :], *heads_vectors, expand],
        )
    (
        rest_weight,
        unit_low,
        normed_low,
        conv_in,
        conv_pre,
        dt_raw,
        y_part,
        scanned,
        states,
    ) = run_forward(
        hidden_low, rest, gain_one[None, :], (my_kernel, my_bias[None, :]), heads_vectors, expand
    )
    gate_weight, out_low, gating, d_gnorm, sums = run_gate(
        gate_out, cot_low, normed_low, scanned, my_gain_two
    )
    middle = run_middle(
        out_places,
        scanned,
        gating,
        d_gnorm,
        cot_low,
        unit_low,
        [sums] + [swap(sums, "seq", mask) for mask in range(1, 4)],
        out_low,
        my_gain_two,
        gain_one[None, :],
        gate_weight,
    )
    block_part, d_gating, d_scanned, d_gain_two, d_gain_gate, *gate_out_grads = middle
    block_rows = lax.psum_scatter(block_part, "seq", scatter_dimension=0, tiled=True)
    if rings:
        gate_out_arrived = swap(gate_out_grads[1], "wshard", 1)
    d_rest, vec_rows, *rest_grads = run_backward(
        out_places,
        unit_low,
        conv_in,
        conv_pre,
        dt_raw,
        y_part,
        states,
        d_scanned,
        my_kernel,
        heads_vectors,
        expand,
        gain_one[None, :],
        rest_weight,
        d_gain_gate,
        d_gain_two,
    )
    near, far = seq_index % 2, seq_index // 2
    if rings:
        *gate_out_sums, rest_send = run_pair(
            gate_places,
            gate_out_grads[0],
            gate_out_arrived,
            [vec_rows],
            [rest_grads[1]],
            [block_rows],
        )
        rest_arrived = swap(rest_send, "wshard", 1)
        gate_out_pieces = [
            swap(gate_out_sums[mask], "wshard", 2 * mask) for mask in range(1, 4)
        ]
        normed_mine, normed_send = run_normed(
            near, d_gating, d_rest, gate_weight, rest_weight, [gate_out_sums[0]]
        )
        gate_out_part, normed_send = run_final(
            [gate_out_sums[0]] + gate_out_pieces, [normed_send], []
        )
        gate_out_near = swap(gate_out_part, "seq", 1)
        rest_sums = run_pair(
            gate_places, rest_grads[0], rest_arrived, [], [], [gate_out_near]
        )
        rest_pieces = [swap(rest_sums[mask], "wshard", 2 * mask) for mask in range(1, 4)]
        gate_out_far = swap(gate_out_part, "seq", 2)
    else:
        every = lax.all_gather(lax.psum(vec_rows, "wshard"), "seq", axis=0, tiled=False)
        normed_mine, normed_send = run_normed(
            near, d_gating, d_rest, gate_weight, rest_weight, []
        )
    normed_arrived = swap(normed_send, "seq", 1)
    normed_sum = normed_mine.astype(jnp.float32) + normed_arrived.astype(jnp.float32)
    normed_far = swap(low(take_block(normed_sum, 1 - far, rows_here)), "seq", 2)
    if rings:
        spots = [seq_index ^ mask for mask in range(4)]
        gate_out_blocks = [gate_out_part, gate_out_near, gate_out_far]
        gate_out_blocks = gate_out_blocks + [swap(gate_out_far, "seq", 1)]
        in_arrays = (in_weight.T, in_first.T, in_second.T)
        updated = run_update_gate(
            spots,
            gate_out_blocks,
            in_arrays,
            (out_weight, out_first, out_second),
            [rest_sums[0]],
        )
        out_first_new, out_second_new, out_weight_new, every = updated[3:]
        rest_part, every = run_final([rest_sums[0]] + rest_pieces, [every], [])
        every_there = swap(every, "wshard", 1)
        every = every.astype(jnp.float32) + every_there.astype(jnp.float32)
    block_out = hidden_rows.astype(jnp.float32) + block_rows.astype(jnp.float32)
    d_normed = take_block(normed_sum, far, rows_here) + normed_far.astype(jnp.float32)
    own_hidden = hidden_rows.astype(jnp.float32)
    own_scale = lax.rsqrt(jnp.mean(own_hidden * own_hidden, axis=-1, keepdims=True) + norm_eps)
    own_unit = own_hidden * own_scale
    d_own = d_normed * gain_one[None, :]
    d_hidden = own_scale * (
        d_own - own_unit * jnp.mean(d_own * own_unit, axis=-1, keepdims=True)
    )
    block_grad = cot_rows.astype(jnp.float32) + d_hidden
    if rings:
        spots, rest_blocks = seq_blocks(rest_part)
        updated = run_update_rest(spots, rest_blocks, in_arrays, updated[:3])
        in_first_new, in_second_new, in_weight_new = [array.T for array in updated]
    else:
        rest_part = lax.psum_scatter(rest_grads[0].T, "wshard", scatter_dimension=0, tiled=True)
        gate_part = lax.psum_scatter(gate_out_grads[0].T, "wshard", scatter_dimension=0, tiled=True)
        gate_every = lax.all_gather(gate_part, "seq", axis=0, tiled=False).astype(jnp.float32)
        rest_every = lax.all_gather(rest_part, "seq", axis=0, tiled=False).astype(jnp.float32)
        out_total = sum_out_grad(gate_out_grads[1], out_weight.shape[0], seq_index, groups)
        in_total = jnp.concatenate(
            [
                merge_heads(gate_every, 1, HEADDIM),
                merge_heads(rest_every[:, :, :local_di], 1, HEADDIM),
                jnp.sum(rest_every[:, :, local_di:channels], axis=0),
                merge_heads(rest_every[:, :, channels : channels + local_heads], 1, 1),
            ],
            1,
        )
        in_first_new, in_second_new, in_weight_new = adamw_step(
            in_weight, in_first, in_second, in_total, matrix_rate, matrix_decay
        )
        out_first_new, out_second_new, out_weight_new = adamw_step(
            out_weight, out_first, out_second, out_total, matrix_rate, matrix_decay
        )
    every = every.reshape(groups, VEC_ROWS * 128)
    cuts = [0, D]
    for extent in (WIDTH * channels, channels, local_di, local_di, lanes, lanes):
        cuts.append(cuts[-1] + extent)
    parts = [every[:, cuts[number] : cuts[number + 1]] for number in range(7)]
    kernel_every = parts[1].reshape(groups, WIDTH, channels)
    kernel_total = jnp.concatenate(
        [
            merge_heads(kernel_every[:, :, :local_di], 1, HEADDIM),
            jnp.sum(kernel_every[:, :, local_di:], axis=0),
        ],
        1,
    )
    skip_every = jnp.sum(parts[4].reshape(groups, local_heads, HEADDIM), axis=2)
    vec_total = jnp.concatenate(
        [
            jnp.sum(parts[0], axis=0),
            merge_heads(parts[3], 0, HEADDIM),
            kernel_total.reshape(-1),
            merge_heads(parts[2][:, :local_di], 0, HEADDIM),
            jnp.sum(parts[2][:, local_di:], axis=0),
            merge_heads(parts[5][:, :local_heads], 0, 1),
            merge_heads(parts[6][:, :local_heads], 0, 1),
            merge_heads(skip_every, 0, 1),
        ]
    )
    vec_first_new, vec_second_new, vec_weight_new = adamw_step(
        vec_weight, vec_first, vec_second, vec_total, vector_rate, 0.0
    )
    return (
        block_out.reshape(1, rows_here, D),
        block_grad.reshape(1, rows_here, D),
        in_first_new,
        in_second_new,
        in_weight_new,
        out_first_new,
        out_second_new,
        out_weight_new,
        vec_first_new,
        vec_second_new,
        vec_weight_new,
    )


def solution(mesh):
    return jax.shard_map(
        shards,
        mesh=mesh,
        in_specs=(
            P("wshard", "seq", None),
            P("wshard", "seq", None),
            P("wshard", None),
            P("wshard", None),
            P("wshard", None),
            P("wshard", None),
            P("wshard", None),
            P("wshard", None),
            P(),
            P(),
            P(),
        ),
        out_specs=(
            P("wshard", "seq", None),
            P("wshard", "seq", None),
            P("wshard", None),
            P("wshard", None),
            P("wshard", None),
            P("wshard", None),
            P("wshard", None),
            P("wshard", None),
            P(),
            P(),
            P(),
        ),
        check_vma=False,
    )
```

```python
import jax
import jax.numpy as jnp
from jax import lax
from jax.experimental import pallas as pl
from jax.experimental.pallas import tpu as pltpu
from jax.sharding import PartitionSpec as P

D = 1024
HEADS = 32
HEADDIM = 64
STATE = 128
WIDTH = 4
BLOCK = 256
STEP = 10
DI = 2048
CONVCH = 2304
VEC_ROWS = 48


norm_eps = 1e-05
beta_one = 0.9
beta_two = 0.95
adam_eps = 1e-08
matrix_rate = 0.05
matrix_decay = 0.1
vector_rate = 0.5


def rms_scale(values):
    return values * lax.rsqrt(jnp.mean(values * values, axis=-1, keepdims=True) + norm_eps)


def split_vector(vector):
    extents = [D, DI, WIDTH * CONVCH, CONVCH, HEADS, HEADS, HEADS]
    pieces = []
    offset = 0
    for extent in extents:
        pieces.append(vector[offset : offset + extent])
        offset = offset + extent
    pieces[2] = pieces[2].reshape(WIDTH, CONVCH)
    return pieces


def dot_nt(left, right, precision=None):
    return lax.dot_general(
        left,
        right,
        (((1,), (1,)), ((), ())),
        precision=precision,
        preferred_element_type=jnp.float32,
    )


def dot_tn(left, right):
    return lax.dot_general(
        left, right, (((0,), (0,)), ((), ())), preferred_element_type=jnp.float32
    )


def dot_nn(left, right, precision=None):
    return jnp.dot(left, right, precision=precision, preferred_element_type=jnp.float32)


def terms_of(values, count):
    terms = []
    for _ in range(count):
        terms.append(values.astype(jnp.bfloat16))
        values = values - terms[-1].astype(jnp.float32)
    return terms


def sum_terms(product, values, count):
    total = None
    for term in terms_of(values, count):
        total = product(term) if total is None else total + product(term)
    return total


def sigmoid(values):
    return 1.0 / (1.0 + jnp.exp(-values))


def low(values):
    return values.astype(jnp.bfloat16)


def lower_mask():
    rows = lax.broadcasted_iota(jnp.int32, (BLOCK, BLOCK), 0)
    return rows >= lax.broadcasted_iota(jnp.int32, (BLOCK, BLOCK), 1)


def decay_sums(dt_raw, dt_bias, a_log, expand):
    shifted = dt_raw + dt_bias
    step = jnp.maximum(shifted, 0.0) + jnp.log1p(jnp.exp(-jnp.abs(shifted)))
    log_decay = -jnp.exp(a_log) * step
    ones = low(jnp.where(lower_mask(), 1.0, 0.0))
    running = sum_terms(lambda term: dot_nn(ones, term), log_decay, 3)
    step_wide = sum_terms(lambda term: dot_nn(term, expand), step, 2)
    running_wide = sum_terms(lambda term: dot_nn(term, expand), running, 3)
    return shifted, step, log_decay, running, step_wide, running_wide


def place_rows(result_ref, place, block):
    rows = block.shape[0]
    result_ref[pl.ds(pl.multiple_of(place * rows, rows), rows), :] = block


def place_columns(result_ref, place, block):
    rows, columns = block.shape
    start = pl.multiple_of(place * columns, columns)
    result_ref[:rows, pl.ds(start, columns)] = block


def forward_kernel(rest_count, places_ref, *refs):
    rest_blocks = refs[:rest_count]
    (
        hidden_ref,
        gain_one_ref,
        conv_ref,
        bias_ref,
        a_log_ref,
        dt_bias_ref,
        skip_ref,
        expand_ref,
        rest_ref,
        unit_ref,
        normed_ref,
        conv_in_ref,
        conv_pre_ref,
        dt_ref,
        y_ref,
        scanned_ref,
        state_ref,
        ext,
        state,
    ) = refs[rest_count:]
    local_di = y_ref.shape[1]
    heads = local_di // HEADDIM
    channels = conv_in_ref.shape[1]

    @pl.when(pl.program_id(0) == 0)
    def _():
        ext[0:8, :] = jnp.zeros((8, ext.shape[1]), jnp.float32)
        state[...] = jnp.zeros_like(state)
        rest_ref[channels:, :] = jnp.zeros_like(rest_ref[channels:, :])
        for number, block in enumerate(rest_blocks):
            place_columns(rest_ref, places_ref[number], block[...])

    hidden = hidden_ref[...].astype(jnp.float32)
    unit = rms_scale(hidden)
    unit_ref[...] = low(unit)
    normed = low(unit * gain_one_ref[...])
    normed_ref[...] = normed
    conv_in = dot_nt(normed, rest_ref[:channels, :])
    conv_in_ref[...] = conv_in
    ext[8 : 8 + BLOCK, :] = conv_in
    conv_pre = bias_ref[...] + conv_ref[WIDTH - 1 : WIDTH, :] * conv_in
    for tap in range(WIDTH - 1):
        first = 8 - WIDTH + 1 + tap
        conv_pre = conv_pre + conv_ref[tap : tap + 1, :] * ext[first : first + BLOCK, :]
    conv_pre_ref[...] = conv_pre
    ext[8 - WIDTH + 1 : 8, :] = ext[8 + BLOCK - WIDTH + 1 : 8 + BLOCK, :]
    conv_low = low(conv_pre * sigmoid(conv_pre))
    inner = conv_low[:, :local_di]
    b_rows = conv_low[:, local_di : local_di + STATE]
    c_rows = conv_low[:, local_di + STATE :]
    dt_raw = low(dot_nt(normed, rest_ref[channels:, :])).astype(jnp.float32)
    dt_ref[...] = dt_raw

    _, _, _, running, step_wide, running_wide = decay_sums(
        dt_raw, dt_bias_ref[...], a_log_ref[...], expand_ref[...]
    )
    running_t = running.T
    b_t = low(b_rows.astype(jnp.float32).T)
    scores = dot_nn(c_rows, b_t)
    mask = lower_mask()
    inner_wide = inner.astype(jnp.float32)
    stepped = step_wide * inner_wide
    stepped_low = low(stepped)
    first_half = lax.broadcasted_iota(jnp.int32, (BLOCK, 2 * HEADDIM), 1) < HEADDIM
    zero = jnp.zeros((), jnp.bfloat16)
    state_ref[...] = state[...].reshape(state_ref.shape)
    held = state[...]
    carried = jnp.exp(running_wide) * dot_nn(c_rows, low(held))
    for pair in range(heads // 2):
        span = slice(pair * 2 * HEADDIM, (pair + 1) * 2 * HEADDIM)
        both = stepped_low[:, span]
        total = carried[:, span]
        for half in range(2):
            head = 2 * pair + half
            differ = running[:, head : head + 1] - running_t[head : head + 1, :]
            mixed = low(jnp.exp(jnp.where(mask, differ, -jnp.inf)) * scores)
            mine = jnp.where(first_half if half == 0 else ~first_half, both, zero)
            total = total + dot_nn(mixed, mine)
        y_ref[:, span] = total
    last = running_wide[BLOCK - 1 : BLOCK, :]
    to_end = jnp.exp(last - running_wide)
    state[...] = jnp.exp(last) * held + dot_nn(b_t, low(to_end * stepped))
    scanned_ref[...] = low(y_ref[...] + skip_ref[...] * inner_wide)


def gate_kernel(count, places_ref, *refs):
    blocks = refs[:count]
    (
        cot_ref,
        normed_ref,
        scanned_ref,
        gain_two_ref,
        gate_ref,
        out_ref,
        gating_ref,
        d_gnorm_ref,
        sums_ref,
    ) = refs[count:]
    local_di = gating_ref.shape[1]

    @pl.when(pl.program_id(0) == 0)
    def _():
        if count == 2:
            gate_ref[...] = blocks[0][...]
            out_ref[...] = blocks[1][...]
            return
        number = 0
        for block in blocks:
            columns = block.shape[1]
            for base in range(0, block.shape[0], 2 * local_di):
                spot = places_ref[number]
                number = number + 1
                place_columns(gate_ref, spot, block[base : base + local_di, :])
                for tile in range(D // columns):
                    first = base + local_di + tile * HEADDIM
                    span = slice(tile * columns, (tile + 1) * columns)
                    place_rows(out_ref.at[:, span], spot, block[first : first + HEADDIM, :])

    gating = dot_nt(normed_ref[...], gate_ref[...])
    gating_ref[...] = gating
    d_gnorm = dot_nt(cot_ref[...], out_ref[...])
    d_gnorm_ref[...] = d_gnorm
    gated = scanned_ref[...].astype(jnp.float32) * (gating * sigmoid(gating))
    ones = jnp.ones((8, local_di), jnp.bfloat16)
    squares = sum_terms(lambda term: dot_nt(ones, term), gated * gated, 2)
    products = d_gnorm * gain_two_ref[...] * gated
    products = sum_terms(lambda term: dot_nt(ones, term), products, 2)
    sums_ref[...] = jnp.where(
        lax.broadcasted_iota(jnp.int32, squares.shape, 0) == 0, squares, products
    )


def middle_kernel(count, places_ref, *refs):
    (
        scanned_ref,
        gating_ref,
        d_gnorm_ref,
        cot_ref,
        unit_ref,
        sums_one_ref,
        sums_two_ref,
        sums_three_ref,
        sums_four_ref,
        out_ref,
        gain_two_ref,
        gain_one_ref,
        gate_weight_ref,
        block_ref,
        d_gating_ref,
        d_scanned_ref,
        d_gain_two_ref,
        d_gain_one_ref,
    ) = refs[:18]
    grad_refs = refs[18 : 18 + count]
    out_sum, gate_sum = refs[18 + count :]
    chunk = pl.program_id(0)

    @pl.when(chunk == 0)
    def _():
        out_sum[...] = jnp.zeros_like(out_sum)
        gate_sum[...] = jnp.zeros_like(gate_sum)
        d_gain_two_ref[...] = jnp.zeros_like(d_gain_two_ref)

    sums = (sums_one_ref[...] + sums_two_ref[...]) + (sums_three_ref[...] + sums_four_ref[...])
    sums = (sums / DI).T
    scale = lax.rsqrt(sums[:, 0:1] + norm_eps)
    slope = scale * scale * sums[:, 1:2]
    gating = gating_ref[...]
    open_part = sigmoid(gating)
    gate = gating * open_part
    scanned = scanned_ref[...].astype(jnp.float32)
    unit = scanned * gate * scale
    d_gnorm = d_gnorm_ref[...]
    gain_two = gain_two_ref[...]
    gnorm = low(unit * gain_two)
    block_ref[...] = low(dot_nn(gnorm, out_ref[...]))
    out_sum[...] += dot_tn(gnorm, cot_ref[...])
    d_gain_two_ref[...] += jnp.sum(d_gnorm * unit, axis=0, keepdims=True)
    d_gated = scale * (d_gnorm * gain_two) - unit * slope
    d_gating = low(d_gated * scanned * (open_part * (1.0 + gating * (1.0 - open_part))))
    d_gating_ref[...] = d_gating
    d_scanned_ref[...] = low(d_gated * gate)
    gate_sum[...] += dot_tn(d_gating, unit_ref[...])

    @pl.when(chunk == pl.num_programs(0) - 1)
    def _():
        weights = gate_weight_ref[...].astype(jnp.float32)
        d_gain_one_ref[...] = jnp.sum(gate_sum[...] * weights, axis=0, keepdims=True)
        gate_sum[...] = gate_sum[...] * gain_one_ref[...]
        local_di = gate_sum.shape[0]
        if grad_refs[0].shape == gate_sum.shape:
            grad_refs[0][...] = low(gate_sum[...])
            grad_refs[1][...] = low(out_sum[...])
            return
        for number, grad_ref in enumerate(grad_refs):
            columns = grad_ref.shape[1]
            for step in range(D // columns // count):
                place = places_ref[number] + step * count
                start = pl.multiple_of(place * columns, columns)
                base = step * 2 * local_di
                grad_ref[base : base + local_di, :] = low(gate_sum[:, pl.ds(start, columns)])
                rows = pl.ds(pl.multiple_of(place * HEADDIM, HEADDIM), HEADDIM)
                for tile in range(D // columns):
                    first = base + local_di + tile * HEADDIM
                    grad_ref[first : first + HEADDIM, :] = low(
                        out_sum[rows, tile * columns : (tile + 1) * columns]
                    )


def backward_kernel(
    grad_count,
    places_ref,
    unit_ref,
    conv_in_ref,
    conv_pre_ref,
    dt_ref,
    y_ref,
    state_ref,
    d_scanned_ref,
    conv_ref,
    a_log_ref,
    dt_bias_ref,
    skip_ref,
    expand_ref,
    gain_one_ref,
    rest_weight_ref,
    d_gain_gate_ref,
    d_gain_two_ref,
    d_rest_ref,
    vec_ref,
    *refs,
):
    grad_refs = refs[:grad_count]
    ext, d_state, later_state, rest_sum = refs[grad_count : grad_count + 4]
    d_kernel_ref, d_conv_bias_ref, d_skip_ref, d_head_ref = refs[grad_count + 4 :]
    local_di = y_ref.shape[1]
    heads = local_di // HEADDIM
    chunk = pl.program_id(0)

    @pl.when(chunk == 0)
    def _():
        ext[BLOCK : BLOCK + 8, :] = jnp.zeros((8, ext.shape[1]), jnp.float32)
        d_state[...] = jnp.zeros_like(d_state)
        later_state[...] = jnp.zeros_like(later_state)
        rest_sum[...] = jnp.zeros_like(rest_sum)
        d_kernel_ref[...] = jnp.zeros_like(d_kernel_ref)
        d_conv_bias_ref[...] = jnp.zeros_like(d_conv_bias_ref)
        d_skip_ref[...] = jnp.zeros_like(d_skip_ref)
        d_head_ref[...] = jnp.zeros_like(d_head_ref)

    expand = expand_ref[...]
    conv_pre = conv_pre_ref[...]
    open_part = sigmoid(conv_pre)
    conv_low = low(conv_pre * open_part)
    inner = conv_low[:, :local_di].astype(jnp.float32)
    b_rows = conv_low[:, local_di : local_di + STATE]
    c_rows = conv_low[:, local_di + STATE :]
    a_log = a_log_ref[...]
    shifted, _, log_decay, running, step_wide, running_wide = decay_sums(
        dt_ref[...], dt_bias_ref[...], a_log, expand
    )
    running_t = running.T
    b_t = low(b_rows.astype(jnp.float32).T)
    c_t = low(c_rows.astype(jnp.float32).T)
    scores = dot_nn(c_rows, b_t)
    scores_t = dot_nn(b_rows, c_t)
    mask = lower_mask()
    rows = lax.broadcasted_iota(jnp.int32, (BLOCK, BLOCK), 0)
    mask_t = rows <= lax.broadcasted_iota(jnp.int32, (BLOCK, BLOCK), 1)
    d_y_low = d_scanned_ref[...]
    d_y = d_y_low.astype(jnp.float32)
    stepped_low = low(step_wide * inner)
    stepped = stepped_low.astype(jnp.float32)
    last = running_wide[BLOCK - 1 : BLOCK, :]
    to_end = jnp.exp(last - running_wide)
    d_later = d_state[...]
    d_later_low = low(d_later)
    held = state_ref[...].reshape(d_state.shape)
    decayed_dy = low(jnp.exp(running_wide) * d_y)
    d_c = dot_nt(decayed_dy, low(held))
    d_b = dot_nt(low(to_end * stepped), d_later_low)
    d_stepped = to_end * dot_nn(b_rows, d_later_low)
    cross = jnp.sum(later_state[...] * d_later, axis=0, keepdims=True)
    d_state[...] = jnp.exp(last) * d_later + dot_nn(c_t, decayed_dy)
    later_state[...] = held
    first_half = lax.broadcasted_iota(jnp.int32, (BLOCK, 2 * HEADDIM), 1) < HEADDIM
    zero = jnp.zeros((), jnp.bfloat16)
    d_scores = jnp.zeros((BLOCK, BLOCK), jnp.float32)
    pieces = []
    for pair in range(heads // 2):
        span = slice(pair * 2 * HEADDIM, (pair + 1) * 2 * HEADDIM)
        total = d_stepped[:, span]
        for half in range(2):
            head = 2 * pair + half
            mine = jnp.where(first_half if half == 0 else ~first_half, d_y_low[:, span], zero)
            column = running[:, head : head + 1]
            row = running_t[head : head + 1, :]
            decay = jnp.exp(jnp.where(mask, column - row, -jnp.inf))
            decay_t = jnp.exp(jnp.where(mask_t, row - column, -jnp.inf))
            d_scores = d_scores + dot_nt(mine, stepped_low[:, span]) * decay
            total = total + dot_nn(low(decay_t * scores_t), mine)
        pieces.append(total)
    d_stepped = jnp.concatenate(pieces, 1)
    d_scores_low = low(d_scores)
    d_c = d_c + dot_nn(d_scores_low, b_rows)
    d_b = d_b + dot_nn(low(d_scores.T), c_rows)
    d_inner = step_wide * d_stepped + skip_ref[...] * d_y
    d_running = d_y * y_ref[...] - d_stepped * stepped
    d_running = sum_terms(lambda term: dot_nt(term, expand), d_running, 2)
    upper = low(jnp.where(mask_t, 1.0, 0.0))
    d_log = sum_terms(lambda term: dot_nn(upper, term), d_running, 3)
    d_log = d_log + sum_terms(lambda term: dot_nt(term, expand), cross, 3)
    d_step = sum_terms(lambda term: dot_nt(term, expand), d_stepped * inner, 2)
    d_step = d_step - jnp.exp(a_log) * d_log
    d_dt = d_step * sigmoid(shifted)
    d_head_ref[0:1, :] += jnp.sum(d_log * log_decay, axis=0, keepdims=True)
    d_head_ref[1:2, :] += jnp.sum(d_dt, axis=0, keepdims=True)
    d_skip_ref[...] += jnp.sum(d_y * inner, axis=0, keepdims=True)

    d_conv_out = jnp.concatenate([d_inner, d_b, d_c], 1)
    d_pre = d_conv_out * (open_part * (1.0 + conv_pre * (1.0 - open_part)))
    ext[0:BLOCK, :] = d_pre
    d_conv_bias_ref[...] += jnp.sum(d_pre, axis=0, keepdims=True)
    conv_in = conv_in_ref[...]
    d_conv_in = jnp.zeros_like(conv_in)
    for tap in range(WIDTH):
        moved = ext[WIDTH - 1 - tap : WIDTH - 1 - tap + BLOCK, :]
        d_conv_in = d_conv_in + conv_ref[tap : tap + 1, :] * moved
        d_kernel_ref[tap : tap + 1, :] += jnp.sum(moved * conv_in, axis=0, keepdims=True)
    ext[BLOCK : BLOCK + 8, :] = ext[0:8, :]
    d_rest = jnp.concatenate([low(d_conv_in), low(d_dt)], 1)
    d_rest_ref[...] = d_rest
    rest_sum[...] += dot_tn(d_rest, unit_ref[...])

    @pl.when(chunk == pl.num_programs(0) - 1)
    def _():
        weights = rest_weight_ref[...].astype(jnp.float32)
        d_gain_one = jnp.sum(rest_sum[...] * weights, axis=0, keepdims=True)
        pieces = [d_gain_one + d_gain_gate_ref[...]]
        pieces = pieces + [d_kernel_ref[tap : tap + 1, :] for tap in range(WIDTH)]
        pieces = pieces + [d_conv_bias_ref[...], d_gain_two_ref[...], d_skip_ref[...]]
        pieces = pieces + [d_head_ref[0:1, :], d_head_ref[1:2, :]]
        row = 0
        for piece in pieces:
            for first in range(0, piece.shape[1], 128):
                vec_ref[row : row + 1, :] = piece[:, first : first + 128]
                row = row + 1
        rest_sum[...] = rest_sum[...] * gain_one_ref[...]
        for number, grad_ref in enumerate(grad_refs):
            columns = grad_ref.shape[1]
            blocks = rest_sum.shape[1] // columns // grad_count
            rows = grad_ref.shape[0] // blocks
            for step in range(blocks):
                place = places_ref[number] + step * grad_count
                start = pl.multiple_of(place * columns, columns)
                grad_ref[step * rows : (step + 1) * rows, :] = low(
                    rest_sum[:rows, pl.ds(start, columns)]
                )


def sum_of(*refs):
    total = refs[0][...].astype(jnp.float32)
    for ref in refs[1:]:
        total = total + ref[...].astype(jnp.float32)
    return total


def pair_kernel(count, extra, places_ref, mine_ref, arrived_ref, *refs):
    for ref in refs[extra + count : len(refs) - count]:
        if extra:
            ref[ref.shape[0] - VEC_ROWS :, :] = low(refs[0][...])
    for number, ref in enumerate(refs[extra + count : len(refs) - count]):
        rows = ref.shape[0] - extra * VEC_ROWS
        here = pl.ds(pl.multiple_of(places_ref[number] * rows, rows), rows)
        ref[:rows, :] = low(sum_of(mine_ref.at[here, :], arrived_ref.at[here, :]))


def hold_kernel(places_ref, *refs):
    rows = refs[0].shape[0]
    for number, ref in enumerate(refs[:-1]):
        refs[-1][number * rows : (number + 1) * rows, :] = ref[...]


def final_kernel(count, places_ref, one_ref, two_ref, three_ref, four_ref, *refs):
    refs[count][...] = low(sum_of(one_ref, two_ref) + sum_of(three_ref, four_ref))


def normed_kernel(
    places_ref, d_gating_ref, d_rest_ref, gate_weight_ref, rest_weight_ref, d_normed_ref
):
    d_normed = dot_nn(d_gating_ref[...], gate_weight_ref[...])
    d_normed_ref[...] = low(d_normed + dot_nn(d_rest_ref[...], rest_weight_ref[...]))


def prepare_kernel(places_ref, in_ref, out_ref, rest_ref, gate_out_ref):
    index = places_ref[0]
    local_di = gate_out_ref.shape[0] // 2
    groups = DI // local_di
    for head in range(HEADS // groups):
        rows = slice(head * HEADDIM, (head + 1) * HEADDIM)
        for base, result_ref in ((0, gate_out_ref), (DI, rest_ref)):
            start = pl.multiple_of(base + (groups * head + index) * HEADDIM, HEADDIM)
            result_ref[rows, :] = low(in_ref[pl.ds(start, HEADDIM), :])
    channels = local_di + 2 * STATE
    rest_ref[local_di:channels, :] = low(in_ref[2 * DI : 2 * DI + 2 * STATE, :])
    rows = rest_ref.shape[0] - channels
    target = lax.broadcasted_iota(jnp.int32, (rows, HEADS), 0)
    source = lax.broadcasted_iota(jnp.int32, (rows, HEADS), 1)
    chosen = (source == groups * target + index) & (target < HEADS // groups)
    steps = low(in_ref[DI + CONVCH :, :])
    rest_ref[channels:, :] = low(dot_nn(jnp.where(chosen, 1.0, 0.0).astype(jnp.bfloat16), steps))
    mine = pl.ds(pl.multiple_of(index * HEADDIM, HEADDIM), HEADDIM)
    columns = gate_out_ref.shape[1]
    for tile in range(D // columns):
        first = local_di + tile * HEADDIM
        gate_out_ref[first : first + HEADDIM, :] = low(
            out_ref[mine, tile * columns : (tile + 1) * columns]
        )


def adamw_store(old_refs, new_refs, rows, columns, grad):
    results = adamw_step(*[ref[rows, columns] for ref in old_refs], grad, matrix_rate, matrix_decay)
    for ref, result in zip(new_refs, results):
        ref[rows, columns] = result


def update_heads(old_refs, new_refs, source, part):
    groups = source.shape[0]
    heads = old_refs[0].shape[0] // HEADDIM // groups
    for head in range(heads):
        start = pl.multiple_of((part * heads + head) * HEADDIM, HEADDIM)
        for group in range(groups):
            first = (head * groups + group) * HEADDIM
            grad = source[group, pl.ds(start, HEADDIM), :].astype(jnp.float32)
            adamw_store(old_refs, new_refs, slice(first, first + HEADDIM), slice(None), grad)


def update_gate_kernel(groups, places_ref, *refs):
    blocks, in_refs, out_refs = refs[:groups], refs[groups : groups + 3], refs[groups + 3 : groups + 6]
    in_new_refs, out_new_refs = refs[groups + 6 : groups + 9], refs[groups + 9 : groups + 12]
    every_ref, gate_out = refs[groups + 12 :]
    chunk = pl.program_id(0)

    @pl.when(chunk == 0)
    def _():
        for number in range(groups):
            gate_out[places_ref[number]] = blocks[number][...]

    local_di = (gate_out.shape[1] - VEC_ROWS) // 2
    every_ref[...] = gate_out[:, 2 * local_di :, :]
    update_heads(in_refs, in_new_refs, gate_out, chunk)
    columns = gate_out.shape[2]
    for tile in range(D // columns):
        first = local_di + tile * HEADDIM
        grad = gate_out[chunk, first : first + HEADDIM, :].astype(jnp.float32)
        span = slice(tile * columns, (tile + 1) * columns)
        adamw_store(out_refs, out_new_refs, slice(None), span, grad)


def update_rest_kernel(groups, places_ref, *refs):
    blocks, in_refs = refs[:groups], refs[groups : groups + 3]
    in_new_refs, (rest,) = refs[groups + 6 : groups + 9], refs[groups + 9 :]
    chunk = pl.program_id(0)

    @pl.when(chunk == 0)
    def _():
        for number in range(groups):
            rest[places_ref[number]] = blocks[number][...]

    @pl.when(chunk < pl.num_programs(0) - 1)
    def _():
        update_heads(in_refs, in_new_refs, rest, chunk)

    @pl.when(chunk == pl.num_programs(0) - 1)
    def _():
        local_di = DI // groups
        channels = local_di + 2 * STATE
        both = rest[0, local_di:channels, :].astype(jnp.float32)
        rows = rest.shape[1] - channels
        steps = jnp.zeros((HEADS, rest.shape[2]), jnp.float32)
        target = lax.broadcasted_iota(jnp.int32, (HEADS, rows), 0)
        source = lax.broadcasted_iota(jnp.int32, (HEADS, rows), 1)
        for group in range(groups):
            if group > 0:
                both = both + rest[group, local_di:channels, :].astype(jnp.float32)
            chosen = jnp.where(target == groups * source + group, 1.0, 0.0).astype(jnp.bfloat16)
            steps = steps + dot_nn(chosen, rest[group, channels:, :])
        after_both = slice(2 * STATE, 2 * STATE + HEADS)
        adamw_store(in_refs, in_new_refs, slice(0, 2 * STATE), slice(None), both)
        adamw_store(in_refs, in_new_refs, after_both, slice(None), steps)


def kernel_params():
    return pltpu.CompilerParams(
        dimension_semantics=("arbitrary",), vmem_limit_bytes=56 * 1024 * 1024
    )


def cost(flops, moved, transcendentals):
    return pl.CostEstimate(flops=flops, bytes_accessed=moved, transcendentals=transcendentals)


def after(kernel, inputs, arrived):
    def run(*refs):
        kernel(*refs[:inputs], *refs[inputs + arrived :])

    return run


def corner(array):
    return pl.BlockSpec((min(16, array.shape[0]), 128), lambda *_: (0, 0))


def fixed(shape):
    return pl.BlockSpec(shape, lambda *_: (0,) * len(shape))


def rows_of(extent, first=0):
    return pl.BlockSpec((BLOCK, extent), lambda q, *_: (q + first, 0))


def struct(shape, dtype=jnp.float32):
    return jax.ShapeDtypeStruct(shape, dtype)


def call(
    kernel, places, inputs, in_specs, outputs, out_specs, scratch, grid, arrived, price, name, same=()
):
    return pl.pallas_call(
        after(kernel, 1 + len(inputs), len(arrived)),
        grid_spec=pltpu.PrefetchScalarGridSpec(
            num_scalar_prefetch=1,
            grid=(grid,),
            in_specs=list(in_specs) + [corner(array) for array in arrived],
            out_specs=out_specs,
            scratch_shapes=scratch,
        ),
        out_shape=outputs,
        input_output_aliases=dict(same),
        compiler_params=kernel_params(),
        cost_estimate=cost(*price),
        name=name,
    )(jnp.stack(places).astype(jnp.int32), *inputs, *arrived)


def run_prepare(index, in_t, out_weight):
    columns = in_t.shape[1]
    local_di = DI // 4
    shapes = [
        (local_di + 2 * STATE + 16, columns),
        (2 * local_di, columns),
    ]
    inputs = [in_t, out_weight]
    return call(
        prepare_kernel,
        [index],
        inputs,
        [fixed(array.shape) for array in inputs],
        [struct(shape, jnp.bfloat16) for shape in shapes],
        [fixed(shape) for shape in shapes],
        [],
        1,
        [],
        (100_000_000, 4_000_000, 0),
        "prepare",
    )


def run_forward(hidden, rest, gain_one, conv, heads_vectors, expand):
    places, blocks = rest
    length = hidden.shape[0]
    chunks = length // BLOCK
    lanes, local_di = expand.shape
    channels = local_di + 2 * STATE
    vectors = [gain_one, *conv, *heads_vectors, expand]
    return call(
        lambda *refs: forward_kernel(len(blocks), *refs),
        places,
        [*blocks, hidden, *vectors],
        [fixed(array.shape) for array in blocks]
        + [rows_of(D)]
        + [fixed(array.shape) for array in vectors],
        [
            struct((channels + lanes, D), jnp.bfloat16),
            struct((length, D), jnp.bfloat16),
            struct((length, D), jnp.bfloat16),
            struct((length, channels)),
            struct((length, channels)),
            struct((length, lanes)),
            struct((length, local_di)),
            struct((length, local_di), jnp.bfloat16),
            struct((chunks, STATE, local_di)),
        ],
        [
            fixed((channels + lanes, D)),
            rows_of(D),
            rows_of(D),
            rows_of(channels),
            rows_of(channels),
            rows_of(lanes),
            rows_of(local_di),
            rows_of(local_di),
            pl.BlockSpec((1, STATE, local_di), lambda q, *_: (q, 0, 0)),
        ],
        [
            pltpu.VMEM((8 + BLOCK, channels), jnp.float32),
            pltpu.VMEM((STATE, local_di), jnp.float32),
        ],
        chunks,
        [],
        (6_000_000_000, 30_000_000, 8_000_000),
        "forward",
    )


def run_gate(gate_out, cot, normed, scanned, gain_two):
    places, blocks = gate_out
    length, local_di = scanned.shape
    return call(
        lambda *refs: gate_kernel(len(blocks), *refs),
        places,
        [*blocks, cot, normed, scanned, gain_two],
        [fixed(array.shape) for array in blocks]
        + [rows_of(D), rows_of(D), rows_of(local_di), fixed((1, local_di))],
        [
            struct((local_di, D), jnp.bfloat16),
            struct((local_di, D), jnp.bfloat16),
            struct((length, local_di)),
            struct((length, local_di)),
            struct((8, length)),
        ],
        [
            fixed((local_di, D)),
            fixed((local_di, D)),
            rows_of(local_di),
            rows_of(local_di),
            pl.BlockSpec((8, BLOCK), lambda q, *_: (0, q)),
        ],
        [],
        length // BLOCK,
        [],
        (2_500_000_000, 12_000_000, 1_000_000),
        "gate",
    )


def run_middle(
    places, scanned, gating, d_gnorm, cot, unit, sums, out, gain_two, gain_one, gate_weight
):
    length, local_di = scanned.shape
    shapes = [(local_di, D)] * 2
    if len(places) > 1:
        shapes = [(2 * local_di * D // 256, 128)] * 2
    return call(
        lambda *refs: middle_kernel(2, *refs),
        places,
        [scanned, gating, d_gnorm, cot, unit, *sums, out, gain_two, gain_one, gate_weight],
        [
            rows_of(local_di),
            rows_of(local_di),
            rows_of(local_di),
            rows_of(D),
            rows_of(D),
        ]
        + [pl.BlockSpec((8, BLOCK), lambda q, *_: (0, q))] * 4
        + [fixed((local_di, D)), fixed((1, local_di)), fixed((1, D)), fixed((local_di, D))],
        [
            struct((length, D), jnp.bfloat16),
            struct((length, local_di), jnp.bfloat16),
            struct((length, local_di), jnp.bfloat16),
            struct((1, local_di)),
            struct((1, D)),
        ]
        + [struct(shape, jnp.bfloat16) for shape in shapes],
        [
            rows_of(D),
            rows_of(local_di),
            rows_of(local_di),
            fixed((1, local_di)),
            fixed((1, D)),
        ]
        + [fixed(shape) for shape in shapes],
        [pltpu.VMEM((local_di, D), jnp.float32), pltpu.VMEM((local_di, D), jnp.float32)],
        length // BLOCK,
        [],
        (4_000_000_000, 15_000_000, 500_000),
        "middle",
    )


def run_backward(
    places,
    unit,
    conv_in,
    conv_pre,
    dt_raw,
    y,
    states,
    d_scanned,
    kernel,
    heads_vectors,
    expand,
    gain_one,
    rest_weight,
    d_gain_gate,
    d_gain_two,
):
    length, local_di = y.shape
    chunks = length // BLOCK
    channels = conv_in.shape[1]
    lanes = expand.shape[0]
    grad = (channels + 16, D) if len(places) == 1 else ((channels + 16) * D // 256, 128)

    def back(extent):
        return pl.BlockSpec((BLOCK, extent), lambda q, *_: (chunks - 1 - q, 0))

    return call(
        lambda *refs: backward_kernel(len(places), *refs),
        places,
        [
            *[unit, conv_in, conv_pre, dt_raw, y, states, d_scanned, kernel],
            *[*heads_vectors, expand, gain_one, rest_weight, d_gain_gate, d_gain_two],
        ],
        [
            back(D),
            back(channels),
            back(channels),
            back(lanes),
            back(local_di),
            pl.BlockSpec((1, STATE, local_di), lambda q, *_: (chunks - 1 - q, 0, 0)),
            back(local_di),
            fixed((WIDTH, channels)),
            fixed((1, lanes)),
            fixed((1, lanes)),
            fixed((1, local_di)),
            fixed((lanes, local_di)),
            fixed((1, D)),
            fixed((channels + lanes, D)),
            fixed((1, D)),
            fixed((1, local_di)),
        ],
        [
            struct((length, channels + lanes), jnp.bfloat16),
            struct((VEC_ROWS, 128)),
        ]
        + [struct(grad, jnp.bfloat16)] * len(places),
        [
            back(channels + lanes),
            fixed((VEC_ROWS, 128)),
        ]
        + [fixed(grad)] * len(places),
        [
            pltpu.VMEM((BLOCK + 8, channels), jnp.float32),
            pltpu.VMEM((STATE, local_di), jnp.float32),
            pltpu.VMEM((STATE, local_di), jnp.float32),
            pltpu.VMEM((channels + lanes, D), jnp.float32),
            pltpu.VMEM((WIDTH, channels), jnp.float32),
            pltpu.VMEM((1, channels), jnp.float32),
            pltpu.VMEM((1, local_di), jnp.float32),
            pltpu.VMEM((2, lanes), jnp.float32),
        ],
        chunks,
        [],
        (14_000_000_000, 40_000_000, 10_000_000),
        "backward",
    )


def run_normed(d_gating, d_rest, gate_weight, rest_weight, arrived):
    length, local_di = d_gating.shape
    rest = d_rest.shape[1]
    return call(
        normed_kernel,
        [jnp.int32(0)],
        [d_gating, d_rest, gate_weight, rest_weight],
        [rows_of(local_di), rows_of(rest), fixed((local_di, D)), fixed((rest, D))],
        struct((length, D), jnp.bfloat16),
        rows_of(D),
        [],
        length // BLOCK,
        arrived,
        (3_000_000_000, 9_000_000, 1000),
        "normed",
    )


def run_pair(places, mine, arrived, extra, through, there):
    rows = mine.shape[0] // len(places) + len(extra) * VEC_ROWS
    block = (rows, mine.shape[1])
    inputs = [mine, arrived, *extra]
    untouched = [pl.BlockSpec(memory_space=pl.ANY)] * len(through)
    return call(
        lambda *refs: pair_kernel(len(through), len(extra), *refs),
        places,
        [*inputs, *through],
        [fixed(array.shape) for array in inputs] + untouched,
        [struct(block, jnp.bfloat16)] * len(places)
        + [struct(array.shape, array.dtype) for array in through],
        [fixed(block)] * len(places) + untouched,
        [],
        1,
        there,
        (2_000_000, 3_000_000, 0),
        "pair",
        [(1 + len(inputs) + number, len(places) + number) for number in range(len(through))],
    )


def run_hold(places, blocks, there):
    rows, columns = blocks[0].shape
    shape = (rows * len(blocks), columns)
    return call(
        hold_kernel,
        places,
        blocks,
        [fixed(block.shape) for block in blocks],
        struct(shape, blocks[0].dtype),
        fixed(shape),
        [],
        1,
        there,
        (0, 2_000_000, 0),
        "hold",
    )


def run_final(terms, through, there):
    untouched = [pl.BlockSpec(memory_space=pl.ANY)] * len(through)
    return call(
        lambda *refs: final_kernel(len(through), *refs),
        [jnp.int32(0)],
        [*terms, *through],
        [fixed(array.shape) for array in terms] + untouched,
        [struct(terms[0].shape, jnp.bfloat16)]
        + [struct(array.shape, array.dtype) for array in through],
        [fixed(terms[0].shape)] + untouched,
        [],
        1,
        there,
        (500_000, 1_000_000, 0),
        "final",
        [(1 + len(terms) + number, 1 + number) for number in range(len(through))],
    )


def run_update_gate(places, blocks, in_arrays, out_arrays, there):
    groups = len(places)
    rows_out = out_arrays[0].shape[0] // groups
    arrays = [*in_arrays, *out_arrays]
    in_spec = pl.BlockSpec((DI // groups, in_arrays[0].shape[1]), lambda q, *_: (q, 0))
    out_spec = pl.BlockSpec((rows_out, D), lambda q, *_: (q, 0))
    specs = [in_spec] * 3 + [out_spec] * 3
    return call(
        lambda *refs: update_gate_kernel(groups, *refs),
        places,
        [*blocks, *arrays],
        [fixed(array.shape) for array in blocks] + specs,
        [struct(array.shape) for array in arrays]
        + [struct((groups, VEC_ROWS, 128), jnp.bfloat16)],
        specs + [fixed((groups, VEC_ROWS, 128))],
        [pltpu.VMEM((groups,) + blocks[0].shape, jnp.bfloat16)],
        groups,
        there,
        (10_000_000, 13_000_000, 500_000),
        "update_gate",
    )


def run_update_rest(places, blocks, in_arrays, so_far):
    groups = len(places)
    spec = pl.BlockSpec((DI // groups, in_arrays[0].shape[1]), lambda q, *_: (q + groups, 0))
    return call(
        lambda *refs: update_rest_kernel(groups, *refs),
        places,
        [*blocks, *in_arrays, *so_far],
        [fixed(array.shape) for array in blocks]
        + [spec] * 3
        + [pl.BlockSpec(memory_space=pl.ANY)] * 3,
        [struct(array.shape) for array in in_arrays],
        [spec] * 3,
        [pltpu.VMEM((groups,) + blocks[0].shape, jnp.bfloat16)],
        groups + 1,
        [],
        (10_000_000, 8_000_000, 500_000),
        "update_rest",
        [(1 + groups + 3 + number, number) for number in range(3)],
    )


def adamw_step(weight, first, second, grad, rate, decay):
    first_new = beta_one * first + (1.0 - beta_one) * grad
    second_new = beta_two * second + (1.0 - beta_two) * grad * grad
    fix_one = 1.0 - beta_one**STEP
    fix_two = 1.0 - beta_two**STEP
    normalized = first_new / fix_one / (jnp.sqrt(second_new / fix_two) + adam_eps)
    return (first_new, second_new, weight - rate * (normalized + decay * weight))


def pick_heads(values, axis, width, index, groups):
    shape = values.shape
    split = shape[:axis] + (HEADS // groups, groups, width) + shape[axis + 1 :]
    taken = lax.dynamic_index_in_dim(values.reshape(split), index, axis + 1, keepdims=False)
    return taken.reshape(shape[:axis] + (HEADS // groups * width,) + shape[axis + 1 :])


def merge_heads(stacked, axis, width):
    groups = stacked.shape[0]
    shape = stacked.shape[1:]
    split = (groups,) + shape[:axis] + (HEADS // groups, width) + shape[axis + 1 :]
    moved = jnp.moveaxis(stacked.reshape(split), 0, axis + 1)
    return moved.reshape(shape[:axis] + (HEADS * width,) + shape[axis + 1 :])


def swap(values, axis, mask):
    route = [(i, i ^ mask) for i in range(lax.axis_size(axis))]
    return lax.ppermute(values, axis, route)


def seq_blocks(rows, far=None):
    index = lax.axis_index("seq")
    far = swap(rows, "seq", 2) if far is None else far
    blocks = [rows, swap(rows, "seq", 1), far, swap(far, "seq", 1)]
    return [index ^ mask for mask in range(4)], blocks


def ring_step(held):
    count = lax.axis_size("wshard")
    return lax.ppermute(held, "wshard", [(i, (i + 2) % count) for i in range(count)])


def ring_blocks(rows):
    count = lax.axis_size("wshard")
    index = lax.axis_index("wshard")
    places, blocks = [], []
    for step in range(count // 2):
        source = (index + count - 2 * step) % count
        places = places + [source, source ^ 1]
        blocks = blocks + [rows, swap(rows, "wshard", 1)]
        if step < count // 2 - 1:
            rows = ring_step(rows)
    return places, blocks


def ring_late(hold_places, rows, arrived):
    count = lax.axis_size("wshard")
    index = lax.axis_index("wshard")
    places = [(index + count - 2 * step) % count for step in range(count // 2)]
    blocks = [rows]
    for _ in range(count // 2 - 1):
        blocks = blocks + [ring_step(blocks[-1])]
    swapped = swap(run_hold(hold_places, blocks, arrived), "wshard", 1)
    return places + [place ^ 1 for place in places], blocks + [swapped]


def take_block(values, index, rows):
    return lax.dynamic_slice_in_dim(values, index * rows, rows, 0)


def gather_out(out_low, seq_index, groups):
    rows = out_low.shape[0]
    if rows % (groups * HEADDIM) == 0:
        mine = pick_rows(out_low, seq_index, groups)
        return lax.all_gather(mine, "wshard", axis=0, tiled=True)
    whole = lax.all_gather(out_low, "wshard", axis=0, tiled=True)
    return pick_heads(whole, 0, HEADDIM, seq_index, groups)


def pick_rows(values, seq_index, groups):
    rows = values.shape[0]
    split = values.reshape(rows // (groups * HEADDIM), groups, HEADDIM, values.shape[1])
    return lax.dynamic_index_in_dim(split, seq_index, 1, keepdims=False).reshape(
        rows // groups, values.shape[1]
    )


def sum_out_grad(grad, rows, seq_index, groups):
    grad = grad.astype(jnp.bfloat16)
    if rows % (groups * HEADDIM) == 0:
        mine = lax.psum_scatter(grad, "wshard", scatter_dimension=0, tiled=True)
        every = lax.all_gather(mine, "seq", axis=0, tiled=False)
        split = every.reshape(groups, rows // (groups * HEADDIM), HEADDIM, grad.shape[1])
        return jnp.moveaxis(split, 0, 1).reshape(rows, grad.shape[1]).astype(jnp.float32)
    blocks = grad.reshape(HEADS // groups, 1, HEADDIM, grad.shape[1])
    here = (jnp.arange(groups) == seq_index)[None, :, None, None]
    spread = jnp.where(here, blocks, jnp.zeros((), jnp.bfloat16)).reshape(DI, grad.shape[1])
    mine = lax.psum_scatter(spread, "wshard", scatter_dimension=0, tiled=True)
    return lax.psum(mine.astype(jnp.float32), "seq")


def shards(
    block_in,
    cotangent,
    in_weight,
    in_first,
    in_second,
    out_weight,
    out_first,
    out_second,
    vec_weight,
    vec_first,
    vec_second,
):
    rows_here = block_in.shape[1]
    groups = lax.axis_size("seq")
    seq_index = lax.axis_index("seq")
    local_heads = HEADS // groups
    local_di = DI // groups
    hidden_rows = block_in.reshape(rows_here, D)
    cot_rows = cotangent.reshape(rows_here, D)
    gain_one, gain_two, kernel, conv_bias, a_log, dt_bias, d_skip = split_vector(vec_weight)

    def heads_of(values, axis, width):
        return pick_heads(values, axis, width, seq_index, groups)

    lanes = 128
    channels = local_di + 2 * STATE
    shard_index = lax.axis_index("wshard")
    rings = lax.axis_size("wshard") == 8
    if rings:
        y, z = shard_index % 2, shard_index // 2
        rest_mine, gate_out_mine = run_prepare(seq_index, in_weight.T, out_weight)
        rest = ring_blocks(rest_mine)
        gate_out_late = gate_out_mine
        gate_places = [z ^ mask for mask in range(4)]
        out_places = [y, 1 - y]
    else:
        in_low = low(in_weight)
        steps_mine = heads_of(in_low[:, DI + CONVCH :], 1, 1)
        rest_mine = jnp.concatenate(
            [
                heads_of(in_low[:, DI : 2 * DI], 1, HEADDIM),
                in_low[:, 2 * DI : 2 * DI + 2 * STATE],
                jnp.pad(steps_mine, ((0, 0), (0, 16 - local_heads))),
            ],
            1,
        )
        gate_mine = heads_of(in_low[:, :DI], 1, HEADDIM)
        origin = [jnp.int32(0)]
        rest = (origin, [lax.all_gather(rest_mine, "wshard", axis=0, tiled=True).T])
        gate_mine = lax.all_gather(gate_mine, "wshard", axis=0, tiled=True).T
        gate_out = (origin, [gate_mine, gather_out(low(out_weight), seq_index, groups)])
        out_places = origin
    hidden_low = lax.all_gather(hidden_rows, "seq", axis=0, tiled=True)
    cot_low = lax.all_gather(cot_rows, "seq", axis=0, tiled=True)
    my_gain_two = heads_of(gain_two, 0, HEADDIM)[None, :]
    my_kernel = jnp.concatenate([heads_of(kernel[:, :DI], 1, HEADDIM), kernel[:, DI:]], 1)
    my_bias = jnp.concatenate([heads_of(conv_bias[:DI], 0, HEADDIM), conv_bias[DI:]], 0)

    def on_lanes(values):
        return jnp.pad(values, (0, lanes - local_heads))[None, :]

    heads_vectors = (
        on_lanes(heads_of(a_log, 0, 1)),
        on_lanes(heads_of(dt_bias, 0, 1)),
        jnp.repeat(heads_of(d_skip, 0, 1), HEADDIM)[None, :],
    )
    expand = (
        jnp.arange(lanes)[:, None] == jnp.arange(local_di)[None, :] // HEADDIM
    ).astype(jnp.bfloat16)
    if rings:
        gate_out = ring_late(
            rest[0],
            gate_out_late,
            rest[1][1::2] + [my_kernel, my_bias[None, :], *heads_vectors, expand],
        )
    (
        rest_weight,
        unit_low,
        normed_low,
        conv_in,
        conv_pre,
        dt_raw,
        y_part,
        scanned,
        states,
    ) = run_forward(
        hidden_low, rest, gain_one[None, :], (my_kernel, my_bias[None, :]), heads_vectors, expand
    )
    gate_weight, out_low, gating, d_gnorm, sums = run_gate(
        gate_out, cot_low, normed_low, scanned, my_gain_two
    )
    middle = run_middle(
        out_places,
        scanned,
        gating,
        d_gnorm,
        cot_low,
        unit_low,
        [sums] + [swap(sums, "seq", mask) for mask in range(1, 4)],
        out_low,
        my_gain_two,
        gain_one[None, :],
        gate_weight,
    )
    block_part, d_gating, d_scanned, d_gain_two, d_gain_gate, *gate_out_grads = middle
    block_rows = lax.psum_scatter(block_part, "seq", scatter_dimension=0, tiled=True)
    if rings:
        gate_out_arrived = swap(gate_out_grads[1], "wshard", 1)
    d_rest, vec_rows, *rest_grads = run_backward(
        out_places,
        unit_low,
        conv_in,
        conv_pre,
        dt_raw,
        y_part,
        states,
        d_scanned,
        my_kernel,
        heads_vectors,
        expand,
        gain_one[None, :],
        rest_weight,
        d_gain_gate,
        d_gain_two,
    )
    if rings:
        *gate_out_sums, rest_send = run_pair(
            gate_places,
            gate_out_grads[0],
            gate_out_arrived,
            [vec_rows],
            [rest_grads[1]],
            [],
        )
        rest_arrived = swap(rest_send, "wshard", 1)
        gate_out_pieces = [
            swap(gate_out_sums[mask], "wshard", 2 * mask) for mask in range(1, 4)
        ]
        d_normed_part = run_normed(
            d_gating, d_rest, gate_weight, rest_weight, [gate_out_sums[0], block_rows]
        )
        rest_sums = run_pair(
            gate_places, rest_grads[0], rest_arrived, [], [], [d_normed_part]
        )
        rest_pieces = [swap(rest_sums[mask], "wshard", 2 * mask) for mask in range(1, 4)]
        gate_out_part, d_normed_part = run_final(
            [gate_out_sums[0]] + gate_out_pieces, [d_normed_part], [rest_sums[0]]
        )
        d_normed = lax.psum_scatter(d_normed_part, "seq", scatter_dimension=0, tiled=True)
        rest_part, gate_out_part = run_final(
            [rest_sums[0]] + rest_pieces, [gate_out_part], []
        )
    else:
        every = lax.all_gather(lax.psum(vec_rows, "wshard"), "seq", axis=0, tiled=False)
        d_normed_part = run_normed(d_gating, d_rest, gate_weight, rest_weight, [])
        d_normed = lax.psum_scatter(d_normed_part, "seq", scatter_dimension=0, tiled=True)
    if rings:
        spots, gate_out_blocks = seq_blocks(gate_out_part)
        in_arrays = (in_weight.T, in_first.T, in_second.T)
        updated = run_update_gate(
            spots,
            gate_out_blocks,
            in_arrays,
            (out_weight, out_first, out_second),
            [],
        )
        out_first_new, out_second_new, out_weight_new, every = updated[3:]
        every_there = swap(every, "wshard", 1)
        every = every.astype(jnp.float32) + every_there.astype(jnp.float32)
    block_out = hidden_rows.astype(jnp.float32) + block_rows.astype(jnp.float32)
    d_normed = d_normed.astype(jnp.float32)
    own_hidden = hidden_rows.astype(jnp.float32)
    own_scale = lax.rsqrt(jnp.mean(own_hidden * own_hidden, axis=-1, keepdims=True) + norm_eps)
    own_unit = own_hidden * own_scale
    d_own = d_normed * gain_one[None, :]
    d_hidden = own_scale * (
        d_own - own_unit * jnp.mean(d_own * own_unit, axis=-1, keepdims=True)
    )
    block_grad = cot_rows.astype(jnp.float32) + d_hidden
    if rings:
        spots, rest_blocks = seq_blocks(rest_part)
        updated = run_update_rest(spots, rest_blocks, in_arrays, updated[:3])
        in_first_new, in_second_new, in_weight_new = [array.T for array in updated]
    else:
        rest_part = lax.psum_scatter(rest_grads[0].T, "wshard", scatter_dimension=0, tiled=True)
        gate_part = lax.psum_scatter(gate_out_grads[0].T, "wshard", scatter_dimension=0, tiled=True)
        gate_every = lax.all_gather(gate_part, "seq", axis=0, tiled=False).astype(jnp.float32)
        rest_every = lax.all_gather(rest_part, "seq", axis=0, tiled=False).astype(jnp.float32)
        out_total = sum_out_grad(gate_out_grads[1], out_weight.shape[0], seq_index, groups)
        in_total = jnp.concatenate(
            [
                merge_heads(gate_every, 1, HEADDIM),
                merge_heads(rest_every[:, :, :local_di], 1, HEADDIM),
                jnp.sum(rest_every[:, :, local_di:channels], axis=0),
                merge_heads(rest_every[:, :, channels : channels + local_heads], 1, 1),
            ],
            1,
        )
        in_first_new, in_second_new, in_weight_new = adamw_step(
            in_weight, in_first, in_second, in_total, matrix_rate, matrix_decay
        )
        out_first_new, out_second_new, out_weight_new = adamw_step(
            out_weight, out_first, out_second, out_total, matrix_rate, matrix_decay
        )
    every = every.reshape(groups, VEC_ROWS * 128)
    cuts = [0, D]
    for extent in (WIDTH * channels, channels, local_di, local_di, lanes, lanes):
        cuts.append(cuts[-1] + extent)
    parts = [every[:, cuts[number] : cuts[number + 1]] for number in range(7)]
    kernel_every = parts[1].reshape(groups, WIDTH, channels)
    kernel_total = jnp.concatenate(
        [
            merge_heads(kernel_every[:, :, :local_di], 1, HEADDIM),
            jnp.sum(kernel_every[:, :, local_di:], axis=0),
        ],
        1,
    )
    skip_every = jnp.sum(parts[4].reshape(groups, local_heads, HEADDIM), axis=2)
    vec_total = jnp.concatenate(
        [
            jnp.sum(parts[0], axis=0),
            merge_heads(parts[3], 0, HEADDIM),
            kernel_total.reshape(-1),
            merge_heads(parts[2][:, :local_di], 0, HEADDIM),
            jnp.sum(parts[2][:, local_di:], axis=0),
            merge_heads(parts[5][:, :local_heads], 0, 1),
            merge_heads(parts[6][:, :local_heads], 0, 1),
            merge_heads(skip_every, 0, 1),
        ]
    )
    vec_first_new, vec_second_new, vec_weight_new = adamw_step(
        vec_weight, vec_first, vec_second, vec_total, vector_rate, 0.0
    )
    return (
        block_out.reshape(1, rows_here, D),
        block_grad.reshape(1, rows_here, D),
        in_first_new,
        in_second_new,
        in_weight_new,
        out_first_new,
        out_second_new,
        out_weight_new,
        vec_first_new,
        vec_second_new,
        vec_weight_new,
    )


def solution(mesh):
    return jax.shard_map(
        shards,
        mesh=mesh,
        in_specs=(
            P("wshard", "seq", None),
            P("wshard", "seq", None),
            P("wshard", None),
            P("wshard", None),
            P("wshard", None),
            P("wshard", None),
            P("wshard", None),
            P("wshard", None),
            P(),
            P(),
            P(),
        ),
        out_specs=(
            P("wshard", "seq", None),
            P("wshard", "seq", None),
            P("wshard", None),
            P("wshard", None),
            P("wshard", None),
            P("wshard", None),
            P("wshard", None),
            P("wshard", None),
            P(),
            P(),
            P(),
        ),
        check_vma=False,
    )
```

```python
import jax
import jax.numpy as jnp
from jax import lax
from jax.experimental import pallas as pl
from jax.experimental.pallas import tpu as pltpu
from jax.sharding import PartitionSpec as P

D = 1024
HEADS = 32
HEADDIM = 64
STATE = 128
WIDTH = 4
BLOCK = 256
STEP = 10
DI = 2048
CONVCH = 2304
VEC_ROWS = 48


norm_eps = 1e-05
beta_one = 0.9
beta_two = 0.95
adam_eps = 1e-08
matrix_rate = 0.05
matrix_decay = 0.1
vector_rate = 0.5


def rms_scale(values):
    return values * lax.rsqrt(jnp.mean(values * values, axis=-1, keepdims=True) + norm_eps)


def split_vector(vector):
    extents = [D, DI, WIDTH * CONVCH, CONVCH, HEADS, HEADS, HEADS]
    pieces = []
    offset = 0
    for extent in extents:
        pieces.append(vector[offset : offset + extent])
        offset = offset + extent
    pieces[2] = pieces[2].reshape(WIDTH, CONVCH)
    return pieces


def dot_nt(left, right, precision=None):
    return lax.dot_general(
        left,
        right,
        (((1,), (1,)), ((), ())),
        precision=precision,
        preferred_element_type=jnp.float32,
    )


def dot_tn(left, right):
    return lax.dot_general(
        left, right, (((0,), (0,)), ((), ())), preferred_element_type=jnp.float32
    )


def dot_nn(left, right, precision=None):
    return jnp.dot(left, right, precision=precision, preferred_element_type=jnp.float32)


def terms_of(values, count):
    terms = []
    for _ in range(count):
        terms.append(values.astype(jnp.bfloat16))
        values = values - terms[-1].astype(jnp.float32)
    return terms


def sum_terms(product, values, count):
    total = None
    for term in terms_of(values, count):
        total = product(term) if total is None else total + product(term)
    return total


def sigmoid(values):
    return 1.0 / (1.0 + jnp.exp(-values))


def low(values):
    return values.astype(jnp.bfloat16)


def lower_mask():
    rows = lax.broadcasted_iota(jnp.int32, (BLOCK, BLOCK), 0)
    return rows >= lax.broadcasted_iota(jnp.int32, (BLOCK, BLOCK), 1)


def decay_sums(dt_raw, dt_bias, a_log, expand):
    shifted = dt_raw + dt_bias
    step = jnp.maximum(shifted, 0.0) + jnp.log1p(jnp.exp(-jnp.abs(shifted)))
    log_decay = -jnp.exp(a_log) * step
    ones = low(jnp.where(lower_mask(), 1.0, 0.0))
    running = sum_terms(lambda term: dot_nn(ones, term), log_decay, 3)
    step_wide = sum_terms(lambda term: dot_nn(term, expand), step, 2)
    running_wide = sum_terms(lambda term: dot_nn(term, expand), running, 3)
    return shifted, step, log_decay, running, step_wide, running_wide


def place_rows(result_ref, place, block):
    rows = block.shape[0]
    result_ref[pl.ds(pl.multiple_of(place * rows, rows), rows), :] = block


def place_columns(result_ref, place, block):
    rows, columns = block.shape
    start = pl.multiple_of(place * columns, columns)
    result_ref[:rows, pl.ds(start, columns)] = block


def forward_kernel(rest_count, places_ref, *refs):
    rest_blocks = refs[:rest_count]
    (
        hidden_ref,
        gain_one_ref,
        conv_ref,
        bias_ref,
        a_log_ref,
        dt_bias_ref,
        skip_ref,
        expand_ref,
        rest_ref,
        unit_ref,
        normed_ref,
        conv_in_ref,
        conv_pre_ref,
        dt_ref,
        y_ref,
        scanned_ref,
        state_ref,
        ext,
        state,
    ) = refs[rest_count:]
    local_di = y_ref.shape[1]
    heads = local_di // HEADDIM
    channels = conv_in_ref.shape[1]

    @pl.when(pl.program_id(0) == 0)
    def _():
        ext[0:8, :] = jnp.zeros((8, ext.shape[1]), jnp.float32)
        state[...] = jnp.zeros_like(state)
        rest_ref[channels:, :] = jnp.zeros_like(rest_ref[channels:, :])
        for number, block in enumerate(rest_blocks):
            place_columns(rest_ref, places_ref[number], block[...])

    hidden = hidden_ref[...].astype(jnp.float32)
    unit = rms_scale(hidden)
    unit_ref[...] = low(unit)
    normed = low(unit * gain_one_ref[...])
    normed_ref[...] = normed
    conv_in = dot_nt(normed, rest_ref[:channels, :])
    conv_in_ref[...] = conv_in
    ext[8 : 8 + BLOCK, :] = conv_in
    conv_pre = bias_ref[...] + conv_ref[WIDTH - 1 : WIDTH, :] * conv_in
    for tap in range(WIDTH - 1):
        first = 8 - WIDTH + 1 + tap
        conv_pre = conv_pre + conv_ref[tap : tap + 1, :] * ext[first : first + BLOCK, :]
    conv_pre_ref[...] = conv_pre
    ext[8 - WIDTH + 1 : 8, :] = ext[8 + BLOCK - WIDTH + 1 : 8 + BLOCK, :]
    conv_low = low(conv_pre * sigmoid(conv_pre))
    inner = conv_low[:, :local_di]
    b_rows = conv_low[:, local_di : local_di + STATE]
    c_rows = conv_low[:, local_di + STATE :]
    dt_raw = low(dot_nt(normed, rest_ref[channels:, :])).astype(jnp.float32)
    dt_ref[...] = dt_raw

    _, _, _, running, step_wide, running_wide = decay_sums(
        dt_raw, dt_bias_ref[...], a_log_ref[...], expand_ref[...]
    )
    running_t = running.T
    b_t = low(b_rows.astype(jnp.float32).T)
    scores = dot_nn(c_rows, b_t)
    mask = lower_mask()
    inner_wide = inner.astype(jnp.float32)
    stepped = step_wide * inner_wide
    stepped_low = low(stepped)
    first_half = lax.broadcasted_iota(jnp.int32, (BLOCK, 2 * HEADDIM), 1) < HEADDIM
    zero = jnp.zeros((), jnp.bfloat16)
    state_ref[...] = state[...].reshape(state_ref.shape)
    held = state[...]
    carried = jnp.exp(running_wide) * dot_nn(c_rows, low(held))
    for pair in range(heads // 2):
        span = slice(pair * 2 * HEADDIM, (pair + 1) * 2 * HEADDIM)
        both = stepped_low[:, span]
        total = carried[:, span]
        for half in range(2):
            head = 2 * pair + half
            differ = running[:, head : head + 1] - running_t[head : head + 1, :]
            mixed = low(jnp.exp(jnp.where(mask, differ, -jnp.inf)) * scores)
            mine = jnp.where(first_half if half == 0 else ~first_half, both, zero)
            total = total + dot_nn(mixed, mine)
        y_ref[:, span] = total
    last = running_wide[BLOCK - 1 : BLOCK, :]
    to_end = jnp.exp(last - running_wide)
    state[...] = jnp.exp(last) * held + dot_nn(b_t, low(to_end * stepped))
    scanned_ref[...] = low(y_ref[...] + skip_ref[...] * inner_wide)


def gate_kernel(count, places_ref, *refs):
    blocks = refs[:count]
    (
        cot_ref,
        normed_ref,
        scanned_ref,
        gain_two_ref,
        gate_ref,
        out_ref,
        gating_ref,
        d_gnorm_ref,
        sums_ref,
    ) = refs[count:]
    local_di = gating_ref.shape[1]

    @pl.when(pl.program_id(0) == 0)
    def _():
        if count == 2:
            gate_ref[...] = blocks[0][...]
            out_ref[...] = blocks[1][...]
            return
        number = 0
        for block in blocks:
            columns = block.shape[1]
            for base in range(0, block.shape[0], 2 * local_di):
                spot = places_ref[number]
                number = number + 1
                place_columns(gate_ref, spot, block[base : base + local_di, :])
                for tile in range(D // columns):
                    first = base + local_di + tile * HEADDIM
                    span = slice(tile * columns, (tile + 1) * columns)
                    place_rows(out_ref.at[:, span], spot, block[first : first + HEADDIM, :])

    gating = dot_nt(normed_ref[...], gate_ref[...])
    gating_ref[...] = gating
    d_gnorm = dot_nt(cot_ref[...], out_ref[...])
    d_gnorm_ref[...] = d_gnorm
    gated = scanned_ref[...].astype(jnp.float32) * (gating * sigmoid(gating))
    ones = jnp.ones((8, local_di), jnp.bfloat16)
    squares = sum_terms(lambda term: dot_nt(ones, term), gated * gated, 2)
    products = d_gnorm * gain_two_ref[...] * gated
    products = sum_terms(lambda term: dot_nt(ones, term), products, 2)
    sums_ref[...] = jnp.where(
        lax.broadcasted_iota(jnp.int32, squares.shape, 0) == 0, squares, products
    )


def middle_kernel(count, places_ref, *refs):
    (
        scanned_ref,
        gating_ref,
        d_gnorm_ref,
        cot_ref,
        unit_ref,
        sums_one_ref,
        sums_two_ref,
        sums_three_ref,
        sums_four_ref,
        out_ref,
        gain_two_ref,
        gain_one_ref,
        gate_weight_ref,
        block_ref,
        d_gating_ref,
        d_scanned_ref,
        d_gain_two_ref,
        d_gain_one_ref,
    ) = refs[:18]
    grad_refs = refs[18 : 18 + count]
    out_sum, gate_sum = refs[18 + count :]
    chunk = pl.program_id(0)

    @pl.when(chunk == 0)
    def _():
        out_sum[...] = jnp.zeros_like(out_sum)
        gate_sum[...] = jnp.zeros_like(gate_sum)
        d_gain_two_ref[...] = jnp.zeros_like(d_gain_two_ref)

    sums = (sums_one_ref[...] + sums_two_ref[...]) + (sums_three_ref[...] + sums_four_ref[...])
    sums = (sums / DI).T
    scale = lax.rsqrt(sums[:, 0:1] + norm_eps)
    slope = scale * scale * sums[:, 1:2]
    gating = gating_ref[...]
    open_part = sigmoid(gating)
    gate = gating * open_part
    scanned = scanned_ref[...].astype(jnp.float32)
    unit = scanned * gate * scale
    d_gnorm = d_gnorm_ref[...]
    gain_two = gain_two_ref[...]
    gnorm = low(unit * gain_two)
    block_ref[...] = low(dot_nn(gnorm, out_ref[...]))
    out_sum[...] += dot_tn(gnorm, cot_ref[...])
    d_gain_two_ref[...] += jnp.sum(d_gnorm * unit, axis=0, keepdims=True)
    d_gated = scale * (d_gnorm * gain_two) - unit * slope
    d_gating = low(d_gated * scanned * (open_part * (1.0 + gating * (1.0 - open_part))))
    d_gating_ref[...] = d_gating
    d_scanned_ref[...] = low(d_gated * gate)
    gate_sum[...] += dot_tn(d_gating, unit_ref[...])

    @pl.when(chunk == pl.num_programs(0) - 1)
    def _():
        weights = gate_weight_ref[...].astype(jnp.float32)
        d_gain_one_ref[...] = jnp.sum(gate_sum[...] * weights, axis=0, keepdims=True)
        gate_sum[...] = gate_sum[...] * gain_one_ref[...]
        local_di = gate_sum.shape[0]
        if grad_refs[0].shape == gate_sum.shape:
            grad_refs[0][...] = low(gate_sum[...])
            grad_refs[1][...] = low(out_sum[...])
            return
        for number, grad_ref in enumerate(grad_refs):
            columns = grad_ref.shape[1]
            for step in range(D // columns // count):
                place = places_ref[number] + step * count
                start = pl.multiple_of(place * columns, columns)
                base = step * 2 * local_di
                grad_ref[base : base + local_di, :] = low(gate_sum[:, pl.ds(start, columns)])
                rows = pl.ds(pl.multiple_of(place * HEADDIM, HEADDIM), HEADDIM)
                for tile in range(D // columns):
                    first = base + local_di + tile * HEADDIM
                    grad_ref[first : first + HEADDIM, :] = low(
                        out_sum[rows, tile * columns : (tile + 1) * columns]
                    )


def backward_kernel(
    grad_count,
    places_ref,
    unit_ref,
    conv_in_ref,
    conv_pre_ref,
    dt_ref,
    y_ref,
    state_ref,
    d_scanned_ref,
    conv_ref,
    a_log_ref,
    dt_bias_ref,
    skip_ref,
    expand_ref,
    gain_one_ref,
    rest_weight_ref,
    d_gain_gate_ref,
    d_gain_two_ref,
    d_rest_ref,
    vec_ref,
    *refs,
):
    grad_refs = refs[:grad_count]
    ext, d_state, later_state, rest_sum = refs[grad_count : grad_count + 4]
    d_kernel_ref, d_conv_bias_ref, d_skip_ref, d_head_ref = refs[grad_count + 4 : grad_count + 8]
    rest_before, unit_before = refs[grad_count + 8 :]
    local_di = y_ref.shape[1]
    heads = local_di // HEADDIM
    chunk = pl.program_id(0)

    @pl.when(chunk == 0)
    def _():
        ext[BLOCK : BLOCK + 8, :] = jnp.zeros((8, ext.shape[1]), jnp.float32)
        d_state[...] = jnp.zeros_like(d_state)
        later_state[...] = jnp.zeros_like(later_state)
        rest_sum[...] = jnp.zeros_like(rest_sum)
        rest_before[...] = jnp.zeros_like(rest_before)
        unit_before[...] = jnp.zeros_like(unit_before)
        d_kernel_ref[...] = jnp.zeros_like(d_kernel_ref)
        d_conv_bias_ref[...] = jnp.zeros_like(d_conv_bias_ref)
        d_skip_ref[...] = jnp.zeros_like(d_skip_ref)
        d_head_ref[...] = jnp.zeros_like(d_head_ref)

    rest_sum[...] += dot_tn(rest_before[...], unit_before[...])
    expand = expand_ref[...]
    conv_pre = conv_pre_ref[...]
    open_part = sigmoid(conv_pre)
    conv_low = low(conv_pre * open_part)
    inner = conv_low[:, :local_di].astype(jnp.float32)
    b_rows = conv_low[:, local_di : local_di + STATE]
    c_rows = conv_low[:, local_di + STATE :]
    a_log = a_log_ref[...]
    shifted, _, log_decay, running, step_wide, running_wide = decay_sums(
        dt_ref[...], dt_bias_ref[...], a_log, expand
    )
    running_t = running.T
    b_t = low(b_rows.astype(jnp.float32).T)
    c_t = low(c_rows.astype(jnp.float32).T)
    scores = dot_nn(c_rows, b_t)
    scores_t = dot_nn(b_rows, c_t)
    mask = lower_mask()
    rows = lax.broadcasted_iota(jnp.int32, (BLOCK, BLOCK), 0)
    mask_t = rows <= lax.broadcasted_iota(jnp.int32, (BLOCK, BLOCK), 1)
    d_y_low = d_scanned_ref[...]
    d_y = d_y_low.astype(jnp.float32)
    stepped_low = low(step_wide * inner)
    stepped = stepped_low.astype(jnp.float32)
    last = running_wide[BLOCK - 1 : BLOCK, :]
    to_end = jnp.exp(last - running_wide)
    d_later = d_state[...]
    d_later_low = low(d_later)
    held = state_ref[...].reshape(d_state.shape)
    decayed_dy = low(jnp.exp(running_wide) * d_y)
    d_c = dot_nt(decayed_dy, low(held))
    d_b = dot_nt(low(to_end * stepped), d_later_low)
    d_stepped = to_end * dot_nn(b_rows, d_later_low)
    cross = jnp.sum(later_state[...] * d_later, axis=0, keepdims=True)
    d_state[...] = jnp.exp(last) * d_later + dot_nn(c_t, decayed_dy)
    later_state[...] = held
    first_half = lax.broadcasted_iota(jnp.int32, (BLOCK, 2 * HEADDIM), 1) < HEADDIM
    zero = jnp.zeros((), jnp.bfloat16)
    d_scores = jnp.zeros((BLOCK, BLOCK), jnp.float32)
    pieces = []
    for pair in range(heads // 2):
        span = slice(pair * 2 * HEADDIM, (pair + 1) * 2 * HEADDIM)
        total = d_stepped[:, span]
        for half in range(2):
            head = 2 * pair + half
            mine = jnp.where(first_half if half == 0 else ~first_half, d_y_low[:, span], zero)
            column = running[:, head : head + 1]
            row = running_t[head : head + 1, :]
            decay = jnp.exp(jnp.where(mask, column - row, -jnp.inf))
            decay_t = jnp.exp(jnp.where(mask_t, row - column, -jnp.inf))
            d_scores = d_scores + dot_nt(mine, stepped_low[:, span]) * decay
            total = total + dot_nn(low(decay_t * scores_t), mine)
        pieces.append(total)
    d_stepped = jnp.concatenate(pieces, 1)
    d_scores_low = low(d_scores)
    d_c = d_c + dot_nn(d_scores_low, b_rows)
    d_b = d_b + dot_nn(low(d_scores.T), c_rows)
    d_inner = step_wide * d_stepped + skip_ref[...] * d_y
    d_running = d_y * y_ref[...] - d_stepped * stepped
    d_running = sum_terms(lambda term: dot_nt(term, expand), d_running, 2)
    upper = low(jnp.where(mask_t, 1.0, 0.0))
    d_log = sum_terms(lambda term: dot_nn(upper, term), d_running, 3)
    d_log = d_log + sum_terms(lambda term: dot_nt(term, expand), cross, 3)
    d_step = sum_terms(lambda term: dot_nt(term, expand), d_stepped * inner, 2)
    d_step = d_step - jnp.exp(a_log) * d_log
    d_dt = d_step * sigmoid(shifted)
    d_head_ref[0:1, :] += jnp.sum(d_log * log_decay, axis=0, keepdims=True)
    d_head_ref[1:2, :] += jnp.sum(d_dt, axis=0, keepdims=True)
    d_skip_ref[...] += jnp.sum(d_y * inner, axis=0, keepdims=True)

    d_conv_out = jnp.concatenate([d_inner, d_b, d_c], 1)
    d_pre = d_conv_out * (open_part * (1.0 + conv_pre * (1.0 - open_part)))
    ext[0:BLOCK, :] = d_pre
    d_conv_bias_ref[...] += jnp.sum(d_pre, axis=0, keepdims=True)
    conv_in = conv_in_ref[...]
    d_conv_in = jnp.zeros_like(conv_in)
    for tap in range(WIDTH):
        moved = ext[WIDTH - 1 - tap : WIDTH - 1 - tap + BLOCK, :]
        d_conv_in = d_conv_in + conv_ref[tap : tap + 1, :] * moved
        d_kernel_ref[tap : tap + 1, :] += jnp.sum(moved * conv_in, axis=0, keepdims=True)
    ext[BLOCK : BLOCK + 8, :] = ext[0:8, :]
    d_rest = jnp.concatenate([low(d_conv_in), low(d_dt)], 1)
    d_rest_ref[...] = d_rest
    rest_before[...] = d_rest
    unit_before[...] = unit_ref[...]

    @pl.when(chunk == pl.num_programs(0) - 1)
    def _():
        rest_sum[...] += dot_tn(d_rest, unit_ref[...])
        weights = rest_weight_ref[...].astype(jnp.float32)
        d_gain_one = jnp.sum(rest_sum[...] * weights, axis=0, keepdims=True)
        pieces = [d_gain_one + d_gain_gate_ref[...]]
        pieces = pieces + [d_kernel_ref[tap : tap + 1, :] for tap in range(WIDTH)]
        pieces = pieces + [d_conv_bias_ref[...], d_gain_two_ref[...], d_skip_ref[...]]
        pieces = pieces + [d_head_ref[0:1, :], d_head_ref[1:2, :]]
        row = 0
        for piece in pieces:
            for first in range(0, piece.shape[1], 128):
                vec_ref[row : row + 1, :] = piece[:, first : first + 128]
                row = row + 1
        rest_sum[...] = rest_sum[...] * gain_one_ref[...]
        for number, grad_ref in enumerate(grad_refs):
            columns = grad_ref.shape[1]
            blocks = rest_sum.shape[1] // columns // grad_count
            rows = grad_ref.shape[0] // blocks
            for step in range(blocks):
                place = places_ref[number] + step * grad_count
                start = pl.multiple_of(place * columns, columns)
                grad_ref[step * rows : (step + 1) * rows, :] = low(
                    rest_sum[:rows, pl.ds(start, columns)]
                )


def sum_of(*refs):
    total = refs[0][...].astype(jnp.float32)
    for ref in refs[1:]:
        total = total + ref[...].astype(jnp.float32)
    return total


def pair_kernel(count, extra, places_ref, mine_ref, arrived_ref, *refs):
    for ref in refs[extra + count : len(refs) - count]:
        if extra:
            ref[ref.shape[0] - VEC_ROWS :, :] = low(refs[0][...])
    for number, ref in enumerate(refs[extra + count : len(refs) - count]):
        rows = ref.shape[0] - extra * VEC_ROWS
        here = pl.ds(pl.multiple_of(places_ref[number] * rows, rows), rows)
        ref[:rows, :] = low(sum_of(mine_ref.at[here, :], arrived_ref.at[here, :]))


def hold_kernel(places_ref, *refs):
    rows = refs[0].shape[0]
    for number, ref in enumerate(refs[:-1]):
        refs[-1][number * rows : (number + 1) * rows, :] = ref[...]


def final_kernel(count, places_ref, one_ref, two_ref, three_ref, four_ref, *refs):
    refs[count][...] = low(sum_of(one_ref, two_ref) + sum_of(three_ref, four_ref))


def normed_kernel(
    places_ref, d_gating_ref, d_rest_ref, gate_weight_ref, rest_weight_ref, mine_ref, send_ref
):
    chunk = pl.program_id(0)
    d_normed = dot_nn(d_gating_ref[...], gate_weight_ref[...])
    d_normed = low(d_normed + dot_nn(d_rest_ref[...], rest_weight_ref[...]))
    here = chunk % 2 == places_ref[0]
    rows = pl.ds(pl.multiple_of(chunk // 2 * BLOCK, BLOCK), BLOCK)

    @pl.when(here)
    def _():
        mine_ref[rows, :] = d_normed

    @pl.when(jnp.logical_not(here))
    def _():
        send_ref[rows, :] = d_normed


def prepare_kernel(places_ref, in_ref, out_ref, rest_ref, gate_out_ref):
    index = places_ref[0]
    local_di = gate_out_ref.shape[0] // 2
    groups = DI // local_di
    for head in range(HEADS // groups):
        rows = slice(head * HEADDIM, (head + 1) * HEADDIM)
        for base, result_ref in ((0, gate_out_ref), (DI, rest_ref)):
            start = pl.multiple_of(base + (groups * head + index) * HEADDIM, HEADDIM)
            result_ref[rows, :] = low(in_ref[pl.ds(start, HEADDIM), :])
    channels = local_di + 2 * STATE
    rest_ref[local_di:channels, :] = low(in_ref[2 * DI : 2 * DI + 2 * STATE, :])
    rows = rest_ref.shape[0] - channels
    target = lax.broadcasted_iota(jnp.int32, (rows, HEADS), 0)
    source = lax.broadcasted_iota(jnp.int32, (rows, HEADS), 1)
    chosen = (source == groups * target + index) & (target < HEADS // groups)
    steps = low(in_ref[DI + CONVCH :, :])
    rest_ref[channels:, :] = low(dot_nn(jnp.where(chosen, 1.0, 0.0).astype(jnp.bfloat16), steps))
    mine = pl.ds(pl.multiple_of(index * HEADDIM, HEADDIM), HEADDIM)
    columns = gate_out_ref.shape[1]
    for tile in range(D // columns):
        first = local_di + tile * HEADDIM
        gate_out_ref[first : first + HEADDIM, :] = low(
            out_ref[mine, tile * columns : (tile + 1) * columns]
        )


def adamw_store(old_refs, new_refs, rows, columns, grad):
    results = adamw_step(*[ref[rows, columns] for ref in old_refs], grad, matrix_rate, matrix_decay)
    for ref, result in zip(new_refs, results):
        ref[rows, columns] = result


def update_heads(old_refs, new_refs, source, part):
    groups = source.shape[0]
    heads = old_refs[0].shape[0] // HEADDIM // groups
    for head in range(heads):
        start = pl.multiple_of((part * heads + head) * HEADDIM, HEADDIM)
        for group in range(groups):
            first = (head * groups + group) * HEADDIM
            grad = source[group, pl.ds(start, HEADDIM), :].astype(jnp.float32)
            adamw_store(old_refs, new_refs, slice(first, first + HEADDIM), slice(None), grad)


def update_gate_kernel(groups, places_ref, *refs):
    blocks, in_refs, out_refs = refs[:groups], refs[groups : groups + 3], refs[groups + 3 : groups + 6]
    in_new_refs, out_new_refs = refs[groups + 6 : groups + 9], refs[groups + 9 : groups + 12]
    every_ref, gate_out = refs[groups + 12 :]
    chunk = pl.program_id(0)

    @pl.when(chunk == 0)
    def _():
        for number in range(groups):
            gate_out[places_ref[number]] = blocks[number][...]

    local_di = (gate_out.shape[1] - VEC_ROWS) // 2
    every_ref[...] = gate_out[:, 2 * local_di :, :]
    update_heads(in_refs, in_new_refs, gate_out, chunk)
    columns = gate_out.shape[2]
    for tile in range(D // columns):
        first = local_di + tile * HEADDIM
        grad = gate_out[chunk, first : first + HEADDIM, :].astype(jnp.float32)
        span = slice(tile * columns, (tile + 1) * columns)
        adamw_store(out_refs, out_new_refs, slice(None), span, grad)


def update_rest_kernel(groups, places_ref, *refs):
    blocks, in_refs = refs[:groups], refs[groups : groups + 3]
    in_new_refs, (rest,) = refs[groups + 6 : groups + 9], refs[groups + 9 :]
    chunk = pl.program_id(0)

    @pl.when(chunk == 0)
    def _():
        for number in range(groups):
            rest[places_ref[number]] = blocks[number][...]

    @pl.when(chunk < pl.num_programs(0) - 1)
    def _():
        update_heads(in_refs, in_new_refs, rest, chunk)

    @pl.when(chunk == pl.num_programs(0) - 1)
    def _():
        local_di = DI // groups
        channels = local_di + 2 * STATE
        both = rest[0, local_di:channels, :].astype(jnp.float32)
        rows = rest.shape[1] - channels
        steps = jnp.zeros((HEADS, rest.shape[2]), jnp.float32)
        target = lax.broadcasted_iota(jnp.int32, (HEADS, rows), 0)
        source = lax.broadcasted_iota(jnp.int32, (HEADS, rows), 1)
        for group in range(groups):
            if group > 0:
                both = both + rest[group, local_di:channels, :].astype(jnp.float32)
            chosen = jnp.where(target == groups * source + group, 1.0, 0.0).astype(jnp.bfloat16)
            steps = steps + dot_nn(chosen, rest[group, channels:, :])
        after_both = slice(2 * STATE, 2 * STATE + HEADS)
        adamw_store(in_refs, in_new_refs, slice(0, 2 * STATE), slice(None), both)
        adamw_store(in_refs, in_new_refs, after_both, slice(None), steps)


def kernel_params():
    return pltpu.CompilerParams(
        dimension_semantics=("arbitrary",), vmem_limit_bytes=56 * 1024 * 1024
    )


def cost(flops, moved, transcendentals):
    return pl.CostEstimate(flops=flops, bytes_accessed=moved, transcendentals=transcendentals)


def after(kernel, inputs, arrived):
    def run(*refs):
        kernel(*refs[:inputs], *refs[inputs + arrived :])

    return run


def corner(array):
    return pl.BlockSpec((min(16, array.shape[0]), 128), lambda *_: (0, 0))


def fixed(shape):
    return pl.BlockSpec(shape, lambda *_: (0,) * len(shape))


def rows_of(extent, first=0):
    return pl.BlockSpec((BLOCK, extent), lambda q, *_: (q + first, 0))


def struct(shape, dtype=jnp.float32):
    return jax.ShapeDtypeStruct(shape, dtype)


def call(
    kernel, places, inputs, in_specs, outputs, out_specs, scratch, grid, arrived, price, name, same=()
):
    return pl.pallas_call(
        after(kernel, 1 + len(inputs), len(arrived)),
        grid_spec=pltpu.PrefetchScalarGridSpec(
            num_scalar_prefetch=1,
            grid=(grid,),
            in_specs=list(in_specs) + [corner(array) for array in arrived],
            out_specs=out_specs,
            scratch_shapes=scratch,
        ),
        out_shape=outputs,
        input_output_aliases=dict(same),
        compiler_params=kernel_params(),
        cost_estimate=cost(*price),
        name=name,
    )(jnp.stack(places).astype(jnp.int32), *inputs, *arrived)


def run_prepare(index, in_t, out_weight):
    columns = in_t.shape[1]
    local_di = DI // 4
    shapes = [
        (local_di + 2 * STATE + 16, columns),
        (2 * local_di, columns),
    ]
    inputs = [in_t, out_weight]
    return call(
        prepare_kernel,
        [index],
        inputs,
        [fixed(array.shape) for array in inputs],
        [struct(shape, jnp.bfloat16) for shape in shapes],
        [fixed(shape) for shape in shapes],
        [],
        1,
        [],
        (100_000_000, 4_000_000, 0),
        "prepare",
    )


def run_forward(hidden, rest, gain_one, conv, heads_vectors, expand):
    places, blocks = rest
    length = hidden.shape[0]
    chunks = length // BLOCK
    lanes, local_di = expand.shape
    channels = local_di + 2 * STATE
    vectors = [gain_one, *conv, *heads_vectors, expand]
    return call(
        lambda *refs: forward_kernel(len(blocks), *refs),
        places,
        [*blocks, hidden, *vectors],
        [fixed(array.shape) for array in blocks]
        + [rows_of(D)]
        + [fixed(array.shape) for array in vectors],
        [
            struct((channels + lanes, D), jnp.bfloat16),
            struct((length, D), jnp.bfloat16),
            struct((length, D), jnp.bfloat16),
            struct((length, channels)),
            struct((length, channels)),
            struct((length, lanes)),
            struct((length, local_di)),
            struct((length, local_di), jnp.bfloat16),
            struct((chunks, STATE, local_di)),
        ],
        [
            fixed((channels + lanes, D)),
            rows_of(D),
            rows_of(D),
            rows_of(channels),
            rows_of(channels),
            rows_of(lanes),
            rows_of(local_di),
            rows_of(local_di),
            pl.BlockSpec((1, STATE, local_di), lambda q, *_: (q, 0, 0)),
        ],
        [
            pltpu.VMEM((8 + BLOCK, channels), jnp.float32),
            pltpu.VMEM((STATE, local_di), jnp.float32),
        ],
        chunks,
        [],
        (6_000_000_000, 30_000_000, 8_000_000),
        "forward",
    )


def run_gate(gate_out, cot, normed, scanned, gain_two):
    places, blocks = gate_out
    length, local_di = scanned.shape
    return call(
        lambda *refs: gate_kernel(len(blocks), *refs),
        places,
        [*blocks, cot, normed, scanned, gain_two],
        [fixed(array.shape) for array in blocks]
        + [rows_of(D), rows_of(D), rows_of(local_di), fixed((1, local_di))],
        [
            struct((local_di, D), jnp.bfloat16),
            struct((local_di, D), jnp.bfloat16),
            struct((length, local_di)),
            struct((length, local_di)),
            struct((8, length)),
        ],
        [
            fixed((local_di, D)),
            fixed((local_di, D)),
            rows_of(local_di),
            rows_of(local_di),
            pl.BlockSpec((8, BLOCK), lambda q, *_: (0, q)),
        ],
        [],
        length // BLOCK,
        [],
        (2_500_000_000, 12_000_000, 1_000_000),
        "gate",
    )


def run_middle(
    places, scanned, gating, d_gnorm, cot, unit, sums, out, gain_two, gain_one, gate_weight
):
    length, local_di = scanned.shape
    shapes = [(local_di, D)] * 2
    if len(places) > 1:
        shapes = [(2 * local_di * D // 256, 128)] * 2
    return call(
        lambda *refs: middle_kernel(2, *refs),
        places,
        [scanned, gating, d_gnorm, cot, unit, *sums, out, gain_two, gain_one, gate_weight],
        [
            rows_of(local_di),
            rows_of(local_di),
            rows_of(local_di),
            rows_of(D),
            rows_of(D),
        ]
        + [pl.BlockSpec((8, BLOCK), lambda q, *_: (0, q))] * 4
        + [fixed((local_di, D)), fixed((1, local_di)), fixed((1, D)), fixed((local_di, D))],
        [
            struct((length, D), jnp.bfloat16),
            struct((length, local_di), jnp.bfloat16),
            struct((length, local_di), jnp.bfloat16),
            struct((1, local_di)),
            struct((1, D)),
        ]
        + [struct(shape, jnp.bfloat16) for shape in shapes],
        [
            rows_of(D),
            rows_of(local_di),
            rows_of(local_di),
            fixed((1, local_di)),
            fixed((1, D)),
        ]
        + [fixed(shape) for shape in shapes],
        [pltpu.VMEM((local_di, D), jnp.float32), pltpu.VMEM((local_di, D), jnp.float32)],
        length // BLOCK,
        [],
        (4_000_000_000, 15_000_000, 500_000),
        "middle",
    )


def run_backward(
    places,
    unit,
    conv_in,
    conv_pre,
    dt_raw,
    y,
    states,
    d_scanned,
    kernel,
    heads_vectors,
    expand,
    gain_one,
    rest_weight,
    d_gain_gate,
    d_gain_two,
):
    length, local_di = y.shape
    chunks = length // BLOCK
    channels = conv_in.shape[1]
    lanes = expand.shape[0]
    grad = (channels + 16, D) if len(places) == 1 else ((channels + 16) * D // 256, 128)

    def back(extent):
        return pl.BlockSpec((BLOCK, extent), lambda q, *_: (chunks - 1 - q, 0))

    return call(
        lambda *refs: backward_kernel(len(places), *refs),
        places,
        [
            *[unit, conv_in, conv_pre, dt_raw, y, states, d_scanned, kernel],
            *[*heads_vectors, expand, gain_one, rest_weight, d_gain_gate, d_gain_two],
        ],
        [
            back(D),
            back(channels),
            back(channels),
            back(lanes),
            back(local_di),
            pl.BlockSpec((1, STATE, local_di), lambda q, *_: (chunks - 1 - q, 0, 0)),
            back(local_di),
            fixed((WIDTH, channels)),
            fixed((1, lanes)),
            fixed((1, lanes)),
            fixed((1, local_di)),
            fixed((lanes, local_di)),
            fixed((1, D)),
            fixed((channels + lanes, D)),
            fixed((1, D)),
            fixed((1, local_di)),
        ],
        [
            struct((length, channels + lanes), jnp.bfloat16),
            struct((VEC_ROWS, 128)),
        ]
        + [struct(grad, jnp.bfloat16)] * len(places),
        [
            back(channels + lanes),
            fixed((VEC_ROWS, 128)),
        ]
        + [fixed(grad)] * len(places),
        [
            pltpu.VMEM((BLOCK + 8, channels), jnp.float32),
            pltpu.VMEM((STATE, local_di), jnp.float32),
            pltpu.VMEM((STATE, local_di), jnp.float32),
            pltpu.VMEM((channels + lanes, D), jnp.float32),
            pltpu.VMEM((WIDTH, channels), jnp.float32),
            pltpu.VMEM((1, channels), jnp.float32),
            pltpu.VMEM((1, local_di), jnp.float32),
            pltpu.VMEM((2, lanes), jnp.float32),
            pltpu.VMEM((BLOCK, channels + lanes), jnp.bfloat16),
            pltpu.VMEM((BLOCK, D), jnp.bfloat16),
        ],
        chunks,
        [],
        (14_000_000_000, 40_000_000, 10_000_000),
        "backward",
    )


def run_normed(parity, d_gating, d_rest, gate_weight, rest_weight, arrived):
    length, local_di = d_gating.shape
    rest = d_rest.shape[1]
    return call(
        normed_kernel,
        [parity],
        [d_gating, d_rest, gate_weight, rest_weight],
        [rows_of(local_di), rows_of(rest), fixed((local_di, D)), fixed((rest, D))],
        [struct((length // 2, D), jnp.bfloat16)] * 2,
        [fixed((length // 2, D))] * 2,
        [],
        length // BLOCK,
        arrived,
        (3_000_000_000, 9_000_000, 1000),
        "normed",
    )


def run_pair(places, mine, arrived, extra, through, there):
    rows = mine.shape[0] // len(places) + len(extra) * VEC_ROWS
    block = (rows, mine.shape[1])
    inputs = [mine, arrived, *extra]
    untouched = [pl.BlockSpec(memory_space=pl.ANY)] * len(through)
    return call(
        lambda *refs: pair_kernel(len(through), len(extra), *refs),
        places,
        [*inputs, *through],
        [fixed(array.shape) for array in inputs] + untouched,
        [struct(block, jnp.bfloat16)] * len(places)
        + [struct(array.shape, array.dtype) for array in through],
        [fixed(block)] * len(places) + untouched,
        [],
        1,
        there,
        (2_000_000, 3_000_000, 0),
        "pair",
        [(1 + len(inputs) + number, len(places) + number) for number in range(len(through))],
    )


def run_hold(places, blocks, there):
    rows, columns = blocks[0].shape
    shape = (rows * len(blocks), columns)
    return call(
        hold_kernel,
        places,
        blocks,
        [fixed(block.shape) for block in blocks],
        struct(shape, blocks[0].dtype),
        fixed(shape),
        [],
        1,
        there,
        (0, 2_000_000, 0),
        "hold",
    )


def run_final(terms, through, there):
    untouched = [pl.BlockSpec(memory_space=pl.ANY)] * len(through)
    return call(
        lambda *refs: final_kernel(len(through), *refs),
        [jnp.int32(0)],
        [*terms, *through],
        [fixed(array.shape) for array in terms] + untouched,
        [struct(terms[0].shape, jnp.bfloat16)]
        + [struct(array.shape, array.dtype) for array in through],
        [fixed(terms[0].shape)] + untouched,
        [],
        1,
        there,
        (500_000, 1_000_000, 0),
        "final",
        [(1 + len(terms) + number, 1 + number) for number in range(len(through))],
    )


def run_update_gate(places, blocks, in_arrays, out_arrays, there):
    groups = len(places)
    rows_out = out_arrays[0].shape[0] // groups
    arrays = [*in_arrays, *out_arrays]
    in_spec = pl.BlockSpec((DI // groups, in_arrays[0].shape[1]), lambda q, *_: (q, 0))
    out_spec = pl.BlockSpec((rows_out, D), lambda q, *_: (q, 0))
    specs = [in_spec] * 3 + [out_spec] * 3
    return call(
        lambda *refs: update_gate_kernel(groups, *refs),
        places,
        [*blocks, *arrays],
        [fixed(array.shape) for array in blocks] + specs,
        [struct(array.shape) for array in arrays]
        + [struct((groups, VEC_ROWS, 128), jnp.bfloat16)],
        specs + [fixed((groups, VEC_ROWS, 128))],
        [pltpu.VMEM((groups,) + blocks[0].shape, jnp.bfloat16)],
        groups,
        there,
        (10_000_000, 13_000_000, 500_000),
        "update_gate",
    )


def run_update_rest(places, blocks, in_arrays, so_far):
    groups = len(places)
    spec = pl.BlockSpec((DI // groups, in_arrays[0].shape[1]), lambda q, *_: (q + groups, 0))
    return call(
        lambda *refs: update_rest_kernel(groups, *refs),
        places,
        [*blocks, *in_arrays, *so_far],
        [fixed(array.shape) for array in blocks]
        + [spec] * 3
        + [pl.BlockSpec(memory_space=pl.ANY)] * 3,
        [struct(array.shape) for array in in_arrays],
        [spec] * 3,
        [pltpu.VMEM((groups,) + blocks[0].shape, jnp.bfloat16)],
        groups + 1,
        [],
        (10_000_000, 8_000_000, 500_000),
        "update_rest",
        [(1 + groups + 3 + number, number) for number in range(3)],
    )


def adamw_step(weight, first, second, grad, rate, decay):
    first_new = beta_one * first + (1.0 - beta_one) * grad
    second_new = beta_two * second + (1.0 - beta_two) * grad * grad
    fix_one = 1.0 - beta_one**STEP
    fix_two = 1.0 - beta_two**STEP
    normalized = first_new / fix_one / (jnp.sqrt(second_new / fix_two) + adam_eps)
    return (first_new, second_new, weight - rate * (normalized + decay * weight))


def pick_heads(values, axis, width, index, groups):
    shape = values.shape
    split = shape[:axis] + (HEADS // groups, groups, width) + shape[axis + 1 :]
    taken = lax.dynamic_index_in_dim(values.reshape(split), index, axis + 1, keepdims=False)
    return taken.reshape(shape[:axis] + (HEADS // groups * width,) + shape[axis + 1 :])


def merge_heads(stacked, axis, width):
    groups = stacked.shape[0]
    shape = stacked.shape[1:]
    split = (groups,) + shape[:axis] + (HEADS // groups, width) + shape[axis + 1 :]
    moved = jnp.moveaxis(stacked.reshape(split), 0, axis + 1)
    return moved.reshape(shape[:axis] + (HEADS * width,) + shape[axis + 1 :])


def swap(values, axis, mask):
    route = [(i, i ^ mask) for i in range(lax.axis_size(axis))]
    return lax.ppermute(values, axis, route)


def seq_blocks(rows, far=None):
    index = lax.axis_index("seq")
    far = swap(rows, "seq", 2) if far is None else far
    blocks = [rows, swap(rows, "seq", 1), far, swap(far, "seq", 1)]
    return [index ^ mask for mask in range(4)], blocks


def ring_step(held):
    count = lax.axis_size("wshard")
    return lax.ppermute(held, "wshard", [(i, (i + 2) % count) for i in range(count)])


def ring_blocks(rows):
    count = lax.axis_size("wshard")
    index = lax.axis_index("wshard")
    places, blocks = [], []
    for step in range(count // 2):
        source = (index + count - 2 * step) % count
        places = places + [source, source ^ 1]
        blocks = blocks + [rows, swap(rows, "wshard", 1)]
        if step < count // 2 - 1:
            rows = ring_step(rows)
    return places, blocks


def ring_late(hold_places, rows, arrived):
    count = lax.axis_size("wshard")
    index = lax.axis_index("wshard")
    places = [(index + count - 2 * step) % count for step in range(count // 2)]
    blocks = [rows]
    for _ in range(count // 2 - 1):
        blocks = blocks + [ring_step(blocks[-1])]
    swapped = swap(run_hold(hold_places, blocks, arrived), "wshard", 1)
    return places + [place ^ 1 for place in places], blocks + [swapped]


def take_block(values, index, rows):
    return lax.dynamic_slice_in_dim(values, index * rows, rows, 0)


def gather_out(out_low, seq_index, groups):
    rows = out_low.shape[0]
    if rows % (groups * HEADDIM) == 0:
        mine = pick_rows(out_low, seq_index, groups)
        return lax.all_gather(mine, "wshard", axis=0, tiled=True)
    whole = lax.all_gather(out_low, "wshard", axis=0, tiled=True)
    return pick_heads(whole, 0, HEADDIM, seq_index, groups)


def pick_rows(values, seq_index, groups):
    rows = values.shape[0]
    split = values.reshape(rows // (groups * HEADDIM), groups, HEADDIM, values.shape[1])
    return lax.dynamic_index_in_dim(split, seq_index, 1, keepdims=False).reshape(
        rows // groups, values.shape[1]
    )


def sum_out_grad(grad, rows, seq_index, groups):
    grad = grad.astype(jnp.bfloat16)
    if rows % (groups * HEADDIM) == 0:
        mine = lax.psum_scatter(grad, "wshard", scatter_dimension=0, tiled=True)
        every = lax.all_gather(mine, "seq", axis=0, tiled=False)
        split = every.reshape(groups, rows // (groups * HEADDIM), HEADDIM, grad.shape[1])
        return jnp.moveaxis(split, 0, 1).reshape(rows, grad.shape[1]).astype(jnp.float32)
    blocks = grad.reshape(HEADS // groups, 1, HEADDIM, grad.shape[1])
    here = (jnp.arange(groups) == seq_index)[None, :, None, None]
    spread = jnp.where(here, blocks, jnp.zeros((), jnp.bfloat16)).reshape(DI, grad.shape[1])
    mine = lax.psum_scatter(spread, "wshard", scatter_dimension=0, tiled=True)
    return lax.psum(mine.astype(jnp.float32), "seq")


def shards(
    block_in,
    cotangent,
    in_weight,
    in_first,
    in_second,
    out_weight,
    out_first,
    out_second,
    vec_weight,
    vec_first,
    vec_second,
):
    rows_here = block_in.shape[1]
    groups = lax.axis_size("seq")
    seq_index = lax.axis_index("seq")
    local_heads = HEADS // groups
    local_di = DI // groups
    hidden_rows = block_in.reshape(rows_here, D)
    cot_rows = cotangent.reshape(rows_here, D)
    gain_one, gain_two, kernel, conv_bias, a_log, dt_bias, d_skip = split_vector(vec_weight)

    def heads_of(values, axis, width):
        return pick_heads(values, axis, width, seq_index, groups)

    lanes = 128
    channels = local_di + 2 * STATE
    shard_index = lax.axis_index("wshard")
    rings = lax.axis_size("wshard") == 8
    if rings:
        y, z = shard_index % 2, shard_index // 2
        rest_mine, gate_out_mine = run_prepare(seq_index, in_weight.T, out_weight)
        rest = ring_blocks(rest_mine)
        gate_out_late = gate_out_mine
        gate_places = [z ^ mask for mask in range(4)]
        out_places = [y, 1 - y]
    else:
        in_low = low(in_weight)
        steps_mine = heads_of(in_low[:, DI + CONVCH :], 1, 1)
        rest_mine = jnp.concatenate(
            [
                heads_of(in_low[:, DI : 2 * DI], 1, HEADDIM),
                in_low[:, 2 * DI : 2 * DI + 2 * STATE],
                jnp.pad(steps_mine, ((0, 0), (0, 16 - local_heads))),
            ],
            1,
        )
        gate_mine = heads_of(in_low[:, :DI], 1, HEADDIM)
        origin = [jnp.int32(0)]
        rest = (origin, [lax.all_gather(rest_mine, "wshard", axis=0, tiled=True).T])
        gate_mine = lax.all_gather(gate_mine, "wshard", axis=0, tiled=True).T
        gate_out = (origin, [gate_mine, gather_out(low(out_weight), seq_index, groups)])
        out_places = origin
    hidden_low = lax.all_gather(hidden_rows, "seq", axis=0, tiled=True)
    cot_low = lax.all_gather(cot_rows, "seq", axis=0, tiled=True)
    my_gain_two = heads_of(gain_two, 0, HEADDIM)[None, :]
    my_kernel = jnp.concatenate([heads_of(kernel[:, :DI], 1, HEADDIM), kernel[:, DI:]], 1)
    my_bias = jnp.concatenate([heads_of(conv_bias[:DI], 0, HEADDIM), conv_bias[DI:]], 0)

    def on_lanes(values):
        return jnp.pad(values, (0, lanes - local_heads))[None, :]

    heads_vectors = (
        on_lanes(heads_of(a_log, 0, 1)),
        on_lanes(heads_of(dt_bias, 0, 1)),
        jnp.repeat(heads_of(d_skip, 0, 1), HEADDIM)[None, :],
    )
    expand = (
        jnp.arange(lanes)[:, None] == jnp.arange(local_di)[None, :] // HEADDIM
    ).astype(jnp.bfloat16)
    if rings:
        gate_out = ring_late(
            rest[0],
            gate_out_late,
            rest[1][1::2] + [my_kernel, my_bias[None, :], *heads_vectors, expand],
        )
    (
        rest_weight,
        unit_low,
        normed_low,
        conv_in,
        conv_pre,
        dt_raw,
        y_part,
        scanned,
        states,
    ) = run_forward(
        hidden_low, rest, gain_one[None, :], (my_kernel, my_bias[None, :]), heads_vectors, expand
    )
    gate_weight, out_low, gating, d_gnorm, sums = run_gate(
        gate_out, cot_low, normed_low, scanned, my_gain_two
    )
    middle = run_middle(
        out_places,
        scanned,
        gating,
        d_gnorm,
        cot_low,
        unit_low,
        [sums] + [swap(sums, "seq", mask) for mask in range(1, 4)],
        out_low,
        my_gain_two,
        gain_one[None, :],
        gate_weight,
    )
    block_part, d_gating, d_scanned, d_gain_two, d_gain_gate, *gate_out_grads = middle
    block_rows = lax.psum_scatter(block_part, "seq", scatter_dimension=0, tiled=True)
    if rings:
        gate_out_arrived = swap(gate_out_grads[1], "wshard", 1)
    d_rest, vec_rows, *rest_grads = run_backward(
        out_places,
        unit_low,
        conv_in,
        conv_pre,
        dt_raw,
        y_part,
        states,
        d_scanned,
        my_kernel,
        heads_vectors,
        expand,
        gain_one[None, :],
        rest_weight,
        d_gain_gate,
        d_gain_two,
    )
    near, far = seq_index % 2, seq_index // 2
    if rings:
        *gate_out_sums, rest_send = run_pair(
            gate_places,
            gate_out_grads[0],
            gate_out_arrived,
            [vec_rows],
            [rest_grads[1]],
            [],
        )
        rest_arrived = swap(rest_send, "wshard", 1)
        gate_out_pieces = [
            swap(gate_out_sums[mask], "wshard", 2 * mask) for mask in range(1, 4)
        ]
        normed_mine, normed_send = run_normed(
            near, d_gating, d_rest, gate_weight, rest_weight, [gate_out_sums[0], block_rows]
        )
        gate_out_part, normed_send = run_final(
            [gate_out_sums[0]] + gate_out_pieces, [normed_send], []
        )
        gate_out_near = swap(gate_out_part, "seq", 1)
        rest_sums = run_pair(
            gate_places, rest_grads[0], rest_arrived, [], [], [gate_out_near]
        )
        rest_pieces = [swap(rest_sums[mask], "wshard", 2 * mask) for mask in range(1, 4)]
        gate_out_far = swap(gate_out_part, "seq", 2)
    else:
        every = lax.all_gather(lax.psum(vec_rows, "wshard"), "seq", axis=0, tiled=False)
        normed_mine, normed_send = run_normed(
            near, d_gating, d_rest, gate_weight, rest_weight, []
        )
    normed_arrived = swap(normed_send, "seq", 1)
    normed_sum = normed_mine.astype(jnp.float32) + normed_arrived.astype(jnp.float32)
    normed_far = swap(low(take_block(normed_sum, 1 - far, rows_here)), "seq", 2)
    if rings:
        spots = [seq_index ^ mask for mask in range(4)]
        gate_out_blocks = [gate_out_part, gate_out_near, gate_out_far]
        gate_out_blocks = gate_out_blocks + [swap(gate_out_far, "seq", 1)]
        in_arrays = (in_weight.T, in_first.T, in_second.T)
        updated = run_update_gate(
            spots,
            gate_out_blocks,
            in_arrays,
            (out_weight, out_first, out_second),
            [rest_sums[0]],
        )
        out_first_new, out_second_new, out_weight_new, every = updated[3:]
        rest_part, every = run_final([rest_sums[0]] + rest_pieces, [every], [])
        every_there = swap(every, "wshard", 1)
        every = every.astype(jnp.float32) + every_there.astype(jnp.float32)
    block_out = hidden_rows.astype(jnp.float32) + block_rows.astype(jnp.float32)
    d_normed = take_block(normed_sum, far, rows_here) + normed_far.astype(jnp.float32)
    own_hidden = hidden_rows.astype(jnp.float32)
    own_scale = lax.rsqrt(jnp.mean(own_hidden * own_hidden, axis=-1, keepdims=True) + norm_eps)
    own_unit = own_hidden * own_scale
    d_own = d_normed * gain_one[None, :]
    d_hidden = own_scale * (
        d_own - own_unit * jnp.mean(d_own * own_unit, axis=-1, keepdims=True)
    )
    block_grad = cot_rows.astype(jnp.float32) + d_hidden
    if rings:
        spots, rest_blocks = seq_blocks(rest_part)
        updated = run_update_rest(spots, rest_blocks, in_arrays, updated[:3])
        in_first_new, in_second_new, in_weight_new = [array.T for array in updated]
    else:
        rest_part = lax.psum_scatter(rest_grads[0].T, "wshard", scatter_dimension=0, tiled=True)
        gate_part = lax.psum_scatter(gate_out_grads[0].T, "wshard", scatter_dimension=0, tiled=True)
        gate_every = lax.all_gather(gate_part, "seq", axis=0, tiled=False).astype(jnp.float32)
        rest_every = lax.all_gather(rest_part, "seq", axis=0, tiled=False).astype(jnp.float32)
        out_total = sum_out_grad(gate_out_grads[1], out_weight.shape[0], seq_index, groups)
        in_total = jnp.concatenate(
            [
                merge_heads(gate_every, 1, HEADDIM),
                merge_heads(rest_every[:, :, :local_di], 1, HEADDIM),
                jnp.sum(rest_every[:, :, local_di:channels], axis=0),
                merge_heads(rest_every[:, :, channels : channels + local_heads], 1, 1),
            ],
            1,
        )
        in_first_new, in_second_new, in_weight_new = adamw_step(
            in_weight, in_first, in_second, in_total, matrix_rate, matrix_decay
        )
        out_first_new, out_second_new, out_weight_new = adamw_step(
            out_weight, out_first, out_second, out_total, matrix_rate, matrix_decay
        )
    every = every.reshape(groups, VEC_ROWS * 128)
    cuts = [0, D]
    for extent in (WIDTH * channels, channels, local_di, local_di, lanes, lanes):
        cuts.append(cuts[-1] + extent)
    parts = [every[:, cuts[number] : cuts[number + 1]] for number in range(7)]
    kernel_every = parts[1].reshape(groups, WIDTH, channels)
    kernel_total = jnp.concatenate(
        [
            merge_heads(kernel_every[:, :, :local_di], 1, HEADDIM),
            jnp.sum(kernel_every[:, :, local_di:], axis=0),
        ],
        1,
    )
    skip_every = jnp.sum(parts[4].reshape(groups, local_heads, HEADDIM), axis=2)
    vec_total = jnp.concatenate(
        [
            jnp.sum(parts[0], axis=0),
            merge_heads(parts[3], 0, HEADDIM),
            kernel_total.reshape(-1),
            merge_heads(parts[2][:, :local_di], 0, HEADDIM),
            jnp.sum(parts[2][:, local_di:], axis=0),
            merge_heads(parts[5][:, :local_heads], 0, 1),
            merge_heads(parts[6][:, :local_heads], 0, 1),
            merge_heads(skip_every, 0, 1),
        ]
    )
    vec_first_new, vec_second_new, vec_weight_new = adamw_step(
        vec_weight, vec_first, vec_second, vec_total, vector_rate, 0.0
    )
    return (
        block_out.reshape(1, rows_here, D),
        block_grad.reshape(1, rows_here, D),
        in_first_new,
        in_second_new,
        in_weight_new,
        out_first_new,
        out_second_new,
        out_weight_new,
        vec_first_new,
        vec_second_new,
        vec_weight_new,
    )


def solution(mesh):
    return jax.shard_map(
        shards,
        mesh=mesh,
        in_specs=(
            P("wshard", "seq", None),
            P("wshard", "seq", None),
            P("wshard", None),
            P("wshard", None),
            P("wshard", None),
            P("wshard", None),
            P("wshard", None),
            P("wshard", None),
            P(),
            P(),
            P(),
        ),
        out_specs=(
            P("wshard", "seq", None),
            P("wshard", "seq", None),
            P("wshard", None),
            P("wshard", None),
            P("wshard", None),
            P("wshard", None),
            P("wshard", None),
            P("wshard", None),
            P(),
            P(),
            P(),
        ),
        check_vma=False,
    )
```
